256 devices in a mesh: depth: 16 (over z, y_lo), pos: 16 (over x, y_hi, core).
Axes of the slice: x: 4, y: 4 (y_hi: 2, y_lo: 2; y = y_hi * 2 + y_lo), z: 8, core: 2. Of those that a mesh axis runs over, the one named last changes fastest.
Arguments:
- transmission: bfloat16 [32, 2, 512, 512], P('depth', None, 'pos'), may hold values from -1.04 to 1.04, as said below
- probe: bfloat16 [2, 256, 256], replicated, may hold values from -4 to 4
- offsets: int32 [32, 2], P('pos'), may hold values from 0 to 256
- measured: float32 [32, 256, 256], P('pos'), may hold values from 0.25 to 2
Outputs:
- slice_grad: float32 [32, 2, 512, 512], P('depth', None, 'pos')
The draws below stay inside these ranges and needn't reach their ends.
Inputs may be any that keep to these rules, and one draw needn't show every extreme that they name: `transmission`: each pair of components is a complex number of modulus between 0.96 and 1.04. `offsets`: each position's 256 x 256 window lies inside the 512 x 512 field.
All inputs are finite; a program needn't handle non-finite values.
Results may differ from the reference program's by a relative error of at most 0.035.
Values may be sent and summed in bfloat16 or wider, within the bound.
A program may use at most 64 MiB of HBM per device.

```python
import math
import jax
import jax.numpy as jnp
from jax import lax

PROBE = 256
WIN = 512
SLICES = 32
POSITIONS = 32


def draw_transmission(key, part):
    key = jax.random.fold_in(key, 11)
    amp_key, phase_key = jax.random.split(key)
    shape = (SLICES, WIN, WIN)
    amplitude = jax.random.uniform(amp_key, shape, jnp.float32, 0.96, 1.04)
    phase_value = jax.random.uniform(phase_key, shape, jnp.float32, -math.pi, math.pi)
    result = jnp.stack([amplitude * jnp.cos(phase_value), amplitude * jnp.sin(phase_value)], axis=1)
    return result.astype(jnp.bfloat16)


def plant(entries, stream_key, least, high):
    shape = entries.shape
    spot = [jax.random.randint(jax.random.fold_in(stream_key, axis), (), 0, shape[axis]) for axis in range(len(shape))]
    entries = entries.at[tuple(spot)].set(least)
    longest = shape.index(max(shape))
    spot[longest] = (spot[longest] + 1) % shape[longest]
    return entries.at[tuple(spot)].set(high)


def level_of(stream_key, shape, pieces, low, high):
    loudness, own = 1.0, jax.random.fold_in(stream_key, 6)
    for axis_at, shards_of in pieces:
        steps = jnp.exp(jax.random.uniform(jax.random.fold_in(own, axis_at), (shards_of,), jnp.float32, low / len(pieces), high / len(pieces)))
        loudness = loudness * jnp.repeat(steps, shape[axis_at] // shards_of).reshape([-1 if axis == axis_at else 1 for axis in range(len(shape))])
    return loudness


def gaussian(key, dims, spread, limit, kind=jnp.bfloat16):
    entries = spread * jax.random.normal(key, dims, jnp.float32)
    return jnp.clip(entries, min=-limit, max=limit).astype(kind)


def setup_inputs(seed: int = 0) -> dict:
    keys = jax.random.split(jax.random.key(seed), 5)
    return {
        "transmission": draw_transmission(jax.random.fold_in(keys[4], 71), 0),
        "probe": gaussian(keys[1], (2, PROBE, PROBE), 0.7, 4.0),
        "offsets": plant(jax.random.randint(keys[2], (POSITIONS, 2), 0, WIN - PROBE + 1), jax.random.fold_in(keys[2], 1), 0, WIN - PROBE).astype(jnp.int32),
        "measured": jnp.clip(0.25 + 1.75 * jax.random.uniform(keys[3], (POSITIONS, PROBE, PROBE), jnp.float32) ** level_of(keys[3], (POSITIONS, PROBE, PROBE), ((0, 16),), -0.2, 0.2), 0.25, 2.0),
    }


PHASE_SCALE = math.pi / 4.0


def round_half(values):
    return lax.optimization_barrier(values.astype(jnp.bfloat16)).astype(jnp.float32)


def propagator(probe_side):
    grid_index = jnp.arange(probe_side, dtype=jnp.int32)
    frequency = ((grid_index + probe_side // 2) % probe_side - probe_side // 2).astype(jnp.float32)
    phase_term = PHASE_SCALE * (frequency[:, None] ** 2 + frequency[None, :] ** 2) / probe_side
    return jnp.cos(phase_term), -jnp.sin(phase_term)


def split_round(field):
    return lax.complex(round_half(jnp.real(field)), round_half(jnp.imag(field)))


def reference(transmission, probe, offsets, measured):
    slice_count = transmission.shape[0]
    probe_side = probe.shape[-1]
    kernel_real, kernel_imag = propagator(probe_side)
    kernel = lax.complex(kernel_real, kernel_imag)
    objects = transmission.astype(jnp.float32)
    entry_wave = lax.complex(probe[0].astype(jnp.float32), probe[1].astype(jnp.float32))
    zero_index = jnp.zeros((), jnp.int32)

    def one_position(window, inputs):
        scan_place, target_block = inputs
        corner = (zero_index, zero_index, scan_place[0].astype(jnp.int32), scan_place[1].astype(jnp.int32))
        patch = lax.dynamic_slice(objects, corner, (slice_count, 2, probe_side, probe_side))
        object_crop = lax.complex(patch[:, 0], patch[:, 1])
        waves = []
        current_wave = entry_wave
        for layer_index in range(slice_count):
            waves.append(current_wave)
            spectrum = kernel * jnp.fft.fft2(object_crop[layer_index] * current_wave, norm="ortho")
            current_wave = split_round(jnp.fft.ifft2(spectrum, norm="ortho"))
        far_field = jnp.fft.fft2(current_wave, norm="ortho")
        intensity = jnp.real(far_field) ** 2 + jnp.imag(far_field) ** 2
        adjoint_wave = split_round(jnp.fft.ifft2((intensity - target_block) * far_field, norm="ortho"))
        gradients = [None] * slice_count
        for layer_index in reversed(range(slice_count)):
            back_field = jnp.fft.ifft2(jnp.conj(kernel) * jnp.fft.fft2(adjoint_wave, norm="ortho"), norm="ortho")
            gradients[layer_index] = jnp.conj(waves[layer_index]) * back_field
            adjoint_wave = split_round(jnp.conj(object_crop[layer_index]) * back_field)
        stacked = jnp.stack(gradients)
        update = jnp.stack([jnp.real(stacked), jnp.imag(stacked)], axis=1)
        current = lax.dynamic_slice(window, corner, (slice_count, 2, probe_side, probe_side))
        window = lax.dynamic_update_slice(window, current + update, corner)
        return window, None

    window = jnp.zeros(transmission.shape, jnp.float32)
    window, _ = lax.scan(one_position, window, (offsets, measured))
    return window
```

```python
import functools
import math

import jax
import jax.numpy as jnp
import ml_dtypes
import numpy as np
from jax import lax
from jax.experimental import pallas as pl
from jax.experimental.pallas import tpu as pltpu
from jax.sharding import PartitionSpec as P


MESH = pl.DeviceIdType.MESH
F32 = jnp.float32
BF16 = jnp.bfloat16
VMEM_LIMIT = 56 * 1024 * 1024


def vmem():
    return pl.BlockSpec(memory_space=pltpu.VMEM)


def place():
    d = lax.axis_index("depth")
    q = lax.axis_index("pos")
    return d // 4, d % 4, q // 4, (q // 2) % 2, q % 2


def hi_lo(table):
    high = table.astype(ml_dtypes.bfloat16)
    low = (table - high.astype(np.float64)).astype(ml_dtypes.bfloat16)
    return np.stack([high, low])


def right_form(matrix):
    return np.block([[matrix.real, matrix.imag], [-matrix.imag, matrix.real]])


@functools.lru_cache(maxsize=None)
def tables(side):
    half = side // 2
    grid = np.arange(side)
    fourier = np.exp(-2j * np.pi * (np.outer(grid, grid) % side) / side) / math.sqrt(side)
    frequency = (grid + half) % side - half
    phase = np.exp(-1j * math.pi * frequency.astype(np.float64) ** 2 / 1024.0)
    circulant = fourier.conj() @ (phase[:, None] * fourier)
    near, far = circulant[:half, :half], circulant[:half, half:]
    sums, differences = right_form((near + far) / 2), right_form((near - far) / 2)
    steps = np.stack([hi_lo(m) for m in (sums, differences, sums.T, differences.T)])
    transforms = np.stack([hi_lo(m) for m in (fourier.real, fourier.imag)])
    return steps, transforms


def dot(a, b):
    return jnp.dot(a, b, preferred_element_type=F32)


def split(x):
    high = x.astype(BF16)
    return high, (x - high.astype(F32)).astype(BF16)


def right_mult(x, high, low):
    a, b = split(x)
    return dot(jnp.concatenate([a, b, a], 1), jnp.concatenate([high, high, low], 0))


def left_mult(high, low, x):
    a, b = split(x)
    return dot(jnp.concatenate([high, high, low], 1), jnp.concatenate([a, b, a], 0))


def propagate(real, imag, right, left):
    half = real.shape[0] // 2
    (rs_h, rs_l), (rd_h, rd_l) = right
    (ls_h, ls_l), (ld_h, ld_l) = left
    plus = jnp.concatenate([real[:, :half] + real[:, half:], imag[:, :half] + imag[:, half:]], 1)
    minus = jnp.concatenate([real[:, :half] - real[:, half:], imag[:, :half] - imag[:, half:]], 1)
    s = right_mult(plus, rs_h, rs_l)
    d = right_mult(minus, rd_h, rd_l)

    def stack(s, d):
        upper = jnp.concatenate([s[:, :half], d[:, :half]], 1)
        lower = jnp.concatenate([s[:, half:], d[:, half:]], 1)
        return jnp.concatenate([upper, lower], 0)

    p = left_mult(ls_h, ls_l, stack(s[:half] + s[half:], d[:half] + d[half:]))
    m = left_mult(ld_h, ld_l, stack(s[:half] - s[half:], d[:half] - d[half:]))
    top, bottom = p + m, p - m

    def spread(upper, lower):
        rows = jnp.concatenate([upper, lower], 0)
        s, d = rows[:, :half], rows[:, half:]
        return jnp.concatenate([s + d, s - d], 1)

    return spread(top[:half], bottom[:half]), spread(top[half:], bottom[half:])


def neighbours(g, j, x, h, core):
    d = 4 * g + j
    q = 4 * x + 2 * h + core
    xy = 2 * x + h
    partners = [(d, 4 * x + 2 * h + 1 - core)]
    for k in range(1, 8):
        partners.append((d, 2 * ((xy + k) % 8) + core))
    for kx in range(4):
        for kj in range(1, 4):
            partners.append((4 * g + (j + kj) % 4, 4 * ((x + kx) % 4) + 2 * h + core))
    return partners


def meet(partners):
    barrier = pltpu.get_barrier_semaphore()
    for partner in partners:
        pl.semaphore_signal(barrier, inc=1, device_id=partner, device_id_type=MESH)
    pl.semaphore_wait(barrier, len(partners))


def remote(src, dst, send, recv, device):
    return pltpu.make_async_remote_copy(
        src_ref=src, dst_ref=dst, send_sem=send, recv_sem=recv, device_id=device, device_id_type=MESH
    )


def window_rows(offset, rows, columns):
    lanes = jnp.concatenate([offset] * (columns // 128), 1)
    shift = lax.broadcasted_iota(jnp.int32, (rows, columns), 1) - lax.broadcasted_iota(
        jnp.int32, (rows, columns), 0
    )
    return jnp.where(shift == lanes, 1.0, 0.0).astype(BF16)


def window_columns(offset, rows, columns):
    lanes = jnp.concatenate([offset] * (columns // 128), 1)
    shift = lax.broadcasted_iota(jnp.int32, (rows, columns), 0) - lax.broadcasted_iota(
        jnp.int32, (rows, columns), 1
    )
    return jnp.where(shift == lanes, 1.0, 0.0).astype(BF16)


def gather_kernel(
    t_ref, off_ref, o_ref, offs_ref, plane, stage,
    s1_send, s1_recv, off_send, off_recv, chip_send, chip_recv, s2_send, s2_recv,
):
    g, j, x, h, core = place()
    d = 4 * g + j
    xy = 2 * x + h
    sibling = (d, 4 * x + 2 * h + 1 - core)
    win = plane.shape[-1]
    side = o_ref.shape[-1]
    meet(neighbours(g, j, x, h, core))

    for k in range(1, 8):
        to = (xy + k) % 8
        tx = to // 2
        remote(
            t_ref.at[tx // 2, tx % 2], plane.at[xy, core], s1_send.at[k], s1_recv.at[k],
            (d, 2 * to + core),
        ).start()
    for k in range(1, 4):
        to = (x + k) % 4
        remote(
            off_ref, offs_ref.at[x], off_send.at[k], off_recv.at[k], (d, 4 * to + 2 * h + core)
        ).start()
    own = t_ref.at[x // 2, x % 2]
    remote(own, plane.at[xy, core], chip_send.at[0], chip_recv.at[0], sibling).start()
    plane[xy, core] = t_ref[x // 2, x % 2]
    offs_ref[x] = off_ref[...]

    for k in range(1, 8):
        come = (xy - k + 8) % 8
        block = plane.at[come, core]
        remote(block, block, s1_send.at[k], s1_recv.at[k], sibling).wait_recv()
        remote(block, block, chip_send.at[k], chip_recv.at[k], sibling).start()
    for k in range(1, 4):
        slot = offs_ref.at[(x - k + 4) % 4]
        remote(slot, slot, off_send.at[k], off_recv.at[k], sibling).wait_recv()
    for k in range(8):
        block = plane.at[(xy - k + 8) % 8, 1 - core]
        remote(block, block, chip_send.at[k], chip_recv.at[k], sibling).wait_recv()

    def target(k, i):
        to_j = core if i == 0 else 3 - core
        to_x = (x + k) % 4
        return to_j, (4 * g + to_j, 4 * to_x + 2 * h + core)

    home = o_ref.at[2 * j + x // 2, x % 2]
    for k in (2, 1, 3, 0):
        for i in range(2):
            slot = 2 * k + i
            position = offs_ref.at[(x + k) % 4]
            pick_rows = window_rows(position[2 * i : 2 * i + 1, :], side, win)
            pick_columns = window_columns(position[2 * i + 1 : 2 * i + 2, :], win, side)
            rows = dot(pick_rows, plane[...].reshape(win, win)).astype(BF16)
            stage[slot] = dot(rows, pick_columns).astype(BF16)
            to_j, device = target(k, i)
            copy = remote(
                stage.at[slot], home, s2_send.at[slot], s2_recv.at[4 * k + (to_j - j + 4) % 4], device
            )
            if k:
                copy.start()
            else:
                pl.when(to_j != j)(copy.start)

                @pl.when(to_j == j)
                def _():
                    o_ref[2 * j + x // 2, x % 2] = stage[slot]

    @pl.when(jnp.logical_or(j == core, j == 3 - core))
    def _():
        for k in range(4):
            for kj in range(4):
                if k or kj:
                    from_x = (x - k + 4) % 4
                    from_j = (j - kj + 4) % 4
                    slot = o_ref.at[2 * from_j + from_x // 2, from_x % 2]
                    remote(slot, slot, s2_send.at[0], s2_recv.at[4 * k + kj], sibling).wait_recv()

    for k in range(1, 8):
        block = t_ref.at[0, 0]
        remote(block, block, s1_send.at[k], s1_recv.at[k], sibling).wait_send()
    for k in range(1, 4):
        remote(off_ref, off_ref, off_send.at[k], off_recv.at[k], sibling).wait_send()
    for k in range(8):
        block = t_ref.at[0, 0]
        remote(block, block, chip_send.at[k], chip_recv.at[k], sibling).wait_send()
    for k in range(4):
        for i in range(2):
            slot = 2 * k + i
            to_j, device = target(k, i)
            copy = remote(stage.at[slot], home, s2_send.at[slot], s2_recv.at[0], device)
            if k:
                copy.wait_send()
            else:
                pl.when(to_j != j)(copy.wait_send)


def chain_kernel(
    o_ref, probe_ref, measured_ref, step_ref, transform_ref, g_ref, wave, stored, out_waves, in_waves,
    send_sem, recv_sem,
):
    g, j, x, h, core = place()
    d = 4 * g + j
    q = 4 * x + 2 * h + core
    last = 3
    count = o_ref.shape[0]
    active = jnp.logical_or(j == core, j == 3 - core)
    ahead = (jnp.minimum(d + 4, 15), q)
    behind = (jnp.maximum(d - 4, 0), q)
    barrier = pltpu.get_barrier_semaphore()

    @pl.when(jnp.logical_and(active, g < last))
    def _():
        pl.semaphore_signal(barrier, inc=1, device_id=ahead, device_id_type=MESH)

    @pl.when(jnp.logical_and(active, g > 0))
    def _():
        pl.semaphore_signal(barrier, inc=1, device_id=behind, device_id_type=MESH)

    @pl.when(active)
    def _():
        pl.semaphore_wait(barrier, jnp.where(jnp.logical_or(g == 0, g == last), 1, 2))

    forward_copy = remote(out_waves.at[0], in_waves.at[0], send_sem.at[0], recv_sem.at[0], ahead)
    backward_copy = remote(out_waves.at[1], in_waves.at[1], send_sem.at[1], recv_sem.at[1], behind)

    def step_tables(right, left):
        pick = lambda m: (step_ref[m, 0], step_ref[m, 1])
        return [pick(m) for m in right], [pick(m) for m in left]

    @pl.when(active)
    def _():
        @pl.when(g == 0)
        def _():
            wave[...] = probe_ref[...].astype(F32)

        @pl.when(g > 0)
        def _():
            forward_copy.wait_recv()
            wave[...] = in_waves[0].astype(F32)

        def forward(s, carry):
            real, imag = wave[0], wave[1]
            stored[s, 0] = real.astype(BF16)
            stored[s, 1] = imag.astype(BF16)
            o_real, o_imag = o_ref[s, 0].astype(F32), o_ref[s, 1].astype(F32)
            right, left = step_tables((0, 1), (2, 3))
            real, imag = propagate(
                o_real * real - o_imag * imag, o_real * imag + o_imag * real, right, left
            )
            wave[0] = real
            wave[1] = imag
            return carry

        lax.fori_loop(0, count, forward, 0)

        @pl.when(g < last)
        def _():
            out_waves[0] = wave[...].astype(BF16)
            forward_copy.start()
            remote(out_waves.at[1], in_waves.at[1], send_sem.at[1], recv_sem.at[1], ahead).wait_recv()
            wave[...] = in_waves[1].astype(F32)

        @pl.when(g == last)
        def _():
            fr = (transform_ref[0, 0], transform_ref[0, 1])
            fi = (transform_ref[1, 0], transform_ref[1, 1])
            target = measured_ref[jnp.where(j == core, 0, 1)]
            real, imag = wave[0], wave[1]
            a = right_mult(real, *fr) - right_mult(imag, *fi)
            b = right_mult(real, *fi) + right_mult(imag, *fr)
            real = left_mult(*fr, a) - left_mult(*fi, b)
            imag = left_mult(*fi, a) + left_mult(*fr, b)
            weight = real * real + imag * imag - target
            real, imag = real * weight, imag * weight
            a = right_mult(real, *fr) + right_mult(imag, *fi)
            b = right_mult(imag, *fr) - right_mult(real, *fi)
            wave[0] = left_mult(*fr, a) + left_mult(*fi, b)
            wave[1] = left_mult(*fr, b) - left_mult(*fi, a)

        def backward(t, carry):
            s = count - 1 - t
            right, left = step_tables((2, 3), (0, 1))
            real, imag = propagate(wave[0], wave[1], right, left)
            p_real, p_imag = stored[s, 0].astype(F32), stored[s, 1].astype(F32)
            g_ref[s, 0] = (p_real * real + p_imag * imag).astype(BF16)
            g_ref[s, 1] = (p_real * imag - p_imag * real).astype(BF16)
            o_real, o_imag = o_ref[s, 0].astype(F32), o_ref[s, 1].astype(F32)
            wave[0] = o_real * real + o_imag * imag
            wave[1] = o_real * imag - o_imag * real
            return carry

        lax.fori_loop(0, count, backward, 0)

        @pl.when(g > 0)
        def _():
            out_waves[1] = wave[...].astype(BF16)
            backward_copy.start()
            backward_copy.wait_send()

        @pl.when(g < last)
        def _():
            forward_copy.wait_send()


def scatter_kernel(
    g_ref, offs_ref, out_ref, patches, total, partial, sibling_sum, reduced, arrived,
    s3_send, s3_recv, chip_send, chip_recv, s4_send, s4_recv,
):
    g, j, x, h, core = place()
    d = 4 * g + j
    xy = 2 * x + h
    sibling = (d, 4 * x + 2 * h + 1 - core)
    win = total.shape[-1]
    side = patches.shape[-1]
    meet(neighbours(g, j, x, h, core))

    active = jnp.logical_or(j == core, j == 3 - core)
    mine = jnp.where(j == core, 0, 1)

    @pl.when(active)
    def _():
        for kx in (2, 1, 3, 0):
            for kj in range(4):
                to_x = (x + kx) % 4
                to_j = (j + kj) % 4
                source = g_ref.at[2 * to_j + to_x // 2, to_x % 2]
                if kx or kj:
                    remote(
                        source, patches.at[2 * x + mine], s3_send.at[4 * kx + kj],
                        s3_recv.at[2 * kx + mine], (4 * g + to_j, 4 * to_x + 2 * h + core),
                    ).start()
                else:
                    patches[2 * x + mine] = g_ref[2 * j + x // 2, x % 2]

    first = True
    for kx in (0, 1, 3, 2):
        for i in range(2):
            from_x = (x - kx + 4) % 4
            from_j = core if i == 0 else 3 - core
            slot = patches.at[2 * from_x + i]
            copy = remote(slot, slot, s3_send.at[0], s3_recv.at[2 * kx + i], sibling)
            if kx:
                copy.wait_recv()
            else:
                pl.when(from_j != j)(copy.wait_recv)
            position = offs_ref.at[from_x]
            put_columns = window_rows(position[2 * i + 1 : 2 * i + 2, :], side, win)
            put_rows = window_columns(position[2 * i : 2 * i + 1, :], win, side)
            wide = dot(slot[...], put_columns).astype(BF16)
            term = dot(put_rows, wide)
            total[...] = term if first else total[...] + term
            first = False

    partial[...] = total[...].reshape(partial.shape).astype(BF16)
    chip_copy = remote(
        partial.at[:, 1 - core], sibling_sum, chip_send.at[0], chip_recv.at[0], sibling
    )
    chip_copy.start()
    chip_copy.wait_recv()
    for k in (4, 3, 5, 2, 6, 1, 7, 0):
        to = (xy + k) % 8
        rows = partial.shape[2]
        start = pl.multiple_of((2 * to + core) * rows, rows)
        value = total[pl.ds(start, rows), :] + sibling_sum[to].astype(F32)
        if k:
            reduced[to] = value.astype(BF16)
            remote(
                reduced.at[to], arrived.at[xy], s4_send.at[k], s4_recv.at[k], (d, 2 * to + core)
            ).start()
        else:
            arrived[xy] = value.astype(BF16)
    for k in range(1, 8):
        slot = arrived.at[(xy - k + 8) % 8]
        remote(slot, slot, s4_send.at[k], s4_recv.at[k], sibling).wait_recv()
    for plane in range(4):
        out_ref[plane // 2, plane % 2] = arrived[2 * plane].astype(F32) + arrived[2 * plane + 1].astype(F32)

    @pl.when(active)
    def _():
        for kx in range(4):
            for kj in range(4):
                if kx or kj:
                    source = g_ref.at[0, 0]
                    remote(source, source, s3_send.at[4 * kx + kj], s3_recv.at[0], sibling).wait_send()

    chip_copy.wait_send()
    for k in range(1, 8):
        slot = reduced.at[0]
        remote(slot, slot, s4_send.at[k], s4_recv.at[k], sibling).wait_send()


def per_device(transmission, probe, offsets, measured):
    layers, _, rows, win = transmission.shape
    side = probe.shape[-1]
    group = 4 * layers
    steps, transforms = tables(side)
    dma = pltpu.SemaphoreType.DMA

    def params(collective_id):
        return pltpu.CompilerParams(
            collective_id=collective_id, has_side_effects=True, vmem_limit_bytes=VMEM_LIMIT
        )

    spread = jnp.broadcast_to(jnp.pad(offsets.reshape(4), (0, 4))[:, None], (8, 128))
    crops, every_offset = pl.pallas_call(
        gather_kernel,
        out_shape=[
            jax.ShapeDtypeStruct((group, 2, side, side), BF16),
            jax.ShapeDtypeStruct((4, 8, 128), jnp.int32),
        ],
        in_specs=[vmem(), vmem()],
        out_specs=[vmem(), vmem()],
        scratch_shapes=[
            pltpu.VMEM((8, 2, rows, win), BF16),
            pltpu.VMEM((8, side, side), BF16),
            dma((8,)), dma((8,)), dma((4,)), dma((4,)), dma((8,)), dma((8,)), dma((8,)), dma((16,)),
        ],
        compiler_params=params(0),
        name="gather_crops",
    )(transmission, spread)

    patches = pl.pallas_call(
        chain_kernel,
        out_shape=jax.ShapeDtypeStruct((group, 2, side, side), BF16),
        in_specs=[vmem()] * 5,
        out_specs=vmem(),
        scratch_shapes=[
            pltpu.VMEM((2, side, side), F32),
            pltpu.VMEM((group, 2, side, side), BF16),
            pltpu.VMEM((2, 2, side, side), BF16),
            pltpu.VMEM((2, 2, side, side), BF16),
            dma((2,)), dma((2,)),
        ],
        compiler_params=params(1),
        name="wave_chain",
    )(crops, probe, measured, jnp.asarray(steps), jnp.asarray(transforms))

    return pl.pallas_call(
        scatter_kernel,
        out_shape=jax.ShapeDtypeStruct((layers, 2, rows, win), F32),
        in_specs=[vmem(), vmem()],
        out_specs=vmem(),
        scratch_shapes=[
            pltpu.VMEM((8, side, side), BF16),
            pltpu.VMEM((win, win), F32),
            pltpu.VMEM((8, 2, rows, win), BF16),
            pltpu.VMEM((8, rows, win), BF16),
            pltpu.VMEM((8, rows, win), BF16),
            pltpu.VMEM((8, rows, win), BF16),
            dma((16,)), dma((8,)), dma((1,)), dma((1,)), dma((8,)), dma((8,)),
        ],
        compiler_params=params(2),
        name="scatter_patches",
    )(patches, every_offset)


def solution(mesh):
    in_specs = (P("depth", None, "pos", None), P(), P("pos", None), P("pos", None, None))
    out_specs = P("depth", None, "pos", None)
    return jax.shard_map(
        per_device, mesh=mesh, in_specs=in_specs, out_specs=out_specs, check_vma=False
    )
```

```python
import functools
import math

import jax
import jax.numpy as jnp
import ml_dtypes
import numpy as np
from jax import lax
from jax.experimental import pallas as pl
from jax.experimental.pallas import tpu as pltpu
from jax.sharding import PartitionSpec as P


MESH = pl.DeviceIdType.MESH
F32 = jnp.float32
BF16 = jnp.bfloat16
VMEM_LIMIT = 56 * 1024 * 1024


def vmem():
    return pl.BlockSpec(memory_space=pltpu.VMEM)


def place():
    d = lax.axis_index("depth")
    q = lax.axis_index("pos")
    return d // 4, d % 4, q // 4, (q // 2) % 2, q % 2


def hi_lo(table, axis):
    high = table.astype(ml_dtypes.bfloat16)
    low = (table - high.astype(np.float64)).astype(ml_dtypes.bfloat16)
    return np.concatenate([high, low], axis)


def right_form(matrix):
    return np.block([[matrix.real, matrix.imag], [-matrix.imag, matrix.real]])


@functools.lru_cache(maxsize=None)
def tables(side):
    half = side // 2
    grid = np.arange(side)
    fourier = np.exp(-2j * np.pi * (np.outer(grid, grid) % side) / side) / math.sqrt(side)
    frequency = (grid + half) % side - half
    phase = np.exp(-1j * math.pi * frequency.astype(np.float64) ** 2 / 1024.0)
    circulant = fourier.conj() @ (phase[:, None] * fourier)
    near, far = circulant[:half, :half], circulant[:half, half:]
    forms = [right_form((near + far) / 2), right_form((near - far) / 2)]
    rights = np.stack([[hi_lo(m, 0) for m in forms], [hi_lo(m.T, 0) for m in forms]])
    lefts = np.stack([[hi_lo(m.T, 1) for m in forms], [hi_lo(m, 1) for m in forms]])
    transforms = np.stack([hi_lo(m, 0) for m in (fourier.real, fourier.imag, -fourier.imag)])
    return rights, lefts, transforms.reshape(3, 2, side, side)


def dot(a, b):
    return jnp.dot(a, b, preferred_element_type=F32)


def cat(parts, axis):
    return jnp.concatenate(parts, axis)


def right_stage(real, imag, right_ref, way):
    half = real.shape[1] // 2
    plus = cat([real[:, :half] + real[:, half:], imag[:, :half] + imag[:, half:]], 1).astype(BF16)
    minus = cat([real[:, :half] - real[:, half:], imag[:, :half] - imag[:, half:]], 1).astype(BF16)
    s = dot(cat([plus, plus], 1), right_ref[way, 0])
    d = dot(cat([minus, minus], 1), right_ref[way, 1])
    return s, d


def keep_middle(middle, s, d, at, rows, half):
    for m, (a, b) in enumerate(((s[:rows] + s[rows:], d[:rows] + d[rows:]), (s[:rows] - s[rows:], d[:rows] - d[rows:]))):
        middle[m, pl.ds(at, rows), :] = cat([a[:, :half], b[:, :half]], 1).astype(BF16)
        middle[m, pl.ds(half + at, rows), :] = cat([a[:, half:], b[:, half:]], 1).astype(BF16)


def left_stage(middle, left_ref, way, at, rows, half):
    def pick(m):
        table = cat([left_ref[way, m, pl.ds(at, rows), :], left_ref[way, m, pl.ds(half + at, rows), :]], 0)
        x = middle[m]
        return dot(table, cat([x, x], 0))

    p, m = pick(0), pick(1)
    top, bottom = p + m, p - m

    def spread(upper, lower):
        s, d = cat([upper[:, :half], lower[:, :half]], 0), cat([upper[:, half:], lower[:, half:]], 0)
        return cat([s + d, s - d], 1)

    return spread(top[:rows], bottom[:rows]), spread(top[rows:], bottom[rows:])


def fourier_right(real, imag, f, inverse):
    r, i, n = f
    up, down = (n, i) if inverse else (i, n)
    x = cat([real, real, imag, imag], 1)
    a = dot(x, cat([r[0], r[1], down[0], down[1]], 0))
    b = dot(x, cat([up[0], up[1], r[0], r[1]], 0))
    return a.astype(BF16), b.astype(BF16)


def fourier_left(real, imag, f, inverse):
    r, i, n = f
    up, down = (n, i) if inverse else (i, n)
    x = cat([real, real, imag, imag], 0)
    a = dot(cat([r[0], r[1], down[0], down[1]], 1), x)
    b = dot(cat([up[0], up[1], r[0], r[1]], 1), x)
    return a, b


def neighbours(g, j, x, h, core):
    d = 4 * g + j
    xy = 2 * x + h
    partners = [(d, 4 * x + 2 * h + 1 - core)]
    for k in range(1, 8):
        partners.append((d, 2 * ((xy + k) % 8) + core))
    for kx in range(4):
        for kj in range(1, 4):
            partners.append((4 * g + (j + kj) % 4, 4 * ((x + kx) % 4) + 2 * h + core))
    return partners


def remote(src, dst, send, recv, device):
    return pltpu.make_async_remote_copy(
        src_ref=src, dst_ref=dst, send_sem=send, recv_sem=recv, device_id=device, device_id_type=MESH
    )


def one_hot(mask):
    return jnp.where(mask, 1.0, 0.0).astype(BF16)


def window_rows(offset, rows, columns):
    lanes = cat([offset] * (columns // 128), 1)
    shift = lax.broadcasted_iota(jnp.int32, (rows, columns), 1) - lax.broadcasted_iota(
        jnp.int32, (rows, columns), 0
    )
    return one_hot(shift == lanes)


def window_columns(offset, rows, columns):
    lanes = cat([offset] * (columns // 128), 1)
    shift = lax.broadcasted_iota(jnp.int32, (rows, columns), 0) - lax.broadcasted_iota(
        jnp.int32, (rows, columns), 1
    )
    return one_hot(shift == lanes)


def window_blocks(offset, first, block, rows, columns):
    lanes = cat([offset] * (columns // 128), 1)
    count = lax.broadcasted_iota(jnp.int32, (rows, columns), 0)
    row = count + (count // block + first) * block
    return one_hot(row - lax.broadcasted_iota(jnp.int32, (rows, columns), 1) == lanes)


CHUNKS = 2


def kernel(
    off_ref, t_ref, probe_ref, measured_hbm, right_hbm, left_hbm, transform_hbm, arrived,
    own_offsets, offs, plane, stage, o_ref, stored, chi, middle, grads, measured_ref, right_ref, left_ref,
    transform_ref, patches, put_columns, put_rows, wide, partial, sibling_sum, reduced,
    load_sem, s1_send, s1_recv, off_send, off_recv, chip_send, chip_recv, s2_send, s2_recv,
    hop_send, hop_recv, s3_send, s3_recv, back_send, back_recv, s4_send, s4_recv,
):
    g, j, x, h, core = place()
    d = 4 * g + j
    q = 4 * x + 2 * h + core
    xy = 2 * x + h
    last = 3
    sibling = (d, 4 * x + 2 * h + 1 - core)
    win = plane.shape[-1]
    side = o_ref.shape[-1]
    half = side // 2
    count = o_ref.shape[0]
    block = plane.shape[2]
    active = jnp.logical_or(j == core, j == 3 - core)
    mine = jnp.where(j == core, 0, 1)
    ahead = (jnp.minimum(d + 4, 15), q)
    behind = (jnp.maximum(d - 4, 0), q)

    loads = [
        pltpu.make_async_copy(right_hbm, right_ref, load_sem.at[0]),
        pltpu.make_async_copy(left_hbm, left_ref, load_sem.at[1]),
        pltpu.make_async_copy(transform_hbm, transform_ref, load_sem.at[2]),
        pltpu.make_async_copy(measured_hbm.at[mine], measured_ref, load_sem.at[3]),
    ]
    barrier = pltpu.get_barrier_semaphore()
    partners = neighbours(g, j, x, h, core)
    for partner in partners:
        pl.semaphore_signal(barrier, inc=1, device_id=partner, device_id_type=MESH)

    @pl.when(jnp.logical_and(active, g < last))
    def _():
        pl.semaphore_signal(barrier, inc=1, device_id=ahead, device_id_type=MESH)

    @pl.when(jnp.logical_and(active, g > 0))
    def _():
        pl.semaphore_signal(barrier, inc=1, device_id=behind, device_id_type=MESH)

    chained = jnp.where(active, jnp.where(jnp.logical_or(g == 0, g == last), 1, 2), 0)
    for load in loads:
        load.start()
    for k in range(4):
        own_offsets[k : k + 1, :] = jnp.full((1, 128), off_ref[k // 2, k % 2], jnp.int32)
        own_offsets[k + 4 : k + 5, :] = jnp.zeros((1, 128), jnp.int32)
    pl.semaphore_wait(barrier, len(partners) + chained)

    for k in (4, 3, 5, 2, 6, 1, 7):
        to = (xy + k) % 8
        tx = to // 2
        remote(
            t_ref.at[tx // 2, tx % 2], plane.at[xy, core], s1_send.at[k], s1_recv.at[k], (d, 2 * to + core)
        ).start()
    for k in range(1, 4):
        to = (x + k) % 4
        remote(
            own_offsets, offs.at[x], off_send.at[k], off_recv.at[k], (d, 4 * to + 2 * h + core)
        ).start()
    own = t_ref.at[x // 2, x % 2]
    remote(own, plane.at[xy, core], chip_send.at[0], chip_recv.at[0], sibling).start()
    plane[xy, core] = t_ref[x // 2, x % 2]
    offs[x] = own_offsets[...]

    for k in (1, 7, 2, 6, 3, 5, 4):
        rows = plane.at[(xy - k + 8) % 8, core]
        remote(rows, rows, s1_send.at[k], s1_recv.at[k], sibling).wait_recv()
        remote(rows, rows, chip_send.at[k], chip_recv.at[k], sibling).start()
    for k in range(1, 4):
        slot = offs.at[(x - k + 4) % 4]
        remote(slot, slot, off_send.at[k], off_recv.at[k], sibling).wait_recv()
    for k in range(8):
        rows = plane.at[(xy - k + 8) % 8, 1 - core]
        remote(rows, rows, chip_send.at[k], chip_recv.at[k], sibling).wait_recv()

    def target(k, i):
        to_j = core if i == 0 else 3 - core
        return to_j, (4 * g + to_j, 4 * ((x + k) % 4) + 2 * h + core)

    own_plane = 2 * j + x // 2
    home = o_ref.at[own_plane, x % 2]
    for i in range(2):
        for k in (2, 1, 3, 0):
            slot = 2 * k + i
            position = offs.at[(x + k) % 4]
            pick_rows = window_rows(position[2 * i : 2 * i + 1, :], side, win)
            pick_columns = window_columns(position[2 * i + 1 : 2 * i + 2, :], win, side)
            rows = dot(pick_rows, plane[...].reshape(win, win)).astype(BF16)
            stage[slot] = dot(rows, pick_columns).astype(BF16)
            to_j, device = target(k, i)
            copy = remote(
                stage.at[slot], home, s2_send.at[slot], s2_recv.at[2 * own_plane + x % 2], device
            )
            if k:
                copy.start()
            else:
                pl.when(to_j != j)(copy.start)

                @pl.when(to_j == j)
                def _():
                    o_ref[own_plane, x % 2] = stage[slot]

    for p in range(8):
        i = p % 2
        put_columns[p] = window_rows(offs[p // 2, 2 * i + 1 : 2 * i + 2, :], side, win)
        for m in range(2):
            first = 1 - core if m == 0 else core
            put_rows[m, :, p * side : (p + 1) * side] = window_blocks(
                offs[p // 2, 2 * i : 2 * i + 1, :], first, block, win // 2, side
            )

    for load in loads:
        load.wait()
    rows = half // CHUNKS
    hop_forward = remote(stored.at[count], stored.at[0], hop_send.at[0], hop_recv.at[0], ahead)
    hop_backward = remote(chi.at[0], chi.at[count], hop_send.at[1], hop_recv.at[1], behind)

    def both(ref, s, c, at):
        return cat([ref[s, c, pl.ds(at, rows), :], ref[s, c, pl.ds(half + at, rows), :]], 0).astype(F32)

    def keep(ref, s, c, at, value):
        value = value.astype(BF16)
        ref[s, c, pl.ds(at, rows), :] = value[:rows]
        ref[s, c, pl.ds(half + at, rows), :] = value[rows:]

    def owner(s, c):
        return 2 * (s % 2) + c, s // 2

    @pl.when(active)
    def _():
        @pl.when(g == 0)
        def _():
            stored[0] = probe_ref[...]

        @pl.when(g > 0)
        def _():
            hop_forward.wait_recv()

        def forward(s, carry):
            for c in range(2):
                from_x, from_j = owner(s, c)
                slot = o_ref.at[s, c]
                copy = remote(slot, slot, s2_send.at[0], s2_recv.at[2 * s + c], sibling)
                pl.when(jnp.logical_or(from_x != x, from_j != j))(copy.wait_recv)
            for part in range(CHUNKS):
                at = part * rows
                real, imag = both(stored, s, 0, at), both(stored, s, 1, at)
                o_real, o_imag = both(o_ref, s, 0, at), both(o_ref, s, 1, at)
                a, b = right_stage(
                    o_real * real - o_imag * imag, o_real * imag + o_imag * real, right_ref, 0
                )
                keep_middle(middle, a, b, at, rows, half)
            for part in range(CHUNKS):
                at = part * rows
                real, imag = left_stage(middle, left_ref, 0, at, rows, half)
                keep(stored, s + 1, 0, at, real)
                keep(stored, s + 1, 1, at, imag)
            return carry

        lax.fori_loop(0, count, forward, 0)

        @pl.when(g < last)
        def _():
            hop_forward.start()
            remote(chi.at[0], chi.at[count], hop_send.at[1], hop_recv.at[1], ahead).wait_recv()

        @pl.when(g == last)
        def _():
            f = [(transform_ref[m, 0], transform_ref[m, 1]) for m in range(3)]
            a, b = fourier_right(stored[count, 0], stored[count, 1], f, False)
            real, imag = fourier_left(a, b, f, False)
            weight = real * real + imag * imag - measured_ref[...]
            a, b = fourier_right((real * weight).astype(BF16), (imag * weight).astype(BF16), f, True)
            real, imag = fourier_left(a, b, f, True)
            chi[count, 0] = real.astype(BF16)
            chi[count, 1] = imag.astype(BF16)

        def backward(t, carry):
            s = count - 1 - t
            for part in range(CHUNKS):
                at = part * rows
                a, b = right_stage(both(chi, s + 1, 0, at), both(chi, s + 1, 1, at), right_ref, 1)
                keep_middle(middle, a, b, at, rows, half)
            for part in range(CHUNKS):
                at = part * rows
                real, imag = left_stage(middle, left_ref, 1, at, rows, half)
                o_real, o_imag = both(o_ref, s, 0, at), both(o_ref, s, 1, at)
                keep(chi, s, 0, at, o_real * real + o_imag * imag)
                keep(chi, s, 1, at, o_real * imag - o_imag * real)
                p_real, p_imag = both(stored, s, 0, at), both(stored, s, 1, at)
                keep(grads, s, 0, at, p_real * real + p_imag * imag)
                keep(grads, s, 1, at, p_real * imag - p_imag * real)
            for c in range(2):
                to_x, to_j = owner(s, c)
                away = jnp.logical_or(to_x != x, to_j != j)
                copy = remote(
                    grads.at[s, c], patches.at[2 * x + mine], s3_send.at[2 * s + c],
                    s3_recv.at[2 * x + mine], (4 * g + to_j, 4 * to_x + 2 * h + core),
                )
                pl.when(away)(copy.start)

                @pl.when(jnp.logical_not(away))
                def _():
                    patches[2 * x + mine] = grads[s, c]
            return carry

        lax.fori_loop(0, count, backward, 0)

        @pl.when(g > 0)
        def _():
            hop_backward.start()

    for kx in range(4):
        for i in range(2):
            from_x = (x - kx + 4) % 4
            from_j = core if i == 0 else 3 - core
            p = 2 * from_x + i
            slot = patches.at[p]
            copy = remote(slot, slot, s3_send.at[0], s3_recv.at[p], sibling)
            if kx:
                copy.wait_recv()
            else:
                pl.when(from_j != j)(copy.wait_recv)
            start = pl.multiple_of(p * side, side)
            wide[pl.ds(start, side), :] = dot(slot[...], put_columns[p]).astype(BF16)

    partial[...] = dot(put_rows[0], wide[...]).reshape(partial.shape).astype(BF16)
    chip_copy = remote(partial, sibling_sum, back_send.at[0], back_recv.at[0], sibling)
    chip_copy.start()
    own_rows = dot(put_rows[1], wide[...]).reshape(partial.shape)
    chip_copy.wait_recv()
    reduced[...] = (own_rows + sibling_sum[...].astype(F32)).astype(BF16)
    for k in (4, 3, 5, 2, 6, 1, 7):
        to = (xy + k) % 8
        remote(reduced.at[to], arrived.at[xy], s4_send.at[k], s4_recv.at[k], (d, 2 * to + core)).start()
    arrived[xy] = reduced[xy]
    for k in range(1, 8):
        slot = arrived.at[(xy - k + 8) % 8]
        remote(slot, slot, s4_send.at[k], s4_recv.at[k], sibling).wait_recv()

    for k in range(1, 8):
        slot = reduced.at[0]
        remote(slot, slot, s1_send.at[k], s1_recv.at[k], sibling).wait_send()
        remote(slot, slot, s4_send.at[k], s4_recv.at[k], sibling).wait_send()
    for k in range(1, 4):
        remote(own_offsets, own_offsets, off_send.at[k], off_recv.at[k], sibling).wait_send()
    for k in range(8):
        slot = reduced.at[0]
        remote(slot, slot, chip_send.at[k], chip_recv.at[k], sibling).wait_send()
    chip_copy.wait_send()
    for i in range(2):
        for k in range(4):
            slot = 2 * k + i
            to_j, device = target(k, i)
            copy = remote(stage.at[slot], home, s2_send.at[slot], s2_recv.at[0], device)
            if k:
                copy.wait_send()
            else:
                pl.when(to_j != j)(copy.wait_send)

    @pl.when(active)
    def _():
        pl.when(g < last)(hop_forward.wait_send)
        pl.when(g > 0)(hop_backward.wait_send)
        for s in range(count):
            for c in range(2):
                to_x, to_j = owner(s, c)
                slot = grads.at[s, c]
                copy = remote(slot, slot, s3_send.at[2 * s + c], s3_recv.at[0], sibling)
                pl.when(jnp.logical_or(to_x != x, to_j != j))(copy.wait_send)


def per_device(transmission, probe, offsets, measured):
    layers, _, rows, win = transmission.shape
    side = probe.shape[-1]
    group = 4 * layers
    rights, lefts, transforms = tables(side)
    dma = pltpu.SemaphoreType.DMA
    hbm = pl.BlockSpec(memory_space=pl.ANY)
    smem = pl.BlockSpec(memory_space=pltpu.SMEM)
    arrived = pl.pallas_call(
        kernel,
        out_shape=jax.ShapeDtypeStruct((8, rows, win), BF16),
        in_specs=[smem, vmem(), vmem(), hbm, hbm, hbm, hbm],
        out_specs=vmem(),
        scratch_shapes=[
            pltpu.VMEM((8, 128), jnp.int32),
            pltpu.VMEM((4, 8, 128), jnp.int32),
            pltpu.VMEM((8, 2, rows, win), BF16),
            pltpu.VMEM((8, side, side), BF16),
            pltpu.VMEM((group, 2, side, side), BF16),
            pltpu.VMEM((group + 1, 2, side, side), BF16),
            pltpu.VMEM((group + 1, 2, side, side), BF16),
            pltpu.VMEM((2, side, side), BF16),
            pltpu.VMEM((group, 2, side, side), BF16),
            pltpu.VMEM((side, side), F32),
            pltpu.VMEM(rights.shape, BF16),
            pltpu.VMEM(lefts.shape, BF16),
            pltpu.VMEM(transforms.shape, BF16),
            pltpu.VMEM((8, side, side), BF16),
            pltpu.VMEM((8, side, win), BF16),
            pltpu.VMEM((2, win // 2, 8 * side), BF16),
            pltpu.VMEM((8 * side, win), BF16),
            pltpu.VMEM((8, rows, win), BF16),
            pltpu.VMEM((8, rows, win), BF16),
            pltpu.VMEM((8, rows, win), BF16),
            dma((4,)), dma((8,)), dma((8,)), dma((4,)), dma((4,)), dma((8,)), dma((8,)), dma((8,)),
            dma((16,)), dma((2,)), dma((2,)), dma((16,)), dma((8,)), dma((1,)), dma((1,)), dma((8,)), dma((8,)),
        ],
        compiler_params=pltpu.CompilerParams(
            collective_id=0, has_side_effects=True, vmem_limit_bytes=VMEM_LIMIT
        ),
        name="ptychography_backward",
    )(
        offsets, transmission, probe, measured,
        jnp.asarray(rights), jnp.asarray(lefts), jnp.asarray(transforms),
    )
    parts = arrived.astype(F32).reshape(layers, 2, 2, rows, win)
    return parts[:, :, 0] + parts[:, :, 1]


def solution(mesh):
    in_specs = (P("depth", None, "pos", None), P(), P("pos", None), P("pos", None, None))
    out_specs = P("depth", None, "pos", None)
    return jax.shard_map(
        per_device, mesh=mesh, in_specs=in_specs, out_specs=out_specs, check_vma=False
    )
```

```python
import functools
import math

import jax
import jax.numpy as jnp
import ml_dtypes
import numpy as np
from jax import lax
from jax.experimental import pallas as pl
from jax.experimental.pallas import tpu as pltpu
from jax.sharding import PartitionSpec as P


MESH = pl.DeviceIdType.MESH
F32 = jnp.float32
BF16 = jnp.bfloat16
VMEM_LIMIT = 56 * 1024 * 1024


def vmem():
    return pl.BlockSpec(memory_space=pltpu.VMEM)


def place():
    d = lax.axis_index("depth")
    q = lax.axis_index("pos")
    return d // 4, d % 4, q // 4, (q // 2) % 2, q % 2


def hi_lo(table, axis):
    high = table.astype(ml_dtypes.bfloat16)
    low = (table - high.astype(np.float64)).astype(ml_dtypes.bfloat16)
    return np.concatenate([high, low], axis)


def right_form(matrix):
    return np.block([[matrix.real, matrix.imag], [-matrix.imag, matrix.real]])


@functools.lru_cache(maxsize=None)
def tables(side):
    half = side // 2
    grid = np.arange(side)
    fourier = np.exp(-2j * np.pi * (np.outer(grid, grid) % side) / side) / math.sqrt(side)
    frequency = (grid + half) % side - half
    phase = np.exp(-1j * math.pi * frequency.astype(np.float64) ** 2 / 1024.0)
    circulant = fourier.conj() @ (phase[:, None] * fourier)
    near, far = circulant[:half, :half], circulant[:half, half:]
    forms = [right_form((near + far) / 2), right_form((near - far) / 2)]
    rights = np.stack([[hi_lo(m, 0) for m in forms], [hi_lo(m.T, 0) for m in forms]])
    lefts = np.stack([[hi_lo(m.T, 1) for m in forms], [hi_lo(m, 1) for m in forms]])
    transforms = np.stack([hi_lo(m, 0) for m in (fourier.real, fourier.imag, -fourier.imag)])
    return rights, lefts, transforms.reshape(3, 2, side, side)


def dot(a, b):
    return jnp.dot(a, b, preferred_element_type=F32)


def cat(parts, axis):
    return jnp.concatenate(parts, axis)


STRIP = 16


def strips(count):
    return range(0, count, STRIP)


def halves(value):
    middle = value.shape[1] // 2
    return value[:, :middle], value[:, middle:]


def put_sums(ref, at, real, imag):
    (a, b), (c, d) = halves(real), halves(imag)
    ref[0, pl.ds(at, STRIP), :] = cat([a + b, c + d], 1).astype(BF16)
    ref[1, pl.ds(at, STRIP), :] = cat([a - b, c - d], 1).astype(BF16)


def propagate(sums, flat, middle, field, right_ref, left_ref, way):
    half = sums.shape[1] // 2
    for m in range(2):
        x = sums[m]
        flat[m] = dot(cat([x, x], 1), right_ref[way, m])
    for r in strips(half):
        s, t = flat[0, pl.ds(r, STRIP), :], flat[0, pl.ds(half + r, STRIP), :]
        d, e = flat[1, pl.ds(r, STRIP), :], flat[1, pl.ds(half + r, STRIP), :]
        for m, (a, b) in enumerate(((s + t, d + e), (s - t, d - e))):
            (a_real, a_imag), (b_real, b_imag) = halves(a), halves(b)
            middle[m, pl.ds(r, STRIP), :] = cat([a_real, b_real], 1).astype(BF16)
            middle[m, pl.ds(half + r, STRIP), :] = cat([a_imag, b_imag], 1).astype(BF16)
    for m in range(2):
        x = middle[m]
        field[m] = dot(left_ref[way, m], cat([x, x], 0))


def spread(field):
    half = field.shape[1] // 2
    for r in strips(half):
        p, u = field[0, pl.ds(r, STRIP), :], field[0, pl.ds(half + r, STRIP), :]
        m, v = field[1, pl.ds(r, STRIP), :], field[1, pl.ds(half + r, STRIP), :]
        for at, real, imag in ((r, p + m, u + v), (half + r, p - m, u - v)):
            (a, b), (c, d) = halves(real), halves(imag)
            yield at, cat([a + b, a - b], 1), cat([c + d, c - d], 1)


def strip(ref, s, c, at):
    return ref[s, c, pl.ds(at, STRIP), :].astype(F32)


def fourier_right(real, imag, f, inverse):
    r, i, n = f
    up, down = (n, i) if inverse else (i, n)
    x = cat([real, real, imag, imag], 1)
    a = dot(x, cat([r[0], r[1], down[0], down[1]], 0))
    b = dot(x, cat([up[0], up[1], r[0], r[1]], 0))
    return a, b


def fourier_left(real, imag, f, inverse):
    r, i, n = f
    up, down = (n, i) if inverse else (i, n)
    x = cat([real, real, imag, imag], 0)
    a = dot(cat([r[0], r[1], down[0], down[1]], 1), x)
    b = dot(cat([up[0], up[1], r[0], r[1]], 1), x)
    return a, b


def neighbours(g, j, x, h, core):
    d = 4 * g + j
    xy = 2 * x + h
    partners = [(d, 4 * x + 2 * h + 1 - core)]
    for k in range(1, 8):
        partners.append((d, 2 * ((xy + k) % 8) + core))
    for kx in range(4):
        for kj in range(1, 4):
            partners.append((4 * g + (j + kj) % 4, 4 * ((x + kx) % 4) + 2 * h + core))
    return partners


def remote(src, dst, send, recv, device):
    return pltpu.make_async_remote_copy(
        src_ref=src, dst_ref=dst, send_sem=send, recv_sem=recv, device_id=device, device_id_type=MESH
    )


def one_hot(mask):
    return jnp.where(mask, 1.0, 0.0).astype(BF16)


def shifts(columns):
    return lax.broadcasted_iota(jnp.int32, (STRIP, columns), 1) - lax.broadcasted_iota(
        jnp.int32, (STRIP, columns), 0
    )


def fill_rows(ref, offset):
    rows, columns = ref.shape
    lanes = cat([offset] * (columns // 128), 1)
    base = shifts(columns)
    for r in strips(rows):
        ref[pl.ds(r, STRIP), :] = one_hot(base == lanes + r)


def fill_columns(ref, offset, row_of=lambda r: r):
    rows, columns = ref.shape
    lanes = cat([offset] * (columns // 128), 1)
    base = shifts(columns)
    for r in strips(rows):
        ref[pl.ds(r, STRIP), :] = one_hot(base == row_of(r) - lanes)


def kernel(
    off_ref, t_ref, probe_ref, measured_hbm, right_hbm, left_hbm, transform_hbm, arrived,
    own_offsets, offs, plane, pick_rows, pick_columns, stage, o_ref, stored, sums, flat, middle, field, grads, measured_ref, right_ref, left_ref,
    transform_ref, patches, put_columns, put_rows, wide, partial, sibling_sum, reduced,
    load_sem, s1_send, s1_recv, off_send, off_recv, chip_send, chip_recv, s2_send, s2_recv,
    hop_send, hop_recv, s3_send, s3_recv, back_send, back_recv, s4_send, s4_recv,
):
    g, j, x, h, core = place()
    d = 4 * g + j
    q = 4 * x + 2 * h + core
    xy = 2 * x + h
    last = 3
    sibling = (d, 4 * x + 2 * h + 1 - core)
    win = plane.shape[-1]
    side = o_ref.shape[-1]
    half = side // 2
    count = o_ref.shape[0]
    block = plane.shape[2]
    active = jnp.logical_or(j == core, j == 3 - core)
    mine = jnp.where(j == core, 0, 1)
    ahead = (jnp.minimum(d + 4, 15), q)
    behind = (jnp.maximum(d - 4, 0), q)

    loads = [
        pltpu.make_async_copy(right_hbm, right_ref, load_sem.at[0]),
        pltpu.make_async_copy(left_hbm, left_ref, load_sem.at[1]),
        pltpu.make_async_copy(transform_hbm, transform_ref, load_sem.at[2]),
        pltpu.make_async_copy(measured_hbm.at[mine], measured_ref, load_sem.at[3]),
    ]
    barrier = pltpu.get_barrier_semaphore()
    partners = neighbours(g, j, x, h, core)
    for partner in partners:
        pl.semaphore_signal(barrier, inc=1, device_id=partner, device_id_type=MESH)

    @pl.when(jnp.logical_and(active, g < last))
    def _():
        pl.semaphore_signal(barrier, inc=1, device_id=ahead, device_id_type=MESH)

    @pl.when(jnp.logical_and(active, g > 0))
    def _():
        pl.semaphore_signal(barrier, inc=1, device_id=behind, device_id_type=MESH)

    chained = jnp.where(active, jnp.where(jnp.logical_or(g == 0, g == last), 1, 2), 0)
    for load in loads:
        load.start()
    for k in range(4):
        own_offsets[k : k + 1, :] = jnp.full((1, 128), off_ref[k // 2, k % 2], jnp.int32)
        own_offsets[k + 4 : k + 5, :] = jnp.zeros((1, 128), jnp.int32)
    pl.semaphore_wait(barrier, len(partners) + chained)

    for k in (4, 3, 5, 2, 6, 1, 7):
        to = (xy + k) % 8
        tx = to // 2
        remote(
            t_ref.at[tx // 2, tx % 2], plane.at[xy, core], s1_send.at[k], s1_recv.at[k], (d, 2 * to + core)
        ).start()
    for k in range(1, 4):
        to = (x + k) % 4
        remote(
            own_offsets, offs.at[x], off_send.at[k], off_recv.at[k], (d, 4 * to + 2 * h + core)
        ).start()
    own = t_ref.at[x // 2, x % 2]
    remote(own, plane.at[xy, core], chip_send.at[0], chip_recv.at[0], sibling).start()
    plane[xy, core] = t_ref[x // 2, x % 2]
    offs[x] = own_offsets[...]

    for k in (1, 7, 2, 6, 3, 5, 4):
        rows = plane.at[(xy - k + 8) % 8, core]
        remote(rows, rows, s1_send.at[k], s1_recv.at[k], sibling).wait_recv()
        remote(rows, rows, chip_send.at[k], chip_recv.at[k], sibling).start()
    for k in range(1, 4):
        slot = offs.at[(x - k + 4) % 4]
        remote(slot, slot, off_send.at[k], off_recv.at[k], sibling).wait_recv()
    for k in range(8):
        rows = plane.at[(xy - k + 8) % 8, 1 - core]
        remote(rows, rows, chip_send.at[k], chip_recv.at[k], sibling).wait_recv()

    def target(k, i):
        to_j = core if i == 0 else 3 - core
        return to_j, (4 * g + to_j, 4 * ((x + k) % 4) + 2 * h + core)

    own_plane = 2 * j + x // 2
    home = o_ref.at[own_plane, x % 2]
    for i in range(2):
        for k in (2, 1, 3, 0):
            slot = 2 * k + i
            position = offs.at[(x + k) % 4]
            fill_rows(pick_rows.at[k % 2], position[2 * i : 2 * i + 1, :])
            fill_columns(pick_columns.at[k % 2], position[2 * i + 1 : 2 * i + 2, :])
            rows = dot(pick_rows[k % 2], plane[...].reshape(win, win)).astype(BF16)
            stage[slot] = dot(rows, pick_columns[k % 2]).astype(BF16)
            to_j, device = target(k, i)
            copy = remote(
                stage.at[slot], home, s2_send.at[slot], s2_recv.at[2 * own_plane + x % 2], device
            )
            if k:
                copy.start()
            else:
                pl.when(to_j != j)(copy.start)

                @pl.when(to_j == j)
                def _():
                    o_ref[own_plane, x % 2] = stage[slot]

    for p in range(8):
        i = p % 2
        fill_rows(put_columns.at[p], offs[p // 2, 2 * i + 1 : 2 * i + 2, :])
        for m in range(2):
            first = 1 - core if m == 0 else core
            fill_columns(
                put_rows.at[m, :, p * side : (p + 1) * side],
                offs[p // 2, 2 * i : 2 * i + 1, :],
                lambda r: r + (r // block + first) * block,
            )

    for load in loads:
        load.wait()
    hop_forward = remote(stored.at[count], stored.at[0], hop_send.at[0], hop_recv.at[0], ahead)
    hop_backward = remote(sums, sums, hop_send.at[1], hop_recv.at[1], behind)

    def owner(s, c):
        return 2 * (s % 2) + c, s // 2

    @pl.when(active)
    def _():
        @pl.when(g == 0)
        def _():
            stored[0] = probe_ref[...]

        @pl.when(g > 0)
        def _():
            hop_forward.wait_recv()

        def wait_crop(s):
            for c in range(2):
                from_x, from_j = owner(s, c)
                slot = o_ref.at[s, c]
                copy = remote(slot, slot, s2_send.at[0], s2_recv.at[2 * s + c], sibling)
                pl.when(jnp.logical_or(from_x != x, from_j != j))(copy.wait_recv)

        def enter(s, at, real, imag):
            o_real, o_imag = strip(o_ref, s, 0, at), strip(o_ref, s, 1, at)
            put_sums(sums, at, o_real * real - o_imag * imag, o_real * imag + o_imag * real)

        def forward(s, carry):
            wait_crop(s + 1)
            propagate(sums, flat, middle, field, right_ref, left_ref, 0)
            for at, real, imag in spread(field):
                stored[s + 1, 0, pl.ds(at, STRIP), :] = real.astype(BF16)
                stored[s + 1, 1, pl.ds(at, STRIP), :] = imag.astype(BF16)
                enter(s + 1, at, real, imag)
            return carry

        wait_crop(0)
        for at in strips(side):
            enter(0, at, strip(stored, 0, 0, at), strip(stored, 0, 1, at))
        lax.fori_loop(0, count - 1, forward, 0)
        propagate(sums, flat, middle, field, right_ref, left_ref, 0)
        for at, real, imag in spread(field):
            stored[count, 0, pl.ds(at, STRIP), :] = real.astype(BF16)
            stored[count, 1, pl.ds(at, STRIP), :] = imag.astype(BF16)

        @pl.when(g < last)
        def _():
            hop_forward.start()
            remote(sums, sums, hop_send.at[1], hop_recv.at[1], ahead).wait_recv()

        @pl.when(g == last)
        def _():
            f = [(transform_ref[m, 0], transform_ref[m, 1]) for m in range(3)]
            a, b = fourier_right(stored[count, 0], stored[count, 1], f, False)
            middle[0] = a.astype(BF16)
            middle[1] = b.astype(BF16)
            a, b = fourier_left(middle[0], middle[1], f, False)
            flat[0] = a
            flat[1] = b
            for at in strips(side):
                real, imag = flat[0, pl.ds(at, STRIP), :], flat[1, pl.ds(at, STRIP), :]
                weight = real * real + imag * imag - measured_ref[pl.ds(at, STRIP), :]
                sums[0, pl.ds(at, STRIP), :] = (real * weight).astype(BF16)
                sums[1, pl.ds(at, STRIP), :] = (imag * weight).astype(BF16)
            a, b = fourier_right(sums[0], sums[1], f, True)
            middle[0] = a.astype(BF16)
            middle[1] = b.astype(BF16)
            a, b = fourier_left(middle[0], middle[1], f, True)
            flat[0] = a
            flat[1] = b
            for at in strips(side):
                put_sums(sums, at, flat[0, pl.ds(at, STRIP), :], flat[1, pl.ds(at, STRIP), :])

        def send_patches(s):
            for c in range(2):
                to_x, to_j = owner(s, c)
                away = jnp.logical_or(to_x != x, to_j != j)
                copy = remote(
                    grads.at[s, c], patches.at[2 * x + mine], s3_send.at[2 * s + c],
                    s3_recv.at[2 * x + mine], (4 * g + to_j, 4 * to_x + 2 * h + core),
                )
                pl.when(away)(copy.start)

                @pl.when(jnp.logical_not(away))
                def _():
                    patches[2 * x + mine] = grads[s, c]

        def backward(t, carry):
            s = count - 1 - t
            propagate(sums, flat, middle, field, right_ref, left_ref, 1)
            for at, real, imag in spread(field):
                o_real, o_imag = strip(o_ref, s, 0, at), strip(o_ref, s, 1, at)
                put_sums(sums, at, o_real * real + o_imag * imag, o_real * imag - o_imag * real)
                p_real, p_imag = strip(stored, s, 0, at), strip(stored, s, 1, at)
                grads[s, 0, pl.ds(at, STRIP), :] = (p_real * real + p_imag * imag).astype(BF16)
                grads[s, 1, pl.ds(at, STRIP), :] = (p_real * imag - p_imag * real).astype(BF16)
            pl.when(g == 0)(functools.partial(send_patches, s))
            return carry

        lax.fori_loop(0, count, backward, 0)

        @pl.when(g > 0)
        def _():
            hop_backward.start()
            hop_backward.wait_send()

            def send(t, carry):
                send_patches(count - 1 - t)
                return carry

            lax.fori_loop(0, count, send, 0)

    for kx in range(4):
        for i in range(2):
            from_x = (x - kx + 4) % 4
            from_j = core if i == 0 else 3 - core
            p = 2 * from_x + i
            slot = patches.at[p]
            copy = remote(slot, slot, s3_send.at[0], s3_recv.at[p], sibling)
            if kx:
                copy.wait_recv()
            else:
                pl.when(from_j != j)(copy.wait_recv)
            start = pl.multiple_of(p * side, side)
            wide[pl.ds(start, side), :] = dot(slot[...], put_columns[p]).astype(BF16)

    partial[...] = dot(put_rows[0], wide[...]).reshape(partial.shape).astype(BF16)
    chip_copy = remote(partial, sibling_sum, back_send.at[0], back_recv.at[0], sibling)
    chip_copy.start()
    own_rows = dot(put_rows[1], wide[...]).reshape(partial.shape)
    chip_copy.wait_recv()
    reduced[...] = (own_rows + sibling_sum[...].astype(F32)).astype(BF16)
    for k in (4, 3, 5, 2, 6, 1, 7):
        to = (xy + k) % 8
        remote(reduced.at[to], arrived.at[xy], s4_send.at[k], s4_recv.at[k], (d, 2 * to + core)).start()
    arrived[xy] = reduced[xy]
    for k in range(1, 8):
        slot = arrived.at[(xy - k + 8) % 8]
        remote(slot, slot, s4_send.at[k], s4_recv.at[k], sibling).wait_recv()

    for k in range(1, 8):
        slot = reduced.at[0]
        remote(slot, slot, s1_send.at[k], s1_recv.at[k], sibling).wait_send()
        remote(slot, slot, s4_send.at[k], s4_recv.at[k], sibling).wait_send()
    for k in range(1, 4):
        remote(own_offsets, own_offsets, off_send.at[k], off_recv.at[k], sibling).wait_send()
    for k in range(8):
        slot = reduced.at[0]
        remote(slot, slot, chip_send.at[k], chip_recv.at[k], sibling).wait_send()
    chip_copy.wait_send()
    for i in range(2):
        for k in range(4):
            slot = 2 * k + i
            to_j, device = target(k, i)
            copy = remote(stage.at[slot], home, s2_send.at[slot], s2_recv.at[0], device)
            if k:
                copy.wait_send()
            else:
                pl.when(to_j != j)(copy.wait_send)

    @pl.when(active)
    def _():
        pl.when(g < last)(hop_forward.wait_send)
        for s in range(count):
            for c in range(2):
                to_x, to_j = owner(s, c)
                slot = grads.at[s, c]
                copy = remote(slot, slot, s3_send.at[2 * s + c], s3_recv.at[0], sibling)
                pl.when(jnp.logical_or(to_x != x, to_j != j))(copy.wait_send)


def per_device(transmission, probe, offsets, measured):
    layers, _, rows, win = transmission.shape
    side = probe.shape[-1]
    group = 4 * layers
    rights, lefts, transforms = tables(side)
    dma = pltpu.SemaphoreType.DMA
    hbm = pl.BlockSpec(memory_space=pl.ANY)
    smem = pl.BlockSpec(memory_space=pltpu.SMEM)
    arrived = pl.pallas_call(
        kernel,
        out_shape=jax.ShapeDtypeStruct((8, rows, win), BF16),
        in_specs=[smem, vmem(), vmem(), hbm, hbm, hbm, hbm],
        out_specs=vmem(),
        scratch_shapes=[
            pltpu.VMEM((8, 128), jnp.int32),
            pltpu.VMEM((4, 8, 128), jnp.int32),
            pltpu.VMEM((8, 2, rows, win), BF16),
            pltpu.VMEM((2, side, win), BF16),
            pltpu.VMEM((2, win, side), BF16),
            pltpu.VMEM((8, side, side), BF16),
            pltpu.VMEM((group, 2, side, side), BF16),
            pltpu.VMEM((group + 1, 2, side, side), BF16),
            pltpu.VMEM((2, side, side), BF16),
            pltpu.VMEM((2, side, side), F32),
            pltpu.VMEM((2, side, side), BF16),
            pltpu.VMEM((2, side, side), F32),
            pltpu.VMEM((group, 2, side, side), BF16),
            pltpu.VMEM((side, side), F32),
            pltpu.VMEM(rights.shape, BF16),
            pltpu.VMEM(lefts.shape, BF16),
            pltpu.VMEM(transforms.shape, BF16),
            pltpu.VMEM((8, side, side), BF16),
            pltpu.VMEM((8, side, win), BF16),
            pltpu.VMEM((2, win // 2, 8 * side), BF16),
            pltpu.VMEM((8 * side, win), BF16),
            pltpu.VMEM((8, rows, win), BF16),
            pltpu.VMEM((8, rows, win), BF16),
            pltpu.VMEM((8, rows, win), BF16),
            dma((4,)), dma((8,)), dma((8,)), dma((4,)), dma((4,)), dma((8,)), dma((8,)), dma((8,)),
            dma((16,)), dma((2,)), dma((2,)), dma((16,)), dma((8,)), dma((1,)), dma((1,)), dma((8,)), dma((8,)),
        ],
        compiler_params=pltpu.CompilerParams(
            collective_id=0, has_side_effects=True, vmem_limit_bytes=VMEM_LIMIT
        ),
        name="ptychography_backward",
    )(
        offsets, transmission, probe, measured,
        jnp.asarray(rights), jnp.asarray(lefts), jnp.asarray(transforms),
    )
    parts = arrived.astype(F32).reshape(layers, 2, 2, rows, win)
    return parts[:, :, 0] + parts[:, :, 1]


def solution(mesh):
    in_specs = (P("depth", None, "pos", None), P(), P("pos", None), P("pos", None, None))
    out_specs = P("depth", None, "pos", None)
    return jax.shard_map(
        per_device, mesh=mesh, in_specs=in_specs, out_specs=out_specs, check_vma=False
    )
```

```python
import functools
import math

import jax
import jax.numpy as jnp
import ml_dtypes
import numpy as np
from jax import lax
from jax.experimental import pallas as pl
from jax.experimental.pallas import tpu as pltpu
from jax.sharding import PartitionSpec as P


MESH = pl.DeviceIdType.MESH
F32 = jnp.float32
BF16 = jnp.bfloat16
VMEM_LIMIT = 56 * 1024 * 1024


def vmem():
    return pl.BlockSpec(memory_space=pltpu.VMEM)


def place():
    d = lax.axis_index("depth")
    q = lax.axis_index("pos")
    return d // 4, d % 4, q // 4, (q // 2) % 2, q % 2


def hi_lo(table, axis):
    high = table.astype(ml_dtypes.bfloat16)
    low = (table - high.astype(np.float64)).astype(ml_dtypes.bfloat16)
    return np.concatenate([high, low], axis)


def right_form(matrix):
    return np.block([[matrix.real, matrix.imag], [-matrix.imag, matrix.real]])


@functools.lru_cache(maxsize=None)
def tables(side):
    half = side // 2
    grid = np.arange(side)
    fourier = np.exp(-2j * np.pi * (np.outer(grid, grid) % side) / side) / math.sqrt(side)
    frequency = (grid + half) % side - half
    phase = np.exp(-1j * math.pi * frequency.astype(np.float64) ** 2 / 1024.0)
    circulant = fourier.conj() @ (phase[:, None] * fourier)
    near, far = circulant[:half, :half], circulant[:half, half:]
    forms = [right_form((near + far) / 2), right_form((near - far) / 2)]
    rights = np.stack([[hi_lo(m, 0) for m in forms], [hi_lo(m.T, 0) for m in forms]])
    order = grid.reshape(2, half // STRIP, STRIP).transpose(1, 0, 2).reshape(side)
    strided = [m[order][:, order] for m in forms]
    lefts = np.stack([[hi_lo(m.T, 1) for m in strided], [hi_lo(m, 1) for m in strided]])
    transforms = np.stack([hi_lo(m, 0) for m in (fourier.real, fourier.imag, -fourier.imag)])
    return rights, lefts, transforms.reshape(3, 2, side, side)


def dot(a, b):
    return jnp.dot(a, b, preferred_element_type=F32)


def cat(parts, axis):
    return jnp.concatenate(parts, axis)


STRIP = 16
BLOCKS = 2


def strips(count):
    return range(0, count, STRIP)


def halves(value):
    middle = value.shape[1] // 2
    return value[:, :middle], value[:, middle:]


def put_sums(ref, at, real, imag):
    (a, b), (c, d) = halves(real), halves(imag)
    ref[0, pl.ds(at, STRIP), :] = cat([a + b, c + d], 1).astype(BF16)
    ref[1, pl.ds(at, STRIP), :] = cat([a - b, c - d], 1).astype(BF16)


def sums_row(row, side):
    half = side // 2
    return 2 * row if row < half else 2 * (row - half) + STRIP


def right_stage(sums, flat, middle, right_ref, way):
    side = sums.shape[1]
    block = side // BLOCKS
    for n in range(BLOCKS):
        for m in range(2):
            x = sums[m, pl.ds(n * block, block), :]
            flat[m, pl.ds(n * block, block), :] = dot(cat([x, x], 1), right_ref[way, m])
        for r in range(n * block, (n + 1) * block, 2 * STRIP):
            s, t = flat[0, pl.ds(r, STRIP), :], flat[0, pl.ds(r + STRIP, STRIP), :]
            d, e = flat[1, pl.ds(r, STRIP), :], flat[1, pl.ds(r + STRIP, STRIP), :]
            for m, (a, b) in enumerate(((s + t, d + e), (s - t, d - e))):
                (a_real, a_imag), (b_real, b_imag) = halves(a), halves(b)
                middle[m, pl.ds(r, STRIP), :] = cat([a_real, b_real], 1).astype(BF16)
                middle[m, pl.ds(r + STRIP, STRIP), :] = cat([a_imag, b_imag], 1).astype(BF16)


def left_stage(middle, field, left_ref, way):
    side = middle.shape[1]
    block = side // BLOCKS
    for n in range(BLOCKS):
        for m in range(2):
            x = middle[m]
            field[m, pl.ds(n * block, block), :] = dot(
                left_ref[way, m, pl.ds(n * block, block), :], cat([x, x], 0)
            )
        for r in range(n * block, (n + 1) * block, 2 * STRIP):
            p, u = field[0, pl.ds(r, STRIP), :], field[0, pl.ds(r + STRIP, STRIP), :]
            m, v = field[1, pl.ds(r, STRIP), :], field[1, pl.ds(r + STRIP, STRIP), :]
            for at, real, imag in ((r // 2, p + m, u + v), (side // 2 + r // 2, p - m, u - v)):
                (a, b), (c, d) = halves(real), halves(imag)
                yield at, cat([a + b, a - b], 1), cat([c + d, c - d], 1)


def strip(ref, s, c, at):
    return ref[s, c, pl.ds(at, STRIP), :].astype(F32)


def fourier_right(real, imag, f, inverse):
    r, i, n = f
    up, down = (n, i) if inverse else (i, n)
    x = cat([real, real, imag, imag], 1)
    a = dot(x, cat([r[0], r[1], down[0], down[1]], 0))
    b = dot(x, cat([up[0], up[1], r[0], r[1]], 0))
    return a, b


def fourier_left(real, imag, f, inverse):
    r, i, n = f
    up, down = (n, i) if inverse else (i, n)
    x = cat([real, real, imag, imag], 0)
    a = dot(cat([r[0], r[1], down[0], down[1]], 1), x)
    b = dot(cat([up[0], up[1], r[0], r[1]], 1), x)
    return a, b


def neighbours(g, j, x, h, core):
    d = 4 * g + j
    xy = 2 * x + h
    partners = [(d, 4 * x + 2 * h + 1 - core)]
    for k in range(1, 8):
        partners.append((d, 2 * ((xy + k) % 8) + core))
    for kx in range(4):
        for kj in range(1, 4):
            partners.append((4 * g + (j + kj) % 4, 4 * ((x + kx) % 4) + 2 * h + core))
    return partners


def remote(src, dst, send, recv, device):
    return pltpu.make_async_remote_copy(
        src_ref=src, dst_ref=dst, send_sem=send, recv_sem=recv, device_id=device, device_id_type=MESH
    )


def one_hot(mask):
    return jnp.where(mask, 1.0, 0.0).astype(BF16)


def shifts(columns):
    return lax.broadcasted_iota(jnp.int32, (STRIP, columns), 1) - lax.broadcasted_iota(
        jnp.int32, (STRIP, columns), 0
    )


def fill_rows(ref, offset):
    rows, columns = ref.shape
    lanes = cat([offset] * (columns // 128), 1)
    base = shifts(columns)
    for r in strips(rows):
        ref[pl.ds(r, STRIP), :] = one_hot(base == lanes + r)


def fill_columns(ref, offset, row_of=lambda r: r):
    rows, columns = ref.shape
    lanes = cat([offset] * (columns // 128), 1)
    base = shifts(columns)
    for r in strips(rows):
        ref[pl.ds(r, STRIP), :] = one_hot(base == row_of(r) - lanes)


def kernel(
    off_ref, t_ref, probe_hbm, measured_hbm, right_hbm, left_hbm, transform_hbm, arrived,
    own_offsets, offs, plane, pick_rows, pick_columns, stage, o_ref, stored, sums, flat, middle, field, grads, measured_ref, right_ref, left_ref,
    transform_ref, patches, put_columns, put_rows, wide, partial, sibling_sum, reduced,
    load_sem, s1_send, s1_recv, off_send, off_recv, chip_send, chip_recv, s2_send, s2_recv,
    hop_send, hop_recv, s3_send, s3_recv, back_send, back_recv, s4_send, s4_recv,
):
    g, j, x, h, core = place()
    d = 4 * g + j
    q = 4 * x + 2 * h + core
    xy = 2 * x + h
    last = 3
    sibling = (d, 4 * x + 2 * h + 1 - core)
    win = plane.shape[-1]
    side = o_ref.shape[-1]
    half = side // 2
    count = o_ref.shape[0]
    block = plane.shape[2]
    active = jnp.logical_or(j == core, j == 3 - core)
    mine = jnp.where(j == core, 0, 1)
    ahead = (jnp.minimum(d + 4, 15), q)
    behind = (jnp.maximum(d - 4, 0), q)

    loads = [
        pltpu.make_async_copy(right_hbm, right_ref, load_sem.at[0]),
        pltpu.make_async_copy(left_hbm, left_ref, load_sem.at[1]),
        pltpu.make_async_copy(transform_hbm, transform_ref, load_sem.at[2]),
        pltpu.make_async_copy(measured_hbm.at[mine], measured_ref, load_sem.at[3]),
    ]
    load_probe = pltpu.make_async_copy(probe_hbm, stored.at[0], load_sem.at[4])
    barrier = pltpu.get_barrier_semaphore()
    partners = neighbours(g, j, x, h, core)
    for partner in partners:
        pl.semaphore_signal(barrier, inc=1, device_id=partner, device_id_type=MESH)

    @pl.when(jnp.logical_and(active, g < last))
    def _():
        pl.semaphore_signal(barrier, inc=1, device_id=ahead, device_id_type=MESH)

    @pl.when(jnp.logical_and(active, g > 0))
    def _():
        pl.semaphore_signal(barrier, inc=1, device_id=behind, device_id_type=MESH)

    chained = jnp.where(active, jnp.where(jnp.logical_or(g == 0, g == last), 1, 2), 0)
    for load in loads:
        load.start()
    pl.when(g == 0)(load_probe.start)
    for k in range(4):
        own_offsets[k : k + 1, :] = jnp.full((1, 128), off_ref[k // 2, k % 2], jnp.int32)
        own_offsets[k + 4 : k + 5, :] = jnp.zeros((1, 128), jnp.int32)
    pl.semaphore_wait(barrier, len(partners) + chained)

    for k in (4, 3, 5, 2, 6, 1, 7):
        to = (xy + k) % 8
        tx = to // 2
        remote(
            t_ref.at[tx // 2, tx % 2], plane.at[xy, core], s1_send.at[k], s1_recv.at[k], (d, 2 * to + core)
        ).start()
    for k in range(1, 4):
        to = (x + k) % 4
        remote(
            own_offsets, offs.at[x], off_send.at[k], off_recv.at[k], (d, 4 * to + 2 * h + core)
        ).start()
    own = t_ref.at[x // 2, x % 2]
    remote(own, plane.at[xy, core], chip_send.at[0], chip_recv.at[0], sibling).start()
    plane[xy, core] = t_ref[x // 2, x % 2]
    offs[x] = own_offsets[...]

    for k in (1, 7, 2, 6, 3, 5, 4):
        rows = plane.at[(xy - k + 8) % 8, core]
        remote(rows, rows, s1_send.at[k], s1_recv.at[k], sibling).wait_recv()
        remote(rows, rows, chip_send.at[k], chip_recv.at[k], sibling).start()
    for k in range(1, 4):
        slot = offs.at[(x - k + 4) % 4]
        remote(slot, slot, off_send.at[k], off_recv.at[k], sibling).wait_recv()
    for k in range(8):
        rows = plane.at[(xy - k + 8) % 8, 1 - core]
        remote(rows, rows, chip_send.at[k], chip_recv.at[k], sibling).wait_recv()

    def target(k, i):
        to_j = core if i == 0 else 3 - core
        return to_j, (4 * g + to_j, 4 * ((x + k) % 4) + 2 * h + core)

    own_plane = 2 * j + x // 2
    home = o_ref.at[own_plane, x % 2]
    for i in (1, 0):
        for k in (2, 1, 3, 0):
            slot = 2 * k + i
            position = offs.at[(x + k) % 4]
            fill_rows(pick_rows.at[k % 2], position[2 * i : 2 * i + 1, :])
            fill_columns(pick_columns.at[k % 2], position[2 * i + 1 : 2 * i + 2, :])
            rows = dot(pick_rows[k % 2], plane[...].reshape(win, win)).astype(BF16)
            stage[slot] = dot(rows, pick_columns[k % 2]).astype(BF16)
            to_j, device = target(k, i)
            copy = remote(
                stage.at[slot], home, s2_send.at[slot], s2_recv.at[2 * own_plane + x % 2], device
            )
            if k:
                copy.start()
            else:
                pl.when(to_j != j)(copy.start)

                @pl.when(to_j == j)
                def _():
                    o_ref[own_plane, x % 2] = stage[slot]

    for p in range(8):
        i = p % 2
        fill_rows(put_columns.at[p], offs[p // 2, 2 * i + 1 : 2 * i + 2, :])
        for m in range(2):
            first = 1 - core if m == 0 else core
            fill_columns(
                put_rows.at[m, :, p * side : (p + 1) * side],
                offs[p // 2, 2 * i : 2 * i + 1, :],
                lambda r: r + (r // block + first) * block,
            )

    for load in loads:
        load.wait()
    pl.when(g == 0)(load_probe.wait)
    hop_forward = remote(stored.at[count], stored.at[0], hop_send.at[0], hop_recv.at[0], ahead)
    hop_backward = remote(middle, middle, hop_send.at[1], hop_recv.at[1], behind)

    def owner(s, c):
        return 2 * (s % 2) + c, s // 2

    @pl.when(active)
    def _():
        @pl.when(g > 0)
        def _():
            hop_forward.wait_recv()

        def wait_crop(s):
            for c in range(2):
                from_x, from_j = owner(s, c)
                slot = o_ref.at[s, c]
                copy = remote(slot, slot, s2_send.at[0], s2_recv.at[2 * s + c], sibling)
                pl.when(jnp.logical_or(from_x != x, from_j != j))(copy.wait_recv)

        def enter(s, at, real, imag):
            o_real, o_imag = strip(o_ref, s, 0, at), strip(o_ref, s, 1, at)
            put_sums(
                sums, sums_row(at, side), o_real * real - o_imag * imag, o_real * imag + o_imag * real
            )

        def keep_wave(s, at, real, imag):
            stored[s, 0, pl.ds(at, STRIP), :] = real.astype(BF16)
            stored[s, 1, pl.ds(at, STRIP), :] = imag.astype(BF16)

        def forward(s, carry):
            wait_crop(s + 1)
            for at, real, imag in left_stage(middle, field, left_ref, 0):
                keep_wave(s + 1, at, real, imag)
                enter(s + 1, at, real, imag)
            right_stage(sums, flat, middle, right_ref, 0)
            return carry

        wait_crop(0)
        for at in strips(side):
            enter(0, at, strip(stored, 0, 0, at), strip(stored, 0, 1, at))
        right_stage(sums, flat, middle, right_ref, 0)
        lax.fori_loop(0, count - 1, forward, 0)
        for at, real, imag in left_stage(middle, field, left_ref, 0):
            keep_wave(count, at, real, imag)

        @pl.when(g < last)
        def _():
            hop_forward.start()
            remote(middle, middle, hop_send.at[1], hop_recv.at[1], ahead).wait_recv()

        @pl.when(g == last)
        def _():
            f = [(transform_ref[m, 0], transform_ref[m, 1]) for m in range(3)]
            a, b = fourier_right(stored[count, 0], stored[count, 1], f, False)
            middle[0] = a.astype(BF16)
            middle[1] = b.astype(BF16)
            a, b = fourier_left(middle[0], middle[1], f, False)
            flat[0] = a
            flat[1] = b
            for at in strips(side):
                real, imag = flat[0, pl.ds(at, STRIP), :], flat[1, pl.ds(at, STRIP), :]
                weight = real * real + imag * imag - measured_ref[pl.ds(at, STRIP), :]
                sums[0, pl.ds(at, STRIP), :] = (real * weight).astype(BF16)
                sums[1, pl.ds(at, STRIP), :] = (imag * weight).astype(BF16)
            a, b = fourier_right(sums[0], sums[1], f, True)
            middle[0] = a.astype(BF16)
            middle[1] = b.astype(BF16)
            a, b = fourier_left(middle[0], middle[1], f, True)
            flat[0] = a
            flat[1] = b
            for at in strips(side):
                put_sums(
                    sums, sums_row(at, side), flat[0, pl.ds(at, STRIP), :], flat[1, pl.ds(at, STRIP), :]
                )
            right_stage(sums, flat, middle, right_ref, 1)

        def send_patches(s):
            for c in range(2):
                to_x, to_j = owner(s, c)
                away = jnp.logical_or(to_x != x, to_j != j)
                copy = remote(
                    grads.at[s, c], patches.at[2 * x + mine], s3_send.at[2 * s + c],
                    s3_recv.at[2 * x + mine], (4 * g + to_j, 4 * to_x + 2 * h + core),
                )
                pl.when(away)(copy.start)

                @pl.when(jnp.logical_not(away))
                def _():
                    patches[2 * x + mine] = grads[s, c]

        def leave(s):
            for at, real, imag in left_stage(middle, field, left_ref, 1):
                o_real, o_imag = strip(o_ref, s, 0, at), strip(o_ref, s, 1, at)
                put_sums(
                    sums, sums_row(at, side), o_real * real + o_imag * imag, o_real * imag - o_imag * real
                )
                p_real, p_imag = strip(stored, s, 0, at), strip(stored, s, 1, at)
                grads[s, 0, pl.ds(at, STRIP), :] = (p_real * real + p_imag * imag).astype(BF16)
                grads[s, 1, pl.ds(at, STRIP), :] = (p_real * imag - p_imag * real).astype(BF16)

        def backward(t, carry):
            s = count - 1 - t
            leave(s)
            right_stage(sums, flat, middle, right_ref, 1)
            pl.when(g == 0)(functools.partial(send_patches, s))
            return carry

        lax.fori_loop(0, count - 1, backward, 0)
        leave(0)
        pl.when(g == 0)(functools.partial(send_patches, 0))

        @pl.when(g > 0)
        def _():
            right_stage(sums, flat, middle, right_ref, 1)
            hop_backward.start()
            hop_backward.wait_send()

            def send(t, carry):
                send_patches(count - 1 - t)
                return carry

            lax.fori_loop(0, count, send, 0)

    for i in (1, 0):
        for kx in range(4):
            from_x = (x - kx + 4) % 4
            from_j = core if i == 0 else 3 - core
            p = 2 * from_x + i
            slot = patches.at[p]
            copy = remote(slot, slot, s3_send.at[0], s3_recv.at[p], sibling)
            if kx:
                copy.wait_recv()
            else:
                pl.when(from_j != j)(copy.wait_recv)
            start = pl.multiple_of(p * side, side)
            wide[pl.ds(start, side), :] = dot(slot[...], put_columns[p]).astype(BF16)

    partial[...] = dot(put_rows[0], wide[...]).reshape(partial.shape).astype(BF16)
    chip_copy = remote(partial, sibling_sum, back_send.at[0], back_recv.at[0], sibling)
    chip_copy.start()
    own_rows = dot(put_rows[1], wide[...]).reshape(partial.shape)
    chip_copy.wait_recv()
    reduced[...] = (own_rows + sibling_sum[...].astype(F32)).astype(BF16)
    for k in (4, 3, 5, 2, 6, 1, 7):
        to = (xy + k) % 8
        remote(reduced.at[to], arrived.at[4 * h + x], s4_send.at[k], s4_recv.at[k], (d, 2 * to + core)).start()
    arrived[4 * h + x] = reduced[xy]
    for k in range(1, 8):
        come = (xy - k + 8) % 8
        slot = arrived.at[4 * (come % 2) + come // 2]
        remote(slot, slot, s4_send.at[k], s4_recv.at[k], sibling).wait_recv()

    for k in range(1, 8):
        slot = reduced.at[0]
        remote(slot, slot, s1_send.at[k], s1_recv.at[k], sibling).wait_send()
        remote(slot, slot, s4_send.at[k], s4_recv.at[k], sibling).wait_send()
    for k in range(1, 4):
        remote(own_offsets, own_offsets, off_send.at[k], off_recv.at[k], sibling).wait_send()
    for k in range(8):
        slot = reduced.at[0]
        remote(slot, slot, chip_send.at[k], chip_recv.at[k], sibling).wait_send()
    chip_copy.wait_send()
    for i in range(2):
        for k in range(4):
            slot = 2 * k + i
            to_j, device = target(k, i)
            copy = remote(stage.at[slot], home, s2_send.at[slot], s2_recv.at[0], device)
            if k:
                copy.wait_send()
            else:
                pl.when(to_j != j)(copy.wait_send)

    @pl.when(active)
    def _():
        pl.when(g < last)(hop_forward.wait_send)
        for s in range(count):
            for c in range(2):
                to_x, to_j = owner(s, c)
                slot = grads.at[s, c]
                copy = remote(slot, slot, s3_send.at[2 * s + c], s3_recv.at[0], sibling)
                pl.when(jnp.logical_or(to_x != x, to_j != j))(copy.wait_send)


def per_device(transmission, probe, offsets, measured):
    layers, _, rows, win = transmission.shape
    side = probe.shape[-1]
    group = 4 * layers
    rights, lefts, transforms = tables(side)
    dma = pltpu.SemaphoreType.DMA
    hbm = pl.BlockSpec(memory_space=pl.ANY)
    smem = pl.BlockSpec(memory_space=pltpu.SMEM)
    arrived = pl.pallas_call(
        kernel,
        out_shape=jax.ShapeDtypeStruct((8, rows, win), BF16),
        in_specs=[smem, vmem(), hbm, hbm, hbm, hbm, hbm],
        out_specs=vmem(),
        scratch_shapes=[
            pltpu.VMEM((8, 128), jnp.int32),
            pltpu.VMEM((4, 8, 128), jnp.int32),
            pltpu.VMEM((8, 2, rows, win), BF16),
            pltpu.VMEM((2, side, win), BF16),
            pltpu.VMEM((2, win, side), BF16),
            pltpu.VMEM((8, side, side), BF16),
            pltpu.VMEM((group, 2, side, side), BF16),
            pltpu.VMEM((group + 1, 2, side, side), BF16),
            pltpu.VMEM((2, side, side), BF16),
            pltpu.VMEM((2, side, side), F32),
            pltpu.VMEM((2, side, side), BF16),
            pltpu.VMEM((2, side, side), F32),
            pltpu.VMEM((group, 2, side, side), BF16),
            pltpu.VMEM((side, side), F32),
            pltpu.VMEM(rights.shape, BF16),
            pltpu.VMEM(lefts.shape, BF16),
            pltpu.VMEM(transforms.shape, BF16),
            pltpu.VMEM((8, side, side), BF16),
            pltpu.VMEM((8, side, win), BF16),
            pltpu.VMEM((2, win // 2, 8 * side), BF16),
            pltpu.VMEM((8 * side, win), BF16),
            pltpu.VMEM((8, rows, win), BF16),
            pltpu.VMEM((8, rows, win), BF16),
            pltpu.VMEM((8, rows, win), BF16),
            dma((5,)), dma((8,)), dma((8,)), dma((4,)), dma((4,)), dma((8,)), dma((8,)), dma((8,)),
            dma((16,)), dma((2,)), dma((2,)), dma((16,)), dma((8,)), dma((1,)), dma((1,)), dma((8,)), dma((8,)),
        ],
        compiler_params=pltpu.CompilerParams(
            collective_id=0, has_side_effects=True, vmem_limit_bytes=VMEM_LIMIT
        ),
        name="ptychography_backward",
    )(
        offsets, transmission, probe, measured,
        jnp.asarray(rights), jnp.asarray(lefts), jnp.asarray(transforms),
    )
    parts = arrived.reshape(2, layers, 2, rows, win)
    return parts[0].astype(F32) + parts[1].astype(F32)


def solution(mesh):
    in_specs = (P("depth", None, "pos", None), P(), P("pos", None), P("pos", None, None))
    out_specs = P("depth", None, "pos", None)
    return jax.shard_map(
        per_device, mesh=mesh, in_specs=in_specs, out_specs=out_specs, check_vma=False
    )
```

```python
import functools
import math

import jax
import jax.numpy as jnp
import ml_dtypes
import numpy as np
from jax import lax
from jax.experimental import pallas as pl
from jax.experimental.pallas import tpu as pltpu
from jax.sharding import PartitionSpec as P


MESH = pl.DeviceIdType.MESH
F32 = jnp.float32
BF16 = jnp.bfloat16
VMEM_LIMIT = 56 * 1024 * 1024


def vmem():
    return pl.BlockSpec(memory_space=pltpu.VMEM)


def place():
    d = lax.axis_index("depth")
    q = lax.axis_index("pos")
    return d // 4, d % 4, q // 4, (q // 2) % 2, q % 2


LANES = 128
STRIP = 16
BLOCKS = 2


def hi_lo(table, axis):
    high = table.astype(ml_dtypes.bfloat16)
    low = (table - high.astype(np.float64)).astype(ml_dtypes.bfloat16)
    return np.concatenate([high, low], axis)


def lane_blocks(table):
    rows, columns = table.shape
    return table.reshape(rows, columns // LANES, LANES).transpose(1, 0, 2)


def right_form(matrix):
    return np.block([[matrix.real, matrix.imag], [-matrix.imag, matrix.real]])


@functools.lru_cache(maxsize=None)
def tables(side):
    half = side // 2
    grid = np.arange(side)
    fourier = np.exp(-2j * np.pi * (np.outer(grid, grid) % side) / side) / math.sqrt(side)
    frequency = (grid + half) % side - half
    phase = np.exp(-1j * math.pi * frequency.astype(np.float64) ** 2 / 1024.0)
    circulant = fourier.conj() @ (phase[:, None] * fourier)
    near, far = circulant[:half, :half], circulant[:half, half:]
    forms = [right_form((near + far) / 2), right_form((near - far) / 2)]
    order = grid.reshape(2, half // STRIP, STRIP).transpose(1, 0, 2).reshape(side)
    strided = [m[order][:, order] for m in forms]
    pack = lambda m, axis: lane_blocks(hi_lo(m, axis))
    rights = np.stack([[pack(m, 0) for m in forms], [pack(m.T, 0) for m in forms]])
    lefts = np.stack([[pack(m.T, 1) for m in strided], [pack(m, 1) for m in strided]])
    transforms = np.stack([pack(m, 0) for m in (fourier.real, fourier.imag, -fourier.imag)])
    return rights, lefts, transforms


def dot(a, b):
    return jnp.dot(a, b, preferred_element_type=F32)


def cat(parts, axis):
    return jnp.concatenate(parts, axis)


def wide_read(ref, *index, rows=slice(None)):
    count = ref.shape[len(index)]
    return cat([ref[(*index, n, rows, slice(None))] for n in range(count)], 1)


def wide_write(ref, *index, value, rows=slice(None)):
    for n in range(ref.shape[len(index)]):
        ref[(*index, n, rows, slice(None))] = value[:, n * LANES : (n + 1) * LANES].astype(ref.dtype)


def strips(count):
    return range(0, count, STRIP)


def read(ref, *index, at):
    return tuple(ref[(*index, n, pl.ds(at, STRIP), slice(None))].astype(F32) for n in range(2))


def write(ref, *index, at, value):
    for n in range(2):
        ref[(*index, n, pl.ds(at, STRIP), slice(None))] = value[n].astype(BF16)


def product(a, b, conj_first):
    (ar, ai), (br, bi) = a, b
    parts = list(zip(ar, ai, br, bi))
    if conj_first:
        return [p * r + q * t for p, q, r, t in parts], [p * t - q * r for p, q, r, t in parts]
    return [p * r - q * t for p, q, r, t in parts], [p * t + q * r for p, q, r, t in parts]


def put_sums(ref, at, field):
    for n, (a, b) in enumerate(field):
        ref[0, n, pl.ds(at, STRIP), :] = (a + b).astype(BF16)
        ref[1, n, pl.ds(at, STRIP), :] = (a - b).astype(BF16)


def sums_row(row, side):
    half = side // 2
    return 2 * row if row < half else 2 * (row - half) + STRIP


def lane_half(ref, m, at, n):
    return ref[m, pl.ds(at, STRIP), n * LANES : (n + 1) * LANES]


def right_stage(sums, flat, middle, right_ref, way):
    side = sums.shape[2]
    block = side // BLOCKS
    for n in range(BLOCKS):
        rows = pl.ds(n * block, block)
        for m in range(2):
            x = wide_read(sums, m, rows=rows)
            flat[m, rows, :] = dot(cat([x, x], 1), wide_read(right_ref, way, m))
        for r in range(n * block, (n + 1) * block, 2 * STRIP):
            for lane in range(2):
                for part in range(2):
                    upper, lower = lane_half(flat, lane, r, part), lane_half(flat, lane, r + STRIP, part)
                    at = pl.ds(r + part * STRIP, STRIP)
                    middle[0, lane, at, :] = (upper + lower).astype(BF16)
                    middle[1, lane, at, :] = (upper - lower).astype(BF16)


def left_stage(middle, field, left_ref, way):
    side = middle.shape[2]
    block = side // BLOCKS
    for n in range(BLOCKS):
        rows = pl.ds(n * block, block)
        for m in range(2):
            x = wide_read(middle, m)
            field[m, rows, :] = dot(wide_read(left_ref, way, m, rows=rows), cat([x, x], 0))
        for r in range(n * block, (n + 1) * block, 2 * STRIP):
            upper, lower = [], []
            for part in range(2):
                s, d = (lane_half(field, 0, r + part * STRIP, lane) for lane in range(2))
                t, e = (lane_half(field, 1, r + part * STRIP, lane) for lane in range(2))
                a, b = s + t, d + e
                upper.append((a + b, a - b))
                a, b = s - t, d - e
                lower.append((a + b, a - b))
            yield r // 2, upper
            yield side // 2 + r // 2, lower


def fourier_right(source, f, inverse):
    r, i, n = f
    up, down = (n, i) if inverse else (i, n)
    real, imag = wide_read(source, 0), wide_read(source, 1)
    x = cat([real, real, imag, imag], 1)
    return dot(x, cat([r, down], 0)), dot(x, cat([up, r], 0))


def fourier_left(source, f, inverse):
    r, i, n = f
    half = r.shape[0] // 2
    up, down = (n, i) if inverse else (i, n)
    real, imag = wide_read(source, 0), wide_read(source, 1)
    x = cat([real, real, imag, imag], 0)
    r, up, down = (cat([m[:half], m[half:]], 1) for m in (r, up, down))
    return dot(cat([r, down], 1), x), dot(cat([up, r], 1), x)


def neighbours(g, j, x, h, core):
    d = 4 * g + j
    xy = 2 * x + h
    partners = [(d, 4 * x + 2 * h + 1 - core)]
    for k in range(1, 8):
        partners.append((d, 2 * ((xy + k) % 8) + core))
    for kx in range(4):
        for kj in range(1, 4):
            partners.append((4 * g + (j + kj) % 4, 4 * ((x + kx) % 4) + 2 * h + core))
    return partners


def remote(src, dst, send, recv, device):
    return pltpu.make_async_remote_copy(
        src_ref=src, dst_ref=dst, send_sem=send, recv_sem=recv, device_id=device, device_id_type=MESH
    )


def one_hot(mask):
    return jnp.where(mask, 1.0, 0.0).astype(BF16)


def shift():
    return lax.broadcasted_iota(jnp.int32, (STRIP, LANES), 1) - lax.broadcasted_iota(
        jnp.int32, (STRIP, LANES), 0
    )


def fill_rows(ref, offset):
    base = shift()
    for r in strips(ref.shape[1]):
        for n in range(ref.shape[0]):
            ref[n, pl.ds(r, STRIP), :] = one_hot(base == offset + (r - n * LANES))


def fill_columns(ref, offset, row_of=lambda r: r):
    base = shift()
    for r in strips(ref.shape[1]):
        for n in range(ref.shape[0]):
            ref[n, pl.ds(r, STRIP), :] = one_hot(base == (row_of(r) - n * LANES) - offset)


def kernel(
    off_ref, t_hbm, probe_hbm, measured_hbm, right_hbm, left_hbm, transform_hbm, arrived,
    t_ref, own_offsets, offs, plane, pick_rows, pick_columns, stage, o_ref, stored, sums, flat, middle, field, grads, measured_ref, right_ref, left_ref,
    transform_ref, patches, put_columns, put_rows, wide, partial, sibling_sum, reduced,
    load_sem, s1_send, s1_recv, off_send, off_recv, chip_send, chip_recv, s2_send, s2_recv,
    hop_send, hop_recv, s3_send, s3_recv, back_send, back_recv, s4_send, s4_recv,
):
    g, j, x, h, core = place()
    d = 4 * g + j
    q = 4 * x + 2 * h + core
    xy = 2 * x + h
    last = 3
    sibling = (d, 4 * x + 2 * h + 1 - core)
    block = plane.shape[3]
    win = 16 * block
    side = o_ref.shape[3]
    count = o_ref.shape[0]
    active = jnp.logical_or(j == core, j == 3 - core)
    mine = jnp.where(j == core, 0, 1)
    ahead = (jnp.minimum(d + 4, 15), q)
    behind = (jnp.maximum(d - 4, 0), q)

    loads = [
        pltpu.make_async_copy(right_hbm, right_ref, load_sem.at[0]),
        pltpu.make_async_copy(left_hbm, left_ref, load_sem.at[1]),
        pltpu.make_async_copy(transform_hbm, transform_ref, load_sem.at[2]),
        pltpu.make_async_copy(measured_hbm.at[mine], measured_ref, load_sem.at[3]),
    ]
    load_probe = [
        pltpu.make_async_copy(probe_hbm.at[:, :, n * LANES : (n + 1) * LANES], stored.at[0, :, n], load_sem.at[4 + n])
        for n in range(2)
    ]
    load_rows = [
        pltpu.make_async_copy(t_hbm.at[:, :, :, n * LANES : (n + 1) * LANES], t_ref.at[:, :, n], load_sem.at[6 + n])
        for n in range(4)
    ]
    for load in load_rows:
        load.start()
    barrier = pltpu.get_barrier_semaphore()
    partners = neighbours(g, j, x, h, core)
    for partner in partners:
        pl.semaphore_signal(barrier, inc=1, device_id=partner, device_id_type=MESH)

    @pl.when(jnp.logical_and(active, g < last))
    def _():
        pl.semaphore_signal(barrier, inc=1, device_id=ahead, device_id_type=MESH)

    @pl.when(jnp.logical_and(active, g > 0))
    def _():
        pl.semaphore_signal(barrier, inc=1, device_id=behind, device_id_type=MESH)

    chained = jnp.where(active, jnp.where(jnp.logical_or(g == 0, g == last), 1, 2), 0)
    for load in loads:
        load.start()
    @pl.when(g == 0)
    def _():
        for load in load_probe:
            load.start()

    for k in range(4):
        own_offsets[k : k + 1, :] = jnp.full((1, 128), off_ref[k // 2, k % 2], jnp.int32)
        own_offsets[k + 4 : k + 5, :] = jnp.zeros((1, 128), jnp.int32)
    for load in load_rows:
        load.wait()
    pl.semaphore_wait(barrier, len(partners) + chained)

    for k in (4, 3, 5, 2, 6, 1, 7):
        to = (xy + k) % 8
        tx = to // 2
        remote(
            t_ref.at[tx // 2, tx % 2], plane.at[xy, core], s1_send.at[k], s1_recv.at[k], (d, 2 * to + core)
        ).start()
    for k in range(1, 4):
        to = (x + k) % 4
        remote(
            own_offsets, offs.at[x], off_send.at[k], off_recv.at[k], (d, 4 * to + 2 * h + core)
        ).start()
    own = t_ref.at[x // 2, x % 2]
    remote(own, plane.at[xy, core], chip_send.at[0], chip_recv.at[0], sibling).start()
    plane[xy, core] = t_ref[x // 2, x % 2]
    offs[x] = own_offsets[...]

    for k in (1, 7, 2, 6, 3, 5, 4):
        rows = plane.at[(xy - k + 8) % 8, core]
        remote(rows, rows, s1_send.at[k], s1_recv.at[k], sibling).wait_recv()
        remote(rows, rows, chip_send.at[k], chip_recv.at[k], sibling).start()
    for k in range(1, 4):
        slot = offs.at[(x - k + 4) % 4]
        remote(slot, slot, off_send.at[k], off_recv.at[k], sibling).wait_recv()
    for k in range(8):
        rows = plane.at[(xy - k + 8) % 8, 1 - core]
        remote(rows, rows, chip_send.at[k], chip_recv.at[k], sibling).wait_recv()

    def target(k, i):
        to_j = core if i == 0 else 3 - core
        return to_j, (4 * g + to_j, 4 * ((x + k) % 4) + 2 * h + core)

    own_plane = 2 * j + x // 2
    home = o_ref.at[own_plane, x % 2]
    for i in (1, 0):
        for k in (2, 1, 3, 0):
            slot = 2 * k + i
            position = offs.at[(x + k) % 4]
            fill_rows(pick_rows.at[k % 2], position[2 * i : 2 * i + 1, :])
            fill_columns(pick_columns.at[k % 2], position[2 * i + 1 : 2 * i + 2, :])
            field_rows = cat([plane[:, :, n].reshape(win, LANES) for n in range(4)], 1)
            rows = dot(wide_read(pick_rows, k % 2), field_rows).astype(BF16)
            wide_write(stage, slot, value=dot(rows, wide_read(pick_columns, k % 2)))
            to_j, device = target(k, i)
            copy = remote(
                stage.at[slot], home, s2_send.at[slot], s2_recv.at[2 * own_plane + x % 2], device
            )
            if k:
                copy.start()
            else:
                pl.when(to_j != j)(copy.start)

                @pl.when(to_j == j)
                def _():
                    o_ref[own_plane, x % 2] = stage[slot]

    for p in range(8):
        i = p % 2
        fill_rows(put_columns.at[p], offs[p // 2, 2 * i + 1 : 2 * i + 2, :])
        for m in range(2):
            first = 1 - core if m == 0 else core
            fill_columns(
                put_rows.at[m, 2 * p : 2 * p + 2],
                offs[p // 2, 2 * i : 2 * i + 1, :],
                lambda r: r + (r // block + first) * block,
            )

    for load in loads:
        load.wait()
    @pl.when(g == 0)
    def _():
        for load in load_probe:
            load.wait()

    hop_forward = remote(stored.at[count], stored.at[0], hop_send.at[0], hop_recv.at[0], ahead)
    hop_backward = remote(middle, middle, hop_send.at[1], hop_recv.at[1], behind)

    def owner(s, c):
        return 2 * (s % 2) + c, s // 2

    @pl.when(active)
    def _():
        @pl.when(g > 0)
        def _():
            hop_forward.wait_recv()

        def wait_crop(s):
            for c in range(2):
                from_x, from_j = owner(s, c)
                slot = o_ref.at[s, c]
                copy = remote(slot, slot, s2_send.at[0], s2_recv.at[2 * s + c], sibling)
                pl.when(jnp.logical_or(from_x != x, from_j != j))(copy.wait_recv)

        def pair(ref, s, at):
            return read(ref, s, 0, at=at), read(ref, s, 1, at=at)

        def keep(ref, s, at, value):
            for c in range(2):
                write(ref, s, c, at=at, value=value[c])

        def enter(s, at, wave):
            put_sums(sums, sums_row(at, side), product(pair(o_ref, s, at), wave, False))

        def forward(s, carry):
            wait_crop(s + 1)
            for at, wave in left_stage(middle, field, left_ref, 0):
                keep(stored, s + 1, at, wave)
                enter(s + 1, at, wave)
            right_stage(sums, flat, middle, right_ref, 0)
            return carry

        wait_crop(0)
        for at in strips(side):
            enter(0, at, pair(stored, 0, at))
        right_stage(sums, flat, middle, right_ref, 0)
        lax.fori_loop(0, count - 1, forward, 0)
        for at, wave in left_stage(middle, field, left_ref, 0):
            keep(stored, count, at, wave)

        @pl.when(g < last)
        def _():
            hop_forward.start()
            remote(middle, middle, hop_send.at[1], hop_recv.at[1], ahead).wait_recv()

        @pl.when(g == last)
        def _():
            f = [wide_read(transform_ref, m) for m in range(3)]

            def both(ref, values):
                for m in range(2):
                    if ref is flat:
                        ref[m] = values[m]
                    else:
                        wide_write(ref, m, value=values[m])

            def from_flat(at):
                return [tuple(lane_half(flat, m, at, n) for n in range(2)) for m in range(2)]

            both(middle, fourier_right(stored.at[count], f, False))
            both(flat, fourier_left(middle, f, False))
            for at in strips(side):
                real, imag = from_flat(at)
                for n in range(2):
                    target_part = measured_ref[pl.ds(at, STRIP), n * LANES : (n + 1) * LANES]
                    weight = real[n] * real[n] + imag[n] * imag[n] - target_part
                    sums[0, n, pl.ds(at, STRIP), :] = (real[n] * weight).astype(BF16)
                    sums[1, n, pl.ds(at, STRIP), :] = (imag[n] * weight).astype(BF16)
            both(middle, fourier_right(sums, f, True))
            both(flat, fourier_left(middle, f, True))
            for at in strips(side):
                put_sums(sums, sums_row(at, side), from_flat(at))
            right_stage(sums, flat, middle, right_ref, 1)

        def send_patches(s):
            for c in range(2):
                to_x, to_j = owner(s, c)
                away = jnp.logical_or(to_x != x, to_j != j)
                copy = remote(
                    grads.at[s, c], patches.at[2 * x + mine], s3_send.at[2 * s + c],
                    s3_recv.at[2 * x + mine], (4 * g + to_j, 4 * to_x + 2 * h + core),
                )
                pl.when(away)(copy.start)

                @pl.when(jnp.logical_not(away))
                def _():
                    patches[2 * x + mine] = grads[s, c]

        def leave(s):
            for at, back in left_stage(middle, field, left_ref, 1):
                put_sums(sums, sums_row(at, side), product(pair(o_ref, s, at), back, True))
                keep(grads, s, at, product(pair(stored, s, at), back, True))

        def backward(t, carry):
            s = count - 1 - t
            leave(s)
            right_stage(sums, flat, middle, right_ref, 1)
            pl.when(g == 0)(functools.partial(send_patches, s))
            return carry

        lax.fori_loop(0, count - 1, backward, 0)
        leave(0)
        pl.when(g == 0)(functools.partial(send_patches, 0))

        @pl.when(g > 0)
        def _():
            right_stage(sums, flat, middle, right_ref, 1)
            hop_backward.start()
            hop_backward.wait_send()

            def send(t, carry):
                send_patches(count - 1 - t)
                return carry

            lax.fori_loop(0, count, send, 0)

    for i in (1, 0):
        for kx in range(4):
            from_x = (x - kx + 4) % 4
            from_j = core if i == 0 else 3 - core
            p = 2 * from_x + i
            slot = patches.at[p]
            copy = remote(slot, slot, s3_send.at[0], s3_recv.at[p], sibling)
            if kx:
                copy.wait_recv()
            else:
                pl.when(from_j != j)(copy.wait_recv)
            start = pl.ds(pl.multiple_of(p * side, side), side)
            wide_write(wide, value=dot(wide_read(patches, p), wide_read(put_columns, p)), rows=start)

    placed = wide_read(wide)
    partial[...] = dot(wide_read(put_rows, 0), placed).reshape(partial.shape).astype(BF16)
    chip_copy = remote(partial, sibling_sum, back_send.at[0], back_recv.at[0], sibling)
    chip_copy.start()
    own_rows = dot(wide_read(put_rows, 1), placed).reshape(partial.shape)
    chip_copy.wait_recv()
    reduced[...] = (own_rows + sibling_sum[...].astype(F32)).astype(BF16)
    for k in (4, 3, 5, 2, 6, 1, 7):
        to = (xy + k) % 8
        remote(reduced.at[to], arrived.at[4 * h + x], s4_send.at[k], s4_recv.at[k], (d, 2 * to + core)).start()
    arrived[4 * h + x] = reduced[xy]
    for k in range(1, 8):
        come = (xy - k + 8) % 8
        slot = arrived.at[4 * (come % 2) + come // 2]
        remote(slot, slot, s4_send.at[k], s4_recv.at[k], sibling).wait_recv()

    for k in range(1, 8):
        slot = reduced.at[0]
        remote(slot, slot, s1_send.at[k], s1_recv.at[k], sibling).wait_send()
        remote(slot, slot, s4_send.at[k], s4_recv.at[k], sibling).wait_send()
    for k in range(1, 4):
        remote(own_offsets, own_offsets, off_send.at[k], off_recv.at[k], sibling).wait_send()
    for k in range(8):
        slot = reduced.at[0]
        remote(slot, slot, chip_send.at[k], chip_recv.at[k], sibling).wait_send()
    chip_copy.wait_send()
    for i in range(2):
        for k in range(4):
            slot = 2 * k + i
            to_j, device = target(k, i)
            copy = remote(stage.at[slot], home, s2_send.at[slot], s2_recv.at[0], device)
            if k:
                copy.wait_send()
            else:
                pl.when(to_j != j)(copy.wait_send)

    @pl.when(active)
    def _():
        pl.when(g < last)(hop_forward.wait_send)
        for s in range(count):
            for c in range(2):
                to_x, to_j = owner(s, c)
                slot = grads.at[s, c]
                copy = remote(slot, slot, s3_send.at[2 * s + c], s3_recv.at[0], sibling)
                pl.when(jnp.logical_or(to_x != x, to_j != j))(copy.wait_send)


def per_device(transmission, probe, offsets, measured):
    layers, _, rows, win = transmission.shape
    side = probe.shape[-1]
    group = 4 * layers
    rights, lefts, transforms = tables(side)
    dma = pltpu.SemaphoreType.DMA
    hbm = pl.BlockSpec(memory_space=pl.ANY)
    smem = pl.BlockSpec(memory_space=pltpu.SMEM)
    arrived = pl.pallas_call(
        kernel,
        out_shape=jax.ShapeDtypeStruct((8, rows, win), BF16),
        in_specs=[smem, hbm, hbm, hbm, hbm, hbm, hbm],
        out_specs=vmem(),
        scratch_shapes=[
            pltpu.VMEM((layers, 2, 4, rows, LANES), BF16),
            pltpu.VMEM((8, LANES), jnp.int32),
            pltpu.VMEM((4, 8, LANES), jnp.int32),
            pltpu.VMEM((8, 2, 4, rows, LANES), BF16),
            pltpu.VMEM((2, 4, side, LANES), BF16),
            pltpu.VMEM((2, 2, win, LANES), BF16),
            pltpu.VMEM((8, 2, side, LANES), BF16),
            pltpu.VMEM((group, 2, 2, side, LANES), BF16),
            pltpu.VMEM((group + 1, 2, 2, side, LANES), BF16),
            pltpu.VMEM((2, 2, side, LANES), BF16),
            pltpu.VMEM((2, side, side), F32),
            pltpu.VMEM((2, 2, side, LANES), BF16),
            pltpu.VMEM((2, side, side), F32),
            pltpu.VMEM((group, 2, 2, side, LANES), BF16),
            pltpu.VMEM((side, side), F32),
            pltpu.VMEM(rights.shape, BF16),
            pltpu.VMEM(lefts.shape, BF16),
            pltpu.VMEM(transforms.shape, BF16),
            pltpu.VMEM((8, 2, side, LANES), BF16),
            pltpu.VMEM((8, 4, side, LANES), BF16),
            pltpu.VMEM((2, 16, win // 2, LANES), BF16),
            pltpu.VMEM((4, 8 * side, LANES), BF16),
            pltpu.VMEM((8, rows, win), BF16),
            pltpu.VMEM((8, rows, win), BF16),
            pltpu.VMEM((8, rows, win), BF16),
            dma((10,)), dma((8,)), dma((8,)), dma((4,)), dma((4,)), dma((8,)), dma((8,)), dma((8,)),
            dma((16,)), dma((2,)), dma((2,)), dma((16,)), dma((8,)), dma((1,)), dma((1,)), dma((8,)), dma((8,)),
        ],
        compiler_params=pltpu.CompilerParams(
            collective_id=0, has_side_effects=True, vmem_limit_bytes=VMEM_LIMIT
        ),
        name="ptychography_backward",
    )(
        offsets, transmission, probe, measured,
        jnp.asarray(rights), jnp.asarray(lefts), jnp.asarray(transforms),
    )
    parts = arrived.reshape(2, layers, 2, rows, win)
    return parts[0].astype(F32) + parts[1].astype(F32)


def solution(mesh):
    in_specs = (P("depth", None, "pos", None), P(), P("pos", None), P("pos", None, None))
    out_specs = P("depth", None, "pos", None)
    return jax.shard_map(
        per_device, mesh=mesh, in_specs=in_specs, out_specs=out_specs, check_vma=False
    )
```

```python
import functools
import math

import jax
import jax.numpy as jnp
import ml_dtypes
import numpy as np
from jax import lax
from jax.experimental import pallas as pl
from jax.experimental.pallas import tpu as pltpu
from jax.sharding import PartitionSpec as P


MESH = pl.DeviceIdType.MESH
F32 = jnp.float32
BF16 = jnp.bfloat16
VMEM_LIMIT = 56 * 1024 * 1024


def vmem():
    return pl.BlockSpec(memory_space=pltpu.VMEM)


def place():
    d = lax.axis_index("depth")
    q = lax.axis_index("pos")
    return d // 4, d % 4, q // 4, (q // 2) % 2, q % 2


def hi_lo(table, axis):
    high = table.astype(ml_dtypes.bfloat16)
    low = (table - high.astype(np.float64)).astype(ml_dtypes.bfloat16)
    return np.concatenate([high, low], axis)


def right_form(matrix):
    return np.block([[matrix.real, matrix.imag], [-matrix.imag, matrix.real]])


@functools.lru_cache(maxsize=None)
def tables(side):
    half = side // 2
    grid = np.arange(side)
    fourier = np.exp(-2j * np.pi * (np.outer(grid, grid) % side) / side) / math.sqrt(side)
    frequency = (grid + half) % side - half
    phase = np.exp(-1j * math.pi * frequency.astype(np.float64) ** 2 / 1024.0)
    circulant = fourier.conj() @ (phase[:, None] * fourier)
    near, far = circulant[:half, :half], circulant[:half, half:]
    forms = [right_form((near + far) / 2), right_form((near - far) / 2)]
    rights = np.stack([[hi_lo(m, 0) for m in forms], [hi_lo(m.T, 0) for m in forms]])
    order = grid.reshape(2, half // STRIP, STRIP).transpose(1, 0, 2).reshape(side)
    strided = [m[order][:, order] for m in forms]

    def strip_pairs(table):
        parts = hi_lo(table, 0).reshape(2, side // STRIP, STRIP, side)
        return parts.transpose(1, 0, 2, 3).reshape(2 * side, side)

    lefts = np.stack([[strip_pairs(m.T) for m in strided], [strip_pairs(m) for m in strided]])
    transforms = np.stack([hi_lo(m, 0) for m in (fourier.real, fourier.imag, -fourier.imag)])
    return rights, lefts, transforms.reshape(3, 2, side, side)


def dot(a, b):
    return jnp.dot(a, b, preferred_element_type=F32)


def cat(parts, axis):
    return jnp.concatenate(parts, axis)


STRIP = 16


def strips(count):
    return range(0, count, STRIP)


def halves(value):
    middle = value.shape[1] // 2
    return value[:, :middle], value[:, middle:]


def put_sums(ref, at, real, imag):
    (a, b), (c, d) = halves(real), halves(imag)
    ref[0, pl.ds(at, STRIP), :] = cat([a + b, c + d], 1).astype(BF16)
    ref[1, pl.ds(at, STRIP), :] = cat([a - b, c - d], 1).astype(BF16)


def sums_row(row, side):
    half = side // 2
    return 2 * row if row < half else 2 * (row - half) + STRIP


def right_stage(sums, flat, middle, right_ref, way):
    side = sums.shape[1]
    for m in range(2):
        x = sums[m]
        flat[m] = dot(cat([x, x], 1), right_ref[way, m])
    for r in range(0, side, 2 * STRIP):
        s, t = flat[0, pl.ds(r, STRIP), :], flat[0, pl.ds(r + STRIP, STRIP), :]
        d, e = flat[1, pl.ds(r, STRIP), :], flat[1, pl.ds(r + STRIP, STRIP), :]
        for m, (a, b) in enumerate(((s + t, d + e), (s - t, d - e))):
            (a_real, a_imag), (b_real, b_imag) = halves(a), halves(b)
            middle[m, pl.ds(r, STRIP), :] = cat([a_real, b_real], 1).astype(BF16)
            middle[m, pl.ds(r + STRIP, STRIP), :] = cat([a_imag, b_imag], 1).astype(BF16)


def left_stage(middle, field, left_ref, way):
    side = middle.shape[1]
    for m in range(2):
        field[m] = dot(left_ref[way, m], middle[m])

    def total(m, r):
        return field[m, pl.ds(2 * r, STRIP), :] + field[m, pl.ds(2 * r + STRIP, STRIP), :]

    for r in range(0, side, 2 * STRIP):
        p, u = total(0, r), total(0, r + STRIP)
        m, v = total(1, r), total(1, r + STRIP)
        for at, real, imag in ((r // 2, p + m, u + v), (side // 2 + r // 2, p - m, u - v)):
            (a, b), (c, d) = halves(real), halves(imag)
            yield at, cat([a + b, a - b], 1), cat([c + d, c - d], 1)


def strip(ref, s, c, at):
    return ref[s, c, pl.ds(at, STRIP), :].astype(F32)


def fourier_right(real, imag, f, inverse):
    r, i, n = f
    up, down = (n, i) if inverse else (i, n)
    x = cat([real, real, imag, imag], 1)
    a = dot(x, cat([r[0], r[1], down[0], down[1]], 0))
    b = dot(x, cat([up[0], up[1], r[0], r[1]], 0))
    return a, b


def fourier_left(real, imag, f, inverse):
    r, i, n = f
    up, down = (n, i) if inverse else (i, n)
    x = cat([real, real, imag, imag], 0)
    a = dot(cat([r[0], r[1], down[0], down[1]], 1), x)
    b = dot(cat([up[0], up[1], r[0], r[1]], 1), x)
    return a, b


def neighbours(g, j, x, h, core):
    d = 4 * g + j
    xy = 2 * x + h
    partners = [(d, 4 * x + 2 * h + 1 - core)]
    for k in range(1, 8):
        partners.append((d, 2 * ((xy + k) % 8) + core))
    for kx in range(4):
        for kj in range(1, 4):
            partners.append((4 * g + (j + kj) % 4, 4 * ((x + kx) % 4) + 2 * h + core))
    return partners


def remote(src, dst, send, recv, device):
    return pltpu.make_async_remote_copy(
        src_ref=src, dst_ref=dst, send_sem=send, recv_sem=recv, device_id=device, device_id_type=MESH
    )


def one_hot(mask):
    return jnp.where(mask, 1.0, 0.0).astype(BF16)


def shifts(columns):
    return lax.broadcasted_iota(jnp.int32, (STRIP, columns), 1) - lax.broadcasted_iota(
        jnp.int32, (STRIP, columns), 0
    )


def fill_rows(ref, offset):
    rows, columns = ref.shape
    lanes = cat([offset] * (columns // 128), 1)
    base = shifts(columns)
    for r in strips(rows):
        ref[pl.ds(r, STRIP), :] = one_hot(base == lanes + r)


def fill_columns(ref, offset, row_of=lambda r: r):
    rows, columns = ref.shape
    lanes = cat([offset] * (columns // 128), 1)
    base = shifts(columns)
    for r in strips(rows):
        ref[pl.ds(r, STRIP), :] = one_hot(base == row_of(r) - lanes)


def kernel(
    off_ref, t_ref, probe_hbm, measured_hbm, right_hbm, left_hbm, transform_hbm, arrived,
    own_offsets, offs, plane, pick_rows, pick_columns, stage, o_ref, stored, sums, flat, middle, field, grads, measured_ref, right_ref, left_ref,
    transform_ref, patches, put_columns, put_rows, wide, partial, sibling_sum, reduced,
    load_sem, s1_send, s1_recv, off_send, off_recv, chip_send, chip_recv, s2_send, s2_recv,
    hop_send, hop_recv, s3_send, s3_recv, back_send, back_recv, s4_send, s4_recv,
):
    g, j, x, h, core = place()
    d = 4 * g + j
    q = 4 * x + 2 * h + core
    xy = 2 * x + h
    last = 3
    sibling = (d, 4 * x + 2 * h + 1 - core)
    win = plane.shape[-1]
    side = o_ref.shape[-1]
    half = side // 2
    count = o_ref.shape[0]
    block = plane.shape[2]
    active = jnp.logical_or(j == core, j == 3 - core)
    mine = jnp.where(j == core, 0, 1)
    ahead = (jnp.minimum(d + 4, 15), q)
    behind = (jnp.maximum(d - 4, 0), q)

    loads = [
        pltpu.make_async_copy(right_hbm, right_ref, load_sem.at[0]),
        pltpu.make_async_copy(left_hbm, left_ref, load_sem.at[1]),
        pltpu.make_async_copy(transform_hbm, transform_ref, load_sem.at[2]),
        pltpu.make_async_copy(measured_hbm.at[mine], measured_ref, load_sem.at[3]),
    ]
    load_probe = pltpu.make_async_copy(probe_hbm, stored.at[0], load_sem.at[4])
    barrier = pltpu.get_barrier_semaphore()
    partners = neighbours(g, j, x, h, core)
    for partner in partners:
        pl.semaphore_signal(barrier, inc=1, device_id=partner, device_id_type=MESH)

    @pl.when(jnp.logical_and(active, g < last))
    def _():
        pl.semaphore_signal(barrier, inc=1, device_id=ahead, device_id_type=MESH)

    @pl.when(jnp.logical_and(active, g > 0))
    def _():
        pl.semaphore_signal(barrier, inc=1, device_id=behind, device_id_type=MESH)

    chained = jnp.where(active, jnp.where(jnp.logical_or(g == 0, g == last), 1, 2), 0)
    for load in loads:
        load.start()
    pl.when(g == 0)(load_probe.start)
    for k in range(4):
        own_offsets[k : k + 1, :] = jnp.full((1, 128), off_ref[k // 2, k % 2], jnp.int32)
        own_offsets[k + 4 : k + 5, :] = jnp.zeros((1, 128), jnp.int32)
    pl.semaphore_wait(barrier, len(partners) + chained)

    for k in range(1, 4):
        to = (x + k) % 4
        remote(
            own_offsets, offs.at[x], off_send.at[k], off_recv.at[k], (d, 4 * to + 2 * h + core)
        ).start()
    for k in (4, 3, 5, 2, 6, 1, 7):
        to = (xy + k) % 8
        tx = to // 2
        remote(
            t_ref.at[tx // 2, tx % 2], plane.at[xy, core], s1_send.at[k], s1_recv.at[k], (d, 2 * to + core)
        ).start()
    own = t_ref.at[x // 2, x % 2]
    remote(own, plane.at[xy, core], chip_send.at[0], chip_recv.at[0], sibling).start()
    plane[xy, core] = t_ref[x // 2, x % 2]
    offs[x] = own_offsets[...]

    for k in range(4):
        if k:
            slot = offs.at[(x - k + 4) % 4]
            remote(slot, slot, off_send.at[k], off_recv.at[k], sibling).wait_recv()
        for i in range(2):
            from_x = (x - k + 4) % 4
            slot = 2 * ((4 - k) % 4) + i
            row, column = offs[from_x, 2 * i : 2 * i + 1, :], offs[from_x, 2 * i + 1 : 2 * i + 2, :]
            fill_rows(pick_rows.at[slot], row)
            fill_columns(pick_columns.at[slot], column)
            fill_rows(put_columns.at[slot], column)
            for m in range(2):
                first = 1 - core if m == 0 else core
                fill_columns(
                    put_rows.at[m, :, slot * side : (slot + 1) * side],
                    row,
                    lambda r: r + (r // block + first) * block,
                )

    for k in (1, 7, 2, 6, 3, 5, 4):
        rows = plane.at[(xy - k + 8) % 8, core]
        remote(rows, rows, s1_send.at[k], s1_recv.at[k], sibling).wait_recv()
        remote(rows, rows, chip_send.at[k], chip_recv.at[k], sibling).start()
    for k in range(8):
        rows = plane.at[(xy - k + 8) % 8, 1 - core]
        remote(rows, rows, chip_send.at[k], chip_recv.at[k], sibling).wait_recv()

    def target(k, i):
        to_j = core if i == 0 else 3 - core
        return to_j, (4 * g + to_j, 4 * ((x + k) % 4) + 2 * h + core)

    own_plane = 2 * j + x // 2
    home = o_ref.at[own_plane, x % 2]
    for i in (1, 0):
        for k in (2, 1, 3, 0):
            slot = 2 * k + i
            rows = dot(pick_rows[slot], plane[...].reshape(win, win)).astype(BF16)
            stage[slot] = dot(rows, pick_columns[slot]).astype(BF16)
            to_j, device = target(k, i)
            copy = remote(
                stage.at[slot], home, s2_send.at[slot], s2_recv.at[2 * own_plane + x % 2], device
            )
            if k:
                copy.start()
            else:
                pl.when(to_j != j)(copy.start)

                @pl.when(to_j == j)
                def _():
                    o_ref[own_plane, x % 2] = stage[slot]

    for load in loads:
        load.wait()
    pl.when(g == 0)(load_probe.wait)
    hop_forward = remote(stored.at[count], stored.at[0], hop_send.at[0], hop_recv.at[0], ahead)
    hop_backward = remote(middle, middle, hop_send.at[1], hop_recv.at[1], behind)

    def owner(s, c):
        return 2 * (s % 2) + c, s // 2

    @pl.when(active)
    def _():
        @pl.when(g > 0)
        def _():
            hop_forward.wait_recv()

        def wait_crop(s):
            for c in range(2):
                from_x, from_j = owner(s, c)
                slot = o_ref.at[s, c]
                copy = remote(slot, slot, s2_send.at[0], s2_recv.at[2 * s + c], sibling)
                pl.when(jnp.logical_or(from_x != x, from_j != j))(copy.wait_recv)

        def enter(s, at, real, imag):
            o_real, o_imag = strip(o_ref, s, 0, at), strip(o_ref, s, 1, at)
            put_sums(
                sums, sums_row(at, side), o_real * real - o_imag * imag, o_real * imag + o_imag * real
            )

        def keep_wave(s, at, real, imag):
            stored[s, 0, pl.ds(at, STRIP), :] = real.astype(BF16)
            stored[s, 1, pl.ds(at, STRIP), :] = imag.astype(BF16)

        def forward(s, carry):
            wait_crop(s + 1)
            for at, real, imag in left_stage(middle, field, left_ref, 0):
                keep_wave(s + 1, at, real, imag)
                enter(s + 1, at, real, imag)
            right_stage(sums, flat, middle, right_ref, 0)
            return carry

        wait_crop(0)
        for at in strips(side):
            enter(0, at, strip(stored, 0, 0, at), strip(stored, 0, 1, at))
        right_stage(sums, flat, middle, right_ref, 0)
        lax.fori_loop(0, count - 1, forward, 0)
        for at, real, imag in left_stage(middle, field, left_ref, 0):
            keep_wave(count, at, real, imag)

        @pl.when(g < last)
        def _():
            hop_forward.start()
            remote(middle, middle, hop_send.at[1], hop_recv.at[1], ahead).wait_recv()

        @pl.when(g == last)
        def _():
            f = [(transform_ref[m, 0], transform_ref[m, 1]) for m in range(3)]
            a, b = fourier_right(stored[count, 0], stored[count, 1], f, False)
            middle[0] = a.astype(BF16)
            middle[1] = b.astype(BF16)
            a, b = fourier_left(middle[0], middle[1], f, False)
            flat[0] = a
            flat[1] = b
            for at in strips(side):
                real, imag = flat[0, pl.ds(at, STRIP), :], flat[1, pl.ds(at, STRIP), :]
                weight = real * real + imag * imag - measured_ref[pl.ds(at, STRIP), :]
                sums[0, pl.ds(at, STRIP), :] = (real * weight).astype(BF16)
                sums[1, pl.ds(at, STRIP), :] = (imag * weight).astype(BF16)
            a, b = fourier_right(sums[0], sums[1], f, True)
            middle[0] = a.astype(BF16)
            middle[1] = b.astype(BF16)
            a, b = fourier_left(middle[0], middle[1], f, True)
            flat[0] = a
            flat[1] = b
            for at in strips(side):
                put_sums(
                    sums, sums_row(at, side), flat[0, pl.ds(at, STRIP), :], flat[1, pl.ds(at, STRIP), :]
                )
            right_stage(sums, flat, middle, right_ref, 1)

        def send_patches(s):
            for c in range(2):
                to_x, to_j = owner(s, c)
                away = jnp.logical_or(to_x != x, to_j != j)
                copy = remote(
                    grads.at[s, c], patches.at[2 * x + mine], s3_send.at[2 * s + c],
                    s3_recv.at[2 * x + mine], (4 * g + to_j, 4 * to_x + 2 * h + core),
                )
                pl.when(away)(copy.start)

                @pl.when(jnp.logical_not(away))
                def _():
                    patches[2 * x + mine] = grads[s, c]

        def leave(s):
            for at, real, imag in left_stage(middle, field, left_ref, 1):
                o_real, o_imag = strip(o_ref, s, 0, at), strip(o_ref, s, 1, at)
                put_sums(
                    sums, sums_row(at, side), o_real * real + o_imag * imag, o_real * imag - o_imag * real
                )
                p_real, p_imag = strip(stored, s, 0, at), strip(stored, s, 1, at)
                grads[s, 0, pl.ds(at, STRIP), :] = (p_real * real + p_imag * imag).astype(BF16)
                grads[s, 1, pl.ds(at, STRIP), :] = (p_real * imag - p_imag * real).astype(BF16)

        def backward(t, carry):
            s = count - 1 - t
            leave(s)
            right_stage(sums, flat, middle, right_ref, 1)
            pl.when(g == 0)(functools.partial(send_patches, s))
            return carry

        lax.fori_loop(0, count - 1, backward, 0)
        leave(0)
        pl.when(g == 0)(functools.partial(send_patches, 0))

        @pl.when(g > 0)
        def _():
            right_stage(sums, flat, middle, right_ref, 1)
            hop_backward.start()
            hop_backward.wait_send()

            def send(t, carry):
                send_patches(count - 1 - t)
                return carry

            lax.fori_loop(0, count, send, 0)

    for i in (1, 0):
        for kx in range(4):
            from_x = (x - kx + 4) % 4
            from_j = core if i == 0 else 3 - core
            p = 2 * from_x + i
            slot = patches.at[p]
            copy = remote(slot, slot, s3_send.at[0], s3_recv.at[p], sibling)
            if kx:
                copy.wait_recv()
            else:
                pl.when(from_j != j)(copy.wait_recv)
            at = 2 * ((4 - kx) % 4) + i
            wide[at * side : (at + 1) * side, :] = dot(slot[...], put_columns[at]).astype(BF16)

    partial[...] = dot(put_rows[0], wide[...]).reshape(partial.shape).astype(BF16)
    chip_copy = remote(partial, sibling_sum, back_send.at[0], back_recv.at[0], sibling)
    chip_copy.start()
    own_rows = dot(put_rows[1], wide[...]).reshape(partial.shape)
    chip_copy.wait_recv()
    reduced[...] = (own_rows + sibling_sum[...].astype(F32)).astype(BF16)
    for k in (4, 3, 5, 2, 6, 1, 7):
        to = (xy + k) % 8
        remote(reduced.at[to], arrived.at[4 * h + x], s4_send.at[k], s4_recv.at[k], (d, 2 * to + core)).start()
    arrived[4 * h + x] = reduced[xy]
    for k in range(1, 8):
        come = (xy - k + 8) % 8
        slot = arrived.at[4 * (come % 2) + come // 2]
        remote(slot, slot, s4_send.at[k], s4_recv.at[k], sibling).wait_recv()

    for k in range(1, 8):
        slot = reduced.at[0]
        remote(slot, slot, s1_send.at[k], s1_recv.at[k], sibling).wait_send()
        remote(slot, slot, s4_send.at[k], s4_recv.at[k], sibling).wait_send()
    for k in range(1, 4):
        remote(own_offsets, own_offsets, off_send.at[k], off_recv.at[k], sibling).wait_send()
    for k in range(8):
        slot = reduced.at[0]
        remote(slot, slot, chip_send.at[k], chip_recv.at[k], sibling).wait_send()
    chip_copy.wait_send()
    for i in range(2):
        for k in range(4):
            slot = 2 * k + i
            to_j, device = target(k, i)
            copy = remote(stage.at[slot], home, s2_send.at[slot], s2_recv.at[0], device)
            if k:
                copy.wait_send()
            else:
                pl.when(to_j != j)(copy.wait_send)

    @pl.when(active)
    def _():
        pl.when(g < last)(hop_forward.wait_send)
        for s in range(count):
            for c in range(2):
                to_x, to_j = owner(s, c)
                slot = grads.at[s, c]
                copy = remote(slot, slot, s3_send.at[2 * s + c], s3_recv.at[0], sibling)
                pl.when(jnp.logical_or(to_x != x, to_j != j))(copy.wait_send)


def per_device(transmission, probe, offsets, measured):
    layers, _, rows, win = transmission.shape
    side = probe.shape[-1]
    group = 4 * layers
    rights, lefts, transforms = tables(side)
    dma = pltpu.SemaphoreType.DMA
    hbm = pl.BlockSpec(memory_space=pl.ANY)
    smem = pl.BlockSpec(memory_space=pltpu.SMEM)
    arrived = pl.pallas_call(
        kernel,
        out_shape=jax.ShapeDtypeStruct((8, rows, win), BF16),
        in_specs=[smem, vmem(), hbm, hbm, hbm, hbm, hbm],
        out_specs=vmem(),
        scratch_shapes=[
            pltpu.VMEM((8, 128), jnp.int32),
            pltpu.VMEM((4, 8, 128), jnp.int32),
            pltpu.VMEM((8, 2, rows, win), BF16),
            pltpu.VMEM((8, side, win), BF16),
            pltpu.VMEM((8, win, side), BF16),
            pltpu.VMEM((8, side, side), BF16),
            pltpu.VMEM((group, 2, side, side), BF16),
            pltpu.VMEM((group + 1, 2, side, side), BF16),
            pltpu.VMEM((2, side, side), BF16),
            pltpu.VMEM((2, side, side), F32),
            pltpu.VMEM((2, side, side), BF16),
            pltpu.VMEM((2, 2 * side, side), F32),
            pltpu.VMEM((group, 2, side, side), BF16),
            pltpu.VMEM((side, side), F32),
            pltpu.VMEM(rights.shape, BF16),
            pltpu.VMEM(lefts.shape, BF16),
            pltpu.VMEM(transforms.shape, BF16),
            pltpu.VMEM((8, side, side), BF16),
            pltpu.VMEM((8, side, win), BF16),
            pltpu.VMEM((2, win // 2, 8 * side), BF16),
            pltpu.VMEM((8 * side, win), BF16),
            pltpu.VMEM((8, rows, win), BF16),
            pltpu.VMEM((8, rows, win), BF16),
            pltpu.VMEM((8, rows, win), BF16),
            dma((5,)), dma((8,)), dma((8,)), dma((4,)), dma((4,)), dma((8,)), dma((8,)), dma((8,)),
            dma((16,)), dma((2,)), dma((2,)), dma((16,)), dma((8,)), dma((1,)), dma((1,)), dma((8,)), dma((8,)),
        ],
        compiler_params=pltpu.CompilerParams(
            collective_id=0, has_side_effects=True, vmem_limit_bytes=VMEM_LIMIT
        ),
        name="ptychography_backward",
    )(
        offsets, transmission, probe, measured,
        jnp.asarray(rights), jnp.asarray(lefts), jnp.asarray(transforms),
    )
    parts = arrived.reshape(2, layers, 2, rows, win)
    return parts[0].astype(F32) + parts[1].astype(F32)


def solution(mesh):
    in_specs = (P("depth", None, "pos", None), P(), P("pos", None), P("pos", None, None))
    out_specs = P("depth", None, "pos", None)
    return jax.shard_map(
        per_device, mesh=mesh, in_specs=in_specs, out_specs=out_specs, check_vma=False
    )
```

```python
import functools
import math

import jax
import jax.numpy as jnp
import ml_dtypes
import numpy as np
from jax import lax
from jax.experimental import pallas as pl
from jax.experimental.pallas import tpu as pltpu
from jax.sharding import PartitionSpec as P


MESH = pl.DeviceIdType.MESH
F32 = jnp.float32
BF16 = jnp.bfloat16
VMEM_LIMIT = 56 * 1024 * 1024


def vmem():
    return pl.BlockSpec(memory_space=pltpu.VMEM)


def place():
    d = lax.axis_index("depth")
    q = lax.axis_index("pos")
    return d // 4, d % 4, q // 4, (q // 2) % 2, q % 2


def hi_lo(table, axis):
    high = table.astype(ml_dtypes.bfloat16)
    low = (table - high.astype(np.float64)).astype(ml_dtypes.bfloat16)
    return np.concatenate([high, low], axis)


def right_form(matrix):
    return np.block([[matrix.real, matrix.imag], [-matrix.imag, matrix.real]])


@functools.lru_cache(maxsize=None)
def tables(side):
    half = side // 2
    grid = np.arange(side)
    fourier = np.exp(-2j * np.pi * (np.outer(grid, grid) % side) / side) / math.sqrt(side)
    frequency = (grid + half) % side - half
    phase = np.exp(-1j * math.pi * frequency.astype(np.float64) ** 2 / 1024.0)
    circulant = fourier.conj() @ (phase[:, None] * fourier)
    near, far = circulant[:half, :half], circulant[:half, half:]
    pieces = [(near + far) / 2, (near - far) / 2]

    def left_form(matrix):
        parts = np.stack([hi_lo(matrix.real, 1), hi_lo(matrix.imag, 1)])
        return parts.reshape(2, half // STRIP, STRIP, side).transpose(1, 0, 2, 3).reshape(side, side)

    ways = [pieces, [m.conj() for m in pieces]]
    rights = np.stack([[hi_lo(right_form(m), 1) for m in way] for way in ways])
    lefts = np.stack([[left_form(m) for m in way] for way in ways])
    transforms = np.stack([hi_lo(m, 0) for m in (fourier.real, fourier.imag, -fourier.imag)])
    return rights, lefts, transforms.reshape(3, 2, side, side)


def dot(a, b):
    return jnp.dot(a, b, preferred_element_type=F32)


def cat(parts, axis):
    return jnp.concatenate(parts, axis)


STRIP = 16


def strips(count):
    return range(0, count, STRIP)


def halves(value):
    middle = value.shape[1] // 2
    return value[:, :middle], value[:, middle:]


def put_sums(ref, at, real, imag):
    (a, b), (c, d) = halves(real), halves(imag)
    ref[0, pl.ds(at, STRIP), :] = cat([a + b, c + d], 1).astype(BF16)
    ref[1, pl.ds(at, STRIP), :] = cat([a - b, c - d], 1).astype(BF16)


def sums_row(row, side):
    half = side // 2
    return 2 * row if row < half else 2 * (row - half) + STRIP


def right_stage(sums, flat, middle, right_ref, way):
    side = sums.shape[1]
    for m in range(2):
        flat[m] = dot(sums[m], right_ref[way, m])

    def total(m, r):
        return flat[m, pl.ds(r, STRIP), :side] + flat[m, pl.ds(r, STRIP), side:]

    for r in range(0, side, 2 * STRIP):
        s, t = total(0, r), total(0, r + STRIP)
        d, e = total(1, r), total(1, r + STRIP)
        for m, (a, b) in enumerate(((s + t, d + e), (s - t, d - e))):
            (a_real, a_imag), (b_real, b_imag) = halves(a), halves(b)
            middle[m, pl.ds(r // 2, STRIP), :] = cat([a_real, b_real, a_imag, b_imag], 1).astype(BF16)


def left_stage(middle, field, left_ref, way):
    side = field.shape[1]
    for m in range(2):
        x = middle[m]
        field[m] = dot(left_ref[way, m], cat([x, x], 0))

    def total(m, r):
        (a, b), (c, d) = halves(field[m, pl.ds(r, STRIP), :]), halves(field[m, pl.ds(r + STRIP, STRIP), :])
        return a - d, c + b

    for r in range(0, side, 2 * STRIP):
        (p, u), (m, v) = total(0, r), total(1, r)
        for at, real, imag in ((r // 2, p + m, u + v), (side // 2 + r // 2, p - m, u - v)):
            (a, b), (c, d) = halves(real), halves(imag)
            yield at, cat([a + b, a - b], 1), cat([c + d, c - d], 1)


def strip(ref, s, c, at):
    return ref[s, c, pl.ds(at, STRIP), :].astype(F32)


def fourier_right(real, imag, f, inverse):
    r, i, n = f
    up, down = (n, i) if inverse else (i, n)
    x = cat([real, real, imag, imag], 1)
    a = dot(x, cat([r[0], r[1], down[0], down[1]], 0))
    b = dot(x, cat([up[0], up[1], r[0], r[1]], 0))
    return a, b


def fourier_left(real, imag, f, inverse):
    r, i, n = f
    up, down = (n, i) if inverse else (i, n)
    x = cat([real, real, imag, imag], 0)
    a = dot(cat([r[0], r[1], down[0], down[1]], 1), x)
    b = dot(cat([up[0], up[1], r[0], r[1]], 1), x)
    return a, b


def neighbours(g, j, x, h, core):
    d = 4 * g + j
    xy = 2 * x + h
    partners = [(d, 4 * x + 2 * h + 1 - core)]
    for k in range(1, 8):
        partners.append((d, 2 * ((xy + k) % 8) + core))
    for kx in range(4):
        for kj in range(1, 4):
            partners.append((4 * g + (j + kj) % 4, 4 * ((x + kx) % 4) + 2 * h + core))
    return partners


def remote(src, dst, send, recv, device):
    return pltpu.make_async_remote_copy(
        src_ref=src, dst_ref=dst, send_sem=send, recv_sem=recv, device_id=device, device_id_type=MESH
    )


def one_hot(mask):
    return jnp.where(mask, 1.0, 0.0).astype(BF16)


def shifts(columns):
    return lax.broadcasted_iota(jnp.int32, (STRIP, columns), 1) - lax.broadcasted_iota(
        jnp.int32, (STRIP, columns), 0
    )


def fill_rows(ref, offset):
    rows, columns = ref.shape
    lanes = cat([offset] * (columns // 128), 1)
    base = shifts(columns)
    for r in strips(rows):
        ref[pl.ds(r, STRIP), :] = one_hot(base == lanes + r)


def fill_columns(ref, offset, row_of=lambda r: r):
    rows, columns = ref.shape
    lanes = cat([offset] * (columns // 128), 1)
    base = shifts(columns)
    for r in strips(rows):
        ref[pl.ds(r, STRIP), :] = one_hot(base == row_of(r) - lanes)


def kernel(
    off_ref, t_ref, probe_hbm, measured_hbm, right_hbm, left_hbm, transform_hbm, arrived,
    own_offsets, offs, plane, pick_rows, pick_columns, stage, o_ref, stored, sums, flat, middle, field, grads, measured_ref, right_ref, left_ref,
    transform_ref, patches, put_columns, put_rows, wide, partial, sibling_sum, reduced,
    load_sem, s1_send, s1_recv, off_send, off_recv, chip_send, chip_recv, s2_send, s2_recv,
    hop_send, hop_recv, s3_send, s3_recv, back_send, back_recv, s4_send, s4_recv,
):
    g, j, x, h, core = place()
    d = 4 * g + j
    q = 4 * x + 2 * h + core
    xy = 2 * x + h
    last = 3
    sibling = (d, 4 * x + 2 * h + 1 - core)
    win = plane.shape[-1]
    side = o_ref.shape[-1]
    half = side // 2
    count = o_ref.shape[0]
    block = plane.shape[2]
    active = jnp.logical_or(j == core, j == 3 - core)
    mine = jnp.where(j == core, 0, 1)
    ahead = (jnp.minimum(d + 4, 15), q)
    behind = (jnp.maximum(d - 4, 0), q)

    loads = [
        pltpu.make_async_copy(right_hbm, right_ref, load_sem.at[0]),
        pltpu.make_async_copy(left_hbm, left_ref, load_sem.at[1]),
        pltpu.make_async_copy(transform_hbm, transform_ref, load_sem.at[2]),
        pltpu.make_async_copy(measured_hbm.at[mine], measured_ref, load_sem.at[3]),
    ]
    load_probe = pltpu.make_async_copy(probe_hbm, stored.at[0], load_sem.at[4])
    barrier = pltpu.get_barrier_semaphore()
    partners = neighbours(g, j, x, h, core)
    for partner in partners:
        pl.semaphore_signal(barrier, inc=1, device_id=partner, device_id_type=MESH)

    @pl.when(jnp.logical_and(active, g < last))
    def _():
        pl.semaphore_signal(barrier, inc=1, device_id=ahead, device_id_type=MESH)

    @pl.when(jnp.logical_and(active, g > 0))
    def _():
        pl.semaphore_signal(barrier, inc=1, device_id=behind, device_id_type=MESH)

    chained = jnp.where(active, jnp.where(jnp.logical_or(g == 0, g == last), 1, 2), 0)
    for load in loads:
        load.start()
    pl.when(g == 0)(load_probe.start)
    for k in range(4):
        own_offsets[k : k + 1, :] = jnp.full((1, 128), off_ref[k // 2, k % 2], jnp.int32)
        own_offsets[k + 4 : k + 5, :] = jnp.zeros((1, 128), jnp.int32)
    pl.semaphore_wait(barrier, len(partners) + chained)

    for k in range(1, 4):
        to = (x + k) % 4
        remote(
            own_offsets, offs.at[x], off_send.at[k], off_recv.at[k], (d, 4 * to + 2 * h + core)
        ).start()
    for k in (4, 3, 5, 2, 6, 1, 7):
        to = (xy + k) % 8
        tx = to // 2
        remote(
            t_ref.at[tx // 2, tx % 2], plane.at[xy, core], s1_send.at[k], s1_recv.at[k], (d, 2 * to + core)
        ).start()
    own = t_ref.at[x // 2, x % 2]
    remote(own, plane.at[xy, core], chip_send.at[0], chip_recv.at[0], sibling).start()
    plane[xy, core] = t_ref[x // 2, x % 2]
    offs[x] = own_offsets[...]

    for k in range(4):
        if k:
            slot = offs.at[(x - k + 4) % 4]
            remote(slot, slot, off_send.at[k], off_recv.at[k], sibling).wait_recv()
        for i in range(2):
            from_x = (x - k + 4) % 4
            slot = 2 * ((4 - k) % 4) + i
            row, column = offs[from_x, 2 * i : 2 * i + 1, :], offs[from_x, 2 * i + 1 : 2 * i + 2, :]
            fill_rows(pick_rows.at[slot], row)
            fill_columns(pick_columns.at[slot], column)
            fill_rows(put_columns.at[slot], column)
            for m in range(2):
                first = 1 - core if m == 0 else core
                fill_columns(
                    put_rows.at[m, :, slot * side : (slot + 1) * side],
                    row,
                    lambda r: r + (r // block + first) * block,
                )

    for k in (1, 7, 2, 6, 3, 5, 4):
        rows = plane.at[(xy - k + 8) % 8, core]
        remote(rows, rows, s1_send.at[k], s1_recv.at[k], sibling).wait_recv()
        remote(rows, rows, chip_send.at[k], chip_recv.at[k], sibling).start()
    for k in range(8):
        rows = plane.at[(xy - k + 8) % 8, 1 - core]
        remote(rows, rows, chip_send.at[k], chip_recv.at[k], sibling).wait_recv()

    def target(k, i):
        to_j = core if i == 0 else 3 - core
        return to_j, (4 * g + to_j, 4 * ((x + k) % 4) + 2 * h + core)

    own_plane = 2 * j + x // 2
    home = o_ref.at[own_plane, x % 2]
    for i in (1, 0):
        for k in (2, 1, 3, 0):
            slot = 2 * k + i
            rows = dot(pick_rows[slot], plane[...].reshape(win, win)).astype(BF16)
            stage[slot] = dot(rows, pick_columns[slot]).astype(BF16)
            to_j, device = target(k, i)
            copy = remote(
                stage.at[slot], home, s2_send.at[slot], s2_recv.at[2 * own_plane + x % 2], device
            )
            if k:
                copy.start()
            else:
                pl.when(to_j != j)(copy.start)

                @pl.when(to_j == j)
                def _():
                    o_ref[own_plane, x % 2] = stage[slot]

    for load in loads:
        load.wait()
    pl.when(g == 0)(load_probe.wait)
    hop_forward = remote(stored.at[count], stored.at[0], hop_send.at[0], hop_recv.at[0], ahead)
    hop_backward = remote(middle, middle, hop_send.at[1], hop_recv.at[1], behind)

    def owner(s, c):
        return 2 * (s % 2) + c, s // 2

    @pl.when(active)
    def _():
        @pl.when(g > 0)
        def _():
            hop_forward.wait_recv()

        def wait_crop(s):
            for c in range(2):
                from_x, from_j = owner(s, c)
                slot = o_ref.at[s, c]
                copy = remote(slot, slot, s2_send.at[0], s2_recv.at[2 * s + c], sibling)
                pl.when(jnp.logical_or(from_x != x, from_j != j))(copy.wait_recv)

        def enter(s, at, real, imag):
            o_real, o_imag = strip(o_ref, s, 0, at), strip(o_ref, s, 1, at)
            put_sums(
                sums, sums_row(at, side), o_real * real - o_imag * imag, o_real * imag + o_imag * real
            )

        def keep_wave(s, at, real, imag):
            stored[s, 0, pl.ds(at, STRIP), :] = real.astype(BF16)
            stored[s, 1, pl.ds(at, STRIP), :] = imag.astype(BF16)

        def forward(s, carry):
            wait_crop(s + 1)
            for at, real, imag in left_stage(middle, field, left_ref, 0):
                keep_wave(s + 1, at, real, imag)
                enter(s + 1, at, real, imag)
            right_stage(sums, flat, middle, right_ref, 0)
            return carry

        wait_crop(0)
        for at in strips(side):
            enter(0, at, strip(stored, 0, 0, at), strip(stored, 0, 1, at))
        right_stage(sums, flat, middle, right_ref, 0)
        lax.fori_loop(0, count - 1, forward, 0)
        for at, real, imag in left_stage(middle, field, left_ref, 0):
            keep_wave(count, at, real, imag)

        @pl.when(g < last)
        def _():
            hop_forward.start()
            remote(middle, middle, hop_send.at[1], hop_recv.at[1], ahead).wait_recv()

        @pl.when(g == last)
        def _():
            f = [(transform_ref[m, 0], transform_ref[m, 1]) for m in range(3)]
            a, b = fourier_right(stored[count, 0], stored[count, 1], f, False)
            grads[0, 0] = a.astype(BF16)
            grads[0, 1] = b.astype(BF16)
            a, b = fourier_left(grads[0, 0], grads[0, 1], f, False)
            flat[0, :, :side] = a
            flat[1, :, :side] = b
            for at in strips(side):
                real, imag = flat[0, pl.ds(at, STRIP), :side], flat[1, pl.ds(at, STRIP), :side]
                weight = real * real + imag * imag - measured_ref[pl.ds(at, STRIP), :]
                sums[0, pl.ds(at, STRIP), :] = (real * weight).astype(BF16)
                sums[1, pl.ds(at, STRIP), :] = (imag * weight).astype(BF16)
            a, b = fourier_right(sums[0], sums[1], f, True)
            grads[0, 0] = a.astype(BF16)
            grads[0, 1] = b.astype(BF16)
            a, b = fourier_left(grads[0, 0], grads[0, 1], f, True)
            flat[0, :, :side] = a
            flat[1, :, :side] = b
            for at in strips(side):
                put_sums(
                    sums, sums_row(at, side),
                    flat[0, pl.ds(at, STRIP), :side], flat[1, pl.ds(at, STRIP), :side],
                )
            right_stage(sums, flat, middle, right_ref, 1)

        def send_patches(s):
            for c in range(2):
                to_x, to_j = owner(s, c)
                away = jnp.logical_or(to_x != x, to_j != j)
                copy = remote(
                    grads.at[s, c], patches.at[2 * x + mine], s3_send.at[2 * s + c],
                    s3_recv.at[2 * x + mine], (4 * g + to_j, 4 * to_x + 2 * h + core),
                )
                pl.when(away)(copy.start)

                @pl.when(jnp.logical_not(away))
                def _():
                    patches[2 * x + mine] = grads[s, c]

        def leave(s):
            for at, real, imag in left_stage(middle, field, left_ref, 1):
                o_real, o_imag = strip(o_ref, s, 0, at), strip(o_ref, s, 1, at)
                put_sums(
                    sums, sums_row(at, side), o_real * real + o_imag * imag, o_real * imag - o_imag * real
                )
                p_real, p_imag = strip(stored, s, 0, at), strip(stored, s, 1, at)
                grads[s, 0, pl.ds(at, STRIP), :] = (p_real * real + p_imag * imag).astype(BF16)
                grads[s, 1, pl.ds(at, STRIP), :] = (p_real * imag - p_imag * real).astype(BF16)

        def backward(t, carry):
            s = count - 1 - t
            leave(s)
            right_stage(sums, flat, middle, right_ref, 1)
            pl.when(g == 0)(functools.partial(send_patches, s))
            return carry

        lax.fori_loop(0, count - 1, backward, 0)
        leave(0)
        pl.when(g == 0)(functools.partial(send_patches, 0))

        @pl.when(g > 0)
        def _():
            right_stage(sums, flat, middle, right_ref, 1)
            hop_backward.start()
            hop_backward.wait_send()

            def send(t, carry):
                send_patches(count - 1 - t)
                return carry

            lax.fori_loop(0, count, send, 0)

    for i in (1, 0):
        for kx in range(4):
            from_x = (x - kx + 4) % 4
            from_j = core if i == 0 else 3 - core
            p = 2 * from_x + i
            slot = patches.at[p]
            copy = remote(slot, slot, s3_send.at[0], s3_recv.at[p], sibling)
            if kx:
                copy.wait_recv()
            else:
                pl.when(from_j != j)(copy.wait_recv)
            at = 2 * ((4 - kx) % 4) + i
            wide[at * side : (at + 1) * side, :] = dot(slot[...], put_columns[at]).astype(BF16)

    partial[...] = dot(put_rows[0], wide[...]).reshape(partial.shape).astype(BF16)
    chip_copy = remote(partial, sibling_sum, back_send.at[0], back_recv.at[0], sibling)
    chip_copy.start()
    own_rows = dot(put_rows[1], wide[...]).reshape(partial.shape)
    chip_copy.wait_recv()
    reduced[...] = (own_rows + sibling_sum[...].astype(F32)).astype(BF16)
    for k in (4, 3, 5, 2, 6, 1, 7):
        to = (xy + k) % 8
        remote(reduced.at[to], arrived.at[4 * h + x], s4_send.at[k], s4_recv.at[k], (d, 2 * to + core)).start()
    arrived[4 * h + x] = reduced[xy]
    for k in range(1, 8):
        come = (xy - k + 8) % 8
        slot = arrived.at[4 * (come % 2) + come // 2]
        remote(slot, slot, s4_send.at[k], s4_recv.at[k], sibling).wait_recv()

    for k in range(1, 8):
        slot = reduced.at[0]
        remote(slot, slot, s1_send.at[k], s1_recv.at[k], sibling).wait_send()
        remote(slot, slot, s4_send.at[k], s4_recv.at[k], sibling).wait_send()
    for k in range(1, 4):
        remote(own_offsets, own_offsets, off_send.at[k], off_recv.at[k], sibling).wait_send()
    for k in range(8):
        slot = reduced.at[0]
        remote(slot, slot, chip_send.at[k], chip_recv.at[k], sibling).wait_send()
    chip_copy.wait_send()
    for i in range(2):
        for k in range(4):
            slot = 2 * k + i
            to_j, device = target(k, i)
            copy = remote(stage.at[slot], home, s2_send.at[slot], s2_recv.at[0], device)
            if k:
                copy.wait_send()
            else:
                pl.when(to_j != j)(copy.wait_send)

    @pl.when(active)
    def _():
        pl.when(g < last)(hop_forward.wait_send)
        for s in range(count):
            for c in range(2):
                to_x, to_j = owner(s, c)
                slot = grads.at[s, c]
                copy = remote(slot, slot, s3_send.at[2 * s + c], s3_recv.at[0], sibling)
                pl.when(jnp.logical_or(to_x != x, to_j != j))(copy.wait_send)


def per_device(transmission, probe, offsets, measured):
    layers, _, rows, win = transmission.shape
    side = probe.shape[-1]
    group = 4 * layers
    rights, lefts, transforms = tables(side)
    dma = pltpu.SemaphoreType.DMA
    hbm = pl.BlockSpec(memory_space=pl.ANY)
    smem = pl.BlockSpec(memory_space=pltpu.SMEM)
    arrived = pl.pallas_call(
        kernel,
        out_shape=jax.ShapeDtypeStruct((8, rows, win), BF16),
        in_specs=[smem, vmem(), hbm, hbm, hbm, hbm, hbm],
        out_specs=vmem(),
        scratch_shapes=[
            pltpu.VMEM((8, 128), jnp.int32),
            pltpu.VMEM((4, 8, 128), jnp.int32),
            pltpu.VMEM((8, 2, rows, win), BF16),
            pltpu.VMEM((8, side, win), BF16),
            pltpu.VMEM((8, win, side), BF16),
            pltpu.VMEM((8, side, side), BF16),
            pltpu.VMEM((group, 2, side, side), BF16),
            pltpu.VMEM((group + 1, 2, side, side), BF16),
            pltpu.VMEM((2, side, side), BF16),
            pltpu.VMEM((2, side, win), F32),
            pltpu.VMEM((2, side // 2, win), BF16),
            pltpu.VMEM((2, side, win), F32),
            pltpu.VMEM((group, 2, side, side), BF16),
            pltpu.VMEM((side, side), F32),
            pltpu.VMEM(rights.shape, BF16),
            pltpu.VMEM(lefts.shape, BF16),
            pltpu.VMEM(transforms.shape, BF16),
            pltpu.VMEM((8, side, side), BF16),
            pltpu.VMEM((8, side, win), BF16),
            pltpu.VMEM((2, win // 2, 8 * side), BF16),
            pltpu.VMEM((8 * side, win), BF16),
            pltpu.VMEM((8, rows, win), BF16),
            pltpu.VMEM((8, rows, win), BF16),
            pltpu.VMEM((8, rows, win), BF16),
            dma((5,)), dma((8,)), dma((8,)), dma((4,)), dma((4,)), dma((8,)), dma((8,)), dma((8,)),
            dma((16,)), dma((2,)), dma((2,)), dma((16,)), dma((8,)), dma((1,)), dma((1,)), dma((8,)), dma((8,)),
        ],
        compiler_params=pltpu.CompilerParams(
            collective_id=0, has_side_effects=True, vmem_limit_bytes=VMEM_LIMIT
        ),
        name="ptychography_backward",
    )(
        offsets, transmission, probe, measured,
        jnp.asarray(rights), jnp.asarray(lefts), jnp.asarray(transforms),
    )
    parts = arrived.reshape(2, layers, 2, rows, win)
    return parts[0].astype(F32) + parts[1].astype(F32)


def solution(mesh):
    in_specs = (P("depth", None, "pos", None), P(), P("pos", None), P("pos", None, None))
    out_specs = P("depth", None, "pos", None)
    return jax.shard_map(
        per_device, mesh=mesh, in_specs=in_specs, out_specs=out_specs, check_vma=False
    )
```

```python
import functools
import math

import jax
import jax.numpy as jnp
import ml_dtypes
import numpy as np
from jax import lax
from jax.experimental import pallas as pl
from jax.experimental.pallas import tpu as pltpu
from jax.sharding import PartitionSpec as P


MESH = pl.DeviceIdType.MESH
F32 = jnp.float32
BF16 = jnp.bfloat16
VMEM_LIMIT = 56 * 1024 * 1024


def vmem():
    return pl.BlockSpec(memory_space=pltpu.VMEM)


def place():
    d = lax.axis_index("depth")
    q = lax.axis_index("pos")
    return d // 4, d % 4, q // 4, (q // 2) % 2, q % 2


def hi_lo(table, axis):
    high = table.astype(ml_dtypes.bfloat16)
    low = (table - high.astype(np.float64)).astype(ml_dtypes.bfloat16)
    return np.concatenate([high, low], axis)


def right_form(matrix):
    return np.block([[matrix.real, matrix.imag], [-matrix.imag, matrix.real]])


@functools.lru_cache(maxsize=None)
def tables(side):
    half = side // 2
    grid = np.arange(side)
    fourier = np.exp(-2j * np.pi * (np.outer(grid, grid) % side) / side) / math.sqrt(side)
    frequency = (grid + half) % side - half
    phase = np.exp(-1j * math.pi * frequency.astype(np.float64) ** 2 / 1024.0)
    circulant = fourier.conj() @ (phase[:, None] * fourier)
    near, far = circulant[:half, :half], circulant[:half, half:]
    forms = [right_form((near + far) / 2), right_form((near - far) / 2)]
    rights = np.stack([[hi_lo(m, 0) for m in forms], [hi_lo(m.T, 0) for m in forms]])
    order = grid.reshape(2, half // STRIP, STRIP).transpose(1, 0, 2).reshape(side)
    strided = [m[order][:, order] for m in forms]
    lefts = np.stack([[hi_lo(m.T, 1) for m in strided], [hi_lo(m, 1) for m in strided]])
    transforms = np.stack([hi_lo(m, 0) for m in (fourier.real, fourier.imag, -fourier.imag)])
    return rights, lefts, transforms.reshape(3, 2, side, side)


def dot(a, b):
    return jnp.dot(a, b, preferred_element_type=F32)


def cat(parts, axis):
    return jnp.concatenate(parts, axis)


STRIP = 16
BLOCKS = 2


def strips(count):
    return range(0, count, STRIP)


def halves(value):
    middle = value.shape[1] // 2
    return value[:, :middle], value[:, middle:]


def put_sums(ref, at, real, imag):
    (a, b), (c, d) = halves(real), halves(imag)
    ref[0, pl.ds(at, STRIP), :] = cat([a + b, c + d], 1).astype(BF16)
    ref[1, pl.ds(at, STRIP), :] = cat([a - b, c - d], 1).astype(BF16)


def sums_row(row, side):
    half = side // 2
    return 2 * row if row < half else 2 * (row - half) + STRIP


def right_stage(sums, flat, middle, right_ref, way):
    side = sums.shape[1]
    block = side // BLOCKS
    for n in range(BLOCKS):
        for m in range(2):
            x = sums[m, pl.ds(n * block, block), :]
            flat[m, pl.ds(n * block, block), :] = dot(cat([x, x], 1), right_ref[way, m])
        for r in range(n * block, (n + 1) * block, 2 * STRIP):
            s, t = flat[0, pl.ds(r, STRIP), :], flat[0, pl.ds(r + STRIP, STRIP), :]
            d, e = flat[1, pl.ds(r, STRIP), :], flat[1, pl.ds(r + STRIP, STRIP), :]
            for m, (a, b) in enumerate(((s + t, d + e), (s - t, d - e))):
                (a_real, a_imag), (b_real, b_imag) = halves(a), halves(b)
                middle[m, pl.ds(r, STRIP), :] = cat([a_real, b_real], 1).astype(BF16)
                middle[m, pl.ds(r + STRIP, STRIP), :] = cat([a_imag, b_imag], 1).astype(BF16)


def left_stage(middle, field, left_ref, way):
    side = middle.shape[1]
    block = side // BLOCKS
    for n in range(BLOCKS):
        for m in range(2):
            x = middle[m]
            field[m, pl.ds(n * block, block), :] = dot(
                left_ref[way, m, pl.ds(n * block, block), :], cat([x, x], 0)
            )
        for r in range(n * block, (n + 1) * block, 2 * STRIP):
            p, u = field[0, pl.ds(r, STRIP), :], field[0, pl.ds(r + STRIP, STRIP), :]
            m, v = field[1, pl.ds(r, STRIP), :], field[1, pl.ds(r + STRIP, STRIP), :]
            for at, real, imag in ((r // 2, p + m, u + v), (side // 2 + r // 2, p - m, u - v)):
                (a, b), (c, d) = halves(real), halves(imag)
                yield at, cat([a + b, a - b], 1), cat([c + d, c - d], 1)


def strip(ref, s, c, at):
    return ref[s, c, pl.ds(at, STRIP), :].astype(F32)


def fourier_right(real, imag, f, inverse):
    r, i, n = f
    up, down = (n, i) if inverse else (i, n)
    x = cat([real, real, imag, imag], 1)
    a = dot(x, cat([r[0], r[1], down[0], down[1]], 0))
    b = dot(x, cat([up[0], up[1], r[0], r[1]], 0))
    return a, b


def fourier_left(real, imag, f, inverse):
    r, i, n = f
    up, down = (n, i) if inverse else (i, n)
    x = cat([real, real, imag, imag], 0)
    a = dot(cat([r[0], r[1], down[0], down[1]], 1), x)
    b = dot(cat([up[0], up[1], r[0], r[1]], 1), x)
    return a, b


def neighbours(g, j, x, h, core):
    d = 4 * g + j
    xy = 2 * x + h
    partners = [(d, 4 * x + 2 * h + 1 - core)]
    for k in range(1, 8):
        partners.append((d, 2 * ((xy + k) % 8) + core))
    for kx in range(4):
        for kj in range(1, 4):
            partners.append((4 * g + (j + kj) % 4, 4 * ((x + kx) % 4) + 2 * h + core))
    return partners


def remote(src, dst, send, recv, device):
    return pltpu.make_async_remote_copy(
        src_ref=src, dst_ref=dst, send_sem=send, recv_sem=recv, device_id=device, device_id_type=MESH
    )


def one_hot(mask):
    return jnp.where(mask, 1.0, 0.0).astype(BF16)


def shifts(columns):
    return lax.broadcasted_iota(jnp.int32, (STRIP, columns), 1) - lax.broadcasted_iota(
        jnp.int32, (STRIP, columns), 0
    )


def fill_rows(ref, offset):
    rows, columns = ref.shape
    lanes = cat([offset] * (columns // 128), 1)
    base = shifts(columns)
    for r in strips(rows):
        ref[pl.ds(r, STRIP), :] = one_hot(base == lanes + r)


def fill_columns(ref, offset, row_of=lambda r: r):
    rows, columns = ref.shape
    lanes = cat([offset] * (columns // 128), 1)
    base = shifts(columns)
    for r in strips(rows):
        ref[pl.ds(r, STRIP), :] = one_hot(base == row_of(r) - lanes)


def kernel(
    off_ref, t_ref, probe_hbm, measured_hbm, right_hbm, left_hbm, transform_hbm, arrived,
    own_offsets, offs, plane, pick_rows, pick_columns, stage, o_ref, stored, sums, flat, middle, field, grads, measured_ref, right_ref, left_ref,
    transform_ref, patches, put_columns, put_rows, wide, total, partial, sibling_sum, reduced,
    load_sem, s1_send, s1_recv, off_send, off_recv, chip_send, chip_recv, s2_send, s2_recv,
    hop_send, hop_recv, s3_send, s3_recv, back_send, back_recv, s4_send, s4_recv,
):
    g, j, x, h, core = place()
    d = 4 * g + j
    q = 4 * x + 2 * h + core
    xy = 2 * x + h
    last = 3
    sibling = (d, 4 * x + 2 * h + 1 - core)
    win = plane.shape[-1]
    side = o_ref.shape[-1]
    half = side // 2
    count = o_ref.shape[0]
    block = plane.shape[2]
    active = jnp.logical_or(j == core, j == 3 - core)
    mine = jnp.where(j == core, 0, 1)
    ahead = (jnp.minimum(d + 4, 15), q)
    behind = (jnp.maximum(d - 4, 0), q)

    loads = [
        pltpu.make_async_copy(right_hbm, right_ref, load_sem.at[0]),
        pltpu.make_async_copy(left_hbm, left_ref, load_sem.at[1]),
        pltpu.make_async_copy(transform_hbm, transform_ref, load_sem.at[2]),
        pltpu.make_async_copy(measured_hbm.at[mine], measured_ref, load_sem.at[3]),
    ]
    load_probe = pltpu.make_async_copy(probe_hbm, stored.at[0], load_sem.at[4])
    barrier = pltpu.get_barrier_semaphore()
    partners = neighbours(g, j, x, h, core)
    for partner in partners:
        pl.semaphore_signal(barrier, inc=1, device_id=partner, device_id_type=MESH)

    @pl.when(jnp.logical_and(active, g < last))
    def _():
        pl.semaphore_signal(barrier, inc=1, device_id=ahead, device_id_type=MESH)

    @pl.when(jnp.logical_and(active, g > 0))
    def _():
        pl.semaphore_signal(barrier, inc=1, device_id=behind, device_id_type=MESH)

    chained = jnp.where(active, jnp.where(jnp.logical_or(g == 0, g == last), 1, 2), 0)
    for load in loads:
        load.start()
    pl.when(g == 0)(load_probe.start)
    for k in range(4):
        own_offsets[k : k + 1, :] = jnp.full((1, 128), off_ref[k // 2, k % 2], jnp.int32)
        own_offsets[k + 4 : k + 5, :] = jnp.zeros((1, 128), jnp.int32)
    pl.semaphore_wait(barrier, len(partners) + chained)

    for k in range(1, 4):
        to = (x + k) % 4
        remote(
            own_offsets, offs.at[x], off_send.at[k], off_recv.at[k], (d, 4 * to + 2 * h + core)
        ).start()
    for k in (4, 3, 5, 2, 6, 1, 7):
        to = (xy + k) % 8
        tx = to // 2
        remote(
            t_ref.at[tx // 2, tx % 2], plane.at[xy, core], s1_send.at[k], s1_recv.at[k], (d, 2 * to + core)
        ).start()
    own = t_ref.at[x // 2, x % 2]
    remote(own, plane.at[xy, core], chip_send.at[0], chip_recv.at[0], sibling).start()
    plane[xy, core] = t_ref[x // 2, x % 2]
    offs[x] = own_offsets[...]

    for i in (1, 0):
        for k in (0, 3, 2, 1):
            from_x = (x - k + 4) % 4
            if k and i:
                slot = offs.at[from_x]
                remote(slot, slot, off_send.at[k], off_recv.at[k], sibling).wait_recv()
            slot = 2 * ((4 - k) % 4) + i
            fill_rows(pick_rows.at[slot], offs[from_x, 2 * i : 2 * i + 1, :])
            fill_columns(pick_columns.at[slot], offs[from_x, 2 * i + 1 : 2 * i + 2, :])

    for k in (1, 7, 2, 6, 3, 5, 4):
        rows = plane.at[(xy - k + 8) % 8, core]
        remote(rows, rows, s1_send.at[k], s1_recv.at[k], sibling).wait_recv()
        remote(rows, rows, chip_send.at[k], chip_recv.at[k], sibling).start()
    for k in range(8):
        rows = plane.at[(xy - k + 8) % 8, 1 - core]
        remote(rows, rows, chip_send.at[k], chip_recv.at[k], sibling).wait_recv()

    def target(k, i):
        to_j = core if i == 0 else 3 - core
        return to_j, (4 * g + to_j, 4 * ((x + k) % 4) + 2 * h + core)

    own_plane = 2 * j + x // 2
    home = o_ref.at[own_plane, x % 2]
    for i in (1, 0):
        for k in (2, 1, 3, 0):
            slot = 2 * k + i
            rows = dot(pick_rows[slot], plane[...].reshape(win, win)).astype(BF16)
            stage[slot] = dot(rows, pick_columns[slot]).astype(BF16)
            to_j, device = target(k, i)
            copy = remote(
                stage.at[slot], home, s2_send.at[slot], s2_recv.at[2 * own_plane + x % 2], device
            )
            if k:
                copy.start()
            else:
                pl.when(to_j != j)(copy.start)

                @pl.when(to_j == j)
                def _():
                    o_ref[own_plane, x % 2] = stage[slot]

    for load in loads:
        load.wait()
    pl.when(g == 0)(load_probe.wait)
    hop_forward = remote(stored.at[count], stored.at[0], hop_send.at[0], hop_recv.at[0], ahead)
    hop_backward = remote(middle, middle, hop_send.at[1], hop_recv.at[1], behind)

    def owner(s, c):
        return 2 * (s % 2) + c, s // 2

    def make_put_tables():
        for i in range(2):
            for k in range(4):
                at = 4 * (1 - i) + k
                from_x = (x + k) % 4
                fill_rows(put_columns.at[at], offs[from_x, 2 * i + 1 : 2 * i + 2, :])
                for m in range(2):
                    first = 1 - core if m == 0 else core
                    fill_columns(
                        put_rows.at[m, 1 - i, :, k * side : (k + 1) * side],
                        offs[from_x, 2 * i : 2 * i + 1, :],
                        lambda r: r + (r // block + first) * block,
                    )

    starts = jnp.logical_and(active, g == 0)
    pl.when(jnp.logical_not(starts))(make_put_tables)

    @pl.when(active)
    def _():
        @pl.when(g > 0)
        def _():
            hop_forward.wait_recv()

        def wait_crop(s):
            for c in range(2):
                from_x, from_j = owner(s, c)
                slot = o_ref.at[s, c]
                copy = remote(slot, slot, s2_send.at[0], s2_recv.at[2 * s + c], sibling)
                pl.when(jnp.logical_or(from_x != x, from_j != j))(copy.wait_recv)

        def enter(s, at, real, imag):
            o_real, o_imag = strip(o_ref, s, 0, at), strip(o_ref, s, 1, at)
            put_sums(
                sums, sums_row(at, side), o_real * real - o_imag * imag, o_real * imag + o_imag * real
            )

        def keep_wave(s, at, real, imag):
            stored[s, 0, pl.ds(at, STRIP), :] = real.astype(BF16)
            stored[s, 1, pl.ds(at, STRIP), :] = imag.astype(BF16)

        def forward(s, carry):
            wait_crop(s + 1)
            for at, real, imag in left_stage(middle, field, left_ref, 0):
                keep_wave(s + 1, at, real, imag)
                enter(s + 1, at, real, imag)
            right_stage(sums, flat, middle, right_ref, 0)
            return carry

        wait_crop(0)
        for at in strips(side):
            enter(0, at, strip(stored, 0, 0, at), strip(stored, 0, 1, at))
        right_stage(sums, flat, middle, right_ref, 0)
        lax.fori_loop(0, count - 1, forward, 0)
        for at, real, imag in left_stage(middle, field, left_ref, 0):
            keep_wave(count, at, real, imag)

        @pl.when(g < last)
        def _():
            hop_forward.start()
            pl.when(g == 0)(make_put_tables)
            remote(middle, middle, hop_send.at[1], hop_recv.at[1], ahead).wait_recv()

        @pl.when(g == last)
        def _():
            f = [(transform_ref[m, 0], transform_ref[m, 1]) for m in range(3)]
            a, b = fourier_right(stored[count, 0], stored[count, 1], f, False)
            middle[0] = a.astype(BF16)
            middle[1] = b.astype(BF16)
            a, b = fourier_left(middle[0], middle[1], f, False)
            flat[0] = a
            flat[1] = b
            for at in strips(side):
                real, imag = flat[0, pl.ds(at, STRIP), :], flat[1, pl.ds(at, STRIP), :]
                weight = real * real + imag * imag - measured_ref[pl.ds(at, STRIP), :]
                sums[0, pl.ds(at, STRIP), :] = (real * weight).astype(BF16)
                sums[1, pl.ds(at, STRIP), :] = (imag * weight).astype(BF16)
            a, b = fourier_right(sums[0], sums[1], f, True)
            middle[0] = a.astype(BF16)
            middle[1] = b.astype(BF16)
            a, b = fourier_left(middle[0], middle[1], f, True)
            flat[0] = a
            flat[1] = b
            for at in strips(side):
                put_sums(
                    sums, sums_row(at, side), flat[0, pl.ds(at, STRIP), :], flat[1, pl.ds(at, STRIP), :]
                )
            right_stage(sums, flat, middle, right_ref, 1)

        def send_patches(s):
            for c in range(2):
                to_x, to_j = owner(s, c)
                away = jnp.logical_or(to_x != x, to_j != j)
                copy = remote(
                    grads.at[s, c], patches.at[2 * x + mine], s3_send.at[2 * s + c],
                    s3_recv.at[2 * x + mine], (4 * g + to_j, 4 * to_x + 2 * h + core),
                )
                pl.when(away)(copy.start)

                @pl.when(jnp.logical_not(away))
                def _():
                    patches[2 * x + mine] = grads[s, c]

        def leave(s):
            for at, real, imag in left_stage(middle, field, left_ref, 1):
                o_real, o_imag = strip(o_ref, s, 0, at), strip(o_ref, s, 1, at)
                put_sums(
                    sums, sums_row(at, side), o_real * real + o_imag * imag, o_real * imag - o_imag * real
                )
                p_real, p_imag = strip(stored, s, 0, at), strip(stored, s, 1, at)
                grads[s, 0, pl.ds(at, STRIP), :] = (p_real * real + p_imag * imag).astype(BF16)
                grads[s, 1, pl.ds(at, STRIP), :] = (p_real * imag - p_imag * real).astype(BF16)

        def backward(t, carry):
            s = count - 1 - t
            leave(s)
            right_stage(sums, flat, middle, right_ref, 1)
            pl.when(g == 0)(functools.partial(send_patches, s))
            return carry

        lax.fori_loop(0, count - 1, backward, 0)
        leave(0)
        pl.when(g == 0)(functools.partial(send_patches, 0))

        @pl.when(g > 0)
        def _():
            right_stage(sums, flat, middle, right_ref, 1)
            hop_backward.start()
            hop_backward.wait_send()

            def send(t, carry):
                send_patches(count - 1 - t)
                return carry

            lax.fori_loop(0, count, send, 0)

    for i in (1, 0):
        group = 1 - i
        for kx in range(4):
            from_x = (x - kx + 4) % 4
            from_j = core if i == 0 else 3 - core
            p = 2 * from_x + i
            slot = patches.at[p]
            copy = remote(slot, slot, s3_send.at[0], s3_recv.at[p], sibling)
            if kx:
                copy.wait_recv()
            else:
                pl.when(from_j != j)(copy.wait_recv)
            at = (4 - kx) % 4
            wide[at * side : (at + 1) * side, :] = dot(slot[...], put_columns[4 * group + at]).astype(BF16)
        if group == 0:
            for m in range(2):
                total[m] = dot(put_rows[m, 0], wide[...])
    partial[...] = (total[0] + dot(put_rows[0, 1], wide[...])).reshape(partial.shape).astype(BF16)
    chip_copy = remote(partial, sibling_sum, back_send.at[0], back_recv.at[0], sibling)
    chip_copy.start()
    own_rows = (total[1] + dot(put_rows[1, 1], wide[...])).reshape(partial.shape)
    chip_copy.wait_recv()
    reduced[...] = (own_rows + sibling_sum[...].astype(F32)).astype(BF16)
    for k in (4, 3, 5, 2, 6, 1, 7):
        to = (xy + k) % 8
        remote(reduced.at[to], arrived.at[4 * h + x], s4_send.at[k], s4_recv.at[k], (d, 2 * to + core)).start()
    arrived[4 * h + x] = reduced[xy]
    for k in range(1, 8):
        come = (xy - k + 8) % 8
        slot = arrived.at[4 * (come % 2) + come // 2]
        remote(slot, slot, s4_send.at[k], s4_recv.at[k], sibling).wait_recv()

    for k in range(1, 8):
        slot = reduced.at[0]
        remote(slot, slot, s1_send.at[k], s1_recv.at[k], sibling).wait_send()
        remote(slot, slot, s4_send.at[k], s4_recv.at[k], sibling).wait_send()
    for k in range(1, 4):
        remote(own_offsets, own_offsets, off_send.at[k], off_recv.at[k], sibling).wait_send()
    for k in range(8):
        slot = reduced.at[0]
        remote(slot, slot, chip_send.at[k], chip_recv.at[k], sibling).wait_send()
    chip_copy.wait_send()
    for i in range(2):
        for k in range(4):
            slot = 2 * k + i
            to_j, device = target(k, i)
            copy = remote(stage.at[slot], home, s2_send.at[slot], s2_recv.at[0], device)
            if k:
                copy.wait_send()
            else:
                pl.when(to_j != j)(copy.wait_send)

    @pl.when(active)
    def _():
        pl.when(g < last)(hop_forward.wait_send)
        for s in range(count):
            for c in range(2):
                to_x, to_j = owner(s, c)
                slot = grads.at[s, c]
                copy = remote(slot, slot, s3_send.at[2 * s + c], s3_recv.at[0], sibling)
                pl.when(jnp.logical_or(to_x != x, to_j != j))(copy.wait_send)


def per_device(transmission, probe, offsets, measured):
    layers, _, rows, win = transmission.shape
    side = probe.shape[-1]
    group = 4 * layers
    rights, lefts, transforms = tables(side)
    dma = pltpu.SemaphoreType.DMA
    hbm = pl.BlockSpec(memory_space=pl.ANY)
    smem = pl.BlockSpec(memory_space=pltpu.SMEM)
    arrived = pl.pallas_call(
        kernel,
        out_shape=jax.ShapeDtypeStruct((8, rows, win), BF16),
        in_specs=[smem, vmem(), hbm, hbm, hbm, hbm, hbm],
        out_specs=vmem(),
        scratch_shapes=[
            pltpu.VMEM((8, 128), jnp.int32),
            pltpu.VMEM((4, 8, 128), jnp.int32),
            pltpu.VMEM((8, 2, rows, win), BF16),
            pltpu.VMEM((8, side, win), BF16),
            pltpu.VMEM((8, win, side), BF16),
            pltpu.VMEM((8, side, side), BF16),
            pltpu.VMEM((group, 2, side, side), BF16),
            pltpu.VMEM((group + 1, 2, side, side), BF16),
            pltpu.VMEM((2, side, side), BF16),
            pltpu.VMEM((2, side, side), F32),
            pltpu.VMEM((2, side, side), BF16),
            pltpu.VMEM((2, side, side), F32),
            pltpu.VMEM((group, 2, side, side), BF16),
            pltpu.VMEM((side, side), F32),
            pltpu.VMEM(rights.shape, BF16),
            pltpu.VMEM(lefts.shape, BF16),
            pltpu.VMEM(transforms.shape, BF16),
            pltpu.VMEM((8, side, side), BF16),
            pltpu.VMEM((8, side, win), BF16),
            pltpu.VMEM((2, 2, win // 2, 4 * side), BF16),
            pltpu.VMEM((4 * side, win), BF16),
            pltpu.VMEM((2, win // 2, win), F32),
            pltpu.VMEM((8, rows, win), BF16),
            pltpu.VMEM((8, rows, win), BF16),
            pltpu.VMEM((8, rows, win), BF16),
            dma((5,)), dma((8,)), dma((8,)), dma((4,)), dma((4,)), dma((8,)), dma((8,)), dma((8,)),
            dma((16,)), dma((2,)), dma((2,)), dma((16,)), dma((8,)), dma((1,)), dma((1,)), dma((8,)), dma((8,)),
        ],
        compiler_params=pltpu.CompilerParams(
            collective_id=0, has_side_effects=True, vmem_limit_bytes=VMEM_LIMIT
        ),
        name="ptychography_backward",
    )(
        offsets, transmission, probe, measured,
        jnp.asarray(rights), jnp.asarray(lefts), jnp.asarray(transforms),
    )
    parts = arrived.reshape(2, layers, 2, rows, win)
    return parts[0].astype(F32) + parts[1].astype(F32)


def solution(mesh):
    in_specs = (P("depth", None, "pos", None), P(), P("pos", None), P("pos", None, None))
    out_specs = P("depth", None, "pos", None)
    return jax.shard_map(
        per_device, mesh=mesh, in_specs=in_specs, out_specs=out_specs, check_vma=False
    )
```

```python
import functools
import math

import jax
import jax.numpy as jnp
import ml_dtypes
import numpy as np
from jax import lax
from jax.experimental import pallas as pl
from jax.experimental.pallas import tpu as pltpu
from jax.sharding import PartitionSpec as P


MESH = pl.DeviceIdType.MESH
F32 = jnp.float32
BF16 = jnp.bfloat16
VMEM_LIMIT = 56 * 1024 * 1024


def vmem():
    return pl.BlockSpec(memory_space=pltpu.VMEM)


def place():
    d = lax.axis_index("depth")
    q = lax.axis_index("pos")
    return d // 4, d % 4, q // 4, (q // 2) % 2, q % 2


def hi_lo(table, axis):
    high = table.astype(ml_dtypes.bfloat16)
    low = (table - high.astype(np.float64)).astype(ml_dtypes.bfloat16)
    return np.concatenate([high, low], axis)


def right_form(matrix):
    return np.block([[matrix.real, matrix.imag], [-matrix.imag, matrix.real]])


@functools.lru_cache(maxsize=None)
def tables(side):
    half = side // 2
    grid = np.arange(side)
    fourier = np.exp(-2j * np.pi * (np.outer(grid, grid) % side) / side) / math.sqrt(side)
    frequency = (grid + half) % side - half
    phase = np.exp(-1j * math.pi * frequency.astype(np.float64) ** 2 / 1024.0)
    circulant = fourier.conj() @ (phase[:, None] * fourier)
    near, far = circulant[:half, :half], circulant[:half, half:]
    forms = [right_form((near + far) / 2), right_form((near - far) / 2)]
    rights = np.stack([[hi_lo(m, 0) for m in forms], [hi_lo(m.T, 0) for m in forms]])
    order = grid.reshape(2, half // STRIP, STRIP).transpose(1, 0, 2).reshape(side)
    strided = [m[order][:, order] for m in forms]
    lefts = np.stack([[hi_lo(m.T, 1) for m in strided], [hi_lo(m, 1) for m in strided]])
    transforms = np.stack([hi_lo(m, 0) for m in (fourier.real, fourier.imag, -fourier.imag)])
    return rights, lefts, transforms.reshape(3, 2, side, side)


def dot(a, b):
    return jnp.dot(a, b, preferred_element_type=F32)


def cat(parts, axis):
    return jnp.concatenate(parts, axis)


STRIP = 16
BLOCKS = 2


def strips(count):
    return range(0, count, STRIP)


def halves(value):
    middle = value.shape[1] // 2
    return value[:, :middle], value[:, middle:]


def put_sums(ref, at, real, imag):
    (a, b), (c, d) = halves(real), halves(imag)
    ref[0, pl.ds(at, STRIP), :] = cat([a + b, c + d], 1).astype(BF16)
    ref[1, pl.ds(at, STRIP), :] = cat([a - b, c - d], 1).astype(BF16)


def sums_row(row, side):
    half = side // 2
    return 2 * row if row < half else 2 * (row - half) + STRIP


def right_stage(sums, flat, middle, right_ref, way):
    side = sums.shape[1]
    block = side // BLOCKS
    for n in range(BLOCKS):
        for m in range(2):
            x = sums[m, pl.ds(n * block, block), :]
            flat[m, pl.ds(n * block, block), :] = dot(cat([x, x], 1), right_ref[way, m])
        for r in range(n * block, (n + 1) * block, 2 * STRIP):
            s, t = flat[0, pl.ds(r, STRIP), :], flat[0, pl.ds(r + STRIP, STRIP), :]
            d, e = flat[1, pl.ds(r, STRIP), :], flat[1, pl.ds(r + STRIP, STRIP), :]
            for m, (a, b) in enumerate(((s + t, d + e), (s - t, d - e))):
                (a_real, a_imag), (b_real, b_imag) = halves(a), halves(b)
                middle[m, pl.ds(r, STRIP), :] = cat([a_real, b_real], 1).astype(BF16)
                middle[m, pl.ds(r + STRIP, STRIP), :] = cat([a_imag, b_imag], 1).astype(BF16)


def left_stage(middle, field, left_ref, way):
    side = middle.shape[1]
    block = side // BLOCKS
    for n in range(BLOCKS):
        for m in range(2):
            x = middle[m]
            field[m, pl.ds(n * block, block), :] = dot(
                left_ref[way, m, pl.ds(n * block, block), :], cat([x, x], 0)
            )
        for r in range(n * block, (n + 1) * block, 2 * STRIP):
            p, u = field[0, pl.ds(r, STRIP), :], field[0, pl.ds(r + STRIP, STRIP), :]
            m, v = field[1, pl.ds(r, STRIP), :], field[1, pl.ds(r + STRIP, STRIP), :]
            for at, real, imag in ((r // 2, p + m, u + v), (side // 2 + r // 2, p - m, u - v)):
                (a, b), (c, d) = halves(real), halves(imag)
                yield at, cat([a + b, a - b], 1), cat([c + d, c - d], 1)


def strip(ref, s, c, at):
    return ref[s, c, pl.ds(at, STRIP), :].astype(F32)


def fourier_right(real, imag, f, inverse):
    r, i, n = f
    up, down = (n, i) if inverse else (i, n)
    x = cat([real, real, imag, imag], 1)
    a = dot(x, cat([r[0], r[1], down[0], down[1]], 0))
    b = dot(x, cat([up[0], up[1], r[0], r[1]], 0))
    return a, b


def fourier_left(real, imag, f, inverse):
    r, i, n = f
    up, down = (n, i) if inverse else (i, n)
    x = cat([real, real, imag, imag], 0)
    a = dot(cat([r[0], r[1], down[0], down[1]], 1), x)
    b = dot(cat([up[0], up[1], r[0], r[1]], 1), x)
    return a, b


def neighbours(g, j, x, h, core):
    d = 4 * g + j
    xy = 2 * x + h
    partners = [(d, 4 * x + 2 * h + 1 - core)]
    for k in range(1, 8):
        partners.append((d, 2 * ((xy + k) % 8) + core))
    for kx in range(4):
        for kj in range(1, 4):
            partners.append((4 * g + (j + kj) % 4, 4 * ((x + kx) % 4) + 2 * h + core))
    return partners


def remote(src, dst, send, recv, device):
    return pltpu.make_async_remote_copy(
        src_ref=src, dst_ref=dst, send_sem=send, recv_sem=recv, device_id=device, device_id_type=MESH
    )


def one_hot(mask):
    return jnp.where(mask, 1.0, 0.0).astype(BF16)


def shifts(columns):
    return lax.broadcasted_iota(jnp.int32, (STRIP, columns), 1) - lax.broadcasted_iota(
        jnp.int32, (STRIP, columns), 0
    )


def fill_rows(ref, offset):
    rows, columns = ref.shape
    lanes = cat([offset] * (columns // 128), 1)
    base = shifts(columns)
    for r in strips(rows):
        ref[pl.ds(r, STRIP), :] = one_hot(base == lanes + r)


def fill_columns(ref, offset, row_of=lambda r: r):
    rows, columns = ref.shape
    lanes = cat([offset] * (columns // 128), 1)
    base = shifts(columns)
    for r in strips(rows):
        ref[pl.ds(r, STRIP), :] = one_hot(base == row_of(r) - lanes)


def kernel(
    off_ref, t_ref, probe_hbm, measured_hbm, right_hbm, left_hbm, transform_hbm, arrived,
    own_offsets, offs, plane, pick_rows, pick_columns, stage, o_ref, stored, sums, flat, middle, field, grads, measured_ref, right_ref, left_ref,
    transform_ref, patches, put_columns, put_rows, wide, total, partial, sibling_sum, reduced,
    crop_relay, patch_relay, crop_relay_send, crop_relay_recv, patch_relay_send, patch_relay_recv,
    load_sem, s1_send, s1_recv, off_send, off_recv, chip_send, chip_recv, s2_send, s2_recv,
    hop_send, hop_recv, s3_send, s3_recv, back_send, back_recv, s4_send, s4_recv,
):
    g, j, x, h, core = place()
    d = 4 * g + j
    q = 4 * x + 2 * h + core
    xy = 2 * x + h
    last = 3
    sibling = (d, 4 * x + 2 * h + 1 - core)
    win = plane.shape[-1]
    side = o_ref.shape[-1]
    half = side // 2
    count = o_ref.shape[0]
    block = plane.shape[2]
    active = jnp.logical_or(j == core, j == 3 - core)
    mine = jnp.where(j == core, 0, 1)
    ahead = (jnp.minimum(d + 4, 15), q)
    behind = (jnp.maximum(d - 4, 0), q)

    loads = [
        pltpu.make_async_copy(right_hbm, right_ref, load_sem.at[0]),
        pltpu.make_async_copy(left_hbm, left_ref, load_sem.at[1]),
        pltpu.make_async_copy(transform_hbm, transform_ref, load_sem.at[2]),
        pltpu.make_async_copy(measured_hbm.at[mine], measured_ref, load_sem.at[3]),
    ]
    load_probe = pltpu.make_async_copy(probe_hbm, stored.at[0], load_sem.at[4])
    barrier = pltpu.get_barrier_semaphore()
    partners = neighbours(g, j, x, h, core)
    relayed = [(4 * g + (j + k) % 4, 4 * ((x + 1) % 4) + 2 * h + 1 - core) for k in range(4)]
    for partner in partners + relayed:
        pl.semaphore_signal(barrier, inc=1, device_id=partner, device_id_type=MESH)

    @pl.when(jnp.logical_and(active, g < last))
    def _():
        pl.semaphore_signal(barrier, inc=1, device_id=ahead, device_id_type=MESH)

    @pl.when(jnp.logical_and(active, g > 0))
    def _():
        pl.semaphore_signal(barrier, inc=1, device_id=behind, device_id_type=MESH)

    chained = jnp.where(active, jnp.where(jnp.logical_or(g == 0, g == last), 1, 2), 0)
    for load in loads:
        load.start()
    pl.when(g == 0)(load_probe.start)
    for k in range(4):
        own_offsets[k : k + 1, :] = jnp.full((1, 128), off_ref[k // 2, k % 2], jnp.int32)
        own_offsets[k + 4 : k + 5, :] = jnp.zeros((1, 128), jnp.int32)
    pl.semaphore_wait(barrier, len(partners) + len(relayed) + chained)

    for k in range(1, 4):
        to = (x + k) % 4
        remote(
            own_offsets, offs.at[x], off_send.at[k], off_recv.at[k], (d, 4 * to + 2 * h + core)
        ).start()
    for k in (4, 3, 5, 2, 6, 1, 7):
        to = (xy + k) % 8
        tx = to // 2
        remote(
            t_ref.at[tx // 2, tx % 2], plane.at[xy, core], s1_send.at[k], s1_recv.at[k], (d, 2 * to + core)
        ).start()
    own = t_ref.at[x // 2, x % 2]
    remote(own, plane.at[xy, core], chip_send.at[0], chip_recv.at[0], sibling).start()
    plane[xy, core] = t_ref[x // 2, x % 2]
    offs[x] = own_offsets[...]

    for i in (1, 0):
        for k in (0, 3, 2, 1):
            from_x = (x - k + 4) % 4
            if k and i:
                slot = offs.at[from_x]
                remote(slot, slot, off_send.at[k], off_recv.at[k], sibling).wait_recv()
            slot = 2 * ((4 - k) % 4) + i
            fill_rows(pick_rows.at[slot], offs[from_x, 2 * i : 2 * i + 1, :])
            fill_columns(pick_columns.at[slot], offs[from_x, 2 * i + 1 : 2 * i + 2, :])

    for k in (1, 7, 2, 6, 3, 5, 4):
        rows = plane.at[(xy - k + 8) % 8, core]
        remote(rows, rows, s1_send.at[k], s1_recv.at[k], sibling).wait_recv()
        remote(rows, rows, chip_send.at[k], chip_recv.at[k], sibling).start()
    for k in range(8):
        rows = plane.at[(xy - k + 8) % 8, 1 - core]
        remote(rows, rows, chip_send.at[k], chip_recv.at[k], sibling).wait_recv()

    def target(k, i):
        to_j = core if i == 0 else 3 - core
        return to_j, (4 * g + to_j, 4 * ((x + k) % 4) + 2 * h + core)

    own_plane = 2 * j + x // 2
    home = o_ref.at[own_plane, x % 2]
    for i in (1, 0):
        for k in (2, 1, 3, 0):
            slot = 2 * k + i
            rows = dot(pick_rows[slot], plane[...].reshape(win, win)).astype(BF16)
            stage[slot] = dot(rows, pick_columns[slot]).astype(BF16)
            to_j, device = target(k, i)
            copy = remote(
                stage.at[slot], home, s2_send.at[slot], s2_recv.at[2 * own_plane + x % 2], device
            )
            if k == 2:
                pl.when(core == 0)(copy.start)
                pl.when(core == 1)(
                    remote(
                        stage.at[slot], crop_relay.at[i], s2_send.at[slot], crop_relay_recv.at[i],
                        (d, 4 * ((x + 3) % 4) + 2 * h + core),
                    ).start
                )
            elif k:
                copy.start()
            else:
                pl.when(to_j != j)(copy.start)

                @pl.when(to_j == j)
                def _():
                    o_ref[own_plane, x % 2] = stage[slot]

    def crop_forward(i):
        from_x = (x + 1) % 4
        from_plane = 2 * j + from_x // 2
        to_j = core if i == 0 else 3 - core
        return remote(
            crop_relay.at[i], o_ref.at[from_plane, from_x % 2], crop_relay_send.at[i],
            s2_recv.at[2 * from_plane + from_x % 2], (4 * g + to_j, 4 * ((x + 3) % 4) + 2 * h + core),
        )

    @pl.when(core == 1)
    def _():
        for i in (1, 0):
            slot = crop_relay.at[i]
            remote(slot, slot, s2_send.at[0], crop_relay_recv.at[i], sibling).wait_recv()
            crop_forward(i).start()

    for load in loads:
        load.wait()
    pl.when(g == 0)(load_probe.wait)
    hop_forward = remote(stored.at[count], stored.at[0], hop_send.at[0], hop_recv.at[0], ahead)
    hop_backward = remote(middle, middle, hop_send.at[1], hop_recv.at[1], behind)

    def owner(s, c):
        return 2 * (s % 2) + c, s // 2

    def make_put_tables():
        for i in range(2):
            for k in range(4):
                at = 4 * (1 - i) + k
                from_x = (x + k) % 4
                fill_rows(put_columns.at[at], offs[from_x, 2 * i + 1 : 2 * i + 2, :])
                for m in range(2):
                    first = 1 - core if m == 0 else core
                    fill_columns(
                        put_rows.at[m, 1 - i, :, k * side : (k + 1) * side],
                        offs[from_x, 2 * i : 2 * i + 1, :],
                        lambda r: r + (r // block + first) * block,
                    )

    starts = jnp.logical_and(active, g == 0)
    pl.when(jnp.logical_not(starts))(make_put_tables)

    @pl.when(active)
    def _():
        @pl.when(g > 0)
        def _():
            hop_forward.wait_recv()

        def wait_crop(s):
            for c in range(2):
                from_x, from_j = owner(s, c)
                slot = o_ref.at[s, c]
                copy = remote(slot, slot, s2_send.at[0], s2_recv.at[2 * s + c], sibling)
                pl.when(jnp.logical_or(from_x != x, from_j != j))(copy.wait_recv)

        def enter(s, at, real, imag):
            o_real, o_imag = strip(o_ref, s, 0, at), strip(o_ref, s, 1, at)
            put_sums(
                sums, sums_row(at, side), o_real * real - o_imag * imag, o_real * imag + o_imag * real
            )

        def keep_wave(s, at, real, imag):
            stored[s, 0, pl.ds(at, STRIP), :] = real.astype(BF16)
            stored[s, 1, pl.ds(at, STRIP), :] = imag.astype(BF16)

        def forward(s, carry):
            wait_crop(s + 1)
            for at, real, imag in left_stage(middle, field, left_ref, 0):
                keep_wave(s + 1, at, real, imag)
                enter(s + 1, at, real, imag)
            right_stage(sums, flat, middle, right_ref, 0)
            return carry

        wait_crop(0)
        for at in strips(side):
            enter(0, at, strip(stored, 0, 0, at), strip(stored, 0, 1, at))
        right_stage(sums, flat, middle, right_ref, 0)
        lax.fori_loop(0, count - 1, forward, 0)
        for at, real, imag in left_stage(middle, field, left_ref, 0):
            keep_wave(count, at, real, imag)

        @pl.when(g < last)
        def _():
            hop_forward.start()
            pl.when(g == 0)(make_put_tables)
            remote(middle, middle, hop_send.at[1], hop_recv.at[1], ahead).wait_recv()

        @pl.when(g == last)
        def _():
            f = [(transform_ref[m, 0], transform_ref[m, 1]) for m in range(3)]
            a, b = fourier_right(stored[count, 0], stored[count, 1], f, False)
            middle[0] = a.astype(BF16)
            middle[1] = b.astype(BF16)
            a, b = fourier_left(middle[0], middle[1], f, False)
            flat[0] = a
            flat[1] = b
            for at in strips(side):
                real, imag = flat[0, pl.ds(at, STRIP), :], flat[1, pl.ds(at, STRIP), :]
                weight = real * real + imag * imag - measured_ref[pl.ds(at, STRIP), :]
                sums[0, pl.ds(at, STRIP), :] = (real * weight).astype(BF16)
                sums[1, pl.ds(at, STRIP), :] = (imag * weight).astype(BF16)
            a, b = fourier_right(sums[0], sums[1], f, True)
            middle[0] = a.astype(BF16)
            middle[1] = b.astype(BF16)
            a, b = fourier_left(middle[0], middle[1], f, True)
            flat[0] = a
            flat[1] = b
            for at in strips(side):
                put_sums(
                    sums, sums_row(at, side), flat[0, pl.ds(at, STRIP), :], flat[1, pl.ds(at, STRIP), :]
                )
            right_stage(sums, flat, middle, right_ref, 1)

        def send_patches(s):
            for c in range(2):
                to_x, to_j = owner(s, c)
                source, send = grads.at[s, c], s3_send.at[2 * s + c]
                away = jnp.logical_or(to_x != x, to_j != j)
                detour = jnp.logical_and(to_x == (x + 2) % 4, to_j % 2 == 1)
                copy = remote(
                    source, patches.at[2 * x + mine], send, s3_recv.at[2 * x + mine],
                    (4 * g + to_j, 4 * to_x + 2 * h + core),
                )
                pl.when(jnp.logical_and(away, jnp.logical_not(detour)))(copy.start)
                pl.when(detour)(
                    remote(
                        source, patch_relay.at[to_j // 2], send, patch_relay_recv.at[to_j // 2],
                        (d, 4 * ((x + 3) % 4) + 2 * h + 1 - core),
                    ).start
                )

                @pl.when(jnp.logical_not(away))
                def _():
                    patches[2 * x + mine] = grads[s, c]

        def leave(s):
            for at, real, imag in left_stage(middle, field, left_ref, 1):
                o_real, o_imag = strip(o_ref, s, 0, at), strip(o_ref, s, 1, at)
                put_sums(
                    sums, sums_row(at, side), o_real * real + o_imag * imag, o_real * imag - o_imag * real
                )
                p_real, p_imag = strip(stored, s, 0, at), strip(stored, s, 1, at)
                grads[s, 0, pl.ds(at, STRIP), :] = (p_real * real + p_imag * imag).astype(BF16)
                grads[s, 1, pl.ds(at, STRIP), :] = (p_real * imag - p_imag * real).astype(BF16)

        def backward(t, carry):
            s = count - 1 - t
            leave(s)
            right_stage(sums, flat, middle, right_ref, 1)
            pl.when(g == 0)(functools.partial(send_patches, s))
            return carry

        lax.fori_loop(0, count - 1, backward, 0)
        leave(0)
        pl.when(g == 0)(functools.partial(send_patches, 0))

        @pl.when(g > 0)
        def _():
            right_stage(sums, flat, middle, right_ref, 1)
            hop_backward.start()
            hop_backward.wait_send()

            def send(t, carry):
                send_patches(count - 1 - t)
                return carry

            lax.fori_loop(0, count, send, 0)

    def patch_forward(n):
        from_x = (x + 1) % 4
        p = 2 * from_x + jnp.where(j == 1 - core, 0, 1)
        return remote(
            patch_relay.at[n], patches.at[p], patch_relay_send.at[n], s3_recv.at[p],
            (4 * g + 2 * n + 1, 4 * ((x + 3) % 4) + 2 * h + 1 - core),
        )

    @pl.when(jnp.logical_not(active))
    def _():
        for n in (1, 0):
            slot = patch_relay.at[n]
            remote(slot, slot, s3_send.at[0], patch_relay_recv.at[n], sibling).wait_recv()
            patch_forward(n).start()

    for i in (1, 0):
        group = 1 - i
        for kx in range(4):
            from_x = (x - kx + 4) % 4
            from_j = core if i == 0 else 3 - core
            p = 2 * from_x + i
            slot = patches.at[p]
            copy = remote(slot, slot, s3_send.at[0], s3_recv.at[p], sibling)
            if kx:
                copy.wait_recv()
            else:
                pl.when(from_j != j)(copy.wait_recv)
            at = (4 - kx) % 4
            wide[at * side : (at + 1) * side, :] = dot(slot[...], put_columns[4 * group + at]).astype(BF16)
        if group == 0:
            for m in range(2):
                total[m] = dot(put_rows[m, 0], wide[...])
    partial[...] = (total[0] + dot(put_rows[0, 1], wide[...])).reshape(partial.shape).astype(BF16)
    chip_copy = remote(partial, sibling_sum, back_send.at[0], back_recv.at[0], sibling)
    chip_copy.start()
    own_rows = (total[1] + dot(put_rows[1, 1], wide[...])).reshape(partial.shape)
    chip_copy.wait_recv()
    reduced[...] = (own_rows + sibling_sum[...].astype(F32)).astype(BF16)
    for k in (4, 3, 5, 2, 6, 1, 7):
        to = (xy + k) % 8
        remote(reduced.at[to], arrived.at[4 * h + x], s4_send.at[k], s4_recv.at[k], (d, 2 * to + core)).start()
    arrived[4 * h + x] = reduced[xy]
    for k in range(1, 8):
        come = (xy - k + 8) % 8
        slot = arrived.at[4 * (come % 2) + come // 2]
        remote(slot, slot, s4_send.at[k], s4_recv.at[k], sibling).wait_recv()

    for k in range(1, 8):
        slot = reduced.at[0]
        remote(slot, slot, s1_send.at[k], s1_recv.at[k], sibling).wait_send()
        remote(slot, slot, s4_send.at[k], s4_recv.at[k], sibling).wait_send()
    for k in range(1, 4):
        remote(own_offsets, own_offsets, off_send.at[k], off_recv.at[k], sibling).wait_send()
    for k in range(8):
        slot = reduced.at[0]
        remote(slot, slot, chip_send.at[k], chip_recv.at[k], sibling).wait_send()
    chip_copy.wait_send()
    for i in range(2):
        for k in range(4):
            slot = 2 * k + i
            to_j, device = target(k, i)
            copy = remote(stage.at[slot], home, s2_send.at[slot], s2_recv.at[0], device)
            if k:
                copy.wait_send()
            else:
                pl.when(to_j != j)(copy.wait_send)

    @pl.when(core == 1)
    def _():
        for i in range(2):
            crop_forward(i).wait_send()

    @pl.when(jnp.logical_not(active))
    def _():
        for n in range(2):
            patch_forward(n).wait_send()

    @pl.when(active)
    def _():
        pl.when(g < last)(hop_forward.wait_send)
        for s in range(count):
            for c in range(2):
                to_x, to_j = owner(s, c)
                slot = grads.at[s, c]
                copy = remote(slot, slot, s3_send.at[2 * s + c], s3_recv.at[0], sibling)
                pl.when(jnp.logical_or(to_x != x, to_j != j))(copy.wait_send)


def per_device(transmission, probe, offsets, measured):
    layers, _, rows, win = transmission.shape
    side = probe.shape[-1]
    group = 4 * layers
    rights, lefts, transforms = tables(side)
    dma = pltpu.SemaphoreType.DMA
    hbm = pl.BlockSpec(memory_space=pl.ANY)
    smem = pl.BlockSpec(memory_space=pltpu.SMEM)
    arrived = pl.pallas_call(
        kernel,
        out_shape=jax.ShapeDtypeStruct((8, rows, win), BF16),
        in_specs=[smem, vmem(), hbm, hbm, hbm, hbm, hbm],
        out_specs=vmem(),
        scratch_shapes=[
            pltpu.VMEM((8, 128), jnp.int32),
            pltpu.VMEM((4, 8, 128), jnp.int32),
            pltpu.VMEM((8, 2, rows, win), BF16),
            pltpu.VMEM((8, side, win), BF16),
            pltpu.VMEM((8, win, side), BF16),
            pltpu.VMEM((8, side, side), BF16),
            pltpu.VMEM((group, 2, side, side), BF16),
            pltpu.VMEM((group + 1, 2, side, side), BF16),
            pltpu.VMEM((2, side, side), BF16),
            pltpu.VMEM((2, side, side), F32),
            pltpu.VMEM((2, side, side), BF16),
            pltpu.VMEM((2, side, side), F32),
            pltpu.VMEM((group, 2, side, side), BF16),
            pltpu.VMEM((side, side), F32),
            pltpu.VMEM(rights.shape, BF16),
            pltpu.VMEM(lefts.shape, BF16),
            pltpu.VMEM(transforms.shape, BF16),
            pltpu.VMEM((8, side, side), BF16),
            pltpu.VMEM((8, side, win), BF16),
            pltpu.VMEM((2, 2, win // 2, 4 * side), BF16),
            pltpu.VMEM((4 * side, win), BF16),
            pltpu.VMEM((2, win // 2, win), F32),
            pltpu.VMEM((8, rows, win), BF16),
            pltpu.VMEM((8, rows, win), BF16),
            pltpu.VMEM((8, rows, win), BF16),
            pltpu.VMEM((2, side, side), BF16),
            pltpu.VMEM((2, side, side), BF16),
            dma((2,)), dma((2,)), dma((2,)), dma((2,)),
            dma((5,)), dma((8,)), dma((8,)), dma((4,)), dma((4,)), dma((8,)), dma((8,)), dma((8,)),
            dma((16,)), dma((2,)), dma((2,)), dma((16,)), dma((8,)), dma((1,)), dma((1,)), dma((8,)), dma((8,)),
        ],
        compiler_params=pltpu.CompilerParams(
            collective_id=0, has_side_effects=True, vmem_limit_bytes=VMEM_LIMIT
        ),
        name="ptychography_backward",
    )(
        offsets, transmission, probe, measured,
        jnp.asarray(rights), jnp.asarray(lefts), jnp.asarray(transforms),
    )
    parts = arrived.reshape(2, layers, 2, rows, win)
    return parts[0].astype(F32) + parts[1].astype(F32)


def solution(mesh):
    in_specs = (P("depth", None, "pos", None), P(), P("pos", None), P("pos", None, None))
    out_specs = P("depth", None, "pos", None)
    return jax.shard_map(
        per_device, mesh=mesh, in_specs=in_specs, out_specs=out_specs, check_vma=False
    )
```

```python
import functools
import math

import jax
import jax.numpy as jnp
import ml_dtypes
import numpy as np
from jax import lax
from jax.experimental import pallas as pl
from jax.experimental.pallas import tpu as pltpu
from jax.sharding import PartitionSpec as P


MESH = pl.DeviceIdType.MESH
F32 = jnp.float32
BF16 = jnp.bfloat16
VMEM_LIMIT = 56 * 1024 * 1024


def vmem():
    return pl.BlockSpec(memory_space=pltpu.VMEM)


def place():
    d = lax.axis_index("depth")
    q = lax.axis_index("pos")
    return d // 4, d % 4, q // 4, (q // 2) % 2, q % 2


def hi_lo(table, axis):
    high = table.astype(ml_dtypes.bfloat16)
    low = (table - high.astype(np.float64)).astype(ml_dtypes.bfloat16)
    return np.concatenate([high, low], axis)


def right_form(matrix):
    return np.block([[matrix.real, matrix.imag], [-matrix.imag, matrix.real]])


@functools.lru_cache(maxsize=None)
def tables(side):
    half = side // 2
    grid = np.arange(side)
    fourier = np.exp(-2j * np.pi * (np.outer(grid, grid) % side) / side) / math.sqrt(side)
    frequency = (grid + half) % side - half
    phase = np.exp(-1j * math.pi * frequency.astype(np.float64) ** 2 / 1024.0)
    circulant = fourier.conj() @ (phase[:, None] * fourier)
    near, far = circulant[:half, :half], circulant[:half, half:]
    forms = [right_form((near + far) / 2), right_form((near - far) / 2)]
    rights = np.stack([[hi_lo(m, 0) for m in forms], [hi_lo(m.T, 0) for m in forms]])
    order = grid.reshape(2, half // STRIP, STRIP).transpose(1, 0, 2).reshape(side)
    strided = [m[order][:, order] for m in forms]
    lefts = np.stack([[hi_lo(m.T, 1) for m in strided], [hi_lo(m, 1) for m in strided]])
    transforms = np.stack([hi_lo(m, 0) for m in (fourier.real, fourier.imag, -fourier.imag)])
    return rights, lefts, transforms.reshape(3, 2, side, side)


def dot(a, b):
    return jnp.dot(a, b, preferred_element_type=F32)


def cat(parts, axis):
    return jnp.concatenate(parts, axis)


STRIP = 16
BLOCKS = 4


def strips(count):
    return range(0, count, STRIP)


def halves(value):
    middle = value.shape[1] // 2
    return value[:, :middle], value[:, middle:]


def put_sums(ref, at, real, imag):
    (a, b), (c, d) = halves(real), halves(imag)
    ref[0, pl.ds(at, STRIP), :] = cat([a + b, c + d], 1).astype(BF16)
    ref[1, pl.ds(at, STRIP), :] = cat([a - b, c - d], 1).astype(BF16)


def sums_row(row, side):
    half = side // 2
    return 2 * row if row < half else 2 * (row - half) + STRIP


def right_stage(sums, flat, middle, right_ref, way, done=lambda n: None):
    side = sums.shape[1]
    block = side // BLOCKS
    for n in range(BLOCKS):
        for m in range(2):
            x = sums[m, pl.ds(n * block, block), :]
            flat[m, pl.ds(n * block, block), :] = dot(cat([x, x], 1), right_ref[way, m])
        for r in range(n * block, (n + 1) * block, 2 * STRIP):
            s, t = flat[0, pl.ds(r, STRIP), :], flat[0, pl.ds(r + STRIP, STRIP), :]
            d, e = flat[1, pl.ds(r, STRIP), :], flat[1, pl.ds(r + STRIP, STRIP), :]
            for m, (a, b) in enumerate(((s + t, d + e), (s - t, d - e))):
                (a_real, a_imag), (b_real, b_imag) = halves(a), halves(b)
                middle[m, pl.ds(r, STRIP), :] = cat([a_real, b_real], 1).astype(BF16)
                middle[m, pl.ds(r + STRIP, STRIP), :] = cat([a_imag, b_imag], 1).astype(BF16)
        done(n)


def left_stage(middle, field, left_ref, way):
    side = middle.shape[1]
    block = side // BLOCKS
    for n in range(BLOCKS):
        for m in range(2):
            x = middle[m]
            field[m, pl.ds(n * block, block), :] = dot(
                left_ref[way, m, pl.ds(n * block, block), :], cat([x, x], 0)
            )
        for r in range(n * block, (n + 1) * block, 2 * STRIP):
            p, u = field[0, pl.ds(r, STRIP), :], field[0, pl.ds(r + STRIP, STRIP), :]
            m, v = field[1, pl.ds(r, STRIP), :], field[1, pl.ds(r + STRIP, STRIP), :]
            for at, real, imag in ((r // 2, p + m, u + v), (side // 2 + r // 2, p - m, u - v)):
                (a, b), (c, d) = halves(real), halves(imag)
                yield at, cat([a + b, a - b], 1), cat([c + d, c - d], 1)


def strip(ref, s, c, at):
    return ref[s, c, pl.ds(at, STRIP), :].astype(F32)


def fourier_right(real, imag, f, inverse):
    r, i, n = f
    up, down = (n, i) if inverse else (i, n)
    x = cat([real, real, imag, imag], 1)
    a = dot(x, cat([r[0], r[1], down[0], down[1]], 0))
    b = dot(x, cat([up[0], up[1], r[0], r[1]], 0))
    return a, b


def fourier_left(real, imag, f, inverse):
    r, i, n = f
    up, down = (n, i) if inverse else (i, n)
    x = cat([real, real, imag, imag], 0)
    a = dot(cat([r[0], r[1], down[0], down[1]], 1), x)
    b = dot(cat([up[0], up[1], r[0], r[1]], 1), x)
    return a, b


def neighbours(g, j, x, h, core):
    d = 4 * g + j
    xy = 2 * x + h
    partners = [(d, 4 * x + 2 * h + 1 - core)]
    for k in range(1, 8):
        partners.append((d, 2 * ((xy + k) % 8) + core))
    for kx in range(4):
        for kj in range(1, 4):
            partners.append((4 * g + (j + kj) % 4, 4 * ((x + kx) % 4) + 2 * h + core))
    return partners


def remote(src, dst, send, recv, device):
    return pltpu.make_async_remote_copy(
        src_ref=src, dst_ref=dst, send_sem=send, recv_sem=recv, device_id=device, device_id_type=MESH
    )


def one_hot(mask):
    return jnp.where(mask, 1.0, 0.0).astype(BF16)


def shifts(columns):
    return lax.broadcasted_iota(jnp.int32, (STRIP, columns), 1) - lax.broadcasted_iota(
        jnp.int32, (STRIP, columns), 0
    )


def fill_rows(ref, offset):
    rows, columns = ref.shape
    lanes = cat([offset] * (columns // 128), 1)
    base = shifts(columns)
    for r in strips(rows):
        ref[pl.ds(r, STRIP), :] = one_hot(base == lanes + r)


def fill_columns(ref, offset, row_of=lambda r: r):
    rows, columns = ref.shape
    lanes = cat([offset] * (columns // 128), 1)
    base = shifts(columns)
    for r in strips(rows):
        ref[pl.ds(r, STRIP), :] = one_hot(base == row_of(r) - lanes)


def kernel(
    off_ref, t_ref, probe_hbm, measured_hbm, right_hbm, left_hbm, transform_hbm, arrived,
    own_offsets, offs, plane, pick_rows, pick_columns, stage, o_ref, stored, sums, flat, middle, field, grads, measured_ref, right_ref, left_ref,
    transform_ref, patches, put_columns, put_rows, wide, total, partial, sibling_sum, reduced,
    crop_relay, patch_relay, crop_relay_send, crop_relay_recv, patch_relay_send, patch_relay_recv,
    load_sem, s1_send, s1_recv, off_send, off_recv, chip_send, chip_recv, s2_send, s2_recv,
    hop_send, hop_recv, s3_send, s3_recv, back_send, back_recv, s4_send, s4_recv,
):
    g, j, x, h, core = place()
    d = 4 * g + j
    q = 4 * x + 2 * h + core
    xy = 2 * x + h
    last = 3
    sibling = (d, 4 * x + 2 * h + 1 - core)
    win = plane.shape[-1]
    side = o_ref.shape[-1]
    half = side // 2
    count = o_ref.shape[0]
    block = plane.shape[2]
    active = jnp.logical_or(j == core, j == 3 - core)
    mine = jnp.where(j == core, 0, 1)
    ahead = (jnp.minimum(d + 4, 15), q)
    behind = (jnp.maximum(d - 4, 0), q)

    loads = [
        pltpu.make_async_copy(right_hbm, right_ref, load_sem.at[0]),
        pltpu.make_async_copy(left_hbm, left_ref, load_sem.at[1]),
        pltpu.make_async_copy(transform_hbm, transform_ref, load_sem.at[2]),
        pltpu.make_async_copy(measured_hbm.at[mine], measured_ref, load_sem.at[3]),
    ]
    load_probe = pltpu.make_async_copy(probe_hbm, stored.at[0], load_sem.at[4])
    barrier = pltpu.get_barrier_semaphore()
    partners = neighbours(g, j, x, h, core)
    relayed = [(4 * g + (j + k) % 4, 4 * ((x + 1) % 4) + 2 * h + 1 - core) for k in range(4)]
    for partner in partners + relayed:
        pl.semaphore_signal(barrier, inc=1, device_id=partner, device_id_type=MESH)

    @pl.when(jnp.logical_and(active, g < last))
    def _():
        pl.semaphore_signal(barrier, inc=1, device_id=ahead, device_id_type=MESH)

    @pl.when(jnp.logical_and(active, g > 0))
    def _():
        pl.semaphore_signal(barrier, inc=1, device_id=behind, device_id_type=MESH)

    chained = jnp.where(active, jnp.where(jnp.logical_or(g == 0, g == last), 1, 2), 0)
    for load in loads:
        load.start()
    pl.when(g == 0)(load_probe.start)
    for k in range(4):
        own_offsets[k : k + 1, :] = jnp.full((1, 128), off_ref[k // 2, k % 2], jnp.int32)
        own_offsets[k + 4 : k + 5, :] = jnp.zeros((1, 128), jnp.int32)
    pl.semaphore_wait(barrier, len(partners) + len(relayed) + chained)

    for k in range(1, 4):
        to = (x + k) % 4
        remote(
            own_offsets, offs.at[x], off_send.at[k], off_recv.at[k], (d, 4 * to + 2 * h + core)
        ).start()
    for k in (4, 3, 5, 2, 6, 1, 7):
        to = (xy + k) % 8
        tx = to // 2
        remote(
            t_ref.at[tx // 2, tx % 2], plane.at[xy, core], s1_send.at[k], s1_recv.at[k], (d, 2 * to + core)
        ).start()
    own = t_ref.at[x // 2, x % 2]
    remote(own, plane.at[xy, core], chip_send.at[0], chip_recv.at[0], sibling).start()
    plane[xy, core] = t_ref[x // 2, x % 2]
    offs[x] = own_offsets[...]

    for i in (1, 0):
        for k in (0, 3, 2, 1):
            from_x = (x - k + 4) % 4
            if k and i:
                slot = offs.at[from_x]
                remote(slot, slot, off_send.at[k], off_recv.at[k], sibling).wait_recv()
            slot = 2 * ((4 - k) % 4) + i
            fill_rows(pick_rows.at[slot], offs[from_x, 2 * i : 2 * i + 1, :])
            fill_columns(pick_columns.at[slot], offs[from_x, 2 * i + 1 : 2 * i + 2, :])

    for k in (1, 7, 2, 6, 3, 5, 4):
        rows = plane.at[(xy - k + 8) % 8, core]
        remote(rows, rows, s1_send.at[k], s1_recv.at[k], sibling).wait_recv()
        remote(rows, rows, chip_send.at[k], chip_recv.at[k], sibling).start()
    for k in range(8):
        rows = plane.at[(xy - k + 8) % 8, 1 - core]
        remote(rows, rows, chip_send.at[k], chip_recv.at[k], sibling).wait_recv()

    def target(k, i):
        to_j = core if i == 0 else 3 - core
        return to_j, (4 * g + to_j, 4 * ((x + k) % 4) + 2 * h + core)

    own_plane = 2 * j + x // 2
    home = o_ref.at[own_plane, x % 2]
    for i in (1, 0):
        for k in (2, 1, 3, 0):
            slot = 2 * k + i
            rows = dot(pick_rows[slot], plane[...].reshape(win, win)).astype(BF16)
            stage[slot] = dot(rows, pick_columns[slot]).astype(BF16)
            to_j, device = target(k, i)
            copy = remote(
                stage.at[slot], home, s2_send.at[slot], s2_recv.at[2 * own_plane + x % 2], device
            )
            if k == 2:
                pl.when(core == 0)(copy.start)
                pl.when(core == 1)(
                    remote(
                        stage.at[slot], crop_relay.at[i], s2_send.at[slot], crop_relay_recv.at[i],
                        (d, 4 * ((x + 3) % 4) + 2 * h + core),
                    ).start
                )
            elif k:
                copy.start()
            else:
                pl.when(to_j != j)(copy.start)

                @pl.when(to_j == j)
                def _():
                    o_ref[own_plane, x % 2] = stage[slot]

    def crop_forward(i):
        from_x = (x + 1) % 4
        from_plane = 2 * j + from_x // 2
        to_j = core if i == 0 else 3 - core
        return remote(
            crop_relay.at[i], o_ref.at[from_plane, from_x % 2], crop_relay_send.at[i],
            s2_recv.at[2 * from_plane + from_x % 2], (4 * g + to_j, 4 * ((x + 3) % 4) + 2 * h + core),
        )

    @pl.when(core == 1)
    def _():
        for i in (1, 0):
            slot = crop_relay.at[i]
            remote(slot, slot, s2_send.at[0], crop_relay_recv.at[i], sibling).wait_recv()
            crop_forward(i).start()

    for load in loads:
        load.wait()
    pl.when(g == 0)(load_probe.wait)
    half = side // 2
    piece = half // 2

    def forward_pieces(n):
        rows = [pl.ds(m * half + n * piece, piece) for m in range(2)]
        return [
            remote(
                stored.at[count, :, rows[m]], stored.at[0, :, rows[m]],
                hop_send.at[2 * n + m], hop_recv.at[2 * n + m], ahead,
            )
            for m in range(2)
        ]

    def backward_piece(n, device):
        rows = middle.at[:, pl.ds(n * half, half)]
        return remote(rows, rows, hop_send.at[4 + n], hop_recv.at[4 + n], device)

    def owner(s, c):
        return 2 * (s % 2) + c, s // 2

    def make_put_tables():
        for i in range(2):
            for k in range(4):
                at = 4 * (1 - i) + k
                from_x = (x + k) % 4
                fill_rows(put_columns.at[at], offs[from_x, 2 * i + 1 : 2 * i + 2, :])
                for m in range(2):
                    first = 1 - core if m == 0 else core
                    fill_columns(
                        put_rows.at[m, 1 - i, :, k * side : (k + 1) * side],
                        offs[from_x, 2 * i : 2 * i + 1, :],
                        lambda r: r + (r // block + first) * block,
                    )

    starts = jnp.logical_and(active, g == 0)
    pl.when(jnp.logical_not(starts))(make_put_tables)

    @pl.when(active)
    def _():
        def wait_crop(s):
            for c in range(2):
                from_x, from_j = owner(s, c)
                slot = o_ref.at[s, c]
                copy = remote(slot, slot, s2_send.at[0], s2_recv.at[2 * s + c], sibling)
                pl.when(jnp.logical_or(from_x != x, from_j != j))(copy.wait_recv)

        def enter(s, at, real, imag):
            o_real, o_imag = strip(o_ref, s, 0, at), strip(o_ref, s, 1, at)
            put_sums(
                sums, sums_row(at, side), o_real * real - o_imag * imag, o_real * imag + o_imag * real
            )

        def keep_wave(s, at, real, imag):
            stored[s, 0, pl.ds(at, STRIP), :] = real.astype(BF16)
            stored[s, 1, pl.ds(at, STRIP), :] = imag.astype(BF16)

        def forward(s, carry):
            wait_crop(s + 1)
            for at, real, imag in left_stage(middle, field, left_ref, 0):
                keep_wave(s + 1, at, real, imag)
                enter(s + 1, at, real, imag)
            right_stage(sums, flat, middle, right_ref, 0)
            return carry

        wait_crop(0)
        for n in range(2):

            @pl.when(g > 0)
            def _():
                for copy in forward_pieces(n):
                    copy.wait_recv()

            for m in range(2):
                for r in strips(piece):
                    at = m * half + n * piece + r
                    enter(0, at, strip(stored, 0, 0, at), strip(stored, 0, 1, at))
        right_stage(sums, flat, middle, right_ref, 0)
        lax.fori_loop(0, count - 1, forward, 0)
        for at, real, imag in left_stage(middle, field, left_ref, 0):
            keep_wave(count, at, real, imag)
            if at >= half and (at + STRIP) % piece == 0:

                @pl.when(g < last)
                def _():
                    for copy in forward_pieces((at - half) // piece):
                        copy.start()

        @pl.when(g < last)
        def _():
            pl.when(g == 0)(make_put_tables)
            for n in range(2):
                backward_piece(n, ahead).wait_recv()

        @pl.when(g == last)
        def _():
            f = [(transform_ref[m, 0], transform_ref[m, 1]) for m in range(3)]
            a, b = fourier_right(stored[count, 0], stored[count, 1], f, False)
            middle[0] = a.astype(BF16)
            middle[1] = b.astype(BF16)
            a, b = fourier_left(middle[0], middle[1], f, False)
            flat[0] = a
            flat[1] = b
            for at in strips(side):
                real, imag = flat[0, pl.ds(at, STRIP), :], flat[1, pl.ds(at, STRIP), :]
                weight = real * real + imag * imag - measured_ref[pl.ds(at, STRIP), :]
                sums[0, pl.ds(at, STRIP), :] = (real * weight).astype(BF16)
                sums[1, pl.ds(at, STRIP), :] = (imag * weight).astype(BF16)
            a, b = fourier_right(sums[0], sums[1], f, True)
            middle[0] = a.astype(BF16)
            middle[1] = b.astype(BF16)
            a, b = fourier_left(middle[0], middle[1], f, True)
            flat[0] = a
            flat[1] = b
            for at in strips(side):
                put_sums(
                    sums, sums_row(at, side), flat[0, pl.ds(at, STRIP), :], flat[1, pl.ds(at, STRIP), :]
                )
            right_stage(sums, flat, middle, right_ref, 1)

        def send_patches(s):
            for c in range(2):
                to_x, to_j = owner(s, c)
                source, send = grads.at[s, c], s3_send.at[2 * s + c]
                away = jnp.logical_or(to_x != x, to_j != j)
                detour = jnp.logical_and(to_x == (x + 2) % 4, to_j % 2 == 1)
                copy = remote(
                    source, patches.at[2 * x + mine], send, s3_recv.at[2 * x + mine],
                    (4 * g + to_j, 4 * to_x + 2 * h + core),
                )
                pl.when(jnp.logical_and(away, jnp.logical_not(detour)))(copy.start)
                pl.when(detour)(
                    remote(
                        source, patch_relay.at[to_j // 2], send, patch_relay_recv.at[to_j // 2],
                        (d, 4 * ((x + 3) % 4) + 2 * h + 1 - core),
                    ).start
                )

                @pl.when(jnp.logical_not(away))
                def _():
                    patches[2 * x + mine] = grads[s, c]

        def leave(s):
            for at, real, imag in left_stage(middle, field, left_ref, 1):
                o_real, o_imag = strip(o_ref, s, 0, at), strip(o_ref, s, 1, at)
                put_sums(
                    sums, sums_row(at, side), o_real * real + o_imag * imag, o_real * imag - o_imag * real
                )
                p_real, p_imag = strip(stored, s, 0, at), strip(stored, s, 1, at)
                grads[s, 0, pl.ds(at, STRIP), :] = (p_real * real + p_imag * imag).astype(BF16)
                grads[s, 1, pl.ds(at, STRIP), :] = (p_real * imag - p_imag * real).astype(BF16)

        def backward(t, carry):
            s = count - 1 - t
            leave(s)
            right_stage(sums, flat, middle, right_ref, 1)
            pl.when(g == 0)(functools.partial(send_patches, s))
            return carry

        lax.fori_loop(0, count - 1, backward, 0)
        leave(0)
        pl.when(g == 0)(functools.partial(send_patches, 0))

        @pl.when(g > 0)
        def _():
            def leave_piece(n):
                if n % 2:
                    backward_piece(n // 2, behind).start()

            right_stage(sums, flat, middle, right_ref, 1, leave_piece)
            for n in range(2):
                backward_piece(n, behind).wait_send()

            def send(t, carry):
                send_patches(count - 1 - t)
                return carry

            lax.fori_loop(0, count, send, 0)

    def patch_forward(n):
        from_x = (x + 1) % 4
        p = 2 * from_x + jnp.where(j == 1 - core, 0, 1)
        return remote(
            patch_relay.at[n], patches.at[p], patch_relay_send.at[n], s3_recv.at[p],
            (4 * g + 2 * n + 1, 4 * ((x + 3) % 4) + 2 * h + 1 - core),
        )

    @pl.when(jnp.logical_not(active))
    def _():
        for n in (1, 0):
            slot = patch_relay.at[n]
            remote(slot, slot, s3_send.at[0], patch_relay_recv.at[n], sibling).wait_recv()
            patch_forward(n).start()

    for i in (1, 0):
        group = 1 - i
        for kx in range(4):
            from_x = (x - kx + 4) % 4
            from_j = core if i == 0 else 3 - core
            p = 2 * from_x + i
            slot = patches.at[p]
            copy = remote(slot, slot, s3_send.at[0], s3_recv.at[p], sibling)
            if kx:
                copy.wait_recv()
            else:
                pl.when(from_j != j)(copy.wait_recv)
            at = (4 - kx) % 4
            wide[at * side : (at + 1) * side, :] = dot(slot[...], put_columns[4 * group + at]).astype(BF16)
        if group == 0:
            for m in range(2):
                total[m] = dot(put_rows[m, 0], wide[...])
    partial[...] = (total[0] + dot(put_rows[0, 1], wide[...])).reshape(partial.shape).astype(BF16)
    chip_copy = remote(partial, sibling_sum, back_send.at[0], back_recv.at[0], sibling)
    chip_copy.start()
    own_rows = (total[1] + dot(put_rows[1, 1], wide[...])).reshape(partial.shape)
    chip_copy.wait_recv()
    reduced[...] = (own_rows + sibling_sum[...].astype(F32)).astype(BF16)
    for k in (4, 3, 5, 2, 6, 1, 7):
        to = (xy + k) % 8
        remote(reduced.at[to], arrived.at[4 * h + x], s4_send.at[k], s4_recv.at[k], (d, 2 * to + core)).start()
    arrived[4 * h + x] = reduced[xy]
    for k in range(1, 8):
        come = (xy - k + 8) % 8
        slot = arrived.at[4 * (come % 2) + come // 2]
        remote(slot, slot, s4_send.at[k], s4_recv.at[k], sibling).wait_recv()

    for k in range(1, 8):
        slot = reduced.at[0]
        remote(slot, slot, s1_send.at[k], s1_recv.at[k], sibling).wait_send()
        remote(slot, slot, s4_send.at[k], s4_recv.at[k], sibling).wait_send()
    for k in range(1, 4):
        remote(own_offsets, own_offsets, off_send.at[k], off_recv.at[k], sibling).wait_send()
    for k in range(8):
        slot = reduced.at[0]
        remote(slot, slot, chip_send.at[k], chip_recv.at[k], sibling).wait_send()
    chip_copy.wait_send()
    for i in range(2):
        for k in range(4):
            slot = 2 * k + i
            to_j, device = target(k, i)
            copy = remote(stage.at[slot], home, s2_send.at[slot], s2_recv.at[0], device)
            if k:
                copy.wait_send()
            else:
                pl.when(to_j != j)(copy.wait_send)

    @pl.when(core == 1)
    def _():
        for i in range(2):
            crop_forward(i).wait_send()

    @pl.when(jnp.logical_not(active))
    def _():
        for n in range(2):
            patch_forward(n).wait_send()

    @pl.when(active)
    def _():
        @pl.when(g < last)
        def _():
            for n in range(2):
                for copy in forward_pieces(n):
                    copy.wait_send()

        for s in range(count):
            for c in range(2):
                to_x, to_j = owner(s, c)
                slot = grads.at[s, c]
                copy = remote(slot, slot, s3_send.at[2 * s + c], s3_recv.at[0], sibling)
                pl.when(jnp.logical_or(to_x != x, to_j != j))(copy.wait_send)


def per_device(transmission, probe, offsets, measured):
    layers, _, rows, win = transmission.shape
    side = probe.shape[-1]
    group = 4 * layers
    rights, lefts, transforms = tables(side)
    dma = pltpu.SemaphoreType.DMA
    hbm = pl.BlockSpec(memory_space=pl.ANY)
    smem = pl.BlockSpec(memory_space=pltpu.SMEM)
    arrived = pl.pallas_call(
        kernel,
        out_shape=jax.ShapeDtypeStruct((8, rows, win), BF16),
        in_specs=[smem, vmem(), hbm, hbm, hbm, hbm, hbm],
        out_specs=vmem(),
        scratch_shapes=[
            pltpu.VMEM((8, 128), jnp.int32),
            pltpu.VMEM((4, 8, 128), jnp.int32),
            pltpu.VMEM((8, 2, rows, win), BF16),
            pltpu.VMEM((8, side, win), BF16),
            pltpu.VMEM((8, win, side), BF16),
            pltpu.VMEM((8, side, side), BF16),
            pltpu.VMEM((group, 2, side, side), BF16),
            pltpu.VMEM((group + 1, 2, side, side), BF16),
            pltpu.VMEM((2, side, side), BF16),
            pltpu.VMEM((2, side, side), F32),
            pltpu.VMEM((2, side, side), BF16),
            pltpu.VMEM((2, side, side), F32),
            pltpu.VMEM((group, 2, side, side), BF16),
            pltpu.VMEM((side, side), F32),
            pltpu.VMEM(rights.shape, BF16),
            pltpu.VMEM(lefts.shape, BF16),
            pltpu.VMEM(transforms.shape, BF16),
            pltpu.VMEM((8, side, side), BF16),
            pltpu.VMEM((8, side, win), BF16),
            pltpu.VMEM((2, 2, win // 2, 4 * side), BF16),
            pltpu.VMEM((4 * side, win), BF16),
            pltpu.VMEM((2, win // 2, win), F32),
            pltpu.VMEM((8, rows, win), BF16),
            pltpu.VMEM((8, rows, win), BF16),
            pltpu.VMEM((8, rows, win), BF16),
            pltpu.VMEM((2, side, side), BF16),
            pltpu.VMEM((2, side, side), BF16),
            dma((2,)), dma((2,)), dma((2,)), dma((2,)),
            dma((5,)), dma((8,)), dma((8,)), dma((4,)), dma((4,)), dma((8,)), dma((8,)), dma((8,)),
            dma((16,)), dma((6,)), dma((6,)), dma((16,)), dma((8,)), dma((1,)), dma((1,)), dma((8,)), dma((8,)),
        ],
        compiler_params=pltpu.CompilerParams(
            collective_id=0, has_side_effects=True, vmem_limit_bytes=VMEM_LIMIT
        ),
        name="ptychography_backward",
    )(
        offsets, transmission, probe, measured,
        jnp.asarray(rights), jnp.asarray(lefts), jnp.asarray(transforms),
    )
    parts = arrived.reshape(2, layers, 2, rows, win)
    return parts[0].astype(F32) + parts[1].astype(F32)


def solution(mesh):
    in_specs = (P("depth", None, "pos", None), P(), P("pos", None), P("pos", None, None))
    out_specs = P("depth", None, "pos", None)
    return jax.shard_map(
        per_device, mesh=mesh, in_specs=in_specs, out_specs=out_specs, check_vma=False
    )
```

```python
import functools
import math

import jax
import jax.numpy as jnp
import ml_dtypes
import numpy as np
from jax import lax
from jax.experimental import pallas as pl
from jax.experimental.pallas import tpu as pltpu
from jax.sharding import PartitionSpec as P


MESH = pl.DeviceIdType.MESH
F32 = jnp.float32
BF16 = jnp.bfloat16
VMEM_LIMIT = 56 * 1024 * 1024


def vmem():
    return pl.BlockSpec(memory_space=pltpu.VMEM)


def place():
    d = lax.axis_index("depth")
    q = lax.axis_index("pos")
    return d // 4, d % 4, q // 4, (q // 2) % 2, q % 2


def hi_lo(table, axis):
    high = table.astype(ml_dtypes.bfloat16)
    low = (table - high.astype(np.float64)).astype(ml_dtypes.bfloat16)
    return np.concatenate([high, low], axis)


def right_form(matrix):
    return np.block([[matrix.real, matrix.imag], [-matrix.imag, matrix.real]])


@functools.lru_cache(maxsize=None)
def tables(side):
    half = side // 2
    grid = np.arange(side)
    fourier = np.exp(-2j * np.pi * (np.outer(grid, grid) % side) / side) / math.sqrt(side)
    frequency = (grid + half) % side - half
    phase = np.exp(-1j * math.pi * frequency.astype(np.float64) ** 2 / 1024.0)
    circulant = fourier.conj() @ (phase[:, None] * fourier)
    near, far = circulant[:half, :half], circulant[:half, half:]
    forms = [right_form((near + far) / 2), right_form((near - far) / 2)]
    rights = np.stack([[hi_lo(m, 0) for m in forms], [hi_lo(m.T, 0) for m in forms]])
    order = grid.reshape(2, half // STRIP, STRIP).transpose(1, 0, 2).reshape(side)
    strided = [m[order][:, order] for m in forms]
    lefts = np.stack([[hi_lo(m.T, 1) for m in strided], [hi_lo(m, 1) for m in strided]])
    transforms = np.stack([hi_lo(m, 0) for m in (fourier.real, fourier.imag, -fourier.imag)])
    return rights, lefts, transforms.reshape(3, 2, side, side)


def dot(a, b):
    return jnp.dot(a, b, preferred_element_type=F32)


def cat(parts, axis):
    return jnp.concatenate(parts, axis)


STRIP = 16
BLOCKS = 2


def strips(count):
    return range(0, count, STRIP)


def halves(value):
    middle = value.shape[1] // 2
    return value[:, :middle], value[:, middle:]


def put_sums(ref, at, real, imag):
    (a, b), (c, d) = halves(real), halves(imag)
    ref[0, pl.ds(at, STRIP), :] = cat([a + b, c + d], 1).astype(BF16)
    ref[1, pl.ds(at, STRIP), :] = cat([a - b, c - d], 1).astype(BF16)


def sums_row(row, side):
    half = side // 2
    return 2 * row if row < half else 2 * (row - half) + STRIP


def right_stage(sums, flat, middle, right_ref, way, done=lambda n: None):
    side = sums.shape[1]
    block = side // BLOCKS
    for n in range(BLOCKS):
        for m in range(2):
            x = sums[m, pl.ds(n * block, block), :]
            flat[m, pl.ds(n * block, block), :] = dot(cat([x, x], 1), right_ref[way, m])
        for r in range(n * block, (n + 1) * block, 2 * STRIP):
            s, t = flat[0, pl.ds(r, STRIP), :], flat[0, pl.ds(r + STRIP, STRIP), :]
            d, e = flat[1, pl.ds(r, STRIP), :], flat[1, pl.ds(r + STRIP, STRIP), :]
            for m, (a, b) in enumerate(((s + t, d + e), (s - t, d - e))):
                (a_real, a_imag), (b_real, b_imag) = halves(a), halves(b)
                middle[m, pl.ds(r, STRIP), :] = cat([a_real, b_real], 1).astype(BF16)
                middle[m, pl.ds(r + STRIP, STRIP), :] = cat([a_imag, b_imag], 1).astype(BF16)
        done(n)


def left_stage(middle, field, left_ref, way):
    side = middle.shape[1]
    block = side // BLOCKS
    for n in range(BLOCKS):
        for m in range(2):
            x = middle[m]
            field[m, pl.ds(n * block, block), :] = dot(
                left_ref[way, m, pl.ds(n * block, block), :], cat([x, x], 0)
            )
        for r in range(n * block, (n + 1) * block, 2 * STRIP):
            p, u = field[0, pl.ds(r, STRIP), :], field[0, pl.ds(r + STRIP, STRIP), :]
            m, v = field[1, pl.ds(r, STRIP), :], field[1, pl.ds(r + STRIP, STRIP), :]
            for at, real, imag in ((r // 2, p + m, u + v), (side // 2 + r // 2, p - m, u - v)):
                (a, b), (c, d) = halves(real), halves(imag)
                yield at, cat([a + b, a - b], 1), cat([c + d, c - d], 1)


def strip(ref, s, c, at):
    return ref[s, c, pl.ds(at, STRIP), :].astype(F32)


def fourier_right(real, imag, f, inverse):
    r, i, n = f
    up, down = (n, i) if inverse else (i, n)
    x = cat([real, real, imag, imag], 1)
    a = dot(x, cat([r[0], r[1], down[0], down[1]], 0))
    b = dot(x, cat([up[0], up[1], r[0], r[1]], 0))
    return a, b


def fourier_left(real, imag, f, inverse):
    r, i, n = f
    up, down = (n, i) if inverse else (i, n)
    x = cat([real, real, imag, imag], 0)
    a = dot(cat([r[0], r[1], down[0], down[1]], 1), x)
    b = dot(cat([up[0], up[1], r[0], r[1]], 1), x)
    return a, b


def neighbours(g, j, x, h, core):
    d = 4 * g + j
    xy = 2 * x + h
    partners = [(d, 4 * x + 2 * h + 1 - core)]
    for k in range(1, 8):
        partners.append((d, 2 * ((xy + k) % 8) + core))
    for kx in range(4):
        for kj in range(1, 4):
            partners.append((4 * g + (j + kj) % 4, 4 * ((x + kx) % 4) + 2 * h + core))
    return partners


def remote(src, dst, send, recv, device):
    return pltpu.make_async_remote_copy(
        src_ref=src, dst_ref=dst, send_sem=send, recv_sem=recv, device_id=device, device_id_type=MESH
    )


def one_hot(mask):
    return jnp.where(mask, 1.0, 0.0).astype(BF16)


def shifts(columns):
    return lax.broadcasted_iota(jnp.int32, (STRIP, columns), 1) - lax.broadcasted_iota(
        jnp.int32, (STRIP, columns), 0
    )


def fill_rows(ref, offset):
    rows, columns = ref.shape
    lanes = cat([offset] * (columns // 128), 1)
    base = shifts(columns)
    for r in strips(rows):
        ref[pl.ds(r, STRIP), :] = one_hot(base == lanes + r)


def fill_columns(ref, offset, row_of=lambda r: r):
    rows, columns = ref.shape
    lanes = cat([offset] * (columns // 128), 1)
    base = shifts(columns)
    for r in strips(rows):
        ref[pl.ds(r, STRIP), :] = one_hot(base == row_of(r) - lanes)


def kernel(
    off_ref, t_ref, probe_hbm, measured_hbm, right_hbm, left_hbm, transform_hbm, arrived,
    own_offsets, offs, plane, pick_rows, pick_columns, stage, o_ref, stored, sums, flat, middle, field, grads, measured_ref, right_ref, left_ref,
    transform_ref, patches, put_columns, put_rows, wide, total, partial, sibling_sum, reduced,
    crop_relay, patch_relay, crop_relay_send, crop_relay_recv, patch_relay_send, patch_relay_recv,
    load_sem, s1_send, s1_recv, off_send, off_recv, chip_send, chip_recv, s2_send, s2_recv,
    hop_send, hop_recv, s3_send, s3_recv, back_send, back_recv, s4_send, s4_recv,
):
    g, j, x, h, core = place()
    d = 4 * g + j
    q = 4 * x + 2 * h + core
    xy = 2 * x + h
    last = 3
    sibling = (d, 4 * x + 2 * h + 1 - core)
    win = plane.shape[-1]
    side = o_ref.shape[-1]
    half = side // 2
    count = o_ref.shape[0]
    block = plane.shape[2]
    active = jnp.logical_or(j == core, j == 3 - core)
    mine = jnp.where(j == core, 0, 1)
    ahead = (jnp.minimum(d + 4, 15), q)
    behind = (jnp.maximum(d - 4, 0), q)

    loads = [
        pltpu.make_async_copy(right_hbm, right_ref, load_sem.at[0]),
        pltpu.make_async_copy(left_hbm, left_ref, load_sem.at[1]),
        pltpu.make_async_copy(transform_hbm, transform_ref, load_sem.at[2]),
        pltpu.make_async_copy(measured_hbm.at[mine], measured_ref, load_sem.at[3]),
    ]
    load_probe = pltpu.make_async_copy(probe_hbm, stored.at[0], load_sem.at[4])
    barrier = pltpu.get_barrier_semaphore()
    partners = neighbours(g, j, x, h, core)
    relayed = [(4 * g + (j + k) % 4, 4 * ((x + 1) % 4) + 2 * h + 1 - core) for k in range(4)]
    for partner in partners + relayed:
        pl.semaphore_signal(barrier, inc=1, device_id=partner, device_id_type=MESH)

    @pl.when(jnp.logical_and(active, g < last))
    def _():
        pl.semaphore_signal(barrier, inc=1, device_id=ahead, device_id_type=MESH)

    @pl.when(jnp.logical_and(active, g > 0))
    def _():
        pl.semaphore_signal(barrier, inc=1, device_id=behind, device_id_type=MESH)

    chained = jnp.where(active, jnp.where(jnp.logical_or(g == 0, g == last), 1, 2), 0)
    for load in loads:
        load.start()
    pl.when(g == 0)(load_probe.start)
    for k in range(4):
        own_offsets[k : k + 1, :] = jnp.full((1, 128), off_ref[k // 2, k % 2], jnp.int32)
        own_offsets[k + 4 : k + 5, :] = jnp.zeros((1, 128), jnp.int32)
    pl.semaphore_wait(barrier, len(partners) + len(relayed) + chained)

    for k in range(1, 4):
        to = (x + k) % 4
        remote(
            own_offsets, offs.at[x], off_send.at[k], off_recv.at[k], (d, 4 * to + 2 * h + core)
        ).start()
    for k in (4, 3, 5, 2, 6, 1, 7):
        to = (xy + k) % 8
        tx = to // 2
        remote(
            t_ref.at[tx // 2, tx % 2], plane.at[xy, core], s1_send.at[k], s1_recv.at[k], (d, 2 * to + core)
        ).start()
    own = t_ref.at[x // 2, x % 2]
    remote(own, plane.at[xy, core], chip_send.at[0], chip_recv.at[0], sibling).start()
    plane[xy, core] = t_ref[x // 2, x % 2]
    offs[x] = own_offsets[...]

    for i in (1, 0):
        for k in (0, 3, 2, 1):
            from_x = (x - k + 4) % 4
            if k and i:
                slot = offs.at[from_x]
                remote(slot, slot, off_send.at[k], off_recv.at[k], sibling).wait_recv()
            slot = 2 * ((4 - k) % 4) + i
            fill_rows(pick_rows.at[slot], offs[from_x, 2 * i : 2 * i + 1, :])
            fill_columns(pick_columns.at[slot], offs[from_x, 2 * i + 1 : 2 * i + 2, :])

    for k in (1, 7, 2, 6, 3, 5, 4):
        rows = plane.at[(xy - k + 8) % 8, core]
        remote(rows, rows, s1_send.at[k], s1_recv.at[k], sibling).wait_recv()
        remote(rows, rows, chip_send.at[k], chip_recv.at[k], sibling).start()
    for k in range(8):
        rows = plane.at[(xy - k + 8) % 8, 1 - core]
        remote(rows, rows, chip_send.at[k], chip_recv.at[k], sibling).wait_recv()

    def target(k, i):
        to_j = core if i == 0 else 3 - core
        return to_j, (4 * g + to_j, 4 * ((x + k) % 4) + 2 * h + core)

    own_plane = 2 * j + x // 2
    home = o_ref.at[own_plane, x % 2]
    for i in (1, 0):
        for k in (2, 1, 3, 0):
            slot = 2 * k + i
            rows = dot(pick_rows[slot], plane[...].reshape(win, win)).astype(BF16)
            stage[slot] = dot(rows, pick_columns[slot]).astype(BF16)
            to_j, device = target(k, i)
            copy = remote(
                stage.at[slot], home, s2_send.at[slot], s2_recv.at[2 * own_plane + x % 2], device
            )
            if k == 2:
                pl.when(core == 0)(copy.start)
                pl.when(core == 1)(
                    remote(
                        stage.at[slot], crop_relay.at[i], s2_send.at[slot], crop_relay_recv.at[i],
                        (d, 4 * ((x + 3) % 4) + 2 * h + core),
                    ).start
                )
            elif k:
                copy.start()
            else:
                pl.when(to_j != j)(copy.start)

                @pl.when(to_j == j)
                def _():
                    o_ref[own_plane, x % 2] = stage[slot]

    def crop_forward(i):
        from_x = (x + 1) % 4
        from_plane = 2 * j + from_x // 2
        to_j = core if i == 0 else 3 - core
        return remote(
            crop_relay.at[i], o_ref.at[from_plane, from_x % 2], crop_relay_send.at[i],
            s2_recv.at[2 * from_plane + from_x % 2], (4 * g + to_j, 4 * ((x + 3) % 4) + 2 * h + core),
        )

    @pl.when(core == 1)
    def _():
        for i in (1, 0):
            slot = crop_relay.at[i]
            remote(slot, slot, s2_send.at[0], crop_relay_recv.at[i], sibling).wait_recv()
            crop_forward(i).start()

    for load in loads:
        load.wait()
    pl.when(g == 0)(load_probe.wait)
    half = side // 2
    piece = half // 2

    def forward_pieces(n):
        rows = [pl.ds(m * half + n * piece, piece) for m in range(2)]
        return [
            remote(
                stored.at[count, :, rows[m]], stored.at[0, :, rows[m]],
                hop_send.at[2 * n + m], hop_recv.at[2 * n + m], ahead,
            )
            for m in range(2)
        ]

    def backward_piece(n, device):
        rows = middle.at[:, pl.ds(n * half, half)]
        return remote(rows, rows, hop_send.at[4 + n], hop_recv.at[4 + n], device)

    def owner(s, c):
        return 2 * (s % 2) + c, s // 2

    def make_put_tables():
        for i in range(2):
            for k in range(4):
                at = 4 * (1 - i) + k
                from_x = (x + k) % 4
                fill_rows(put_columns.at[at], offs[from_x, 2 * i + 1 : 2 * i + 2, :])
                for m in range(2):
                    first = 1 - core if m == 0 else core
                    fill_columns(
                        put_rows.at[m, 1 - i, :, k * side : (k + 1) * side],
                        offs[from_x, 2 * i : 2 * i + 1, :],
                        lambda r: r + (r // block + first) * block,
                    )

    starts = jnp.logical_and(active, g == 0)
    pl.when(jnp.logical_not(starts))(make_put_tables)

    @pl.when(active)
    def _():
        def wait_crop(s):
            for c in range(2):
                from_x, from_j = owner(s, c)
                slot = o_ref.at[s, c]
                copy = remote(slot, slot, s2_send.at[0], s2_recv.at[2 * s + c], sibling)
                pl.when(jnp.logical_or(from_x != x, from_j != j))(copy.wait_recv)

        def enter(s, at, real, imag):
            o_real, o_imag = strip(o_ref, s, 0, at), strip(o_ref, s, 1, at)
            put_sums(
                sums, sums_row(at, side), o_real * real - o_imag * imag, o_real * imag + o_imag * real
            )

        def keep_wave(s, at, real, imag):
            stored[s, 0, pl.ds(at, STRIP), :] = real.astype(BF16)
            stored[s, 1, pl.ds(at, STRIP), :] = imag.astype(BF16)

        def forward(s, carry):
            wait_crop(s + 1)
            for at, real, imag in left_stage(middle, field, left_ref, 0):
                keep_wave(s + 1, at, real, imag)
                enter(s + 1, at, real, imag)
            right_stage(sums, flat, middle, right_ref, 0)
            return carry

        wait_crop(0)
        for n in range(2):

            @pl.when(g > 0)
            def _():
                for copy in forward_pieces(n):
                    copy.wait_recv()

            for m in range(2):
                for r in strips(piece):
                    at = m * half + n * piece + r
                    enter(0, at, strip(stored, 0, 0, at), strip(stored, 0, 1, at))
        right_stage(sums, flat, middle, right_ref, 0)
        lax.fori_loop(0, jnp.where(g == last, count - 2, count - 1), forward, 0)

        @pl.when(g < last)
        def _():
            for at, real, imag in left_stage(middle, field, left_ref, 0):
                keep_wave(count, at, real, imag)
                if at >= half and (at + STRIP) % piece == 0:
                    for copy in forward_pieces((at - half) // piece):
                        copy.start()
            pl.when(g == 0)(make_put_tables)
            for n in range(2):
                backward_piece(n, ahead).wait_recv()

        def leave(s, field_strips):
            for at, real, imag in field_strips:
                o_real, o_imag = strip(o_ref, s, 0, at), strip(o_ref, s, 1, at)
                put_sums(
                    sums, sums_row(at, side), o_real * real + o_imag * imag, o_real * imag - o_imag * real
                )
                p_real, p_imag = stored[s, 0, pl.ds(at, STRIP), :], stored[s, 1, pl.ds(at, STRIP), :]
                real, imag = real.astype(BF16), imag.astype(BF16)
                grads[s, 0, pl.ds(at, STRIP), :] = p_real * real + p_imag * imag
                grads[s, 1, pl.ds(at, STRIP), :] = p_real * imag - p_imag * real

        @pl.when(g == last)
        def _():
            final = count - 1
            leaving, turned = grads.at[0], grads.at[1]
            f = [(transform_ref[m, 0], transform_ref[m, 1]) for m in range(3)]

            def flat_strip(m, at):
                return flat[m, pl.ds(at, STRIP), :]

            def transformed(source, inverse):
                turned[0], turned[1] = (v.astype(BF16) for v in fourier_right(source[0], source[1], f, inverse))
                flat[0], flat[1] = fourier_left(turned[0], turned[1], f, inverse)

            wait_crop(final)
            for at, real, imag in left_stage(middle, field, left_ref, 0):
                keep_wave(final, at, real, imag)
                o_real, o_imag = strip(o_ref, final, 0, at), strip(o_ref, final, 1, at)
                leaving[0, pl.ds(at, STRIP), :] = (o_real * real - o_imag * imag).astype(BF16)
                leaving[1, pl.ds(at, STRIP), :] = (o_real * imag + o_imag * real).astype(BF16)
            transformed(leaving, False)
            for at in strips(side):
                real, imag = flat_strip(0, at), flat_strip(1, at)
                weight = real * real + imag * imag - measured_ref[pl.ds(at, STRIP), :]
                sums[0, pl.ds(at, STRIP), :] = (real * weight).astype(BF16)
                sums[1, pl.ds(at, STRIP), :] = (imag * weight).astype(BF16)
            transformed(sums, True)
            leave(final, ((at, flat_strip(0, at), flat_strip(1, at)) for at in strips(side)))
            right_stage(sums, flat, middle, right_ref, 1)

        def send_patches(s):
            for c in range(2):
                to_x, to_j = owner(s, c)
                source, send = grads.at[s, c], s3_send.at[2 * s + c]
                away = jnp.logical_or(to_x != x, to_j != j)
                detour = jnp.logical_and(to_x == (x + 2) % 4, to_j % 2 == 1)
                copy = remote(
                    source, patches.at[2 * x + mine], send, s3_recv.at[2 * x + mine],
                    (4 * g + to_j, 4 * to_x + 2 * h + core),
                )
                pl.when(jnp.logical_and(away, jnp.logical_not(detour)))(copy.start)
                pl.when(detour)(
                    remote(
                        source, patch_relay.at[to_j // 2], send, patch_relay_recv.at[to_j // 2],
                        (d, 4 * ((x + 3) % 4) + 2 * h + 1 - core),
                    ).start
                )

                @pl.when(jnp.logical_not(away))
                def _():
                    patches[2 * x + mine] = grads[s, c]

        def backward(t, carry):
            s = count - 1 - t
            leave(s, left_stage(middle, field, left_ref, 1))
            right_stage(sums, flat, middle, right_ref, 1)
            pl.when(g == 0)(functools.partial(send_patches, s))
            return carry

        lax.fori_loop(jnp.where(g == last, 1, 0), count - 1, backward, 0)
        leave(0, left_stage(middle, field, left_ref, 1))
        pl.when(g == 0)(functools.partial(send_patches, 0))

        @pl.when(g > 0)
        def _():
            def leave_piece(n):
                backward_piece(n, behind).start()

            right_stage(sums, flat, middle, right_ref, 1, leave_piece)
            for n in range(2):
                backward_piece(n, behind).wait_send()

            def send(t, carry):
                send_patches(count - 1 - t)
                return carry

            lax.fori_loop(0, count, send, 0)

    def patch_forward(n):
        from_x = (x + 1) % 4
        p = 2 * from_x + jnp.where(j == 1 - core, 0, 1)
        return remote(
            patch_relay.at[n], patches.at[p], patch_relay_send.at[n], s3_recv.at[p],
            (4 * g + 2 * n + 1, 4 * ((x + 3) % 4) + 2 * h + 1 - core),
        )

    @pl.when(jnp.logical_not(active))
    def _():
        for n in (1, 0):
            slot = patch_relay.at[n]
            remote(slot, slot, s3_send.at[0], patch_relay_recv.at[n], sibling).wait_recv()
            patch_forward(n).start()

    for i in (1, 0):
        group = 1 - i
        for kx in range(4):
            from_x = (x - kx + 4) % 4
            from_j = core if i == 0 else 3 - core
            p = 2 * from_x + i
            slot = patches.at[p]
            copy = remote(slot, slot, s3_send.at[0], s3_recv.at[p], sibling)
            if kx:
                copy.wait_recv()
            else:
                pl.when(from_j != j)(copy.wait_recv)
            at = (4 - kx) % 4
            wide[at * side : (at + 1) * side, :] = dot(slot[...], put_columns[4 * group + at]).astype(BF16)
        if group == 0:
            for m in range(2):
                total[m] = dot(put_rows[m, 0], wide[...])
    partial[...] = (total[0] + dot(put_rows[0, 1], wide[...])).reshape(partial.shape).astype(BF16)
    chip_copy = remote(partial, sibling_sum, back_send.at[0], back_recv.at[0], sibling)
    chip_copy.start()
    own_rows = (total[1] + dot(put_rows[1, 1], wide[...])).reshape(partial.shape)
    chip_copy.wait_recv()
    reduced[...] = (own_rows + sibling_sum[...].astype(F32)).astype(BF16)
    for k in (4, 3, 5, 2, 6, 1, 7):
        to = (xy + k) % 8
        remote(reduced.at[to], arrived.at[4 * h + x], s4_send.at[k], s4_recv.at[k], (d, 2 * to + core)).start()
    arrived[4 * h + x] = reduced[xy]
    for k in range(1, 8):
        come = (xy - k + 8) % 8
        slot = arrived.at[4 * (come % 2) + come // 2]
        remote(slot, slot, s4_send.at[k], s4_recv.at[k], sibling).wait_recv()

    for k in range(1, 8):
        slot = reduced.at[0]
        remote(slot, slot, s1_send.at[k], s1_recv.at[k], sibling).wait_send()
        remote(slot, slot, s4_send.at[k], s4_recv.at[k], sibling).wait_send()
    for k in range(1, 4):
        remote(own_offsets, own_offsets, off_send.at[k], off_recv.at[k], sibling).wait_send()
    for k in range(8):
        slot = reduced.at[0]
        remote(slot, slot, chip_send.at[k], chip_recv.at[k], sibling).wait_send()
    chip_copy.wait_send()
    for i in range(2):
        for k in range(4):
            slot = 2 * k + i
            to_j, device = target(k, i)
            copy = remote(stage.at[slot], home, s2_send.at[slot], s2_recv.at[0], device)
            if k:
                copy.wait_send()
            else:
                pl.when(to_j != j)(copy.wait_send)

    @pl.when(core == 1)
    def _():
        for i in range(2):
            crop_forward(i).wait_send()

    @pl.when(jnp.logical_not(active))
    def _():
        for n in range(2):
            patch_forward(n).wait_send()

    @pl.when(active)
    def _():
        @pl.when(g < last)
        def _():
            for n in range(2):
                for copy in forward_pieces(n):
                    copy.wait_send()

        for s in range(count):
            for c in range(2):
                to_x, to_j = owner(s, c)
                slot = grads.at[s, c]
                copy = remote(slot, slot, s3_send.at[2 * s + c], s3_recv.at[0], sibling)
                pl.when(jnp.logical_or(to_x != x, to_j != j))(copy.wait_send)


def per_device(transmission, probe, offsets, measured):
    layers, _, rows, win = transmission.shape
    side = probe.shape[-1]
    group = 4 * layers
    rights, lefts, transforms = tables(side)
    dma = pltpu.SemaphoreType.DMA
    hbm = pl.BlockSpec(memory_space=pl.ANY)
    smem = pl.BlockSpec(memory_space=pltpu.SMEM)
    arrived = pl.pallas_call(
        kernel,
        out_shape=jax.ShapeDtypeStruct((8, rows, win), BF16),
        in_specs=[smem, vmem(), hbm, hbm, hbm, hbm, hbm],
        out_specs=vmem(),
        scratch_shapes=[
            pltpu.VMEM((8, 128), jnp.int32),
            pltpu.VMEM((4, 8, 128), jnp.int32),
            pltpu.VMEM((8, 2, rows, win), BF16),
            pltpu.VMEM((8, side, win), BF16),
            pltpu.VMEM((8, win, side), BF16),
            pltpu.VMEM((8, side, side), BF16),
            pltpu.VMEM((group, 2, side, side), BF16),
            pltpu.VMEM((group + 1, 2, side, side), BF16),
            pltpu.VMEM((2, side, side), BF16),
            pltpu.VMEM((2, side, side), F32),
            pltpu.VMEM((2, side, side), BF16),
            pltpu.VMEM((2, side, side), F32),
            pltpu.VMEM((group, 2, side, side), BF16),
            pltpu.VMEM((side, side), F32),
            pltpu.VMEM(rights.shape, BF16),
            pltpu.VMEM(lefts.shape, BF16),
            pltpu.VMEM(transforms.shape, BF16),
            pltpu.VMEM((8, side, side), BF16),
            pltpu.VMEM((8, side, win), BF16),
            pltpu.VMEM((2, 2, win // 2, 4 * side), BF16),
            pltpu.VMEM((4 * side, win), BF16),
            pltpu.VMEM((2, win // 2, win), F32),
            pltpu.VMEM((8, rows, win), BF16),
            pltpu.VMEM((8, rows, win), BF16),
            pltpu.VMEM((8, rows, win), BF16),
            pltpu.VMEM((2, side, side), BF16),
            pltpu.VMEM((2, side, side), BF16),
            dma((2,)), dma((2,)), dma((2,)), dma((2,)),
            dma((5,)), dma((8,)), dma((8,)), dma((4,)), dma((4,)), dma((8,)), dma((8,)), dma((8,)),
            dma((16,)), dma((6,)), dma((6,)), dma((16,)), dma((8,)), dma((1,)), dma((1,)), dma((8,)), dma((8,)),
        ],
        compiler_params=pltpu.CompilerParams(
            collective_id=0, has_side_effects=True, vmem_limit_bytes=VMEM_LIMIT
        ),
        name="ptychography_backward",
    )(
        offsets, transmission, probe, measured,
        jnp.asarray(rights), jnp.asarray(lefts), jnp.asarray(transforms),
    )
    parts = arrived.reshape(2, layers, 2, rows, win)
    return parts[0].astype(F32) + parts[1].astype(F32)


def solution(mesh):
    in_specs = (P("depth", None, "pos", None), P(), P("pos", None), P("pos", None, None))
    out_specs = P("depth", None, "pos", None)
    return jax.shard_map(
        per_device, mesh=mesh, in_specs=in_specs, out_specs=out_specs, check_vma=False
    )
```

```python
import functools
import math

import jax
import jax.numpy as jnp
import ml_dtypes
import numpy as np
from jax import lax
from jax.experimental import pallas as pl
from jax.experimental.pallas import tpu as pltpu
from jax.sharding import PartitionSpec as P


MESH = pl.DeviceIdType.MESH
F32 = jnp.float32
BF16 = jnp.bfloat16
VMEM_LIMIT = 56 * 1024 * 1024


def vmem():
    return pl.BlockSpec(memory_space=pltpu.VMEM)


def place():
    d = lax.axis_index("depth")
    q = lax.axis_index("pos")
    return d // 4, d % 4, q // 4, (q // 2) % 2, q % 2


def hi_lo(table, axis):
    high = table.astype(ml_dtypes.bfloat16)
    low = (table - high.astype(np.float64)).astype(ml_dtypes.bfloat16)
    return np.concatenate([high, low], axis)


def right_form(matrix):
    return np.block([[matrix.real, matrix.imag], [-matrix.imag, matrix.real]])


@functools.lru_cache(maxsize=None)
def tables(side):
    half = side // 2
    grid = np.arange(side)
    fourier = np.exp(-2j * np.pi * (np.outer(grid, grid) % side) / side) / math.sqrt(side)
    frequency = (grid + half) % side - half
    phase = np.exp(-1j * math.pi * frequency.astype(np.float64) ** 2 / 1024.0)
    circulant = fourier.conj() @ (phase[:, None] * fourier)
    near, far = circulant[:half, :half], circulant[:half, half:]
    forms = [right_form((near + far) / 2), right_form((near - far) / 2)]
    rights = np.stack([[hi_lo(m, 0) for m in forms], [hi_lo(m.T, 0) for m in forms]])
    order = grid.reshape(2, half // STRIP, STRIP).transpose(1, 0, 2).reshape(side)
    strided = [m[order][:, order] for m in forms]
    lefts = np.stack([[hi_lo(m.T, 1) for m in strided], [hi_lo(m, 1) for m in strided]])
    transforms = np.stack([hi_lo(m, 0) for m in (fourier.real, fourier.imag, -fourier.imag)])
    return rights, lefts, transforms.reshape(3, 2, side, side)


def dot(a, b):
    return jnp.dot(a, b, preferred_element_type=F32)


def cat(parts, axis):
    return jnp.concatenate(parts, axis)


STRIP = 16
BLOCKS = 2


def strips(count):
    return range(0, count, STRIP)


def halves(value):
    middle = value.shape[1] // 2
    return value[:, :middle], value[:, middle:]


def put_sums(ref, at, real, imag):
    (a, b), (c, d) = halves(real), halves(imag)
    ref[0, pl.ds(at, STRIP), :] = cat([a + b, c + d], 1).astype(BF16)
    ref[1, pl.ds(at, STRIP), :] = cat([a - b, c - d], 1).astype(BF16)


def sums_row(row, side):
    half = side // 2
    return 2 * row if row < half else 2 * (row - half) + STRIP


def right_stage(sums, flat, middle, right_ref, way, done=lambda n: None):
    side = sums.shape[1]
    block = side // BLOCKS
    for n in range(BLOCKS):
        for m in range(2):
            x = sums[m, pl.ds(n * block, block), :]
            flat[m, pl.ds(n * block, block), :] = dot(cat([x, x], 1), right_ref[way, m])
        for r in range(n * block, (n + 1) * block, 2 * STRIP):
            s, t = flat[0, pl.ds(r, STRIP), :], flat[0, pl.ds(r + STRIP, STRIP), :]
            d, e = flat[1, pl.ds(r, STRIP), :], flat[1, pl.ds(r + STRIP, STRIP), :]
            for m, (a, b) in enumerate(((s + t, d + e), (s - t, d - e))):
                (a_real, a_imag), (b_real, b_imag) = halves(a), halves(b)
                middle[m, pl.ds(r, STRIP), :] = cat([a_real, b_real], 1).astype(BF16)
                middle[m, pl.ds(r + STRIP, STRIP), :] = cat([a_imag, b_imag], 1).astype(BF16)
        done(n)


def left_stage(middle, field, left_ref, way):
    side = middle.shape[1]
    block = side // BLOCKS
    for n in range(BLOCKS):
        for m in range(2):
            x = middle[m]
            field[m, pl.ds(n * block, block), :] = dot(
                left_ref[way, m, pl.ds(n * block, block), :], cat([x, x], 0)
            )
        for r in range(n * block, (n + 1) * block, 2 * STRIP):
            p, u = field[0, pl.ds(r, STRIP), :], field[0, pl.ds(r + STRIP, STRIP), :]
            m, v = field[1, pl.ds(r, STRIP), :], field[1, pl.ds(r + STRIP, STRIP), :]
            for at, real, imag in ((r // 2, p + m, u + v), (side // 2 + r // 2, p - m, u - v)):
                (a, b), (c, d) = halves(real), halves(imag)
                yield at, cat([a + b, a - b], 1), cat([c + d, c - d], 1)


def strip(ref, s, c, at):
    return ref[s, c, pl.ds(at, STRIP), :].astype(F32)


def fourier_right(real, imag, f, inverse):
    r, i, n = f
    up, down = (n, i) if inverse else (i, n)
    x = cat([real, real, imag, imag], 1)
    a = dot(x, cat([r[0], r[1], down[0], down[1]], 0))
    b = dot(x, cat([up[0], up[1], r[0], r[1]], 0))
    return a, b


def fourier_left(real, imag, f, inverse):
    r, i, n = f
    up, down = (n, i) if inverse else (i, n)
    x = cat([real, real, imag, imag], 0)
    a = dot(cat([r[0], r[1], down[0], down[1]], 1), x)
    b = dot(cat([up[0], up[1], r[0], r[1]], 1), x)
    return a, b


def neighbours(g, j, x, h, core):
    d = 4 * g + j
    xy = 2 * x + h
    partners = [(d, 4 * x + 2 * h + 1 - core)]
    for k in range(1, 8):
        partners.append((d, 2 * ((xy + k) % 8) + core))
    for kx in range(4):
        for kj in range(1, 4):
            partners.append((4 * g + (j + kj) % 4, 4 * ((x + kx) % 4) + 2 * h + core))
    return partners


def remote(src, dst, send, recv, device):
    return pltpu.make_async_remote_copy(
        src_ref=src, dst_ref=dst, send_sem=send, recv_sem=recv, device_id=device, device_id_type=MESH
    )


def one_hot(mask):
    return jnp.where(mask, 1.0, 0.0).astype(BF16)


def shifts(columns):
    return lax.broadcasted_iota(jnp.int32, (STRIP, columns), 1) - lax.broadcasted_iota(
        jnp.int32, (STRIP, columns), 0
    )


def fill_rows(ref, offset):
    rows, columns = ref.shape
    lanes = cat([offset] * (columns // 128), 1)
    base = shifts(columns)
    for r in strips(rows):
        ref[pl.ds(r, STRIP), :] = one_hot(base == lanes + r)


def fill_columns(ref, offset, row_of=lambda r: r):
    rows, columns = ref.shape
    lanes = cat([offset] * (columns // 128), 1)
    base = shifts(columns)
    for r in strips(rows):
        ref[pl.ds(r, STRIP), :] = one_hot(base == row_of(r) - lanes)


def kernel(
    off_ref, t_hbm, probe_hbm, measured_hbm, right_hbm, left_hbm, transform_hbm, arrived,
    own_offsets, offs, plane, pick_rows, pick_columns, stage, o_ref, stored, sums, flat, middle, field, grads, measured_ref, right_ref, left_ref,
    transform_ref, patches, put_columns, put_rows, wide, total, partial, sibling_sum, reduced,
    crop_relay, patch_relay, crop_relay_send, crop_relay_recv, patch_relay_send, patch_relay_recv,
    load_sem, s1_send, s1_recv, off_send, off_recv, chip_send, chip_recv, s2_send, s2_recv,
    hop_send, hop_recv, s3_send, s3_recv, back_send, back_recv, s4_send, s4_recv,
):
    g, j, x, h, core = place()
    d = 4 * g + j
    q = 4 * x + 2 * h + core
    xy = 2 * x + h
    last = 3
    sibling = (d, 4 * x + 2 * h + 1 - core)
    win = plane.shape[-1]
    side = o_ref.shape[-1]
    half = side // 2
    count = o_ref.shape[0]
    block = plane.shape[2]
    active = jnp.logical_or(j == core, j == 3 - core)
    mine = jnp.where(j == core, 0, 1)
    ahead = (jnp.minimum(d + 4, 15), q)
    behind = (jnp.maximum(d - 4, 0), q)

    loads = [
        pltpu.make_async_copy(right_hbm, right_ref, load_sem.at[0]),
        pltpu.make_async_copy(left_hbm, left_ref, load_sem.at[1]),
        pltpu.make_async_copy(transform_hbm, transform_ref, load_sem.at[2]),
        pltpu.make_async_copy(measured_hbm.at[mine], measured_ref, load_sem.at[3]),
    ]
    load_probe = pltpu.make_async_copy(probe_hbm, stored.at[0], load_sem.at[4])
    barrier = pltpu.get_barrier_semaphore()
    partners = neighbours(g, j, x, h, core)
    relayed = [(4 * g + (j + k) % 4, 4 * ((x + 1) % 4) + 2 * h + 1 - core) for k in range(4)]
    for partner in partners + relayed:
        pl.semaphore_signal(barrier, inc=1, device_id=partner, device_id_type=MESH)

    @pl.when(jnp.logical_and(active, g < last))
    def _():
        pl.semaphore_signal(barrier, inc=1, device_id=ahead, device_id_type=MESH)

    @pl.when(jnp.logical_and(active, g > 0))
    def _():
        pl.semaphore_signal(barrier, inc=1, device_id=behind, device_id_type=MESH)

    chained = jnp.where(active, jnp.where(jnp.logical_or(g == 0, g == last), 1, 2), 0)
    for load in loads:
        load.start()
    pl.when(g == 0)(load_probe.start)
    for k in range(4):
        own_offsets[k : k + 1, :] = jnp.full((1, 128), off_ref[k // 2, k % 2], jnp.int32)
        own_offsets[k + 4 : k + 5, :] = jnp.zeros((1, 128), jnp.int32)
    pl.semaphore_wait(barrier, len(partners) + len(relayed) + chained)

    for k in range(1, 4):
        to = (x + k) % 4
        remote(
            own_offsets, offs.at[x], off_send.at[k], off_recv.at[k], (d, 4 * to + 2 * h + core)
        ).start()
    for k in (4, 3, 5, 2, 6, 1, 7):
        to = (xy + k) % 8
        tx = to // 2
        remote(
            t_hbm.at[tx // 2, tx % 2], plane.at[xy, core], s1_send.at[k], s1_recv.at[k], (d, 2 * to + core)
        ).start()
    own = t_hbm.at[x // 2, x % 2]
    remote(own, plane.at[xy, core], chip_send.at[0], chip_recv.at[0], sibling).start()
    own_copy = pltpu.make_async_copy(own, plane.at[xy, core], load_sem.at[5])
    own_copy.start()
    offs[x] = own_offsets[...]

    for i in (1, 0):
        for k in (0, 3, 2, 1):
            from_x = (x - k + 4) % 4
            if k and i:
                slot = offs.at[from_x]
                remote(slot, slot, off_send.at[k], off_recv.at[k], sibling).wait_recv()
            slot = 2 * ((4 - k) % 4) + i
            fill_rows(pick_rows.at[slot], offs[from_x, 2 * i : 2 * i + 1, :])
            fill_columns(pick_columns.at[slot], offs[from_x, 2 * i + 1 : 2 * i + 2, :])

    for k in (1, 7, 2, 6, 3, 5, 4):
        rows = plane.at[(xy - k + 8) % 8, core]
        remote(rows, rows, s1_send.at[k], s1_recv.at[k], sibling).wait_recv()
        remote(rows, rows, chip_send.at[k], chip_recv.at[k], sibling).start()
    for k in range(8):
        rows = plane.at[(xy - k + 8) % 8, 1 - core]
        remote(rows, rows, chip_send.at[k], chip_recv.at[k], sibling).wait_recv()

    own_copy.wait()

    def target(k, i):
        to_j = core if i == 0 else 3 - core
        return to_j, (4 * g + to_j, 4 * ((x + k) % 4) + 2 * h + core)

    own_plane = 2 * j + x // 2
    home = o_ref.at[own_plane, x % 2]
    for i in (1, 0):
        for k in (2, 1, 3, 0):
            slot = 2 * k + i
            rows = dot(pick_rows[slot], plane[...].reshape(win, win)).astype(BF16)
            stage[slot] = dot(rows, pick_columns[slot]).astype(BF16)
            to_j, device = target(k, i)
            copy = remote(
                stage.at[slot], home, s2_send.at[slot], s2_recv.at[2 * own_plane + x % 2], device
            )
            if k == 2:
                pl.when(core == 0)(copy.start)
                pl.when(core == 1)(
                    remote(
                        stage.at[slot], crop_relay.at[i], s2_send.at[slot], crop_relay_recv.at[i],
                        (d, 4 * ((x + 3) % 4) + 2 * h + core),
                    ).start
                )
            elif k:
                copy.start()
            else:
                pl.when(to_j != j)(copy.start)

                @pl.when(to_j == j)
                def _():
                    o_ref[own_plane, x % 2] = stage[slot]

    def crop_forward(i):
        from_x = (x + 1) % 4
        from_plane = 2 * j + from_x // 2
        to_j = core if i == 0 else 3 - core
        return remote(
            crop_relay.at[i], o_ref.at[from_plane, from_x % 2], crop_relay_send.at[i],
            s2_recv.at[2 * from_plane + from_x % 2], (4 * g + to_j, 4 * ((x + 3) % 4) + 2 * h + core),
        )

    @pl.when(core == 1)
    def _():
        for i in (1, 0):
            slot = crop_relay.at[i]
            remote(slot, slot, s2_send.at[0], crop_relay_recv.at[i], sibling).wait_recv()
            crop_forward(i).start()

    for load in loads:
        load.wait()
    pl.when(g == 0)(load_probe.wait)
    half = side // 2
    piece = half // 2

    def forward_pieces(n):
        rows = [pl.ds(m * half + n * piece, piece) for m in range(2)]
        return [
            remote(
                stored.at[count, :, rows[m]], stored.at[0, :, rows[m]],
                hop_send.at[2 * n + m], hop_recv.at[2 * n + m], ahead,
            )
            for m in range(2)
        ]

    def backward_piece(n, device):
        rows = middle.at[:, pl.ds(n * half, half)]
        return remote(rows, rows, hop_send.at[4 + n], hop_recv.at[4 + n], device)

    def owner(s, c):
        return 2 * (s % 2) + c, s // 2

    def make_put_tables():
        for i in range(2):
            for k in range(4):
                at = 4 * (1 - i) + k
                from_x = (x + k) % 4
                fill_rows(put_columns.at[at], offs[from_x, 2 * i + 1 : 2 * i + 2, :])
                for m in range(2):
                    first = 1 - core if m == 0 else core
                    fill_columns(
                        put_rows.at[m, 1 - i, :, k * side : (k + 1) * side],
                        offs[from_x, 2 * i : 2 * i + 1, :],
                        lambda r: r + (r // block + first) * block,
                    )

    starts = jnp.logical_and(active, g == 0)
    pl.when(jnp.logical_not(starts))(make_put_tables)

    @pl.when(active)
    def _():
        def wait_crop(s):
            for c in range(2):
                from_x, from_j = owner(s, c)
                slot = o_ref.at[s, c]
                copy = remote(slot, slot, s2_send.at[0], s2_recv.at[2 * s + c], sibling)
                pl.when(jnp.logical_or(from_x != x, from_j != j))(copy.wait_recv)

        def enter(s, at, real, imag):
            o_real, o_imag = strip(o_ref, s, 0, at), strip(o_ref, s, 1, at)
            put_sums(
                sums, sums_row(at, side), o_real * real - o_imag * imag, o_real * imag + o_imag * real
            )

        def keep_wave(s, at, real, imag):
            stored[s, 0, pl.ds(at, STRIP), :] = real.astype(BF16)
            stored[s, 1, pl.ds(at, STRIP), :] = imag.astype(BF16)

        def forward(s, carry):
            wait_crop(s + 1)
            for at, real, imag in left_stage(middle, field, left_ref, 0):
                keep_wave(s + 1, at, real, imag)
                enter(s + 1, at, real, imag)
            right_stage(sums, flat, middle, right_ref, 0)
            return carry

        wait_crop(0)
        for n in range(2):

            @pl.when(g > 0)
            def _():
                for copy in forward_pieces(n):
                    copy.wait_recv()

            for m in range(2):
                for r in strips(piece):
                    at = m * half + n * piece + r
                    enter(0, at, strip(stored, 0, 0, at), strip(stored, 0, 1, at))
        right_stage(sums, flat, middle, right_ref, 0)
        lax.fori_loop(0, jnp.where(g == last, count - 2, count - 1), forward, 0)

        @pl.when(g < last)
        def _():
            for at, real, imag in left_stage(middle, field, left_ref, 0):
                keep_wave(count, at, real, imag)
                if at >= half and (at + STRIP) % piece == 0:
                    for copy in forward_pieces((at - half) // piece):
                        copy.start()
            pl.when(g == 0)(make_put_tables)
            for n in range(2):
                backward_piece(n, ahead).wait_recv()

        def leave(s, field_strips):
            for at, real, imag in field_strips:
                real, imag = real.astype(BF16), imag.astype(BF16)
                o_real, o_imag = o_ref[s, 0, pl.ds(at, STRIP), :], o_ref[s, 1, pl.ds(at, STRIP), :]
                put_sums(
                    sums, sums_row(at, side), o_real * real + o_imag * imag, o_real * imag - o_imag * real
                )
                p_real, p_imag = stored[s, 0, pl.ds(at, STRIP), :], stored[s, 1, pl.ds(at, STRIP), :]
                grads[s, 0, pl.ds(at, STRIP), :] = p_real * real + p_imag * imag
                grads[s, 1, pl.ds(at, STRIP), :] = p_real * imag - p_imag * real

        @pl.when(g == last)
        def _():
            final = count - 1
            leaving, turned = grads.at[0], grads.at[1]
            f = [(transform_ref[m, 0], transform_ref[m, 1]) for m in range(3)]

            def flat_strip(m, at):
                return flat[m, pl.ds(at, STRIP), :]

            def transformed(source, inverse):
                turned[0], turned[1] = (v.astype(BF16) for v in fourier_right(source[0], source[1], f, inverse))
                flat[0], flat[1] = fourier_left(turned[0], turned[1], f, inverse)

            wait_crop(final)
            for at, real, imag in left_stage(middle, field, left_ref, 0):
                keep_wave(final, at, real, imag)
                o_real, o_imag = strip(o_ref, final, 0, at), strip(o_ref, final, 1, at)
                leaving[0, pl.ds(at, STRIP), :] = (o_real * real - o_imag * imag).astype(BF16)
                leaving[1, pl.ds(at, STRIP), :] = (o_real * imag + o_imag * real).astype(BF16)
            transformed(leaving, False)
            for at in strips(side):
                real, imag = flat_strip(0, at), flat_strip(1, at)
                weight = real * real + imag * imag - measured_ref[pl.ds(at, STRIP), :]
                sums[0, pl.ds(at, STRIP), :] = (real * weight).astype(BF16)
                sums[1, pl.ds(at, STRIP), :] = (imag * weight).astype(BF16)
            transformed(sums, True)
            leave(final, ((at, flat_strip(0, at), flat_strip(1, at)) for at in strips(side)))
            right_stage(sums, flat, middle, right_ref, 1)

        def send_patches(s):
            for c in range(2):
                to_x, to_j = owner(s, c)
                source, send = grads.at[s, c], s3_send.at[2 * s + c]
                away = jnp.logical_or(to_x != x, to_j != j)
                detour = jnp.logical_and(to_x == (x + 2) % 4, to_j % 2 == 1)
                copy = remote(
                    source, patches.at[2 * x + mine], send, s3_recv.at[2 * x + mine],
                    (4 * g + to_j, 4 * to_x + 2 * h + core),
                )
                pl.when(jnp.logical_and(away, jnp.logical_not(detour)))(copy.start)
                pl.when(detour)(
                    remote(
                        source, patch_relay.at[to_j // 2], send, patch_relay_recv.at[to_j // 2],
                        (d, 4 * ((x + 3) % 4) + 2 * h + 1 - core),
                    ).start
                )

                @pl.when(jnp.logical_not(away))
                def _():
                    patches[2 * x + mine] = grads[s, c]

        def backward(t, carry):
            s = count - 1 - t
            leave(s, left_stage(middle, field, left_ref, 1))
            right_stage(sums, flat, middle, right_ref, 1)
            pl.when(g == 0)(functools.partial(send_patches, s))
            return carry

        lax.fori_loop(jnp.where(g == last, 1, 0), count - 1, backward, 0)
        leave(0, left_stage(middle, field, left_ref, 1))
        pl.when(g == 0)(functools.partial(send_patches, 0))

        @pl.when(g > 0)
        def _():
            def leave_piece(n):
                backward_piece(n, behind).start()

            right_stage(sums, flat, middle, right_ref, 1, leave_piece)
            for n in range(2):
                backward_piece(n, behind).wait_send()

            def send(t, carry):
                send_patches(count - 1 - t)
                return carry

            lax.fori_loop(0, count, send, 0)

    def patch_forward(n):
        from_x = (x + 1) % 4
        p = 2 * from_x + jnp.where(j == 1 - core, 0, 1)
        return remote(
            patch_relay.at[n], patches.at[p], patch_relay_send.at[n], s3_recv.at[p],
            (4 * g + 2 * n + 1, 4 * ((x + 3) % 4) + 2 * h + 1 - core),
        )

    @pl.when(jnp.logical_not(active))
    def _():
        for n in (1, 0):
            slot = patch_relay.at[n]
            remote(slot, slot, s3_send.at[0], patch_relay_recv.at[n], sibling).wait_recv()
            patch_forward(n).start()

    for i in (1, 0):
        group = 1 - i
        for kx in range(4):
            from_x = (x - kx + 4) % 4
            from_j = core if i == 0 else 3 - core
            p = 2 * from_x + i
            slot = patches.at[p]
            copy = remote(slot, slot, s3_send.at[0], s3_recv.at[p], sibling)
            if kx:
                copy.wait_recv()
            else:
                pl.when(from_j != j)(copy.wait_recv)
            at = (4 - kx) % 4
            wide[at * side : (at + 1) * side, :] = dot(slot[...], put_columns[4 * group + at]).astype(BF16)
        if group == 0:
            for m in range(2):
                total[m] = dot(put_rows[m, 0], wide[...])
    partial[...] = (total[0] + dot(put_rows[0, 1], wide[...])).reshape(partial.shape).astype(BF16)
    chip_copy = remote(partial, sibling_sum, back_send.at[0], back_recv.at[0], sibling)
    chip_copy.start()
    own_rows = (total[1] + dot(put_rows[1, 1], wide[...])).reshape(partial.shape)
    chip_copy.wait_recv()
    reduced[...] = (own_rows + sibling_sum[...].astype(F32)).astype(BF16)
    for k in (4, 3, 5, 2, 6, 1, 7):
        to = (xy + k) % 8
        remote(reduced.at[to], arrived.at[4 * h + x], s4_send.at[k], s4_recv.at[k], (d, 2 * to + core)).start()
    kept = pltpu.make_async_copy(reduced.at[xy], arrived.at[4 * h + x], load_sem.at[6])
    kept.start()
    for k in range(1, 8):
        come = (xy - k + 8) % 8
        slot = arrived.at[4 * (come % 2) + come // 2]
        remote(slot, slot, s4_send.at[k], s4_recv.at[k], sibling).wait_recv()

    kept.wait()

    for k in range(1, 8):
        slot = reduced.at[0]
        remote(slot, slot, s1_send.at[k], s1_recv.at[k], sibling).wait_send()
        remote(slot, slot, s4_send.at[k], s4_recv.at[k], sibling).wait_send()
    for k in range(1, 4):
        remote(own_offsets, own_offsets, off_send.at[k], off_recv.at[k], sibling).wait_send()
    for k in range(8):
        slot = reduced.at[0]
        remote(slot, slot, chip_send.at[k], chip_recv.at[k], sibling).wait_send()
    chip_copy.wait_send()
    for i in range(2):
        for k in range(4):
            slot = 2 * k + i
            to_j, device = target(k, i)
            copy = remote(stage.at[slot], home, s2_send.at[slot], s2_recv.at[0], device)
            if k:
                copy.wait_send()
            else:
                pl.when(to_j != j)(copy.wait_send)

    @pl.when(core == 1)
    def _():
        for i in range(2):
            crop_forward(i).wait_send()

    @pl.when(jnp.logical_not(active))
    def _():
        for n in range(2):
            patch_forward(n).wait_send()

    @pl.when(active)
    def _():
        @pl.when(g < last)
        def _():
            for n in range(2):
                for copy in forward_pieces(n):
                    copy.wait_send()

        for s in range(count):
            for c in range(2):
                to_x, to_j = owner(s, c)
                slot = grads.at[s, c]
                copy = remote(slot, slot, s3_send.at[2 * s + c], s3_recv.at[0], sibling)
                pl.when(jnp.logical_or(to_x != x, to_j != j))(copy.wait_send)


def sum_kernel(arrived, out_ref):
    planes = out_ref.shape[0]
    for plane in range(planes):
        for r in strips(out_ref.shape[1]):
            rows = pl.ds(r, STRIP)
            out_ref[plane, rows, :] = arrived[plane, rows, :].astype(F32) + arrived[planes + plane, rows, :].astype(F32)


def per_device(transmission, probe, offsets, measured):
    layers, _, rows, win = transmission.shape
    side = probe.shape[-1]
    group = 4 * layers
    rights, lefts, transforms = tables(side)
    dma = pltpu.SemaphoreType.DMA
    hbm = pl.BlockSpec(memory_space=pl.ANY)
    smem = pl.BlockSpec(memory_space=pltpu.SMEM)
    arrived = pl.pallas_call(
        kernel,
        out_shape=jax.ShapeDtypeStruct((8, rows, win), BF16),
        in_specs=[smem, hbm, hbm, hbm, hbm, hbm, hbm],
        out_specs=hbm,
        scratch_shapes=[
            pltpu.VMEM((8, 128), jnp.int32),
            pltpu.VMEM((4, 8, 128), jnp.int32),
            pltpu.VMEM((8, 2, rows, win), BF16),
            pltpu.VMEM((8, side, win), BF16),
            pltpu.VMEM((8, win, side), BF16),
            pltpu.VMEM((8, side, side), BF16),
            pltpu.VMEM((group, 2, side, side), BF16),
            pltpu.VMEM((group + 1, 2, side, side), BF16),
            pltpu.VMEM((2, side, side), BF16),
            pltpu.VMEM((2, side, side), F32),
            pltpu.VMEM((2, side, side), BF16),
            pltpu.VMEM((2, side, side), F32),
            pltpu.VMEM((group, 2, side, side), BF16),
            pltpu.VMEM((side, side), F32),
            pltpu.VMEM(rights.shape, BF16),
            pltpu.VMEM(lefts.shape, BF16),
            pltpu.VMEM(transforms.shape, BF16),
            pltpu.VMEM((8, side, side), BF16),
            pltpu.VMEM((8, side, win), BF16),
            pltpu.VMEM((2, 2, win // 2, 4 * side), BF16),
            pltpu.VMEM((4 * side, win), BF16),
            pltpu.VMEM((2, win // 2, win), F32),
            pltpu.VMEM((8, rows, win), BF16),
            pltpu.VMEM((8, rows, win), BF16),
            pltpu.VMEM((8, rows, win), BF16),
            pltpu.VMEM((2, side, side), BF16),
            pltpu.VMEM((2, side, side), BF16),
            dma((2,)), dma((2,)), dma((2,)), dma((2,)),
            dma((7,)), dma((8,)), dma((8,)), dma((4,)), dma((4,)), dma((8,)), dma((8,)), dma((8,)),
            dma((16,)), dma((6,)), dma((6,)), dma((16,)), dma((8,)), dma((1,)), dma((1,)), dma((8,)), dma((8,)),
        ],
        compiler_params=pltpu.CompilerParams(
            collective_id=0, has_side_effects=True, vmem_limit_bytes=VMEM_LIMIT
        ),
        name="ptychography_backward",
    )(
        offsets, transmission, probe, measured,
        jnp.asarray(rights), jnp.asarray(lefts), jnp.asarray(transforms),
    )
    gradient = pl.pallas_call(
        sum_kernel,
        out_shape=jax.ShapeDtypeStruct((2 * layers, rows, win), F32),
        in_specs=[vmem()],
        out_specs=vmem(),
        name="sum_halves",
    )(arrived)
    return gradient.reshape(layers, 2, rows, win)


def solution(mesh):
    in_specs = (P("depth", None, "pos", None), P(), P("pos", None), P("pos", None, None))
    out_specs = P("depth", None, "pos", None)
    return jax.shard_map(
        per_device, mesh=mesh, in_specs=in_specs, out_specs=out_specs, check_vma=False
    )
```

```python
import functools
import math

import jax
import jax.numpy as jnp
import ml_dtypes
import numpy as np
from jax import lax
from jax.experimental import pallas as pl
from jax.experimental.pallas import tpu as pltpu
from jax.sharding import PartitionSpec as P


MESH = pl.DeviceIdType.MESH
F32 = jnp.float32
BF16 = jnp.bfloat16
VMEM_LIMIT = 56 * 1024 * 1024


def vmem():
    return pl.BlockSpec(memory_space=pltpu.VMEM)


def place():
    d = lax.axis_index("depth")
    q = lax.axis_index("pos")
    return d // 4, d % 4, q // 4, (q // 2) % 2, q % 2


def hi_lo(table, axis):
    high = table.astype(ml_dtypes.bfloat16)
    low = (table - high.astype(np.float64)).astype(ml_dtypes.bfloat16)
    return np.concatenate([high, low], axis)


def right_form(matrix):
    return np.block([[matrix.real, matrix.imag], [-matrix.imag, matrix.real]])


@functools.lru_cache(maxsize=None)
def tables(side):
    half = side // 2
    grid = np.arange(side)
    fourier = np.exp(-2j * np.pi * (np.outer(grid, grid) % side) / side) / math.sqrt(side)
    frequency = (grid + half) % side - half
    phase = np.exp(-1j * math.pi * frequency.astype(np.float64) ** 2 / 1024.0)
    circulant = fourier.conj() @ (phase[:, None] * fourier)
    near, far = circulant[:half, :half], circulant[:half, half:]
    forms = [right_form((near + far) / 2), right_form((near - far) / 2)]
    rights = np.stack([[hi_lo(m, 0) for m in forms], [hi_lo(m.T, 0) for m in forms]])
    order = grid.reshape(2, half // STRIP, STRIP).transpose(1, 0, 2).reshape(side)
    strided = [m[order][:, order] for m in forms]

    def strip_pairs(table):
        parts = hi_lo(table, 0).reshape(2, side // STRIP, STRIP, side)
        return parts.transpose(1, 0, 2, 3).reshape(2 * side, side)

    lefts = np.stack([[strip_pairs(m.T) for m in strided], [strip_pairs(m) for m in strided]])
    transforms = np.stack([hi_lo(m, 0) for m in (fourier.real, fourier.imag, -fourier.imag)])
    return rights, lefts, transforms.reshape(3, 2, side, side)


def dot(a, b):
    return jnp.dot(a, b, preferred_element_type=F32)


def cat(parts, axis):
    return jnp.concatenate(parts, axis)


STRIP = 16
BLOCKS = 2


def strips(count):
    return range(0, count, STRIP)


def halves(value):
    middle = value.shape[1] // 2
    return value[:, :middle], value[:, middle:]


def put_sums(ref, at, real, imag):
    (a, b), (c, d) = halves(real), halves(imag)
    ref[0, pl.ds(at, STRIP), :] = cat([a + b, c + d], 1).astype(BF16)
    ref[1, pl.ds(at, STRIP), :] = cat([a - b, c - d], 1).astype(BF16)


def sums_row(row, side):
    half = side // 2
    return 2 * row if row < half else 2 * (row - half) + STRIP


def right_stage(sums, flat, middle, right_ref, way, done=lambda n: None):
    side = sums.shape[1]
    block = side // BLOCKS
    for n in range(BLOCKS):
        for m in range(2):
            x = sums[m, pl.ds(n * block, block), :]
            flat[m, pl.ds(n * block, block), :] = dot(cat([x, x], 1), right_ref[way, m])
        for r in range(n * block, (n + 1) * block, 2 * STRIP):
            s, t = flat[0, pl.ds(r, STRIP), :], flat[0, pl.ds(r + STRIP, STRIP), :]
            d, e = flat[1, pl.ds(r, STRIP), :], flat[1, pl.ds(r + STRIP, STRIP), :]
            for m, (a, b) in enumerate(((s + t, d + e), (s - t, d - e))):
                (a_real, a_imag), (b_real, b_imag) = halves(a), halves(b)
                middle[m, pl.ds(r, STRIP), :] = cat([a_real, b_real], 1).astype(BF16)
                middle[m, pl.ds(r + STRIP, STRIP), :] = cat([a_imag, b_imag], 1).astype(BF16)
        done(n)


def left_stage(middle, field, left_ref, way):
    side = middle.shape[1]
    block = side // BLOCKS

    def total(m, r):
        return field[m, pl.ds(2 * r, STRIP), :] + field[m, pl.ds(2 * r + STRIP, STRIP), :]

    for n in range(BLOCKS):
        rows = pl.ds(2 * n * block, 2 * block)
        for m in range(2):
            field[m, rows, :] = dot(left_ref[way, m, rows, :], middle[m])
        for r in range(n * block, (n + 1) * block, 2 * STRIP):
            p, u = total(0, r), total(0, r + STRIP)
            m, v = total(1, r), total(1, r + STRIP)
            for at, real, imag in ((r // 2, p + m, u + v), (side // 2 + r // 2, p - m, u - v)):
                (a, b), (c, d) = halves(real), halves(imag)
                yield at, cat([a + b, a - b], 1), cat([c + d, c - d], 1)


def strip(ref, s, c, at):
    return ref[s, c, pl.ds(at, STRIP), :].astype(F32)


def fourier_right(real, imag, f, inverse):
    r, i, n = f
    up, down = (n, i) if inverse else (i, n)
    x = cat([real, real, imag, imag], 1)
    a = dot(x, cat([r[0], r[1], down[0], down[1]], 0))
    b = dot(x, cat([up[0], up[1], r[0], r[1]], 0))
    return a, b


def fourier_left(real, imag, f, inverse):
    r, i, n = f
    up, down = (n, i) if inverse else (i, n)
    x = cat([real, real, imag, imag], 0)
    a = dot(cat([r[0], r[1], down[0], down[1]], 1), x)
    b = dot(cat([up[0], up[1], r[0], r[1]], 1), x)
    return a, b


def neighbours(g, j, x, h, core):
    d = 4 * g + j
    xy = 2 * x + h
    partners = [(d, 4 * x + 2 * h + 1 - core)]
    for k in range(1, 8):
        partners.append((d, 2 * ((xy + k) % 8) + core))
    for kx in range(4):
        for kj in range(1, 4):
            partners.append((4 * g + (j + kj) % 4, 4 * ((x + kx) % 4) + 2 * h + core))
    return partners


def remote(src, dst, send, recv, device):
    return pltpu.make_async_remote_copy(
        src_ref=src, dst_ref=dst, send_sem=send, recv_sem=recv, device_id=device, device_id_type=MESH
    )


def one_hot(mask):
    return jnp.where(mask, 1.0, 0.0).astype(BF16)


def shifts(columns):
    return lax.broadcasted_iota(jnp.int32, (STRIP, columns), 1) - lax.broadcasted_iota(
        jnp.int32, (STRIP, columns), 0
    )


def fill_rows(ref, offset):
    rows, columns = ref.shape
    lanes = cat([offset] * (columns // 128), 1)
    base = shifts(columns)
    for r in strips(rows):
        ref[pl.ds(r, STRIP), :] = one_hot(base == lanes + r)


def fill_columns(ref, offset, row_of=lambda r: r):
    rows, columns = ref.shape
    lanes = cat([offset] * (columns // 128), 1)
    base = shifts(columns)
    for r in strips(rows):
        ref[pl.ds(r, STRIP), :] = one_hot(base == row_of(r) - lanes)


def kernel(
    off_ref, t_hbm, probe_hbm, measured_hbm, right_hbm, left_hbm, transform_hbm, arrived,
    own_offsets, offs, plane, pick_rows, pick_columns, stage, o_ref, stored, sums, flat, middle, field, grads, measured_ref, right_ref, left_ref,
    transform_ref, patches, put_columns, put_rows, wide, total, partial, sibling_sum, reduced,
    crop_relay, patch_relay, crop_relay_send, crop_relay_recv, patch_relay_send, patch_relay_recv,
    load_sem, s1_send, s1_recv, off_send, off_recv, chip_send, chip_recv, s2_send, s2_recv,
    hop_send, hop_recv, s3_send, s3_recv, back_send, back_recv, s4_send, s4_recv,
):
    g, j, x, h, core = place()
    d = 4 * g + j
    q = 4 * x + 2 * h + core
    xy = 2 * x + h
    last = 3
    sibling = (d, 4 * x + 2 * h + 1 - core)
    win = plane.shape[-1]
    side = o_ref.shape[-1]
    half = side // 2
    count = o_ref.shape[0]
    block = plane.shape[2]
    active = jnp.logical_or(j == core, j == 3 - core)
    mine = jnp.where(j == core, 0, 1)
    ahead = (jnp.minimum(d + 4, 15), q)
    behind = (jnp.maximum(d - 4, 0), q)

    loads = [
        pltpu.make_async_copy(right_hbm, right_ref, load_sem.at[0]),
        pltpu.make_async_copy(left_hbm, left_ref, load_sem.at[1]),
        pltpu.make_async_copy(transform_hbm, transform_ref, load_sem.at[2]),
        pltpu.make_async_copy(measured_hbm.at[mine], measured_ref, load_sem.at[3]),
    ]
    load_probe = pltpu.make_async_copy(probe_hbm, stored.at[0], load_sem.at[4])
    barrier = pltpu.get_barrier_semaphore()
    partners = neighbours(g, j, x, h, core)
    relayed = [(4 * g + (j + k) % 4, 4 * ((x + 1) % 4) + 2 * h + 1 - core) for k in range(4)]
    for partner in partners + relayed:
        pl.semaphore_signal(barrier, inc=1, device_id=partner, device_id_type=MESH)

    @pl.when(jnp.logical_and(active, g < last))
    def _():
        pl.semaphore_signal(barrier, inc=1, device_id=ahead, device_id_type=MESH)

    @pl.when(jnp.logical_and(active, g > 0))
    def _():
        pl.semaphore_signal(barrier, inc=1, device_id=behind, device_id_type=MESH)

    chained = jnp.where(active, jnp.where(jnp.logical_or(g == 0, g == last), 1, 2), 0)
    for load in loads:
        load.start()
    pl.when(g == 0)(load_probe.start)
    for k in range(4):
        own_offsets[k : k + 1, :] = jnp.full((1, 128), off_ref[k // 2, k % 2], jnp.int32)
        own_offsets[k + 4 : k + 5, :] = jnp.zeros((1, 128), jnp.int32)
    pl.semaphore_wait(barrier, len(partners) + len(relayed) + chained)

    for k in range(1, 4):
        to = (x + k) % 4
        remote(
            own_offsets, offs.at[x], off_send.at[k], off_recv.at[k], (d, 4 * to + 2 * h + core)
        ).start()
    for k in (4, 3, 5, 2, 6, 1, 7):
        to = (xy + k) % 8
        tx = to // 2
        remote(
            t_hbm.at[tx // 2, tx % 2], plane.at[xy, core], s1_send.at[k], s1_recv.at[k], (d, 2 * to + core)
        ).start()
    own = t_hbm.at[x // 2, x % 2]
    remote(own, plane.at[xy, core], chip_send.at[0], chip_recv.at[0], sibling).start()
    own_copy = pltpu.make_async_copy(own, plane.at[xy, core], load_sem.at[5])
    own_copy.start()
    offs[x] = own_offsets[...]

    for i in (1, 0):
        for k in (0, 3, 2, 1):
            from_x = (x - k + 4) % 4
            if k and i:
                slot = offs.at[from_x]
                remote(slot, slot, off_send.at[k], off_recv.at[k], sibling).wait_recv()
            slot = 2 * ((4 - k) % 4) + i
            fill_rows(pick_rows.at[slot], offs[from_x, 2 * i : 2 * i + 1, :])
            fill_columns(pick_columns.at[slot], offs[from_x, 2 * i + 1 : 2 * i + 2, :])

    for k in (1, 7, 2, 6, 3, 5, 4):
        rows = plane.at[(xy - k + 8) % 8, core]
        remote(rows, rows, s1_send.at[k], s1_recv.at[k], sibling).wait_recv()
        remote(rows, rows, chip_send.at[k], chip_recv.at[k], sibling).start()
    for k in range(8):
        rows = plane.at[(xy - k + 8) % 8, 1 - core]
        remote(rows, rows, chip_send.at[k], chip_recv.at[k], sibling).wait_recv()

    own_copy.wait()

    def target(k, i):
        to_j = core if i == 0 else 3 - core
        return to_j, (4 * g + to_j, 4 * ((x + k) % 4) + 2 * h + core)

    own_plane = 2 * j + x // 2
    home = o_ref.at[own_plane, x % 2]
    for i in (1, 0):
        for k in (2, 1, 3, 0):
            slot = 2 * k + i
            rows = dot(pick_rows[slot], plane[...].reshape(win, win)).astype(BF16)
            stage[slot] = dot(rows, pick_columns[slot]).astype(BF16)
            to_j, device = target(k, i)
            copy = remote(
                stage.at[slot], home, s2_send.at[slot], s2_recv.at[2 * own_plane + x % 2], device
            )
            if k == 2:
                pl.when(core == 0)(copy.start)
                pl.when(core == 1)(
                    remote(
                        stage.at[slot], crop_relay.at[i], s2_send.at[slot], crop_relay_recv.at[i],
                        (d, 4 * ((x + 3) % 4) + 2 * h + core),
                    ).start
                )
            elif k:
                copy.start()
            else:
                pl.when(to_j != j)(copy.start)

                @pl.when(to_j == j)
                def _():
                    o_ref[own_plane, x % 2] = stage[slot]

    def crop_forward(i):
        from_x = (x + 1) % 4
        from_plane = 2 * j + from_x // 2
        to_j = core if i == 0 else 3 - core
        return remote(
            crop_relay.at[i], o_ref.at[from_plane, from_x % 2], crop_relay_send.at[i],
            s2_recv.at[2 * from_plane + from_x % 2], (4 * g + to_j, 4 * ((x + 3) % 4) + 2 * h + core),
        )

    @pl.when(core == 1)
    def _():
        for i in (1, 0):
            slot = crop_relay.at[i]
            remote(slot, slot, s2_send.at[0], crop_relay_recv.at[i], sibling).wait_recv()
            crop_forward(i).start()

    for load in loads:
        load.wait()
    pl.when(g == 0)(load_probe.wait)
    half = side // 2
    piece = half // 2

    def forward_pieces(n):
        rows = [pl.ds(m * half + n * piece, piece) for m in range(2)]
        return [
            remote(
                stored.at[count, :, rows[m]], stored.at[0, :, rows[m]],
                hop_send.at[2 * n + m], hop_recv.at[2 * n + m], ahead,
            )
            for m in range(2)
        ]

    def backward_piece(n, device):
        rows = middle.at[:, pl.ds(n * half, half)]
        return remote(rows, rows, hop_send.at[4 + n], hop_recv.at[4 + n], device)

    def owner(s, c):
        return 2 * (s % 2) + c, s // 2

    def make_put_tables():
        for i in range(2):
            for k in range(4):
                at = 4 * (1 - i) + k
                from_x = (x + k) % 4
                fill_rows(put_columns.at[at], offs[from_x, 2 * i + 1 : 2 * i + 2, :])
                for m in range(2):
                    first = 1 - core if m == 0 else core
                    fill_columns(
                        put_rows.at[m, 1 - i, :, k * side : (k + 1) * side],
                        offs[from_x, 2 * i : 2 * i + 1, :],
                        lambda r: r + (r // block + first) * block,
                    )

    starts = jnp.logical_and(active, g == 0)
    pl.when(jnp.logical_not(starts))(make_put_tables)

    @pl.when(active)
    def _():
        def wait_crop(s):
            for c in range(2):
                from_x, from_j = owner(s, c)
                slot = o_ref.at[s, c]
                copy = remote(slot, slot, s2_send.at[0], s2_recv.at[2 * s + c], sibling)
                pl.when(jnp.logical_or(from_x != x, from_j != j))(copy.wait_recv)

        def enter(s, at, real, imag):
            o_real, o_imag = strip(o_ref, s, 0, at), strip(o_ref, s, 1, at)
            put_sums(
                sums, sums_row(at, side), o_real * real - o_imag * imag, o_real * imag + o_imag * real
            )

        def keep_wave(s, at, real, imag):
            stored[s, 0, pl.ds(at, STRIP), :] = real.astype(BF16)
            stored[s, 1, pl.ds(at, STRIP), :] = imag.astype(BF16)

        def forward(s, carry):
            wait_crop(s + 1)
            for at, real, imag in left_stage(middle, field, left_ref, 0):
                keep_wave(s + 1, at, real, imag)
                enter(s + 1, at, real, imag)
            right_stage(sums, flat, middle, right_ref, 0)
            return carry

        wait_crop(0)
        for n in range(2):

            @pl.when(g > 0)
            def _():
                for copy in forward_pieces(n):
                    copy.wait_recv()

            for m in range(2):
                for r in strips(piece):
                    at = m * half + n * piece + r
                    enter(0, at, strip(stored, 0, 0, at), strip(stored, 0, 1, at))
        right_stage(sums, flat, middle, right_ref, 0)
        lax.fori_loop(0, jnp.where(g == last, count - 2, count - 1), forward, 0)

        @pl.when(g < last)
        def _():
            for at, real, imag in left_stage(middle, field, left_ref, 0):
                keep_wave(count, at, real, imag)
                if at >= half and (at + STRIP) % piece == 0:
                    for copy in forward_pieces((at - half) // piece):
                        copy.start()
            pl.when(g == 0)(make_put_tables)
            for n in range(2):
                backward_piece(n, ahead).wait_recv()

        def leave(s, field_strips):
            for at, real, imag in field_strips:
                real, imag = real.astype(BF16), imag.astype(BF16)
                o_real, o_imag = o_ref[s, 0, pl.ds(at, STRIP), :], o_ref[s, 1, pl.ds(at, STRIP), :]
                put_sums(
                    sums, sums_row(at, side), o_real * real + o_imag * imag, o_real * imag - o_imag * real
                )
                p_real, p_imag = stored[s, 0, pl.ds(at, STRIP), :], stored[s, 1, pl.ds(at, STRIP), :]
                grads[s, 0, pl.ds(at, STRIP), :] = p_real * real + p_imag * imag
                grads[s, 1, pl.ds(at, STRIP), :] = p_real * imag - p_imag * real

        @pl.when(g == last)
        def _():
            final = count - 1
            leaving, turned = grads.at[0], grads.at[1]
            f = [(transform_ref[m, 0], transform_ref[m, 1]) for m in range(3)]

            def flat_strip(m, at):
                return flat[m, pl.ds(at, STRIP), :]

            def transformed(source, inverse):
                turned[0], turned[1] = (v.astype(BF16) for v in fourier_right(source[0], source[1], f, inverse))
                flat[0], flat[1] = fourier_left(turned[0], turned[1], f, inverse)

            wait_crop(final)
            for at, real, imag in left_stage(middle, field, left_ref, 0):
                keep_wave(final, at, real, imag)
                o_real, o_imag = strip(o_ref, final, 0, at), strip(o_ref, final, 1, at)
                leaving[0, pl.ds(at, STRIP), :] = (o_real * real - o_imag * imag).astype(BF16)
                leaving[1, pl.ds(at, STRIP), :] = (o_real * imag + o_imag * real).astype(BF16)
            transformed(leaving, False)
            for at in strips(side):
                real, imag = flat_strip(0, at), flat_strip(1, at)
                weight = real * real + imag * imag - measured_ref[pl.ds(at, STRIP), :]
                sums[0, pl.ds(at, STRIP), :] = (real * weight).astype(BF16)
                sums[1, pl.ds(at, STRIP), :] = (imag * weight).astype(BF16)
            transformed(sums, True)
            leave(final, ((at, flat_strip(0, at), flat_strip(1, at)) for at in strips(side)))
            right_stage(sums, flat, middle, right_ref, 1)

        def send_patches(s):
            for c in range(2):
                to_x, to_j = owner(s, c)
                source, send = grads.at[s, c], s3_send.at[2 * s + c]
                away = jnp.logical_or(to_x != x, to_j != j)
                detour = jnp.logical_and(to_x == (x + 2) % 4, to_j % 2 == 1)
                copy = remote(
                    source, patches.at[2 * x + mine], send, s3_recv.at[2 * x + mine],
                    (4 * g + to_j, 4 * to_x + 2 * h + core),
                )
                pl.when(jnp.logical_and(away, jnp.logical_not(detour)))(copy.start)
                pl.when(detour)(
                    remote(
                        source, patch_relay.at[to_j // 2], send, patch_relay_recv.at[to_j // 2],
                        (d, 4 * ((x + 3) % 4) + 2 * h + 1 - core),
                    ).start
                )

                @pl.when(jnp.logical_not(away))
                def _():
                    patches[2 * x + mine] = grads[s, c]

        def backward(t, carry):
            s = count - 1 - t
            leave(s, left_stage(middle, field, left_ref, 1))
            right_stage(sums, flat, middle, right_ref, 1)
            pl.when(g == 0)(functools.partial(send_patches, s))
            return carry

        lax.fori_loop(jnp.where(g == last, 1, 0), count - 1, backward, 0)
        leave(0, left_stage(middle, field, left_ref, 1))
        pl.when(g == 0)(functools.partial(send_patches, 0))

        @pl.when(g > 0)
        def _():
            def leave_piece(n):
                backward_piece(n, behind).start()

            right_stage(sums, flat, middle, right_ref, 1, leave_piece)
            for n in range(2):
                backward_piece(n, behind).wait_send()

            def send(t, carry):
                send_patches(count - 1 - t)
                return carry

            lax.fori_loop(0, count, send, 0)

    def patch_forward(n):
        from_x = (x + 1) % 4
        p = 2 * from_x + jnp.where(j == 1 - core, 0, 1)
        return remote(
            patch_relay.at[n], patches.at[p], patch_relay_send.at[n], s3_recv.at[p],
            (4 * g + 2 * n + 1, 4 * ((x + 3) % 4) + 2 * h + 1 - core),
        )

    @pl.when(jnp.logical_not(active))
    def _():
        for n in (1, 0):
            slot = patch_relay.at[n]
            remote(slot, slot, s3_send.at[0], patch_relay_recv.at[n], sibling).wait_recv()
            patch_forward(n).start()

    for i in (1, 0):
        group = 1 - i
        for kx in range(4):
            from_x = (x - kx + 4) % 4
            from_j = core if i == 0 else 3 - core
            p = 2 * from_x + i
            slot = patches.at[p]
            copy = remote(slot, slot, s3_send.at[0], s3_recv.at[p], sibling)
            if kx:
                copy.wait_recv()
            else:
                pl.when(from_j != j)(copy.wait_recv)
            at = (4 - kx) % 4
            wide[at * side : (at + 1) * side, :] = dot(slot[...], put_columns[4 * group + at]).astype(BF16)
        if group == 0:
            for m in range(2):
                total[m] = dot(put_rows[m, 0], wide[...])
    partial[...] = (total[0] + dot(put_rows[0, 1], wide[...])).reshape(partial.shape).astype(BF16)
    chip_copy = remote(partial, sibling_sum, back_send.at[0], back_recv.at[0], sibling)
    chip_copy.start()
    own_rows = (total[1] + dot(put_rows[1, 1], wide[...])).reshape(partial.shape)
    chip_copy.wait_recv()
    reduced[...] = (own_rows + sibling_sum[...].astype(F32)).astype(BF16)
    for k in (4, 3, 5, 2, 6, 1, 7):
        to = (xy + k) % 8
        remote(reduced.at[to], arrived.at[4 * h + x], s4_send.at[k], s4_recv.at[k], (d, 2 * to + core)).start()
    kept = pltpu.make_async_copy(reduced.at[xy], arrived.at[4 * h + x], load_sem.at[6])
    kept.start()
    for k in range(1, 8):
        come = (xy - k + 8) % 8
        slot = arrived.at[4 * (come % 2) + come // 2]
        remote(slot, slot, s4_send.at[k], s4_recv.at[k], sibling).wait_recv()

    kept.wait()

    for k in range(1, 8):
        slot = reduced.at[0]
        remote(slot, slot, s1_send.at[k], s1_recv.at[k], sibling).wait_send()
        remote(slot, slot, s4_send.at[k], s4_recv.at[k], sibling).wait_send()
    for k in range(1, 4):
        remote(own_offsets, own_offsets, off_send.at[k], off_recv.at[k], sibling).wait_send()
    for k in range(8):
        slot = reduced.at[0]
        remote(slot, slot, chip_send.at[k], chip_recv.at[k], sibling).wait_send()
    chip_copy.wait_send()
    for i in range(2):
        for k in range(4):
            slot = 2 * k + i
            to_j, device = target(k, i)
            copy = remote(stage.at[slot], home, s2_send.at[slot], s2_recv.at[0], device)
            if k:
                copy.wait_send()
            else:
                pl.when(to_j != j)(copy.wait_send)

    @pl.when(core == 1)
    def _():
        for i in range(2):
            crop_forward(i).wait_send()

    @pl.when(jnp.logical_not(active))
    def _():
        for n in range(2):
            patch_forward(n).wait_send()

    @pl.when(active)
    def _():
        @pl.when(g < last)
        def _():
            for n in range(2):
                for copy in forward_pieces(n):
                    copy.wait_send()

        for s in range(count):
            for c in range(2):
                to_x, to_j = owner(s, c)
                slot = grads.at[s, c]
                copy = remote(slot, slot, s3_send.at[2 * s + c], s3_recv.at[0], sibling)
                pl.when(jnp.logical_or(to_x != x, to_j != j))(copy.wait_send)


def sum_kernel(arrived, out_ref):
    planes = out_ref.shape[0]
    for plane in range(planes):
        for r in strips(out_ref.shape[1]):
            rows = pl.ds(r, STRIP)
            out_ref[plane, rows, :] = arrived[plane, rows, :].astype(F32) + arrived[planes + plane, rows, :].astype(F32)


def per_device(transmission, probe, offsets, measured):
    layers, _, rows, win = transmission.shape
    side = probe.shape[-1]
    group = 4 * layers
    rights, lefts, transforms = tables(side)
    dma = pltpu.SemaphoreType.DMA
    hbm = pl.BlockSpec(memory_space=pl.ANY)
    smem = pl.BlockSpec(memory_space=pltpu.SMEM)
    arrived = pl.pallas_call(
        kernel,
        out_shape=jax.ShapeDtypeStruct((8, rows, win), BF16),
        in_specs=[smem, hbm, hbm, hbm, hbm, hbm, hbm],
        out_specs=hbm,
        scratch_shapes=[
            pltpu.VMEM((8, 128), jnp.int32),
            pltpu.VMEM((4, 8, 128), jnp.int32),
            pltpu.VMEM((8, 2, rows, win), BF16),
            pltpu.VMEM((8, side, win), BF16),
            pltpu.VMEM((8, win, side), BF16),
            pltpu.VMEM((8, side, side), BF16),
            pltpu.VMEM((group, 2, side, side), BF16),
            pltpu.VMEM((group + 1, 2, side, side), BF16),
            pltpu.VMEM((2, side, side), BF16),
            pltpu.VMEM((2, side, side), F32),
            pltpu.VMEM((2, side, side), BF16),
            pltpu.VMEM((2, 2 * side, side), F32),
            pltpu.VMEM((group, 2, side, side), BF16),
            pltpu.VMEM((side, side), F32),
            pltpu.VMEM(rights.shape, BF16),
            pltpu.VMEM(lefts.shape, BF16),
            pltpu.VMEM(transforms.shape, BF16),
            pltpu.VMEM((8, side, side), BF16),
            pltpu.VMEM((8, side, win), BF16),
            pltpu.VMEM((2, 2, win // 2, 4 * side), BF16),
            pltpu.VMEM((4 * side, win), BF16),
            pltpu.VMEM((2, win // 2, win), F32),
            pltpu.VMEM((8, rows, win), BF16),
            pltpu.VMEM((8, rows, win), BF16),
            pltpu.VMEM((8, rows, win), BF16),
            pltpu.VMEM((2, side, side), BF16),
            pltpu.VMEM((2, side, side), BF16),
            dma((2,)), dma((2,)), dma((2,)), dma((2,)),
            dma((7,)), dma((8,)), dma((8,)), dma((4,)), dma((4,)), dma((8,)), dma((8,)), dma((8,)),
            dma((16,)), dma((6,)), dma((6,)), dma((16,)), dma((8,)), dma((1,)), dma((1,)), dma((8,)), dma((8,)),
        ],
        compiler_params=pltpu.CompilerParams(
            collective_id=0, has_side_effects=True, vmem_limit_bytes=VMEM_LIMIT
        ),
        name="ptychography_backward",
    )(
        offsets, transmission, probe, measured,
        jnp.asarray(rights), jnp.asarray(lefts), jnp.asarray(transforms),
    )
    gradient = pl.pallas_call(
        sum_kernel,
        out_shape=jax.ShapeDtypeStruct((2 * layers, rows, win), F32),
        in_specs=[vmem()],
        out_specs=vmem(),
        name="sum_halves",
    )(arrived)
    return gradient.reshape(layers, 2, rows, win)


def solution(mesh):
    in_specs = (P("depth", None, "pos", None), P(), P("pos", None), P("pos", None, None))
    out_specs = P("depth", None, "pos", None)
    return jax.shard_map(
        per_device, mesh=mesh, in_specs=in_specs, out_specs=out_specs, check_vma=False
    )
```

```python
import functools
import math

import jax
import jax.numpy as jnp
import ml_dtypes
import numpy as np
from jax import lax
from jax.experimental import pallas as pl
from jax.experimental.pallas import tpu as pltpu
from jax.sharding import PartitionSpec as P


MESH = pl.DeviceIdType.MESH
F32 = jnp.float32
BF16 = jnp.bfloat16
VMEM_LIMIT = 56 * 1024 * 1024


def vmem():
    return pl.BlockSpec(memory_space=pltpu.VMEM)


def place():
    d = lax.axis_index("depth")
    q = lax.axis_index("pos")
    return d // 4, d % 4, q // 4, (q // 2) % 2, q % 2


def hi_lo(table, axis):
    high = table.astype(ml_dtypes.bfloat16)
    low = (table - high.astype(np.float64)).astype(ml_dtypes.bfloat16)
    return np.concatenate([high, low], axis)


def right_form(matrix):
    return np.block([[matrix.real, matrix.imag], [-matrix.imag, matrix.real]])


@functools.lru_cache(maxsize=None)
def tables(side):
    half = side // 2
    grid = np.arange(side)
    fourier = np.exp(-2j * np.pi * (np.outer(grid, grid) % side) / side) / math.sqrt(side)
    frequency = (grid + half) % side - half
    phase = np.exp(-1j * math.pi * frequency.astype(np.float64) ** 2 / 1024.0)
    circulant = fourier.conj() @ (phase[:, None] * fourier)
    near, far = circulant[:half, :half], circulant[:half, half:]
    forms = [right_form((near + far) / 2), right_form((near - far) / 2)]
    rights = np.stack([[hi_lo(m, 0) for m in forms], [hi_lo(m.T, 0) for m in forms]])
    order = grid.reshape(2, half // STRIP, STRIP).transpose(1, 0, 2).reshape(side)
    strided = [m[order][:, order] for m in forms]

    def strip_pairs(table):
        parts = hi_lo(table, 0).reshape(2, side // STRIP, STRIP, side)
        return parts.transpose(1, 0, 2, 3).reshape(2 * side, side)

    lefts = np.stack([[strip_pairs(m.T) for m in strided], [strip_pairs(m) for m in strided]])
    transforms = np.stack([hi_lo(m, 0) for m in (fourier.real, fourier.imag, -fourier.imag)])
    return rights, lefts, transforms.reshape(3, 2, side, side)


def dot(a, b):
    return jnp.dot(a, b, preferred_element_type=F32)


def cat(parts, axis):
    return jnp.concatenate(parts, axis)


STRIP = 16
BLOCKS = 2


def strips(count):
    return range(0, count, STRIP)


def halves(value):
    middle = value.shape[1] // 2
    return value[:, :middle], value[:, middle:]


def put_sums(ref, at, real, imag):
    (a, b), (c, d) = halves(real), halves(imag)
    ref[0, pl.ds(at, STRIP), :] = cat([a + b, c + d], 1).astype(BF16)
    ref[1, pl.ds(at, STRIP), :] = cat([a - b, c - d], 1).astype(BF16)


def sums_row(row, side):
    half = side // 2
    return 2 * row if row < half else 2 * (row - half) + STRIP


def right_stage(sums, flat, middle, right_ref, way, done=lambda n: None):
    side = sums.shape[1]
    block = side // BLOCKS
    for n in range(BLOCKS):
        for m in range(2):
            x = sums[m, pl.ds(n * block, block), :]
            flat[m, pl.ds(n * block, block), :] = dot(cat([x, x], 1), right_ref[way, m])
        for r in range(n * block, (n + 1) * block, 2 * STRIP):
            s, t = flat[0, pl.ds(r, STRIP), :], flat[0, pl.ds(r + STRIP, STRIP), :]
            d, e = flat[1, pl.ds(r, STRIP), :], flat[1, pl.ds(r + STRIP, STRIP), :]
            for m, (a, b) in enumerate(((s + t, d + e), (s - t, d - e))):
                (a_real, a_imag), (b_real, b_imag) = halves(a), halves(b)
                middle[m, pl.ds(r, STRIP), :] = cat([a_real, b_real], 1).astype(BF16)
                middle[m, pl.ds(r + STRIP, STRIP), :] = cat([a_imag, b_imag], 1).astype(BF16)
        done(n)


def left_stage(middle, field, left_ref, way):
    side = middle.shape[1]
    block = side // BLOCKS

    def total(m, r):
        return field[m, pl.ds(2 * r, STRIP), :] + field[m, pl.ds(2 * r + STRIP, STRIP), :]

    for n in range(BLOCKS):
        rows = pl.ds(2 * n * block, 2 * block)
        for m in range(2):
            field[m, rows, :] = dot(left_ref[way, m, rows, :], middle[m])
        for r in range(n * block, (n + 1) * block, 2 * STRIP):
            p, u = total(0, r), total(0, r + STRIP)
            m, v = total(1, r), total(1, r + STRIP)
            for at, real, imag in ((r // 2, p + m, u + v), (side // 2 + r // 2, p - m, u - v)):
                (a, b), (c, d) = halves(real), halves(imag)
                yield at, cat([a + b, a - b], 1), cat([c + d, c - d], 1)


def strip(ref, s, c, at):
    return ref[s, c, pl.ds(at, STRIP), :].astype(F32)


def fourier_right(real, imag, f, inverse):
    r, i, n = f
    up, down = (n, i) if inverse else (i, n)
    x = cat([real, real, imag, imag], 1)
    a = dot(x, cat([r[0], r[1], down[0], down[1]], 0))
    b = dot(x, cat([up[0], up[1], r[0], r[1]], 0))
    return a, b


def fourier_left(real, imag, f, inverse):
    r, i, n = f
    up, down = (n, i) if inverse else (i, n)
    x = cat([real, real, imag, imag], 0)
    a = dot(cat([r[0], r[1], down[0], down[1]], 1), x)
    b = dot(cat([up[0], up[1], r[0], r[1]], 1), x)
    return a, b


def neighbours(g, j, x, h, core):
    d = 4 * g + j
    xy = 2 * x + h
    partners = [(d, 4 * x + 2 * h + 1 - core)]
    for k in range(1, 8):
        partners.append((d, 2 * ((xy + k) % 8) + core))
    for kx in range(4):
        for kj in range(1, 4):
            partners.append((4 * g + (j + kj) % 4, 4 * ((x + kx) % 4) + 2 * h + core))
    return partners


def remote(src, dst, send, recv, device):
    return pltpu.make_async_remote_copy(
        src_ref=src, dst_ref=dst, send_sem=send, recv_sem=recv, device_id=device, device_id_type=MESH
    )


def one_hot(mask):
    return jnp.where(mask, 1.0, 0.0).astype(BF16)


def shifts(columns):
    return lax.broadcasted_iota(jnp.int32, (STRIP, columns), 1) - lax.broadcasted_iota(
        jnp.int32, (STRIP, columns), 0
    )


def fill_rows(ref, offset):
    rows, columns = ref.shape
    lanes = cat([offset] * (columns // 128), 1)
    base = shifts(columns)
    for r in strips(rows):
        ref[pl.ds(r, STRIP), :] = one_hot(base == lanes + r)


def fill_columns(ref, offset, row_of=lambda r: r):
    rows, columns = ref.shape
    lanes = cat([offset] * (columns // 128), 1)
    base = shifts(columns)
    for r in strips(rows):
        ref[pl.ds(r, STRIP), :] = one_hot(base == row_of(r) - lanes)


def kernel(
    off_ref, t_hbm, probe_hbm, measured_hbm, right_hbm, left_hbm, transform_hbm, arrived,
    own_offsets, offs, plane, pick_rows, pick_columns, stage, o_ref, stored, sums, flat, middle, field, grads, measured_ref, right_ref, left_ref,
    transform_ref, patches, put_columns, put_rows, wide, total, partial, sibling_sum, reduced,
    crop_relay, patch_relay, row_relay, crop_relay_send, crop_relay_recv, patch_relay_send, patch_relay_recv,
    row_relay_send, row_relay_recv,
    load_sem, s1_send, s1_recv, off_send, off_recv, chip_send, chip_recv, s2_send, s2_recv,
    hop_send, hop_recv, s3_send, s3_recv, back_send, back_recv, s4_send, s4_recv,
):
    g, j, x, h, core = place()
    d = 4 * g + j
    q = 4 * x + 2 * h + core
    xy = 2 * x + h
    last = 3
    sibling = (d, 4 * x + 2 * h + 1 - core)
    win = plane.shape[-1]
    side = o_ref.shape[-1]
    half = side // 2
    count = o_ref.shape[0]
    block = plane.shape[2]
    active = jnp.logical_or(j == core, j == 3 - core)
    mine = jnp.where(j == core, 0, 1)
    ahead = (jnp.minimum(d + 4, 15), q)
    behind = (jnp.maximum(d - 4, 0), q)

    loads = [
        pltpu.make_async_copy(right_hbm, right_ref, load_sem.at[0]),
        pltpu.make_async_copy(left_hbm, left_ref, load_sem.at[1]),
        pltpu.make_async_copy(transform_hbm, transform_ref, load_sem.at[2]),
        pltpu.make_async_copy(measured_hbm.at[mine], measured_ref, load_sem.at[3]),
    ]
    load_probe = pltpu.make_async_copy(probe_hbm, stored.at[0], load_sem.at[4])
    barrier = pltpu.get_barrier_semaphore()
    partners = neighbours(g, j, x, h, core)
    relayed = [(4 * g + (j + k) % 4, 4 * ((x + 1) % 4) + 2 * h + 1 - core) for k in range(4)]
    across = 4 * g + j + 1 - 2 * (j % 2)
    below_h = jnp.where(j % 2 == 1, h, 1 - h)
    above_h = 1 - below_h
    above = [(across, 4 * k + 2 * above_h + core) for k in range(4)]
    for partner in partners + relayed + above:
        pl.semaphore_signal(barrier, inc=1, device_id=partner, device_id_type=MESH)

    @pl.when(jnp.logical_and(active, g < last))
    def _():
        pl.semaphore_signal(barrier, inc=1, device_id=ahead, device_id_type=MESH)

    @pl.when(jnp.logical_and(active, g > 0))
    def _():
        pl.semaphore_signal(barrier, inc=1, device_id=behind, device_id_type=MESH)

    chained = jnp.where(active, jnp.where(jnp.logical_or(g == 0, g == last), 1, 2), 0)
    for load in loads:
        load.start()
    pl.when(g == 0)(load_probe.start)
    for k in range(4):
        own_offsets[k : k + 1, :] = jnp.full((1, 128), off_ref[k // 2, k % 2], jnp.int32)
        own_offsets[k + 4 : k + 5, :] = jnp.zeros((1, 128), jnp.int32)
    pl.semaphore_wait(barrier, len(partners) + len(relayed) + len(above) + chained)

    for k in range(1, 4):
        to = (x + k) % 4
        remote(
            own_offsets, offs.at[x], off_send.at[k], off_recv.at[k], (d, 4 * to + 2 * h + core)
        ).start()
    def send_blocks(stage_at, source_of, target_ref, send_sem, recv_sem):
        for k in (3, 5, 1, 7, 4, 2, 6):
            to = (xy + k) % 8
            source = source_of(to)
            copy = remote(source, target_ref, send_sem.at[k], recv_sem.at[k], (d, 2 * to + core))
            if k % 2:
                n = 4 * stage_at + k // 2
                pl.when(core == 0)(copy.start)
                pl.when(core == 1)(
                    remote(
                        source, row_relay.at[n], send_sem.at[k], row_relay_recv.at[n],
                        (across, 4 * (to // 2) + 2 * below_h + core),
                    ).start
                )
            else:
                copy.start()

    def forward_block(stage_at, k, target_of, recv_sem):
        n = 4 * stage_at + k // 2
        to = 2 * x + 1 - above_h
        come = (to - k + 8) % 8
        return remote(
            row_relay.at[n], target_of(come), row_relay_send.at[n], recv_sem.at[k], (across, 2 * to + core)
        )

    def forward_blocks(stage_at, target_of, recv_sem):
        @pl.when(core == 1)
        def _():
            for k in (3, 5, 1, 7):
                n = 4 * stage_at + k // 2
                slot = row_relay.at[n]
                remote(slot, slot, row_relay_send.at[n], row_relay_recv.at[n], sibling).wait_recv()
                forward_block(stage_at, k, target_of, recv_sem).start()

    def row_slot(come):
        return plane.at[come, core]

    def sum_slot(come):
        return arrived.at[4 * (come % 2) + come // 2]

    send_blocks(0, lambda to: t_hbm.at[to // 2 // 2, to // 2 % 2], row_slot(xy), s1_send, s1_recv)
    own = t_hbm.at[x // 2, x % 2]
    remote(own, plane.at[xy, core], chip_send.at[0], chip_recv.at[0], sibling).start()
    own_copy = pltpu.make_async_copy(own, plane.at[xy, core], load_sem.at[5])
    own_copy.start()
    offs[x] = own_offsets[...]

    for i in (1, 0):
        for k in (0, 3, 2, 1):
            from_x = (x - k + 4) % 4
            if k and i:
                slot = offs.at[from_x]
                remote(slot, slot, off_send.at[k], off_recv.at[k], sibling).wait_recv()
            slot = 2 * ((4 - k) % 4) + i
            fill_rows(pick_rows.at[slot], offs[from_x, 2 * i : 2 * i + 1, :])
            fill_columns(pick_columns.at[slot], offs[from_x, 2 * i + 1 : 2 * i + 2, :])

    forward_blocks(0, row_slot, s1_recv)
    for k in (2, 6, 4, 1, 7, 3, 5):
        rows = plane.at[(xy - k + 8) % 8, core]
        remote(rows, rows, s1_send.at[k], s1_recv.at[k], sibling).wait_recv()
        remote(rows, rows, chip_send.at[k], chip_recv.at[k], sibling).start()
    for k in range(8):
        rows = plane.at[(xy - k + 8) % 8, 1 - core]
        remote(rows, rows, chip_send.at[k], chip_recv.at[k], sibling).wait_recv()

    own_copy.wait()

    def target(k, i):
        to_j = core if i == 0 else 3 - core
        return to_j, (4 * g + to_j, 4 * ((x + k) % 4) + 2 * h + core)

    own_plane = 2 * j + x // 2
    home = o_ref.at[own_plane, x % 2]
    for i in (1, 0):
        for k in (2, 1, 3, 0):
            slot = 2 * k + i
            rows = dot(pick_rows[slot], plane[...].reshape(win, win)).astype(BF16)
            stage[slot] = dot(rows, pick_columns[slot]).astype(BF16)
            to_j, device = target(k, i)
            copy = remote(
                stage.at[slot], home, s2_send.at[slot], s2_recv.at[2 * own_plane + x % 2], device
            )
            if k == 2:
                pl.when(core == 0)(copy.start)
                pl.when(core == 1)(
                    remote(
                        stage.at[slot], crop_relay.at[i], s2_send.at[slot], crop_relay_recv.at[i],
                        (d, 4 * ((x + 3) % 4) + 2 * h + core),
                    ).start
                )
            elif k:
                copy.start()
            else:
                pl.when(to_j != j)(copy.start)

                @pl.when(to_j == j)
                def _():
                    o_ref[own_plane, x % 2] = stage[slot]

    def crop_forward(i):
        from_x = (x + 1) % 4
        from_plane = 2 * j + from_x // 2
        to_j = core if i == 0 else 3 - core
        return remote(
            crop_relay.at[i], o_ref.at[from_plane, from_x % 2], crop_relay_send.at[i],
            s2_recv.at[2 * from_plane + from_x % 2], (4 * g + to_j, 4 * ((x + 3) % 4) + 2 * h + core),
        )

    @pl.when(core == 1)
    def _():
        for i in (1, 0):
            slot = crop_relay.at[i]
            remote(slot, slot, s2_send.at[0], crop_relay_recv.at[i], sibling).wait_recv()
            crop_forward(i).start()

    for load in loads:
        load.wait()
    pl.when(g == 0)(load_probe.wait)
    half = side // 2
    piece = half // 2

    def forward_pieces(n):
        rows = [pl.ds(m * half + n * piece, piece) for m in range(2)]
        return [
            remote(
                stored.at[count, :, rows[m]], stored.at[0, :, rows[m]],
                hop_send.at[2 * n + m], hop_recv.at[2 * n + m], ahead,
            )
            for m in range(2)
        ]

    def backward_piece(n, device):
        rows = middle.at[:, pl.ds(n * half, half)]
        return remote(rows, rows, hop_send.at[4 + n], hop_recv.at[4 + n], device)

    def owner(s, c):
        return 2 * (s % 2) + c, s // 2

    def make_put_tables():
        for i in range(2):
            for k in range(4):
                at = 4 * (1 - i) + k
                from_x = (x + k) % 4
                fill_rows(put_columns.at[at], offs[from_x, 2 * i + 1 : 2 * i + 2, :])
                for m in range(2):
                    first = 1 - core if m == 0 else core
                    fill_columns(
                        put_rows.at[m, 1 - i, :, k * side : (k + 1) * side],
                        offs[from_x, 2 * i : 2 * i + 1, :],
                        lambda r: r + (r // block + first) * block,
                    )

    starts = jnp.logical_and(active, g == 0)
    pl.when(jnp.logical_not(starts))(make_put_tables)

    @pl.when(active)
    def _():
        def wait_crop(s):
            for c in range(2):
                from_x, from_j = owner(s, c)
                slot = o_ref.at[s, c]
                copy = remote(slot, slot, s2_send.at[0], s2_recv.at[2 * s + c], sibling)
                pl.when(jnp.logical_or(from_x != x, from_j != j))(copy.wait_recv)

        def enter(s, at, real, imag):
            o_real, o_imag = strip(o_ref, s, 0, at), strip(o_ref, s, 1, at)
            put_sums(
                sums, sums_row(at, side), o_real * real - o_imag * imag, o_real * imag + o_imag * real
            )

        def keep_wave(s, at, real, imag):
            stored[s, 0, pl.ds(at, STRIP), :] = real.astype(BF16)
            stored[s, 1, pl.ds(at, STRIP), :] = imag.astype(BF16)

        def forward(s, carry):
            wait_crop(s + 1)
            for at, real, imag in left_stage(middle, field, left_ref, 0):
                keep_wave(s + 1, at, real, imag)
                enter(s + 1, at, real, imag)
            right_stage(sums, flat, middle, right_ref, 0)
            return carry

        wait_crop(0)
        for n in range(2):

            @pl.when(g > 0)
            def _():
                for copy in forward_pieces(n):
                    copy.wait_recv()

            for m in range(2):
                for r in strips(piece):
                    at = m * half + n * piece + r
                    enter(0, at, strip(stored, 0, 0, at), strip(stored, 0, 1, at))
        right_stage(sums, flat, middle, right_ref, 0)
        lax.fori_loop(0, jnp.where(g == last, count - 2, count - 1), forward, 0)

        @pl.when(g < last)
        def _():
            for at, real, imag in left_stage(middle, field, left_ref, 0):
                keep_wave(count, at, real, imag)
                if at >= half and (at + STRIP) % piece == 0:
                    for copy in forward_pieces((at - half) // piece):
                        copy.start()
            pl.when(g == 0)(make_put_tables)
            for n in range(2):
                backward_piece(n, ahead).wait_recv()

        def leave(s, field_strips):
            for at, real, imag in field_strips:
                real, imag = real.astype(BF16), imag.astype(BF16)
                o_real, o_imag = o_ref[s, 0, pl.ds(at, STRIP), :], o_ref[s, 1, pl.ds(at, STRIP), :]
                put_sums(
                    sums, sums_row(at, side), o_real * real + o_imag * imag, o_real * imag - o_imag * real
                )
                p_real, p_imag = stored[s, 0, pl.ds(at, STRIP), :], stored[s, 1, pl.ds(at, STRIP), :]
                grads[s, 0, pl.ds(at, STRIP), :] = p_real * real + p_imag * imag
                grads[s, 1, pl.ds(at, STRIP), :] = p_real * imag - p_imag * real

        @pl.when(g == last)
        def _():
            final = count - 1
            leaving, turned = grads.at[0], grads.at[1]
            f = [(transform_ref[m, 0], transform_ref[m, 1]) for m in range(3)]

            def flat_strip(m, at):
                return flat[m, pl.ds(at, STRIP), :]

            def transformed(source, inverse):
                turned[0], turned[1] = (v.astype(BF16) for v in fourier_right(source[0], source[1], f, inverse))
                flat[0], flat[1] = fourier_left(turned[0], turned[1], f, inverse)

            wait_crop(final)
            for at, real, imag in left_stage(middle, field, left_ref, 0):
                keep_wave(final, at, real, imag)
                o_real, o_imag = strip(o_ref, final, 0, at), strip(o_ref, final, 1, at)
                leaving[0, pl.ds(at, STRIP), :] = (o_real * real - o_imag * imag).astype(BF16)
                leaving[1, pl.ds(at, STRIP), :] = (o_real * imag + o_imag * real).astype(BF16)
            transformed(leaving, False)
            for at in strips(side):
                real, imag = flat_strip(0, at), flat_strip(1, at)
                weight = real * real + imag * imag - measured_ref[pl.ds(at, STRIP), :]
                sums[0, pl.ds(at, STRIP), :] = (real * weight).astype(BF16)
                sums[1, pl.ds(at, STRIP), :] = (imag * weight).astype(BF16)
            transformed(sums, True)
            leave(final, ((at, flat_strip(0, at), flat_strip(1, at)) for at in strips(side)))
            right_stage(sums, flat, middle, right_ref, 1)

        def send_patches(s):
            for c in range(2):
                to_x, to_j = owner(s, c)
                source, send = grads.at[s, c], s3_send.at[2 * s + c]
                away = jnp.logical_or(to_x != x, to_j != j)
                detour = jnp.logical_and(to_x == (x + 2) % 4, to_j % 2 == 1)
                copy = remote(
                    source, patches.at[2 * x + mine], send, s3_recv.at[2 * x + mine],
                    (4 * g + to_j, 4 * to_x + 2 * h + core),
                )
                pl.when(jnp.logical_and(away, jnp.logical_not(detour)))(copy.start)
                pl.when(detour)(
                    remote(
                        source, patch_relay.at[to_j // 2], send, patch_relay_recv.at[to_j // 2],
                        (d, 4 * ((x + 3) % 4) + 2 * h + 1 - core),
                    ).start
                )

                @pl.when(jnp.logical_not(away))
                def _():
                    patches[2 * x + mine] = grads[s, c]

        def backward(t, carry):
            s = count - 1 - t
            leave(s, left_stage(middle, field, left_ref, 1))
            right_stage(sums, flat, middle, right_ref, 1)
            pl.when(g == 0)(functools.partial(send_patches, s))
            return carry

        lax.fori_loop(jnp.where(g == last, 1, 0), count - 1, backward, 0)
        leave(0, left_stage(middle, field, left_ref, 1))
        pl.when(g == 0)(functools.partial(send_patches, 0))

        @pl.when(g > 0)
        def _():
            def leave_piece(n):
                backward_piece(n, behind).start()

            right_stage(sums, flat, middle, right_ref, 1, leave_piece)
            for n in range(2):
                backward_piece(n, behind).wait_send()

            def send(t, carry):
                send_patches(count - 1 - t)
                return carry

            lax.fori_loop(0, count, send, 0)

    def patch_forward(n):
        from_x = (x + 1) % 4
        p = 2 * from_x + jnp.where(j == 1 - core, 0, 1)
        return remote(
            patch_relay.at[n], patches.at[p], patch_relay_send.at[n], s3_recv.at[p],
            (4 * g + 2 * n + 1, 4 * ((x + 3) % 4) + 2 * h + 1 - core),
        )

    @pl.when(jnp.logical_not(active))
    def _():
        for n in (1, 0):
            slot = patch_relay.at[n]
            remote(slot, slot, s3_send.at[0], patch_relay_recv.at[n], sibling).wait_recv()
            patch_forward(n).start()

    for i in (1, 0):
        group = 1 - i
        for kx in range(4):
            from_x = (x - kx + 4) % 4
            from_j = core if i == 0 else 3 - core
            p = 2 * from_x + i
            slot = patches.at[p]
            copy = remote(slot, slot, s3_send.at[0], s3_recv.at[p], sibling)
            if kx:
                copy.wait_recv()
            else:
                pl.when(from_j != j)(copy.wait_recv)
            at = (4 - kx) % 4
            wide[at * side : (at + 1) * side, :] = dot(slot[...], put_columns[4 * group + at]).astype(BF16)
        if group == 0:
            for m in range(2):
                total[m] = dot(put_rows[m, 0], wide[...])
    partial[...] = (total[0] + dot(put_rows[0, 1], wide[...])).reshape(partial.shape).astype(BF16)
    chip_copy = remote(partial, sibling_sum, back_send.at[0], back_recv.at[0], sibling)
    chip_copy.start()
    own_rows = (total[1] + dot(put_rows[1, 1], wide[...])).reshape(partial.shape)
    chip_copy.wait_recv()
    reduced[...] = (own_rows + sibling_sum[...].astype(F32)).astype(BF16)
    send_blocks(1, lambda to: reduced.at[to], sum_slot(xy), s4_send, s4_recv)
    kept = pltpu.make_async_copy(reduced.at[xy], arrived.at[4 * h + x], load_sem.at[6])
    kept.start()
    forward_blocks(1, sum_slot, s4_recv)
    for k in range(1, 8):
        slot = sum_slot((xy - k + 8) % 8)
        remote(slot, slot, s4_send.at[k], s4_recv.at[k], sibling).wait_recv()
    kept.wait()

    for k in range(1, 8):
        slot = reduced.at[0]
        remote(slot, slot, s1_send.at[k], s1_recv.at[k], sibling).wait_send()
        remote(slot, slot, s4_send.at[k], s4_recv.at[k], sibling).wait_send()
    for k in range(1, 4):
        remote(own_offsets, own_offsets, off_send.at[k], off_recv.at[k], sibling).wait_send()
    for k in range(8):
        slot = reduced.at[0]
        remote(slot, slot, chip_send.at[k], chip_recv.at[k], sibling).wait_send()
    chip_copy.wait_send()
    for i in range(2):
        for k in range(4):
            slot = 2 * k + i
            to_j, device = target(k, i)
            copy = remote(stage.at[slot], home, s2_send.at[slot], s2_recv.at[0], device)
            if k:
                copy.wait_send()
            else:
                pl.when(to_j != j)(copy.wait_send)

    @pl.when(core == 1)
    def _():
        for i in range(2):
            crop_forward(i).wait_send()
        for k in (1, 3, 5, 7):
            forward_block(0, k, row_slot, s1_recv).wait_send()
            forward_block(1, k, sum_slot, s4_recv).wait_send()

    @pl.when(jnp.logical_not(active))
    def _():
        for n in range(2):
            patch_forward(n).wait_send()

    @pl.when(active)
    def _():
        @pl.when(g < last)
        def _():
            for n in range(2):
                for copy in forward_pieces(n):
                    copy.wait_send()

        for s in range(count):
            for c in range(2):
                to_x, to_j = owner(s, c)
                slot = grads.at[s, c]
                copy = remote(slot, slot, s3_send.at[2 * s + c], s3_recv.at[0], sibling)
                pl.when(jnp.logical_or(to_x != x, to_j != j))(copy.wait_send)


def sum_kernel(arrived, out_ref):
    planes = out_ref.shape[0]
    for plane in range(planes):
        for r in strips(out_ref.shape[1]):
            rows = pl.ds(r, STRIP)
            out_ref[plane, rows, :] = arrived[plane, rows, :].astype(F32) + arrived[planes + plane, rows, :].astype(F32)


def per_device(transmission, probe, offsets, measured):
    layers, _, rows, win = transmission.shape
    side = probe.shape[-1]
    group = 4 * layers
    rights, lefts, transforms = tables(side)
    dma = pltpu.SemaphoreType.DMA
    hbm = pl.BlockSpec(memory_space=pl.ANY)
    smem = pl.BlockSpec(memory_space=pltpu.SMEM)
    arrived = pl.pallas_call(
        kernel,
        out_shape=jax.ShapeDtypeStruct((8, rows, win), BF16),
        in_specs=[smem, hbm, hbm, hbm, hbm, hbm, hbm],
        out_specs=hbm,
        scratch_shapes=[
            pltpu.VMEM((8, 128), jnp.int32),
            pltpu.VMEM((4, 8, 128), jnp.int32),
            pltpu.VMEM((8, 2, rows, win), BF16),
            pltpu.VMEM((8, side, win), BF16),
            pltpu.VMEM((8, win, side), BF16),
            pltpu.VMEM((8, side, side), BF16),
            pltpu.VMEM((group, 2, side, side), BF16),
            pltpu.VMEM((group + 1, 2, side, side), BF16),
            pltpu.VMEM((2, side, side), BF16),
            pltpu.VMEM((2, side, side), F32),
            pltpu.VMEM((2, side, side), BF16),
            pltpu.VMEM((2, 2 * side, side), F32),
            pltpu.VMEM((group, 2, side, side), BF16),
            pltpu.VMEM((side, side), F32),
            pltpu.VMEM(rights.shape, BF16),
            pltpu.VMEM(lefts.shape, BF16),
            pltpu.VMEM(transforms.shape, BF16),
            pltpu.VMEM((8, side, side), BF16),
            pltpu.VMEM((8, side, win), BF16),
            pltpu.VMEM((2, 2, win // 2, 4 * side), BF16),
            pltpu.VMEM((4 * side, win), BF16),
            pltpu.VMEM((2, win // 2, win), F32),
            pltpu.VMEM((8, rows, win), BF16),
            pltpu.VMEM((8, rows, win), BF16),
            pltpu.VMEM((8, rows, win), BF16),
            pltpu.VMEM((2, side, side), BF16),
            pltpu.VMEM((2, side, side), BF16),
            pltpu.VMEM((8, rows, win), BF16),
            dma((2,)), dma((2,)), dma((2,)), dma((2,)), dma((8,)), dma((8,)),
            dma((7,)), dma((8,)), dma((8,)), dma((4,)), dma((4,)), dma((8,)), dma((8,)), dma((8,)),
            dma((16,)), dma((6,)), dma((6,)), dma((16,)), dma((8,)), dma((1,)), dma((1,)), dma((8,)), dma((8,)),
        ],
        compiler_params=pltpu.CompilerParams(
            collective_id=0, has_side_effects=True, vmem_limit_bytes=VMEM_LIMIT
        ),
        name="ptychography_backward",
    )(
        offsets, transmission, probe, measured,
        jnp.asarray(rights), jnp.asarray(lefts), jnp.asarray(transforms),
    )
    gradient = pl.pallas_call(
        sum_kernel,
        out_shape=jax.ShapeDtypeStruct((2 * layers, rows, win), F32),
        in_specs=[vmem()],
        out_specs=vmem(),
        name="sum_halves",
    )(arrived)
    return gradient.reshape(layers, 2, rows, win)


def solution(mesh):
    in_specs = (P("depth", None, "pos", None), P(), P("pos", None), P("pos", None, None))
    out_specs = P("depth", None, "pos", None)
    return jax.shard_map(
        per_device, mesh=mesh, in_specs=in_specs, out_specs=out_specs, check_vma=False
    )
```

```python
import functools
import math

import jax
import jax.numpy as jnp
import ml_dtypes
import numpy as np
from jax import lax
from jax.experimental import pallas as pl
from jax.experimental.pallas import tpu as pltpu
from jax.sharding import PartitionSpec as P


MESH = pl.DeviceIdType.MESH
F32 = jnp.float32
BF16 = jnp.bfloat16
VMEM_LIMIT = 56 * 1024 * 1024


def vmem():
    return pl.BlockSpec(memory_space=pltpu.VMEM)


def place():
    d = lax.axis_index("depth")
    q = lax.axis_index("pos")
    return d // 4, d % 4, q // 4, (q // 2) % 2, q % 2


def hi_lo(table, axis):
    high = table.astype(ml_dtypes.bfloat16)
    low = (table - high.astype(np.float64)).astype(ml_dtypes.bfloat16)
    return np.concatenate([high, low], axis)


def right_form(matrix):
    return np.block([[matrix.real, matrix.imag], [-matrix.imag, matrix.real]])


@functools.lru_cache(maxsize=None)
def tables(side):
    half = side // 2
    grid = np.arange(side)
    fourier = np.exp(-2j * np.pi * (np.outer(grid, grid) % side) / side) / math.sqrt(side)
    frequency = (grid + half) % side - half
    phase = np.exp(-1j * math.pi * frequency.astype(np.float64) ** 2 / 1024.0)
    circulant = fourier.conj() @ (phase[:, None] * fourier)
    near, far = circulant[:half, :half], circulant[:half, half:]
    forms = [right_form((near + far) / 2), right_form((near - far) / 2)]
    rights = np.stack([[hi_lo(m, 0) for m in forms], [hi_lo(m.T, 0) for m in forms]])
    order = grid.reshape(2, half // STRIP, STRIP).transpose(1, 0, 2).reshape(side)
    strided = [m[order][:, order] for m in forms]

    def strip_pairs(table):
        parts = hi_lo(table, 0).reshape(2, side // STRIP, STRIP, side)
        return parts.transpose(1, 0, 2, 3).reshape(2 * side, side)

    lefts = np.stack([[strip_pairs(m.T) for m in strided], [strip_pairs(m) for m in strided]])
    transforms = np.stack([hi_lo(m, 0) for m in (fourier.real, fourier.imag, -fourier.imag)])
    return rights, lefts, transforms.reshape(3, 2, side, side)


def dot(a, b):
    return jnp.dot(a, b, preferred_element_type=F32)


def cat(parts, axis):
    return jnp.concatenate(parts, axis)


STRIP = 16
BLOCKS = 2


def strips(count):
    return range(0, count, STRIP)


def halves(value):
    middle = value.shape[1] // 2
    return value[:, :middle], value[:, middle:]


def put_sums(ref, at, real, imag):
    (a, b), (c, d) = halves(real), halves(imag)
    ref[0, pl.ds(at, STRIP), :] = cat([a + b, c + d], 1).astype(BF16)
    ref[1, pl.ds(at, STRIP), :] = cat([a - b, c - d], 1).astype(BF16)


def sums_row(row, side):
    half = side // 2
    return 2 * row if row < half else 2 * (row - half) + STRIP


def right_stage(sums, flat, middle, right_ref, way, done=lambda n: None):
    side = sums.shape[1]
    block = side // BLOCKS
    for n in range(BLOCKS):
        for m in range(2):
            x = sums[m, pl.ds(n * block, block), :]
            flat[m, pl.ds(n * block, block), :] = dot(cat([x, x], 1), right_ref[way, m])
        for r in range(n * block, (n + 1) * block, 2 * STRIP):
            s, t = flat[0, pl.ds(r, STRIP), :], flat[0, pl.ds(r + STRIP, STRIP), :]
            d, e = flat[1, pl.ds(r, STRIP), :], flat[1, pl.ds(r + STRIP, STRIP), :]
            for m, (a, b) in enumerate(((s + t, d + e), (s - t, d - e))):
                (a_real, a_imag), (b_real, b_imag) = halves(a), halves(b)
                middle[m, pl.ds(r, STRIP), :] = cat([a_real, b_real], 1).astype(BF16)
                middle[m, pl.ds(r + STRIP, STRIP), :] = cat([a_imag, b_imag], 1).astype(BF16)
        done(n)


def left_stage(middle, field, left_ref, way):
    side = middle.shape[1]
    block = side // BLOCKS

    def total(m, r):
        return field[m, pl.ds(2 * r, STRIP), :] + field[m, pl.ds(2 * r + STRIP, STRIP), :]

    for n in range(BLOCKS):
        rows = pl.ds(2 * n * block, 2 * block)
        for m in range(2):
            field[m, rows, :] = dot(left_ref[way, m, rows, :], middle[m])
        for r in range(n * block, (n + 1) * block, 2 * STRIP):
            p, u = total(0, r), total(0, r + STRIP)
            m, v = total(1, r), total(1, r + STRIP)
            for at, real, imag in ((r // 2, p + m, u + v), (side // 2 + r // 2, p - m, u - v)):
                (a, b), (c, d) = halves(real), halves(imag)
                yield at, cat([a + b, a - b], 1), cat([c + d, c - d], 1)


def strip(ref, s, c, at):
    return ref[s, c, pl.ds(at, STRIP), :].astype(F32)


def fourier_right(real, imag, f, inverse):
    r, i, n = f
    up, down = (n, i) if inverse else (i, n)
    x = cat([real, real, imag, imag], 1)
    a = dot(x, cat([r[0], r[1], down[0], down[1]], 0))
    b = dot(x, cat([up[0], up[1], r[0], r[1]], 0))
    return a, b


def fourier_left(real, imag, f, inverse):
    r, i, n = f
    up, down = (n, i) if inverse else (i, n)
    x = cat([real, real, imag, imag], 0)
    a = dot(cat([r[0], r[1], down[0], down[1]], 1), x)
    b = dot(cat([up[0], up[1], r[0], r[1]], 1), x)
    return a, b


def neighbours(g, j, x, h, core):
    d = 4 * g + j
    xy = 2 * x + h
    partners = [(d, 4 * x + 2 * h + 1 - core)]
    for k in range(1, 8):
        partners.append((d, 2 * ((xy + k) % 8) + core))
    for kx in range(4):
        for kj in range(1, 4):
            partners.append((4 * g + (j + kj) % 4, 4 * ((x + kx) % 4) + 2 * h + core))
    return partners


def remote(src, dst, send, recv, device):
    return pltpu.make_async_remote_copy(
        src_ref=src, dst_ref=dst, send_sem=send, recv_sem=recv, device_id=device, device_id_type=MESH
    )


def one_hot(mask):
    return jnp.where(mask, 1.0, 0.0).astype(BF16)


def shifts(columns):
    return lax.broadcasted_iota(jnp.int32, (STRIP, columns), 1) - lax.broadcasted_iota(
        jnp.int32, (STRIP, columns), 0
    )


def fill_rows(ref, offset):
    rows, columns = ref.shape
    lanes = cat([offset] * (columns // 128), 1)
    base = shifts(columns)
    for r in strips(rows):
        ref[pl.ds(r, STRIP), :] = one_hot(base == lanes + r)


def fill_columns(ref, offset, row_of=lambda r: r):
    rows, columns = ref.shape
    lanes = cat([offset] * (columns // 128), 1)
    base = shifts(columns)
    for r in strips(rows):
        ref[pl.ds(r, STRIP), :] = one_hot(base == row_of(r) - lanes)


def kernel(
    off_ref, t_hbm, probe_hbm, measured_hbm, right_hbm, left_hbm, transform_hbm, arrived,
    own_offsets, offs, plane, pick_rows, pick_columns, stage, o_ref, stored, sums, flat, middle, field, grads, measured_ref, right_ref, left_ref,
    transform_ref, patches, put_columns, put_rows, wide, total, partial, sibling_sum, reduced,
    crop_relay, patch_relay, crop_relay_send, crop_relay_recv, patch_relay_send, patch_relay_recv,
    load_sem, s1_send, s1_recv, off_send, off_recv, chip_send, chip_recv, s2_send, s2_recv,
    hop_send, hop_recv, s3_send, s3_recv, back_send, back_recv, s4_send, s4_recv,
):
    g, j, x, h, core = place()
    d = 4 * g + j
    q = 4 * x + 2 * h + core
    xy = 2 * x + h
    last = 3
    sibling = (d, 4 * x + 2 * h + 1 - core)
    win = plane.shape[-1]
    side = o_ref.shape[-1]
    half = side // 2
    count = o_ref.shape[0]
    block = plane.shape[2]
    active = jnp.logical_or(j == core, j == 3 - core)
    mine = jnp.where(j == core, 0, 1)
    ahead = (jnp.minimum(d + 4, 15), q)
    behind = (jnp.maximum(d - 4, 0), q)

    loads = [
        pltpu.make_async_copy(right_hbm, right_ref, load_sem.at[0]),
        pltpu.make_async_copy(left_hbm, left_ref, load_sem.at[1]),
        pltpu.make_async_copy(transform_hbm, transform_ref, load_sem.at[2]),
        pltpu.make_async_copy(measured_hbm.at[mine], measured_ref, load_sem.at[3]),
    ]
    load_probe = pltpu.make_async_copy(probe_hbm, stored.at[0], load_sem.at[4])
    barrier = pltpu.get_barrier_semaphore()
    partners = neighbours(g, j, x, h, core)
    relayed = [(4 * g + (j + k) % 4, 4 * ((x + 1) % 4) + 2 * h + 1 - core) for k in range(4)]
    for partner in partners + relayed:
        pl.semaphore_signal(barrier, inc=1, device_id=partner, device_id_type=MESH)

    @pl.when(jnp.logical_and(active, g < last))
    def _():
        pl.semaphore_signal(barrier, inc=1, device_id=ahead, device_id_type=MESH)

    @pl.when(jnp.logical_and(active, g > 0))
    def _():
        pl.semaphore_signal(barrier, inc=1, device_id=behind, device_id_type=MESH)

    chained = jnp.where(active, jnp.where(jnp.logical_or(g == 0, g == last), 1, 2), 0)
    for load in loads:
        load.start()
    pl.when(g == 0)(load_probe.start)
    for k in range(4):
        own_offsets[k : k + 1, :] = jnp.full((1, 128), off_ref[k // 2, k % 2], jnp.int32)
        own_offsets[k + 4 : k + 5, :] = jnp.zeros((1, 128), jnp.int32)
    pl.semaphore_wait(barrier, len(partners) + len(relayed) + chained)

    for k in range(1, 4):
        to = (x + k) % 4
        remote(
            own_offsets, offs.at[x], off_send.at[k], off_recv.at[k], (d, 4 * to + 2 * h + core)
        ).start()
    for k in (4, 3, 5, 2, 6, 1, 7):
        to = (xy + k) % 8
        tx = to // 2
        remote(
            t_hbm.at[tx // 2, tx % 2], plane.at[xy, core], s1_send.at[k], s1_recv.at[k], (d, 2 * to + core)
        ).start()
    own = t_hbm.at[x // 2, x % 2]
    remote(own, plane.at[xy, core], chip_send.at[0], chip_recv.at[0], sibling).start()
    own_copy = pltpu.make_async_copy(own, plane.at[xy, core], load_sem.at[5])
    own_copy.start()
    offs[x] = own_offsets[...]

    for i in (1, 0):
        for k in (0, 3, 2, 1):
            from_x = (x - k + 4) % 4
            if k and i:
                slot = offs.at[from_x]
                remote(slot, slot, off_send.at[k], off_recv.at[k], sibling).wait_recv()
            slot = 2 * ((4 - k) % 4) + i
            fill_rows(pick_rows.at[slot], offs[from_x, 2 * i : 2 * i + 1, :])
            fill_columns(pick_columns.at[slot], offs[from_x, 2 * i + 1 : 2 * i + 2, :])

    for k in (1, 7, 2, 6, 3, 5, 4):
        rows = plane.at[(xy - k + 8) % 8, core]
        remote(rows, rows, s1_send.at[k], s1_recv.at[k], sibling).wait_recv()
        remote(rows, rows, chip_send.at[k], chip_recv.at[k], sibling).start()
    for k in range(8):
        rows = plane.at[(xy - k + 8) % 8, 1 - core]
        remote(rows, rows, chip_send.at[k], chip_recv.at[k], sibling).wait_recv()

    own_copy.wait()

    def target(k, i):
        to_j = core if i == 0 else 3 - core
        return to_j, (4 * g + to_j, 4 * ((x + k) % 4) + 2 * h + core)

    own_plane = 2 * j + x // 2
    home = o_ref.at[own_plane, x % 2]
    for i in (1, 0):
        for k in (2, 1, 3, 0):
            slot = 2 * k + i
            rows = dot(pick_rows[slot], plane[...].reshape(win, win)).astype(BF16)
            stage[slot] = dot(rows, pick_columns[slot]).astype(BF16)
            to_j, device = target(k, i)
            copy = remote(
                stage.at[slot], home, s2_send.at[slot], s2_recv.at[2 * own_plane + x % 2], device
            )
            if k == 2:
                pl.when(core == 0)(copy.start)
                pl.when(core == 1)(
                    remote(
                        stage.at[slot], crop_relay.at[i], s2_send.at[slot], crop_relay_recv.at[i],
                        (d, 4 * ((x + 3) % 4) + 2 * h + core),
                    ).start
                )
            elif k:
                copy.start()
            else:
                pl.when(to_j != j)(copy.start)

                @pl.when(to_j == j)
                def _():
                    o_ref[own_plane, x % 2] = stage[slot]

    def crop_forward(i):
        from_x = (x + 1) % 4
        from_plane = 2 * j + from_x // 2
        to_j = core if i == 0 else 3 - core
        return remote(
            crop_relay.at[i], o_ref.at[from_plane, from_x % 2], crop_relay_send.at[i],
            s2_recv.at[2 * from_plane + from_x % 2], (4 * g + to_j, 4 * ((x + 3) % 4) + 2 * h + core),
        )

    @pl.when(core == 1)
    def _():
        for i in (1, 0):
            slot = crop_relay.at[i]
            remote(slot, slot, s2_send.at[0], crop_relay_recv.at[i], sibling).wait_recv()
            crop_forward(i).start()

    for load in loads:
        load.wait()
    pl.when(g == 0)(load_probe.wait)
    half = side // 2
    piece = half // 2

    def forward_pieces(n):
        rows = [pl.ds(m * half + n * piece, piece) for m in range(2)]
        return [
            remote(
                stored.at[count, :, rows[m]], stored.at[0, :, rows[m]],
                hop_send.at[2 * n + m], hop_recv.at[2 * n + m], ahead,
            )
            for m in range(2)
        ]

    def backward_piece(n, device):
        rows = middle.at[:, pl.ds(n * half, half)]
        return remote(rows, rows, hop_send.at[4 + n], hop_recv.at[4 + n], device)

    def owner(s, c):
        return 2 * (s % 2) + c, s // 2

    def make_put_tables():
        for i in range(2):
            for k in range(4):
                at = 4 * (1 - i) + k
                from_x = (x + k) % 4
                fill_rows(put_columns.at[at], offs[from_x, 2 * i + 1 : 2 * i + 2, :])
                for m in range(2):
                    first = 1 - core if m == 0 else core
                    fill_columns(
                        put_rows.at[m, 1 - i, :, k * side : (k + 1) * side],
                        offs[from_x, 2 * i : 2 * i + 1, :],
                        lambda r: r + (r // block + first) * block,
                    )

    starts = jnp.logical_and(active, g == 0)
    pl.when(jnp.logical_not(starts))(make_put_tables)

    @pl.when(active)
    def _():
        def wait_crop(s):
            for c in range(2):
                from_x, from_j = owner(s, c)
                slot = o_ref.at[s, c]
                copy = remote(slot, slot, s2_send.at[0], s2_recv.at[2 * s + c], sibling)
                pl.when(jnp.logical_or(from_x != x, from_j != j))(copy.wait_recv)

        def enter(s, at, real, imag):
            o_real, o_imag = strip(o_ref, s, 0, at), strip(o_ref, s, 1, at)
            put_sums(
                sums, sums_row(at, side), o_real * real - o_imag * imag, o_real * imag + o_imag * real
            )

        def keep_wave(s, at, real, imag):
            stored[s, 0, pl.ds(at, STRIP), :] = real.astype(BF16)
            stored[s, 1, pl.ds(at, STRIP), :] = imag.astype(BF16)

        def forward(s, carry):
            wait_crop(s + 1)
            for at, real, imag in left_stage(middle, field, left_ref, 0):
                keep_wave(s + 1, at, real, imag)
                enter(s + 1, at, real, imag)
            right_stage(sums, flat, middle, right_ref, 0)
            return carry

        wait_crop(0)
        for n in range(2):

            @pl.when(g > 0)
            def _():
                for copy in forward_pieces(n):
                    copy.wait_recv()

            for m in range(2):
                for r in strips(piece):
                    at = m * half + n * piece + r
                    enter(0, at, strip(stored, 0, 0, at), strip(stored, 0, 1, at))
        right_stage(sums, flat, middle, right_ref, 0)
        def forward_pair(n, carry):
            forward(2 * n, carry)
            return forward(2 * n + 1, carry)

        lax.fori_loop(0, (count - 2) // 2, forward_pair, 0)

        @pl.when(g < last)
        def _():
            forward(count - 2, 0)
            for at, real, imag in left_stage(middle, field, left_ref, 0):
                keep_wave(count, at, real, imag)
                if at >= half and (at + STRIP) % piece == 0:
                    for copy in forward_pieces((at - half) // piece):
                        copy.start()
            pl.when(g == 0)(make_put_tables)
            for n in range(2):
                backward_piece(n, ahead).wait_recv()

        def leave(s, field_strips):
            for at, real, imag in field_strips:
                real, imag = real.astype(BF16), imag.astype(BF16)
                o_real, o_imag = o_ref[s, 0, pl.ds(at, STRIP), :], o_ref[s, 1, pl.ds(at, STRIP), :]
                put_sums(
                    sums, sums_row(at, side), o_real * real + o_imag * imag, o_real * imag - o_imag * real
                )
                p_real, p_imag = stored[s, 0, pl.ds(at, STRIP), :], stored[s, 1, pl.ds(at, STRIP), :]
                grads[s, 0, pl.ds(at, STRIP), :] = p_real * real + p_imag * imag
                grads[s, 1, pl.ds(at, STRIP), :] = p_real * imag - p_imag * real

        @pl.when(g == last)
        def _():
            final = count - 1
            leaving, turned = grads.at[0], grads.at[1]
            f = [(transform_ref[m, 0], transform_ref[m, 1]) for m in range(3)]

            def flat_strip(m, at):
                return flat[m, pl.ds(at, STRIP), :]

            def transformed(source, inverse):
                turned[0], turned[1] = (v.astype(BF16) for v in fourier_right(source[0], source[1], f, inverse))
                flat[0], flat[1] = fourier_left(turned[0], turned[1], f, inverse)

            wait_crop(final)
            for at, real, imag in left_stage(middle, field, left_ref, 0):
                keep_wave(final, at, real, imag)
                o_real, o_imag = strip(o_ref, final, 0, at), strip(o_ref, final, 1, at)
                leaving[0, pl.ds(at, STRIP), :] = (o_real * real - o_imag * imag).astype(BF16)
                leaving[1, pl.ds(at, STRIP), :] = (o_real * imag + o_imag * real).astype(BF16)
            transformed(leaving, False)
            for at in strips(side):
                real, imag = flat_strip(0, at), flat_strip(1, at)
                weight = real * real + imag * imag - measured_ref[pl.ds(at, STRIP), :]
                sums[0, pl.ds(at, STRIP), :] = (real * weight).astype(BF16)
                sums[1, pl.ds(at, STRIP), :] = (imag * weight).astype(BF16)
            transformed(sums, True)
            leave(final, ((at, flat_strip(0, at), flat_strip(1, at)) for at in strips(side)))
            right_stage(sums, flat, middle, right_ref, 1)

        def send_patches(s):
            for c in range(2):
                to_x, to_j = owner(s, c)
                source, send = grads.at[s, c], s3_send.at[2 * s + c]
                away = jnp.logical_or(to_x != x, to_j != j)
                detour = jnp.logical_and(to_x == (x + 2) % 4, to_j % 2 == 1)
                copy = remote(
                    source, patches.at[2 * x + mine], send, s3_recv.at[2 * x + mine],
                    (4 * g + to_j, 4 * to_x + 2 * h + core),
                )
                pl.when(jnp.logical_and(away, jnp.logical_not(detour)))(copy.start)
                pl.when(detour)(
                    remote(
                        source, patch_relay.at[to_j // 2], send, patch_relay_recv.at[to_j // 2],
                        (d, 4 * ((x + 3) % 4) + 2 * h + 1 - core),
                    ).start
                )

                @pl.when(jnp.logical_not(away))
                def _():
                    patches[2 * x + mine] = grads[s, c]

        def backward(s):
            leave(s, left_stage(middle, field, left_ref, 1))
            right_stage(sums, flat, middle, right_ref, 1)

        def send_pair(s):
            pl.when(g == 0)(functools.partial(send_patches, s))
            pl.when(g == 0)(functools.partial(send_patches, s - 1))

        def backward_pair(t, carry):
            s = count - 2 - 2 * t
            backward(s)
            backward(s - 1)
            send_pair(s)
            return carry

        pl.when(g < last)(functools.partial(backward, count - 1))
        pl.when(g == 0)(functools.partial(send_patches, count - 1))
        lax.fori_loop(0, (count - 2) // 2, backward_pair, 0)
        leave(0, left_stage(middle, field, left_ref, 1))
        pl.when(g == 0)(functools.partial(send_patches, 0))

        @pl.when(g > 0)
        def _():
            def leave_piece(n):
                backward_piece(n, behind).start()

            right_stage(sums, flat, middle, right_ref, 1, leave_piece)
            for n in range(2):
                backward_piece(n, behind).wait_send()

            def send(t, carry):
                send_patches(count - 1 - t)
                return carry

            lax.fori_loop(0, count, send, 0)

    def patch_forward(n):
        from_x = (x + 1) % 4
        p = 2 * from_x + jnp.where(j == 1 - core, 0, 1)
        return remote(
            patch_relay.at[n], patches.at[p], patch_relay_send.at[n], s3_recv.at[p],
            (4 * g + 2 * n + 1, 4 * ((x + 3) % 4) + 2 * h + 1 - core),
        )

    @pl.when(jnp.logical_not(active))
    def _():
        for n in (1, 0):
            slot = patch_relay.at[n]
            remote(slot, slot, s3_send.at[0], patch_relay_recv.at[n], sibling).wait_recv()
            patch_forward(n).start()

    for i in (1, 0):
        group = 1 - i
        for kx in (0, 1, 3, 2):
            from_x = (x - kx + 4) % 4
            from_j = core if i == 0 else 3 - core
            p = 2 * from_x + i
            slot = patches.at[p]
            copy = remote(slot, slot, s3_send.at[0], s3_recv.at[p], sibling)
            if kx:
                copy.wait_recv()
            else:
                pl.when(from_j != j)(copy.wait_recv)
            at = (4 - kx) % 4
            wide[at * side : (at + 1) * side, :] = dot(slot[...], put_columns[4 * group + at]).astype(BF16)
        if group == 0:
            for m in range(2):
                total[m] = dot(put_rows[m, 0], wide[...])
    partial[...] = (total[0] + dot(put_rows[0, 1], wide[...])).reshape(partial.shape).astype(BF16)
    chip_copy = remote(partial, sibling_sum, back_send.at[0], back_recv.at[0], sibling)
    chip_copy.start()
    own_rows = (total[1] + dot(put_rows[1, 1], wide[...])).reshape(partial.shape)
    chip_copy.wait_recv()
    reduced[...] = (own_rows + sibling_sum[...].astype(F32)).astype(BF16)
    for k in (4, 3, 5, 2, 6, 1, 7):
        to = (xy + k) % 8
        remote(reduced.at[to], arrived.at[4 * h + x], s4_send.at[k], s4_recv.at[k], (d, 2 * to + core)).start()
    kept = pltpu.make_async_copy(reduced.at[xy], arrived.at[4 * h + x], load_sem.at[6])
    kept.start()
    for k in range(1, 8):
        come = (xy - k + 8) % 8
        slot = arrived.at[4 * (come % 2) + come // 2]
        remote(slot, slot, s4_send.at[k], s4_recv.at[k], sibling).wait_recv()

    kept.wait()

    for k in range(1, 8):
        slot = reduced.at[0]
        remote(slot, slot, s1_send.at[k], s1_recv.at[k], sibling).wait_send()
        remote(slot, slot, s4_send.at[k], s4_recv.at[k], sibling).wait_send()
    for k in range(1, 4):
        remote(own_offsets, own_offsets, off_send.at[k], off_recv.at[k], sibling).wait_send()
    for k in range(8):
        slot = reduced.at[0]
        remote(slot, slot, chip_send.at[k], chip_recv.at[k], sibling).wait_send()
    chip_copy.wait_send()
    for i in range(2):
        for k in range(4):
            slot = 2 * k + i
            to_j, device = target(k, i)
            copy = remote(stage.at[slot], home, s2_send.at[slot], s2_recv.at[0], device)
            if k:
                copy.wait_send()
            else:
                pl.when(to_j != j)(copy.wait_send)

    @pl.when(core == 1)
    def _():
        for i in range(2):
            crop_forward(i).wait_send()

    @pl.when(jnp.logical_not(active))
    def _():
        for n in range(2):
            patch_forward(n).wait_send()

    @pl.when(active)
    def _():
        @pl.when(g < last)
        def _():
            for n in range(2):
                for copy in forward_pieces(n):
                    copy.wait_send()

        for s in range(count):
            for c in range(2):
                to_x, to_j = owner(s, c)
                slot = grads.at[s, c]
                copy = remote(slot, slot, s3_send.at[2 * s + c], s3_recv.at[0], sibling)
                pl.when(jnp.logical_or(to_x != x, to_j != j))(copy.wait_send)


def sum_kernel(arrived, out_ref):
    planes = out_ref.shape[0]
    for plane in range(planes):
        for r in strips(out_ref.shape[1]):
            rows = pl.ds(r, STRIP)
            out_ref[plane, rows, :] = arrived[plane, rows, :].astype(F32) + arrived[planes + plane, rows, :].astype(F32)


def per_device(transmission, probe, offsets, measured):
    layers, _, rows, win = transmission.shape
    side = probe.shape[-1]
    group = 4 * layers
    rights, lefts, transforms = tables(side)
    dma = pltpu.SemaphoreType.DMA
    hbm = pl.BlockSpec(memory_space=pl.ANY)
    smem = pl.BlockSpec(memory_space=pltpu.SMEM)
    arrived = pl.pallas_call(
        kernel,
        out_shape=jax.ShapeDtypeStruct((8, rows, win), BF16),
        in_specs=[smem, hbm, hbm, hbm, hbm, hbm, hbm],
        out_specs=hbm,
        scratch_shapes=[
            pltpu.VMEM((8, 128), jnp.int32),
            pltpu.VMEM((4, 8, 128), jnp.int32),
            pltpu.VMEM((8, 2, rows, win), BF16),
            pltpu.VMEM((8, side, win), BF16),
            pltpu.VMEM((8, win, side), BF16),
            pltpu.VMEM((8, side, side), BF16),
            pltpu.VMEM((group, 2, side, side), BF16),
            pltpu.VMEM((group + 1, 2, side, side), BF16),
            pltpu.VMEM((2, side, side), BF16),
            pltpu.VMEM((2, side, side), F32),
            pltpu.VMEM((2, side, side), BF16),
            pltpu.VMEM((2, 2 * side, side), F32),
            pltpu.VMEM((group, 2, side, side), BF16),
            pltpu.VMEM((side, side), F32),
            pltpu.VMEM(rights.shape, BF16),
            pltpu.VMEM(lefts.shape, BF16),
            pltpu.VMEM(transforms.shape, BF16),
            pltpu.VMEM((8, side, side), BF16),
            pltpu.VMEM((8, side, win), BF16),
            pltpu.VMEM((2, 2, win // 2, 4 * side), BF16),
            pltpu.VMEM((4 * side, win), BF16),
            pltpu.VMEM((2, win // 2, win), F32),
            pltpu.VMEM((8, rows, win), BF16),
            pltpu.VMEM((8, rows, win), BF16),
            pltpu.VMEM((8, rows, win), BF16),
            pltpu.VMEM((2, side, side), BF16),
            pltpu.VMEM((2, side, side), BF16),
            dma((2,)), dma((2,)), dma((2,)), dma((2,)),
            dma((7,)), dma((8,)), dma((8,)), dma((4,)), dma((4,)), dma((8,)), dma((8,)), dma((8,)),
            dma((16,)), dma((6,)), dma((6,)), dma((16,)), dma((8,)), dma((1,)), dma((1,)), dma((8,)), dma((8,)),
        ],
        compiler_params=pltpu.CompilerParams(
            collective_id=0, has_side_effects=True, vmem_limit_bytes=VMEM_LIMIT
        ),
        name="ptychography_backward",
    )(
        offsets, transmission, probe, measured,
        jnp.asarray(rights), jnp.asarray(lefts), jnp.asarray(transforms),
    )
    gradient = pl.pallas_call(
        sum_kernel,
        out_shape=jax.ShapeDtypeStruct((2 * layers, rows, win), F32),
        in_specs=[vmem()],
        out_specs=vmem(),
        name="sum_halves",
    )(arrived)
    return gradient.reshape(layers, 2, rows, win)


def solution(mesh):
    in_specs = (P("depth", None, "pos", None), P(), P("pos", None), P("pos", None, None))
    out_specs = P("depth", None, "pos", None)
    return jax.shard_map(
        per_device, mesh=mesh, in_specs=in_specs, out_specs=out_specs, check_vma=False
    )
```

```python
import functools
import math

import jax
import jax.numpy as jnp
import ml_dtypes
import numpy as np
from jax import lax
from jax.experimental import pallas as pl
from jax.experimental.pallas import tpu as pltpu
from jax.sharding import PartitionSpec as P


MESH = pl.DeviceIdType.MESH
F32 = jnp.float32
BF16 = jnp.bfloat16
VMEM_LIMIT = 56 * 1024 * 1024


def vmem():
    return pl.BlockSpec(memory_space=pltpu.VMEM)


def place():
    d = lax.axis_index("depth")
    q = lax.axis_index("pos")
    return d // 4, d % 4, q // 4, (q // 2) % 2, q % 2


def hi_lo(table, axis):
    high = table.astype(ml_dtypes.bfloat16)
    low = (table - high.astype(np.float64)).astype(ml_dtypes.bfloat16)
    return np.concatenate([high, low], axis)


def right_form(matrix):
    return np.block([[matrix.real, matrix.imag], [-matrix.imag, matrix.real]])


@functools.lru_cache(maxsize=None)
def tables(side):
    half = side // 2
    grid = np.arange(side)
    fourier = np.exp(-2j * np.pi * (np.outer(grid, grid) % side) / side) / math.sqrt(side)
    frequency = (grid + half) % side - half
    phase = np.exp(-1j * math.pi * frequency.astype(np.float64) ** 2 / 1024.0)
    circulant = fourier.conj() @ (phase[:, None] * fourier)
    near, far = circulant[:half, :half], circulant[:half, half:]
    forms = [right_form((near + far) / 2), right_form((near - far) / 2)]
    rights = np.stack([[hi_lo(m, 0) for m in forms], [hi_lo(m.T, 0) for m in forms]])
    order = grid.reshape(2, half // STRIP, STRIP).transpose(1, 0, 2).reshape(side)
    strided = [m[order][:, order] for m in forms]

    def strip_pairs(table):
        parts = hi_lo(table, 0).reshape(2, side // STRIP, STRIP, side)
        return parts.transpose(1, 0, 2, 3).reshape(2 * side, side)

    lefts = np.stack([[strip_pairs(m.T) for m in strided], [strip_pairs(m) for m in strided]])
    transforms = np.stack([hi_lo(m, 0) for m in (fourier.real, fourier.imag, -fourier.imag)])
    return rights, lefts, transforms.reshape(3, 2, side, side)


def dot(a, b):
    return jnp.dot(a, b, preferred_element_type=F32)


def cat(parts, axis):
    return jnp.concatenate(parts, axis)


STRIP = 16
BLOCKS = 2


def strips(count):
    return range(0, count, STRIP)


def halves(value):
    middle = value.shape[1] // 2
    return value[:, :middle], value[:, middle:]


def put_sums(ref, at, real, imag):
    (a, b), (c, d) = halves(real), halves(imag)
    ref[0, pl.ds(at, STRIP), :] = cat([a + b, c + d], 1).astype(BF16)
    ref[1, pl.ds(at, STRIP), :] = cat([a - b, c - d], 1).astype(BF16)


def sums_row(row, side):
    half = side // 2
    return 2 * row if row < half else 2 * (row - half) + STRIP


def right_stage(sums, flat, middle, right_ref, way, done=lambda n: None):
    side = sums.shape[1]
    block = side // BLOCKS
    for n in range(BLOCKS):
        for m in range(2):
            x = sums[m, pl.ds(n * block, block), :]
            flat[m, pl.ds(n * block, block), :] = dot(cat([x, x], 1), right_ref[way, m]).astype(BF16)
        for r in range(n * block, (n + 1) * block, 2 * STRIP):
            s, t = flat[0, pl.ds(r, STRIP), :], flat[0, pl.ds(r + STRIP, STRIP), :]
            d, e = flat[1, pl.ds(r, STRIP), :], flat[1, pl.ds(r + STRIP, STRIP), :]
            for m, (a, b) in enumerate(((s + t, d + e), (s - t, d - e))):
                (a_real, a_imag), (b_real, b_imag) = halves(a), halves(b)
                middle[m, pl.ds(r, STRIP), :] = cat([a_real, b_real], 1).astype(BF16)
                middle[m, pl.ds(r + STRIP, STRIP), :] = cat([a_imag, b_imag], 1).astype(BF16)
        done(n)


def left_stage(middle, field, left_ref, way):
    side = middle.shape[1]
    block = side // BLOCKS

    def total(m, r):
        return field[m, pl.ds(2 * r, STRIP), :] + field[m, pl.ds(2 * r + STRIP, STRIP), :]

    for n in range(BLOCKS):
        rows = pl.ds(2 * n * block, 2 * block)
        for m in range(2):
            field[m, rows, :] = dot(left_ref[way, m, rows, :], middle[m])
        for r in range(n * block, (n + 1) * block, 2 * STRIP):
            p, u = total(0, r), total(0, r + STRIP)
            m, v = total(1, r), total(1, r + STRIP)
            for at, real, imag in ((r // 2, p + m, u + v), (side // 2 + r // 2, p - m, u - v)):
                (a, b), (c, d) = halves(real), halves(imag)
                yield at, cat([a + b, a - b], 1), cat([c + d, c - d], 1)


def strip(ref, s, c, at):
    return ref[s, c, pl.ds(at, STRIP), :].astype(F32)


def fourier_right(real, imag, f, inverse):
    r, i, n = f
    up, down = (n, i) if inverse else (i, n)
    x = cat([real, real, imag, imag], 1)
    a = dot(x, cat([r[0], r[1], down[0], down[1]], 0))
    b = dot(x, cat([up[0], up[1], r[0], r[1]], 0))
    return a, b


def fourier_left(real, imag, f, inverse):
    r, i, n = f
    up, down = (n, i) if inverse else (i, n)
    x = cat([real, real, imag, imag], 0)
    a = dot(cat([r[0], r[1], down[0], down[1]], 1), x)
    b = dot(cat([up[0], up[1], r[0], r[1]], 1), x)
    return a, b


def neighbours(g, j, x, h, core):
    d = 4 * g + j
    xy = 2 * x + h
    partners = [(d, 4 * x + 2 * h + 1 - core)]
    for k in range(1, 8):
        partners.append((d, 2 * ((xy + k) % 8) + core))
    for kx in range(4):
        for kj in range(1, 4):
            partners.append((4 * g + (j + kj) % 4, 4 * ((x + kx) % 4) + 2 * h + core))
    return partners


def remote(src, dst, send, recv, device):
    return pltpu.make_async_remote_copy(
        src_ref=src, dst_ref=dst, send_sem=send, recv_sem=recv, device_id=device, device_id_type=MESH
    )


def one_hot(mask):
    return jnp.where(mask, 1.0, 0.0).astype(BF16)


def shifts(columns):
    return lax.broadcasted_iota(jnp.int32, (STRIP, columns), 1) - lax.broadcasted_iota(
        jnp.int32, (STRIP, columns), 0
    )


def fill_rows(ref, offset):
    rows, columns = ref.shape
    lanes = cat([offset] * (columns // 128), 1)
    base = shifts(columns)
    for r in strips(rows):
        ref[pl.ds(r, STRIP), :] = one_hot(base == lanes + r)


def fill_columns(ref, offset, row_of=lambda r: r):
    rows, columns = ref.shape
    lanes = cat([offset] * (columns // 128), 1)
    base = shifts(columns)
    for r in strips(rows):
        ref[pl.ds(r, STRIP), :] = one_hot(base == row_of(r) - lanes)


def kernel(
    off_ref, t_hbm, probe_hbm, measured_hbm, right_hbm, left_hbm, transform_hbm, arrived,
    own_offsets, offs, plane, pick_rows, pick_columns, stage, o_ref, stored, sums, flat, middle, field, grads, measured_ref, right_ref, left_ref,
    transform_ref, patches, put_columns, put_rows, wide, total, partial, sibling_sum, reduced,
    crop_relay, patch_relay, crop_relay_send, crop_relay_recv, patch_relay_send, patch_relay_recv,
    load_sem, s1_send, s1_recv, off_send, off_recv, chip_send, chip_recv, s2_send, s2_recv,
    hop_send, hop_recv, s3_send, s3_recv, back_send, back_recv, s4_send, s4_recv,
):
    g, j, x, h, core = place()
    d = 4 * g + j
    q = 4 * x + 2 * h + core
    xy = 2 * x + h
    last = 3
    sibling = (d, 4 * x + 2 * h + 1 - core)
    win = plane.shape[-1]
    side = o_ref.shape[-1]
    half = side // 2
    count = o_ref.shape[0]
    block = plane.shape[2]
    active = jnp.logical_or(j == core, j == 3 - core)
    mine = jnp.where(j == core, 0, 1)
    ahead = (jnp.minimum(d + 4, 15), q)
    behind = (jnp.maximum(d - 4, 0), q)

    loads = [
        pltpu.make_async_copy(right_hbm, right_ref, load_sem.at[0]),
        pltpu.make_async_copy(left_hbm, left_ref, load_sem.at[1]),
        pltpu.make_async_copy(transform_hbm, transform_ref, load_sem.at[2]),
        pltpu.make_async_copy(measured_hbm.at[mine], measured_ref, load_sem.at[3]),
    ]
    load_probe = pltpu.make_async_copy(probe_hbm, stored.at[0], load_sem.at[4])
    barrier = pltpu.get_barrier_semaphore()
    partners = neighbours(g, j, x, h, core)
    relayed = [(4 * g + (j + k) % 4, 4 * ((x + 1) % 4) + 2 * h + 1 - core) for k in range(4)]
    for partner in partners + relayed:
        pl.semaphore_signal(barrier, inc=1, device_id=partner, device_id_type=MESH)

    @pl.when(jnp.logical_and(active, g < last))
    def _():
        pl.semaphore_signal(barrier, inc=1, device_id=ahead, device_id_type=MESH)

    @pl.when(jnp.logical_and(active, g > 0))
    def _():
        pl.semaphore_signal(barrier, inc=1, device_id=behind, device_id_type=MESH)

    chained = jnp.where(active, jnp.where(jnp.logical_or(g == 0, g == last), 1, 2), 0)
    for load in loads:
        load.start()
    pl.when(g == 0)(load_probe.start)
    for k in range(4):
        own_offsets[k : k + 1, :] = jnp.full((1, 128), off_ref[k // 2, k % 2], jnp.int32)
        own_offsets[k + 4 : k + 5, :] = jnp.zeros((1, 128), jnp.int32)
    pl.semaphore_wait(barrier, len(partners) + len(relayed) + chained)

    for k in range(1, 4):
        to = (x + k) % 4
        remote(
            own_offsets, offs.at[x], off_send.at[k], off_recv.at[k], (d, 4 * to + 2 * h + core)
        ).start()
    for k in (4, 3, 5, 2, 6, 1, 7):
        to = (xy + k) % 8
        tx = to // 2
        remote(
            t_hbm.at[tx // 2, tx % 2], plane.at[xy, core], s1_send.at[k], s1_recv.at[k], (d, 2 * to + core)
        ).start()
    own = t_hbm.at[x // 2, x % 2]
    remote(own, plane.at[xy, core], chip_send.at[0], chip_recv.at[0], sibling).start()
    own_copy = pltpu.make_async_copy(own, plane.at[xy, core], load_sem.at[5])
    own_copy.start()
    offs[x] = own_offsets[...]

    for i in (1, 0):
        for k in (0, 3, 2, 1):
            from_x = (x - k + 4) % 4
            if k and i:
                slot = offs.at[from_x]
                remote(slot, slot, off_send.at[k], off_recv.at[k], sibling).wait_recv()
            slot = 2 * ((4 - k) % 4) + i
            fill_rows(pick_rows.at[slot], offs[from_x, 2 * i : 2 * i + 1, :])
            fill_columns(pick_columns.at[slot], offs[from_x, 2 * i + 1 : 2 * i + 2, :])

    for k in (1, 7, 2, 6, 3, 5, 4):
        rows = plane.at[(xy - k + 8) % 8, core]
        remote(rows, rows, s1_send.at[k], s1_recv.at[k], sibling).wait_recv()
        remote(rows, rows, chip_send.at[k], chip_recv.at[k], sibling).start()
    for k in range(8):
        rows = plane.at[(xy - k + 8) % 8, 1 - core]
        remote(rows, rows, chip_send.at[k], chip_recv.at[k], sibling).wait_recv()

    own_copy.wait()

    def target(k, i):
        to_j = core if i == 0 else 3 - core
        return to_j, (4 * g + to_j, 4 * ((x + k) % 4) + 2 * h + core)

    own_plane = 2 * j + x // 2
    home = o_ref.at[own_plane, x % 2]
    for i in (1, 0):
        for k in (2, 1, 3, 0):
            slot = 2 * k + i
            rows = dot(pick_rows[slot], plane[...].reshape(win, win)).astype(BF16)
            stage[slot] = dot(rows, pick_columns[slot]).astype(BF16)
            to_j, device = target(k, i)
            copy = remote(
                stage.at[slot], home, s2_send.at[slot], s2_recv.at[2 * own_plane + x % 2], device
            )
            if k == 2:
                pl.when(core == 0)(copy.start)
                pl.when(core == 1)(
                    remote(
                        stage.at[slot], crop_relay.at[i], s2_send.at[slot], crop_relay_recv.at[i],
                        (d, 4 * ((x + 3) % 4) + 2 * h + core),
                    ).start
                )
            elif k:
                copy.start()
            else:
                pl.when(to_j != j)(copy.start)

                @pl.when(to_j == j)
                def _():
                    o_ref[own_plane, x % 2] = stage[slot]

    def crop_forward(i):
        from_x = (x + 1) % 4
        from_plane = 2 * j + from_x // 2
        to_j = core if i == 0 else 3 - core
        return remote(
            crop_relay.at[i], o_ref.at[from_plane, from_x % 2], crop_relay_send.at[i],
            s2_recv.at[2 * from_plane + from_x % 2], (4 * g + to_j, 4 * ((x + 3) % 4) + 2 * h + core),
        )

    @pl.when(core == 1)
    def _():
        for i in (1, 0):
            slot = crop_relay.at[i]
            remote(slot, slot, s2_send.at[0], crop_relay_recv.at[i], sibling).wait_recv()
            crop_forward(i).start()

    for load in loads:
        load.wait()
    pl.when(g == 0)(load_probe.wait)
    half = side // 2
    piece = half // 2

    def forward_pieces(n):
        rows = [pl.ds(m * half + n * piece, piece) for m in range(2)]
        return [
            remote(
                stored.at[count, :, rows[m]], stored.at[0, :, rows[m]],
                hop_send.at[2 * n + m], hop_recv.at[2 * n + m], ahead,
            )
            for m in range(2)
        ]

    def backward_piece(n, device):
        rows = middle.at[:, pl.ds(n * half, half)]
        return remote(rows, rows, hop_send.at[4 + n], hop_recv.at[4 + n], device)

    def owner(s, c):
        return 2 * (s % 2) + c, s // 2

    def make_put_tables():
        for i in range(2):
            for k in range(4):
                at = 4 * (1 - i) + k
                from_x = (x + k) % 4
                fill_rows(put_columns.at[at], offs[from_x, 2 * i + 1 : 2 * i + 2, :])
                for m in range(2):
                    first = 1 - core if m == 0 else core
                    fill_columns(
                        put_rows.at[m, 1 - i, :, k * side : (k + 1) * side],
                        offs[from_x, 2 * i : 2 * i + 1, :],
                        lambda r: r + (r // block + first) * block,
                    )

    starts = jnp.logical_and(active, g == 0)
    pl.when(jnp.logical_not(starts))(make_put_tables)

    @pl.when(active)
    def _():
        def wait_crop(s):
            for c in range(2):
                from_x, from_j = owner(s, c)
                slot = o_ref.at[s, c]
                copy = remote(slot, slot, s2_send.at[0], s2_recv.at[2 * s + c], sibling)
                pl.when(jnp.logical_or(from_x != x, from_j != j))(copy.wait_recv)

        def enter(s, at, real, imag):
            o_real, o_imag = strip(o_ref, s, 0, at), strip(o_ref, s, 1, at)
            put_sums(
                sums, sums_row(at, side), o_real * real - o_imag * imag, o_real * imag + o_imag * real
            )

        def keep_wave(s, at, real, imag):
            stored[s, 0, pl.ds(at, STRIP), :] = real.astype(BF16)
            stored[s, 1, pl.ds(at, STRIP), :] = imag.astype(BF16)

        def forward(s, carry):
            wait_crop(s + 1)
            for at, real, imag in left_stage(middle, field, left_ref, 0):
                keep_wave(s + 1, at, real, imag)
                enter(s + 1, at, real, imag)
            right_stage(sums, flat, middle, right_ref, 0)
            return carry

        wait_crop(0)
        for n in range(2):

            @pl.when(g > 0)
            def _():
                for copy in forward_pieces(n):
                    copy.wait_recv()

            for m in range(2):
                for r in strips(piece):
                    at = m * half + n * piece + r
                    enter(0, at, strip(stored, 0, 0, at), strip(stored, 0, 1, at))
        right_stage(sums, flat, middle, right_ref, 0)
        def forward_pair(n, carry):
            forward(2 * n, carry)
            return forward(2 * n + 1, carry)

        lax.fori_loop(0, (count - 2) // 2, forward_pair, 0)

        @pl.when(g < last)
        def _():
            forward(count - 2, 0)
            for at, real, imag in left_stage(middle, field, left_ref, 0):
                keep_wave(count, at, real, imag)
                if at >= half and (at + STRIP) % piece == 0:
                    for copy in forward_pieces((at - half) // piece):
                        copy.start()
            pl.when(g == 0)(make_put_tables)
            for n in range(2):
                backward_piece(n, ahead).wait_recv()

        def leave(s, field_strips):
            for at, real, imag in field_strips:
                real, imag = real.astype(BF16), imag.astype(BF16)
                o_real, o_imag = o_ref[s, 0, pl.ds(at, STRIP), :], o_ref[s, 1, pl.ds(at, STRIP), :]
                put_sums(
                    sums, sums_row(at, side), o_real * real + o_imag * imag, o_real * imag - o_imag * real
                )
                p_real, p_imag = stored[s, 0, pl.ds(at, STRIP), :], stored[s, 1, pl.ds(at, STRIP), :]
                grads[s, 0, pl.ds(at, STRIP), :] = p_real * real + p_imag * imag
                grads[s, 1, pl.ds(at, STRIP), :] = p_real * imag - p_imag * real

        @pl.when(g == last)
        def _():
            final = count - 1
            leaving, turned = grads.at[0], grads.at[1]
            f = [(transform_ref[m, 0], transform_ref[m, 1]) for m in range(3)]

            def field_strip(m, at):
                return field[m, pl.ds(at, STRIP), :]

            def transformed(source, inverse):
                turned[0], turned[1] = (v.astype(BF16) for v in fourier_right(source[0], source[1], f, inverse))
                real, imag = fourier_left(turned[0], turned[1], f, inverse)
                field[0, :side, :] = real
                field[1, :side, :] = imag

            wait_crop(final)
            for at, real, imag in left_stage(middle, field, left_ref, 0):
                keep_wave(final, at, real, imag)
                o_real, o_imag = strip(o_ref, final, 0, at), strip(o_ref, final, 1, at)
                leaving[0, pl.ds(at, STRIP), :] = (o_real * real - o_imag * imag).astype(BF16)
                leaving[1, pl.ds(at, STRIP), :] = (o_real * imag + o_imag * real).astype(BF16)
            transformed(leaving, False)
            for at in strips(side):
                real, imag = field_strip(0, at), field_strip(1, at)
                weight = real * real + imag * imag - measured_ref[pl.ds(at, STRIP), :]
                sums[0, pl.ds(at, STRIP), :] = (real * weight).astype(BF16)
                sums[1, pl.ds(at, STRIP), :] = (imag * weight).astype(BF16)
            transformed(sums, True)
            leave(final, ((at, field_strip(0, at), field_strip(1, at)) for at in strips(side)))
            right_stage(sums, flat, middle, right_ref, 1)

        def send_patches(s):
            for c in range(2):
                to_x, to_j = owner(s, c)
                source, send = grads.at[s, c], s3_send.at[2 * s + c]
                away = jnp.logical_or(to_x != x, to_j != j)
                detour = jnp.logical_and(to_x == (x + 2) % 4, to_j % 2 == 1)
                copy = remote(
                    source, patches.at[2 * x + mine], send, s3_recv.at[2 * x + mine],
                    (4 * g + to_j, 4 * to_x + 2 * h + core),
                )
                pl.when(jnp.logical_and(away, jnp.logical_not(detour)))(copy.start)
                pl.when(detour)(
                    remote(
                        source, patch_relay.at[to_j // 2], send, patch_relay_recv.at[to_j // 2],
                        (d, 4 * ((x + 3) % 4) + 2 * h + 1 - core),
                    ).start
                )

                @pl.when(jnp.logical_not(away))
                def _():
                    patches[2 * x + mine] = grads[s, c]

        def backward(s):
            leave(s, left_stage(middle, field, left_ref, 1))
            right_stage(sums, flat, middle, right_ref, 1)

        def send_pair(s):
            pl.when(g == 0)(functools.partial(send_patches, s))
            pl.when(g == 0)(functools.partial(send_patches, s - 1))

        def backward_pair(t, carry):
            s = count - 2 - 2 * t
            backward(s)
            backward(s - 1)
            send_pair(s)
            return carry

        pl.when(g < last)(functools.partial(backward, count - 1))
        pl.when(g == 0)(functools.partial(send_patches, count - 1))
        lax.fori_loop(0, (count - 2) // 2, backward_pair, 0)
        leave(0, left_stage(middle, field, left_ref, 1))
        pl.when(g == 0)(functools.partial(send_patches, 0))

        @pl.when(g > 0)
        def _():
            def leave_piece(n):
                backward_piece(n, behind).start()

            right_stage(sums, flat, middle, right_ref, 1, leave_piece)
            for n in range(2):
                backward_piece(n, behind).wait_send()

            def send(t, carry):
                send_patches(count - 1 - t)
                return carry

            lax.fori_loop(0, count, send, 0)

    def patch_forward(n):
        from_x = (x + 1) % 4
        p = 2 * from_x + jnp.where(j == 1 - core, 0, 1)
        return remote(
            patch_relay.at[n], patches.at[p], patch_relay_send.at[n], s3_recv.at[p],
            (4 * g + 2 * n + 1, 4 * ((x + 3) % 4) + 2 * h + 1 - core),
        )

    @pl.when(jnp.logical_not(active))
    def _():
        for n in (1, 0):
            slot = patch_relay.at[n]
            remote(slot, slot, s3_send.at[0], patch_relay_recv.at[n], sibling).wait_recv()
            patch_forward(n).start()

    for i in (1, 0):
        group = 1 - i
        for kx in (0, 1, 3, 2):
            from_x = (x - kx + 4) % 4
            from_j = core if i == 0 else 3 - core
            p = 2 * from_x + i
            slot = patches.at[p]
            copy = remote(slot, slot, s3_send.at[0], s3_recv.at[p], sibling)
            if kx:
                copy.wait_recv()
            else:
                pl.when(from_j != j)(copy.wait_recv)
            at = (4 - kx) % 4
            wide[at * side : (at + 1) * side, :] = dot(slot[...], put_columns[4 * group + at]).astype(BF16)
        if group == 0:
            for m in range(2):
                total[m] = dot(put_rows[m, 0], wide[...])
    partial[...] = (total[0] + dot(put_rows[0, 1], wide[...])).reshape(partial.shape).astype(BF16)
    chip_copy = remote(partial, sibling_sum, back_send.at[0], back_recv.at[0], sibling)
    chip_copy.start()
    own_rows = (total[1] + dot(put_rows[1, 1], wide[...])).reshape(partial.shape)
    chip_copy.wait_recv()
    reduced[...] = (own_rows + sibling_sum[...].astype(F32)).astype(BF16)
    for k in (4, 3, 5, 2, 6, 1, 7):
        to = (xy + k) % 8
        remote(reduced.at[to], arrived.at[4 * h + x], s4_send.at[k], s4_recv.at[k], (d, 2 * to + core)).start()
    kept = pltpu.make_async_copy(reduced.at[xy], arrived.at[4 * h + x], load_sem.at[6])
    kept.start()
    for k in range(1, 8):
        come = (xy - k + 8) % 8
        slot = arrived.at[4 * (come % 2) + come // 2]
        remote(slot, slot, s4_send.at[k], s4_recv.at[k], sibling).wait_recv()

    kept.wait()

    for k in range(1, 8):
        slot = reduced.at[0]
        remote(slot, slot, s1_send.at[k], s1_recv.at[k], sibling).wait_send()
        remote(slot, slot, s4_send.at[k], s4_recv.at[k], sibling).wait_send()
    for k in range(1, 4):
        remote(own_offsets, own_offsets, off_send.at[k], off_recv.at[k], sibling).wait_send()
    for k in range(8):
        slot = reduced.at[0]
        remote(slot, slot, chip_send.at[k], chip_recv.at[k], sibling).wait_send()
    chip_copy.wait_send()
    for i in range(2):
        for k in range(4):
            slot = 2 * k + i
            to_j, device = target(k, i)
            copy = remote(stage.at[slot], home, s2_send.at[slot], s2_recv.at[0], device)
            if k:
                copy.wait_send()
            else:
                pl.when(to_j != j)(copy.wait_send)

    @pl.when(core == 1)
    def _():
        for i in range(2):
            crop_forward(i).wait_send()

    @pl.when(jnp.logical_not(active))
    def _():
        for n in range(2):
            patch_forward(n).wait_send()

    @pl.when(active)
    def _():
        @pl.when(g < last)
        def _():
            for n in range(2):
                for copy in forward_pieces(n):
                    copy.wait_send()

        for s in range(count):
            for c in range(2):
                to_x, to_j = owner(s, c)
                slot = grads.at[s, c]
                copy = remote(slot, slot, s3_send.at[2 * s + c], s3_recv.at[0], sibling)
                pl.when(jnp.logical_or(to_x != x, to_j != j))(copy.wait_send)


def sum_kernel(arrived, out_ref):
    planes = out_ref.shape[0]
    for plane in range(planes):
        for r in strips(out_ref.shape[1]):
            rows = pl.ds(r, STRIP)
            out_ref[plane, rows, :] = arrived[plane, rows, :].astype(F32) + arrived[planes + plane, rows, :].astype(F32)


def per_device(transmission, probe, offsets, measured):
    layers, _, rows, win = transmission.shape
    side = probe.shape[-1]
    group = 4 * layers
    rights, lefts, transforms = tables(side)
    dma = pltpu.SemaphoreType.DMA
    hbm = pl.BlockSpec(memory_space=pl.ANY)
    smem = pl.BlockSpec(memory_space=pltpu.SMEM)
    arrived = pl.pallas_call(
        kernel,
        out_shape=jax.ShapeDtypeStruct((8, rows, win), BF16),
        in_specs=[smem, hbm, hbm, hbm, hbm, hbm, hbm],
        out_specs=hbm,
        scratch_shapes=[
            pltpu.VMEM((8, 128), jnp.int32),
            pltpu.VMEM((4, 8, 128), jnp.int32),
            pltpu.VMEM((8, 2, rows, win), BF16),
            pltpu.VMEM((8, side, win), BF16),
            pltpu.VMEM((8, win, side), BF16),
            pltpu.VMEM((8, side, side), BF16),
            pltpu.VMEM((group, 2, side, side), BF16),
            pltpu.VMEM((group + 1, 2, side, side), BF16),
            pltpu.VMEM((2, side, side), BF16),
            pltpu.VMEM((2, side, side), BF16),
            pltpu.VMEM((2, side, side), BF16),
            pltpu.VMEM((2, 2 * side, side), F32),
            pltpu.VMEM((group, 2, side, side), BF16),
            pltpu.VMEM((side, side), F32),
            pltpu.VMEM(rights.shape, BF16),
            pltpu.VMEM(lefts.shape, BF16),
            pltpu.VMEM(transforms.shape, BF16),
            pltpu.VMEM((8, side, side), BF16),
            pltpu.VMEM((8, side, win), BF16),
            pltpu.VMEM((2, 2, win // 2, 4 * side), BF16),
            pltpu.VMEM((4 * side, win), BF16),
            pltpu.VMEM((2, win // 2, win), F32),
            pltpu.VMEM((8, rows, win), BF16),
            pltpu.VMEM((8, rows, win), BF16),
            pltpu.VMEM((8, rows, win), BF16),
            pltpu.VMEM((2, side, side), BF16),
            pltpu.VMEM((2, side, side), BF16),
            dma((2,)), dma((2,)), dma((2,)), dma((2,)),
            dma((7,)), dma((8,)), dma((8,)), dma((4,)), dma((4,)), dma((8,)), dma((8,)), dma((8,)),
            dma((16,)), dma((6,)), dma((6,)), dma((16,)), dma((8,)), dma((1,)), dma((1,)), dma((8,)), dma((8,)),
        ],
        compiler_params=pltpu.CompilerParams(
            collective_id=0, has_side_effects=True, vmem_limit_bytes=VMEM_LIMIT
        ),
        name="ptychography_backward",
    )(
        offsets, transmission, probe, measured,
        jnp.asarray(rights), jnp.asarray(lefts), jnp.asarray(transforms),
    )
    gradient = pl.pallas_call(
        sum_kernel,
        out_shape=jax.ShapeDtypeStruct((2 * layers, rows, win), F32),
        in_specs=[vmem()],
        out_specs=vmem(),
        name="sum_halves",
    )(arrived)
    return gradient.reshape(layers, 2, rows, win)


def solution(mesh):
    in_specs = (P("depth", None, "pos", None), P(), P("pos", None), P("pos", None, None))
    out_specs = P("depth", None, "pos", None)
    return jax.shard_map(
        per_device, mesh=mesh, in_specs=in_specs, out_specs=out_specs, check_vma=False
    )
```

```python
import functools
import math

import jax
import jax.numpy as jnp
import ml_dtypes
import numpy as np
from jax import lax
from jax.experimental import pallas as pl
from jax.experimental.pallas import tpu as pltpu
from jax.sharding import PartitionSpec as P


MESH = pl.DeviceIdType.MESH
F32 = jnp.float32
BF16 = jnp.bfloat16
VMEM_LIMIT = 56 * 1024 * 1024


def vmem():
    return pl.BlockSpec(memory_space=pltpu.VMEM)


def place():
    d = lax.axis_index("depth")
    q = lax.axis_index("pos")
    return d // 4, d % 4, q // 4, (q // 2) % 2, q % 2


def hi_lo(table, axis):
    high = table.astype(ml_dtypes.bfloat16)
    low = (table - high.astype(np.float64)).astype(ml_dtypes.bfloat16)
    return np.concatenate([high, low], axis)


def right_form(matrix):
    return np.block([[matrix.real, matrix.imag], [-matrix.imag, matrix.real]])


@functools.lru_cache(maxsize=None)
def tables(side):
    half = side // 2
    grid = np.arange(side)
    fourier = np.exp(-2j * np.pi * (np.outer(grid, grid) % side) / side) / math.sqrt(side)
    frequency = (grid + half) % side - half
    phase = np.exp(-1j * math.pi * frequency.astype(np.float64) ** 2 / 1024.0)
    circulant = fourier.conj() @ (phase[:, None] * fourier)
    near, far = circulant[:half, :half], circulant[:half, half:]
    forms = [right_form((near + far) / 2), right_form((near - far) / 2)]
    rights = np.stack([[hi_lo(m, 0) for m in forms], [hi_lo(m.T, 0) for m in forms]])
    order = grid.reshape(2, half // STRIP, STRIP).transpose(1, 0, 2).reshape(side)
    strided = [m[order][:, order] for m in forms]

    def strip_pairs(table):
        parts = hi_lo(table, 0).reshape(2, side // STRIP, STRIP, side)
        return parts.transpose(1, 0, 2, 3).reshape(2 * side, side)

    lefts = np.stack([[strip_pairs(m.T) for m in strided], [strip_pairs(m) for m in strided]])
    transforms = np.stack([hi_lo(m, 0) for m in (fourier.real, fourier.imag, -fourier.imag)])
    return rights, lefts, transforms.reshape(3, 2, side, side)


def dot(a, b):
    return jnp.dot(a, b, preferred_element_type=F32)


def cat(parts, axis):
    return jnp.concatenate(parts, axis)


STRIP = 16
BLOCKS = 2


def strips(count):
    return range(0, count, STRIP)


def halves(value):
    middle = value.shape[1] // 2
    return value[:, :middle], value[:, middle:]


def put_sums(ref, at, real, imag):
    (a, b), (c, d) = halves(real), halves(imag)
    ref[0, pl.ds(at, STRIP), :] = cat([a + b, c + d], 1).astype(BF16)
    ref[1, pl.ds(at, STRIP), :] = cat([a - b, c - d], 1).astype(BF16)


def sums_row(row, side):
    half = side // 2
    return 2 * row if row < half else 2 * (row - half) + STRIP


def right_stage(sums, flat, middle, right_ref, way, done=lambda n: None):
    side = sums.shape[1]
    block = side // BLOCKS
    for n in range(BLOCKS):
        for m in range(2):
            x = sums[m, pl.ds(n * block, block), :]
            flat[m, pl.ds(n * block, block), :] = dot(cat([x, x], 1), right_ref[way, m])
        for r in range(n * block, (n + 1) * block, 2 * STRIP):
            s, t = flat[0, pl.ds(r, STRIP), :], flat[0, pl.ds(r + STRIP, STRIP), :]
            d, e = flat[1, pl.ds(r, STRIP), :], flat[1, pl.ds(r + STRIP, STRIP), :]
            for m, (a, b) in enumerate(((s + t, d + e), (s - t, d - e))):
                (a_real, a_imag), (b_real, b_imag) = halves(a), halves(b)
                middle[m, pl.ds(r, STRIP), :] = cat([a_real, b_real], 1).astype(BF16)
                middle[m, pl.ds(r + STRIP, STRIP), :] = cat([a_imag, b_imag], 1).astype(BF16)
        done(n)


def left_stage(middle, field, left_ref, way):
    side = middle.shape[1]
    block = side // BLOCKS

    def total(m, r):
        return field[m, pl.ds(2 * r, STRIP), :] + field[m, pl.ds(2 * r + STRIP, STRIP), :]

    for n in range(BLOCKS):
        rows = pl.ds(2 * n * block, 2 * block)
        for m in range(2):
            field[m, rows, :] = dot(left_ref[way, m, rows, :], middle[m])
        for r in range(n * block, (n + 1) * block, 2 * STRIP):
            p, u = total(0, r), total(0, r + STRIP)
            m, v = total(1, r), total(1, r + STRIP)
            for at, real, imag in ((r // 2, p + m, u + v), (side // 2 + r // 2, p - m, u - v)):
                (a, b), (c, d) = halves(real), halves(imag)
                yield at, cat([a + b, a - b], 1), cat([c + d, c - d], 1)


def strip(ref, s, c, at):
    return ref[s, c, pl.ds(at, STRIP), :].astype(F32)


def fourier_right(real, imag, f, inverse):
    r, i, n = f
    up, down = (n, i) if inverse else (i, n)
    x = cat([real, real, imag, imag], 1)
    a = dot(x, cat([r[0], r[1], down[0], down[1]], 0))
    b = dot(x, cat([up[0], up[1], r[0], r[1]], 0))
    return a, b


def fourier_left(real, imag, f, inverse):
    r, i, n = f
    up, down = (n, i) if inverse else (i, n)
    x = cat([real, real, imag, imag], 0)
    a = dot(cat([r[0], r[1], down[0], down[1]], 1), x)
    b = dot(cat([up[0], up[1], r[0], r[1]], 1), x)
    return a, b


def neighbours(g, j, x, h, core):
    d = 4 * g + j
    xy = 2 * x + h
    partners = [(d, 4 * x + 2 * h + 1 - core)]
    for k in range(1, 8):
        partners.append((d, 2 * ((xy + k) % 8) + core))
    for kx in range(4):
        for kj in range(1, 4):
            partners.append((4 * g + (j + kj) % 4, 4 * ((x + kx) % 4) + 2 * h + core))
    return partners


def remote(src, dst, send, recv, device):
    return pltpu.make_async_remote_copy(
        src_ref=src, dst_ref=dst, send_sem=send, recv_sem=recv, device_id=device, device_id_type=MESH
    )


def one_hot(mask):
    return jnp.where(mask, 1.0, 0.0).astype(BF16)


def shifts(columns):
    return lax.broadcasted_iota(jnp.int32, (STRIP, columns), 1) - lax.broadcasted_iota(
        jnp.int32, (STRIP, columns), 0
    )


def fill_rows(ref, offset):
    rows, columns = ref.shape
    lanes = cat([offset] * (columns // 128), 1)
    base = shifts(columns)
    for r in strips(rows):
        ref[pl.ds(r, STRIP), :] = one_hot(base == lanes + r)


def fill_columns(ref, offset, row_of=lambda r: r):
    rows, columns = ref.shape
    lanes = cat([offset] * (columns // 128), 1)
    base = shifts(columns)
    for r in strips(rows):
        ref[pl.ds(r, STRIP), :] = one_hot(base == row_of(r) - lanes)


def kernel(
    off_ref, t_hbm, probe_hbm, measured_hbm, right_hbm, left_hbm, transform_hbm, arrived,
    own_offsets, offs, plane, pick_rows, pick_columns, stage, o_ref, stored, sums, flat, middle, field, grads, measured_ref, right_ref, left_ref,
    transform_ref, patches, put_columns, put_rows, wide, total, partial, sibling_sum, reduced,
    crop_relay, patch_relay, crop_relay_send, crop_relay_recv, patch_relay_send, patch_relay_recv,
    load_sem, s1_send, s1_recv, off_send, off_recv, chip_send, chip_recv, s2_send, s2_recv,
    hop_send, hop_recv, s3_send, s3_recv, back_send, back_recv, s4_send, s4_recv,
):
    g, j, x, h, core = place()
    d = 4 * g + j
    q = 4 * x + 2 * h + core
    xy = 2 * x + h
    last = 3
    sibling = (d, 4 * x + 2 * h + 1 - core)
    win = plane.shape[-1]
    side = o_ref.shape[-1]
    half = side // 2
    count = o_ref.shape[0]
    block = plane.shape[2]
    active = jnp.logical_or(j == core, j == 3 - core)
    mine = jnp.where(j == core, 0, 1)
    ahead = (jnp.minimum(d + 4, 15), q)
    behind = (jnp.maximum(d - 4, 0), q)

    loads = [
        pltpu.make_async_copy(right_hbm, right_ref, load_sem.at[0]),
        pltpu.make_async_copy(left_hbm, left_ref, load_sem.at[1]),
        pltpu.make_async_copy(transform_hbm, transform_ref, load_sem.at[2]),
        pltpu.make_async_copy(measured_hbm.at[mine], measured_ref, load_sem.at[3]),
    ]
    load_probe = pltpu.make_async_copy(probe_hbm, stored.at[0], load_sem.at[4])
    barrier = pltpu.get_barrier_semaphore()
    partners = neighbours(g, j, x, h, core)
    relayed = [(4 * g + (j + k) % 4, 4 * ((x + 1) % 4) + 2 * h + 1 - core) for k in range(4)]
    for partner in partners + relayed:
        pl.semaphore_signal(barrier, inc=1, device_id=partner, device_id_type=MESH)

    @pl.when(jnp.logical_and(active, g < last))
    def _():
        pl.semaphore_signal(barrier, inc=1, device_id=ahead, device_id_type=MESH)

    @pl.when(jnp.logical_and(active, g > 0))
    def _():
        pl.semaphore_signal(barrier, inc=1, device_id=behind, device_id_type=MESH)

    chained = jnp.where(active, jnp.where(jnp.logical_or(g == 0, g == last), 1, 2), 0)
    for load in loads:
        load.start()
    pl.when(g == 0)(load_probe.start)
    for k in range(4):
        own_offsets[k : k + 1, :] = jnp.full((1, 128), off_ref[k // 2, k % 2], jnp.int32)
        own_offsets[k + 4 : k + 5, :] = jnp.zeros((1, 128), jnp.int32)
    pl.semaphore_wait(barrier, len(partners) + len(relayed) + chained)

    for k in range(1, 4):
        to = (x + k) % 4
        remote(
            own_offsets, offs.at[x], off_send.at[k], off_recv.at[k], (d, 4 * to + 2 * h + core)
        ).start()
    for k in (4, 3, 5, 2, 6, 1, 7):
        to = (xy + k) % 8
        tx = to // 2
        remote(
            t_hbm.at[tx // 2, tx % 2], plane.at[xy, core], s1_send.at[k], s1_recv.at[k], (d, 2 * to + core)
        ).start()
    own = t_hbm.at[x // 2, x % 2]
    remote(own, plane.at[xy, core], chip_send.at[0], chip_recv.at[0], sibling).start()
    own_copy = pltpu.make_async_copy(own, plane.at[xy, core], load_sem.at[5])
    own_copy.start()
    offs[x] = own_offsets[...]

    for i in (1, 0):
        for k in (0, 3, 2, 1):
            from_x = (x - k + 4) % 4
            if k and i:
                slot = offs.at[from_x]
                remote(slot, slot, off_send.at[k], off_recv.at[k], sibling).wait_recv()
            slot = 2 * ((4 - k) % 4) + i
            fill_rows(pick_rows.at[slot], offs[from_x, 2 * i : 2 * i + 1, :])
            fill_columns(pick_columns.at[slot], offs[from_x, 2 * i + 1 : 2 * i + 2, :])

    for k in (1, 7, 2, 6, 3, 5, 4):
        rows = plane.at[(xy - k + 8) % 8, core]
        remote(rows, rows, s1_send.at[k], s1_recv.at[k], sibling).wait_recv()
        remote(rows, rows, chip_send.at[k], chip_recv.at[k], sibling).start()
    for k in range(8):
        rows = plane.at[(xy - k + 8) % 8, 1 - core]
        remote(rows, rows, chip_send.at[k], chip_recv.at[k], sibling).wait_recv()

    own_copy.wait()

    def target(k, i):
        to_j = core if i == 0 else 3 - core
        return to_j, (4 * g + to_j, 4 * ((x + k) % 4) + 2 * h + core)

    own_plane = 2 * j + x // 2
    home = o_ref.at[own_plane, x % 2]
    for i in (1, 0):
        for k in (2, 1, 3, 0):
            slot = 2 * k + i
            rows = dot(pick_rows[slot], plane[...].reshape(win, win)).astype(BF16)
            stage[slot] = dot(rows, pick_columns[slot]).astype(BF16)
            to_j, device = target(k, i)
            copy = remote(
                stage.at[slot], home, s2_send.at[slot], s2_recv.at[2 * own_plane + x % 2], device
            )
            if k == 2 and i == 1:
                remote(
                    stage.at[slot], crop_relay, s2_send.at[slot], crop_relay_recv.at[0],
                    (d, 4 * ((x + 3) % 4) + 2 * h + core),
                ).start()
            elif k:
                copy.start()
            else:
                pl.when(to_j != j)(copy.start)

                @pl.when(to_j == j)
                def _():
                    o_ref[own_plane, x % 2] = stage[slot]

    from_plane = 2 * j + (x + 1) % 4 // 2
    crop_forward = remote(
        crop_relay, o_ref.at[from_plane, (x + 1) % 2], crop_relay_send.at[0],
        s2_recv.at[2 * from_plane + (x + 1) % 2], (4 * g + 3 - core, 4 * ((x + 3) % 4) + 2 * h + core),
    )
    remote(crop_relay, crop_relay, s2_send.at[0], crop_relay_recv.at[0], sibling).wait_recv()
    crop_forward.start()

    for load in loads:
        load.wait()
    pl.when(g == 0)(load_probe.wait)
    half = side // 2
    piece = half // 2

    def forward_pieces(n):
        rows = [pl.ds(m * half + n * piece, piece) for m in range(2)]
        return [
            remote(
                stored.at[count, :, rows[m]], stored.at[0, :, rows[m]],
                hop_send.at[2 * n + m], hop_recv.at[2 * n + m], ahead,
            )
            for m in range(2)
        ]

    def backward_piece(n, device):
        rows = middle.at[:, pl.ds(n * half, half)]
        return remote(rows, rows, hop_send.at[4 + n], hop_recv.at[4 + n], device)

    def owner(s, c):
        return 2 * (s % 2) + c, s // 2

    def make_put_tables():
        for i in range(2):
            for k in range(4):
                at = 4 * (1 - i) + k
                from_x = (x + k) % 4
                fill_rows(put_columns.at[at], offs[from_x, 2 * i + 1 : 2 * i + 2, :])
                for m in range(2):
                    first = 1 - core if m == 0 else core
                    fill_columns(
                        put_rows.at[m, 1 - i, :, k * side : (k + 1) * side],
                        offs[from_x, 2 * i : 2 * i + 1, :],
                        lambda r: r + (r // block + first) * block,
                    )

    starts = jnp.logical_and(active, g == 0)
    pl.when(jnp.logical_not(starts))(make_put_tables)

    @pl.when(active)
    def _():
        def wait_crop(s):
            for c in range(2):
                from_x, from_j = owner(s, c)
                slot = o_ref.at[s, c]
                copy = remote(slot, slot, s2_send.at[0], s2_recv.at[2 * s + c], sibling)
                pl.when(jnp.logical_or(from_x != x, from_j != j))(copy.wait_recv)

        def enter(s, at, real, imag):
            o_real, o_imag = strip(o_ref, s, 0, at), strip(o_ref, s, 1, at)
            put_sums(
                sums, sums_row(at, side), o_real * real - o_imag * imag, o_real * imag + o_imag * real
            )

        def keep_wave(s, at, real, imag):
            stored[s, 0, pl.ds(at, STRIP), :] = real.astype(BF16)
            stored[s, 1, pl.ds(at, STRIP), :] = imag.astype(BF16)

        def forward(s, carry):
            wait_crop(s + 1)
            for at, real, imag in left_stage(middle, field, left_ref, 0):
                keep_wave(s + 1, at, real, imag)
                enter(s + 1, at, real, imag)
            right_stage(sums, flat, middle, right_ref, 0)
            return carry

        wait_crop(0)
        for n in range(2):

            @pl.when(g > 0)
            def _():
                for copy in forward_pieces(n):
                    copy.wait_recv()

            for m in range(2):
                for r in strips(piece):
                    at = m * half + n * piece + r
                    enter(0, at, strip(stored, 0, 0, at), strip(stored, 0, 1, at))
        right_stage(sums, flat, middle, right_ref, 0)
        def forward_pair(n, carry):
            forward(2 * n, carry)
            return forward(2 * n + 1, carry)

        lax.fori_loop(0, (count - 2) // 2, forward_pair, 0)

        @pl.when(g < last)
        def _():
            forward(count - 2, 0)
            for at, real, imag in left_stage(middle, field, left_ref, 0):
                keep_wave(count, at, real, imag)
                if at >= half and (at + STRIP) % piece == 0:
                    for copy in forward_pieces((at - half) // piece):
                        copy.start()
            pl.when(g == 0)(make_put_tables)
            for n in range(2):
                backward_piece(n, ahead).wait_recv()

        def leave(s, field_strips):
            for at, real, imag in field_strips:
                real, imag = real.astype(BF16), imag.astype(BF16)
                o_real, o_imag = o_ref[s, 0, pl.ds(at, STRIP), :], o_ref[s, 1, pl.ds(at, STRIP), :]
                put_sums(
                    sums, sums_row(at, side), o_real * real + o_imag * imag, o_real * imag - o_imag * real
                )
                p_real, p_imag = stored[s, 0, pl.ds(at, STRIP), :], stored[s, 1, pl.ds(at, STRIP), :]
                grads[s, 0, pl.ds(at, STRIP), :] = p_real * real + p_imag * imag
                grads[s, 1, pl.ds(at, STRIP), :] = p_real * imag - p_imag * real

        @pl.when(g == last)
        def _():
            final = count - 1
            leaving, turned = grads.at[0], grads.at[1]
            f = [(transform_ref[m, 0], transform_ref[m, 1]) for m in range(3)]

            def flat_strip(m, at):
                return flat[m, pl.ds(at, STRIP), :]

            def transformed(source, inverse):
                turned[0], turned[1] = (v.astype(BF16) for v in fourier_right(source[0], source[1], f, inverse))
                flat[0], flat[1] = fourier_left(turned[0], turned[1], f, inverse)

            wait_crop(final)
            for at, real, imag in left_stage(middle, field, left_ref, 0):
                keep_wave(final, at, real, imag)
                o_real, o_imag = strip(o_ref, final, 0, at), strip(o_ref, final, 1, at)
                leaving[0, pl.ds(at, STRIP), :] = (o_real * real - o_imag * imag).astype(BF16)
                leaving[1, pl.ds(at, STRIP), :] = (o_real * imag + o_imag * real).astype(BF16)
            transformed(leaving, False)
            for at in strips(side):
                real, imag = flat_strip(0, at), flat_strip(1, at)
                weight = real * real + imag * imag - measured_ref[pl.ds(at, STRIP), :]
                sums[0, pl.ds(at, STRIP), :] = (real * weight).astype(BF16)
                sums[1, pl.ds(at, STRIP), :] = (imag * weight).astype(BF16)
            transformed(sums, True)
            leave(final, ((at, flat_strip(0, at), flat_strip(1, at)) for at in strips(side)))
            right_stage(sums, flat, middle, right_ref, 1)

        def send_patches(s):
            for c in range(2):
                to_x, to_j = owner(s, c)
                source, send = grads.at[s, c], s3_send.at[2 * s + c]
                away = jnp.logical_or(to_x != x, to_j != j)
                detour = jnp.logical_and(to_x == (x + 2) % 4, to_j % 2 == 1)
                copy = remote(
                    source, patches.at[2 * x + mine], send, s3_recv.at[2 * x + mine],
                    (4 * g + to_j, 4 * to_x + 2 * h + core),
                )
                pl.when(jnp.logical_and(away, jnp.logical_not(detour)))(copy.start)
                pl.when(detour)(
                    remote(
                        source, patch_relay.at[to_j // 2], send, patch_relay_recv.at[to_j // 2],
                        (d, 4 * ((x + 3) % 4) + 2 * h + 1 - core),
                    ).start
                )

                @pl.when(jnp.logical_not(away))
                def _():
                    patches[2 * x + mine] = grads[s, c]

        def backward(s):
            leave(s, left_stage(middle, field, left_ref, 1))
            right_stage(sums, flat, middle, right_ref, 1)

        def send_pair(s):
            pl.when(g == 0)(functools.partial(send_patches, s))
            pl.when(g == 0)(functools.partial(send_patches, s - 1))

        def backward_pair(t, carry):
            s = count - 2 - 2 * t
            backward(s)
            backward(s - 1)
            send_pair(s)
            return carry

        pl.when(g < last)(functools.partial(backward, count - 1))
        pl.when(g == 0)(functools.partial(send_patches, count - 1))
        lax.fori_loop(0, (count - 2) // 2, backward_pair, 0)
        leave(0, left_stage(middle, field, left_ref, 1))
        pl.when(g == 0)(functools.partial(send_patches, 0))

        @pl.when(g > 0)
        def _():
            def leave_piece(n):
                backward_piece(n, behind).start()

            right_stage(sums, flat, middle, right_ref, 1, leave_piece)
            for n in range(2):
                backward_piece(n, behind).wait_send()

            def send(t, carry):
                send_patches(count - 1 - t)
                return carry

            lax.fori_loop(0, count, send, 0)

    def patch_forward(n):
        from_x = (x + 1) % 4
        p = 2 * from_x + jnp.where(j == 1 - core, 0, 1)
        return remote(
            patch_relay.at[n], patches.at[p], patch_relay_send.at[n], s3_recv.at[p],
            (4 * g + 2 * n + 1, 4 * ((x + 3) % 4) + 2 * h + 1 - core),
        )

    @pl.when(jnp.logical_not(active))
    def _():
        for n in (1, 0):
            slot = patch_relay.at[n]
            remote(slot, slot, s3_send.at[0], patch_relay_recv.at[n], sibling).wait_recv()
            patch_forward(n).start()

    for i in (1, 0):
        group = 1 - i
        for kx in (0, 1, 3, 2):
            from_x = (x - kx + 4) % 4
            from_j = core if i == 0 else 3 - core
            p = 2 * from_x + i
            slot = patches.at[p]
            copy = remote(slot, slot, s3_send.at[0], s3_recv.at[p], sibling)
            if kx:
                copy.wait_recv()
            else:
                pl.when(from_j != j)(copy.wait_recv)
            at = (4 - kx) % 4
            wide[at * side : (at + 1) * side, :] = dot(slot[...], put_columns[4 * group + at]).astype(BF16)
        if group == 0:
            for m in range(2):
                total[m] = dot(put_rows[m, 0], wide[...])
    partial[...] = (total[0] + dot(put_rows[0, 1], wide[...])).reshape(partial.shape).astype(BF16)
    chip_copy = remote(partial, sibling_sum, back_send.at[0], back_recv.at[0], sibling)
    chip_copy.start()
    own_rows = (total[1] + dot(put_rows[1, 1], wide[...])).reshape(partial.shape)
    chip_copy.wait_recv()
    reduced[...] = (own_rows + sibling_sum[...].astype(F32)).astype(BF16)
    for k in (4, 3, 5, 2, 6, 1, 7):
        to = (xy + k) % 8
        remote(reduced.at[to], arrived.at[4 * h + x], s4_send.at[k], s4_recv.at[k], (d, 2 * to + core)).start()
    kept = pltpu.make_async_copy(reduced.at[xy], arrived.at[4 * h + x], load_sem.at[6])
    kept.start()
    for k in range(1, 8):
        come = (xy - k + 8) % 8
        slot = arrived.at[4 * (come % 2) + come // 2]
        remote(slot, slot, s4_send.at[k], s4_recv.at[k], sibling).wait_recv()

    kept.wait()

    for k in range(1, 8):
        slot = reduced.at[0]
        remote(slot, slot, s1_send.at[k], s1_recv.at[k], sibling).wait_send()
        remote(slot, slot, s4_send.at[k], s4_recv.at[k], sibling).wait_send()
    for k in range(1, 4):
        remote(own_offsets, own_offsets, off_send.at[k], off_recv.at[k], sibling).wait_send()
    for k in range(8):
        slot = reduced.at[0]
        remote(slot, slot, chip_send.at[k], chip_recv.at[k], sibling).wait_send()
    chip_copy.wait_send()
    for i in range(2):
        for k in range(4):
            slot = 2 * k + i
            to_j, device = target(k, i)
            copy = remote(stage.at[slot], home, s2_send.at[slot], s2_recv.at[0], device)
            if k:
                copy.wait_send()
            else:
                pl.when(to_j != j)(copy.wait_send)

    crop_forward.wait_send()

    @pl.when(jnp.logical_not(active))
    def _():
        for n in range(2):
            patch_forward(n).wait_send()

    @pl.when(active)
    def _():
        @pl.when(g < last)
        def _():
            for n in range(2):
                for copy in forward_pieces(n):
                    copy.wait_send()

        for s in range(count):
            for c in range(2):
                to_x, to_j = owner(s, c)
                slot = grads.at[s, c]
                copy = remote(slot, slot, s3_send.at[2 * s + c], s3_recv.at[0], sibling)
                pl.when(jnp.logical_or(to_x != x, to_j != j))(copy.wait_send)


def sum_kernel(arrived, out_ref):
    planes = out_ref.shape[0]
    for plane in range(planes):
        for r in strips(out_ref.shape[1]):
            rows = pl.ds(r, STRIP)
            out_ref[plane, rows, :] = arrived[plane, rows, :].astype(F32) + arrived[planes + plane, rows, :].astype(F32)


def per_device(transmission, probe, offsets, measured):
    layers, _, rows, win = transmission.shape
    side = probe.shape[-1]
    group = 4 * layers
    rights, lefts, transforms = tables(side)
    dma = pltpu.SemaphoreType.DMA
    hbm = pl.BlockSpec(memory_space=pl.ANY)
    smem = pl.BlockSpec(memory_space=pltpu.SMEM)
    arrived = pl.pallas_call(
        kernel,
        out_shape=jax.ShapeDtypeStruct((8, rows, win), BF16),
        in_specs=[smem, hbm, hbm, hbm, hbm, hbm, hbm],
        out_specs=hbm,
        scratch_shapes=[
            pltpu.VMEM((8, 128), jnp.int32),
            pltpu.VMEM((4, 8, 128), jnp.int32),
            pltpu.VMEM((8, 2, rows, win), BF16),
            pltpu.VMEM((8, side, win), BF16),
            pltpu.VMEM((8, win, side), BF16),
            pltpu.VMEM((8, side, side), BF16),
            pltpu.VMEM((group, 2, side, side), BF16),
            pltpu.VMEM((group + 1, 2, side, side), BF16),
            pltpu.VMEM((2, side, side), BF16),
            pltpu.VMEM((2, side, side), F32),
            pltpu.VMEM((2, side, side), BF16),
            pltpu.VMEM((2, 2 * side, side), F32),
            pltpu.VMEM((group, 2, side, side), BF16),
            pltpu.VMEM((side, side), F32),
            pltpu.VMEM(rights.shape, BF16),
            pltpu.VMEM(lefts.shape, BF16),
            pltpu.VMEM(transforms.shape, BF16),
            pltpu.VMEM((8, side, side), BF16),
            pltpu.VMEM((8, side, win), BF16),
            pltpu.VMEM((2, 2, win // 2, 4 * side), BF16),
            pltpu.VMEM((4 * side, win), BF16),
            pltpu.VMEM((2, win // 2, win), F32),
            pltpu.VMEM((8, rows, win), BF16),
            pltpu.VMEM((8, rows, win), BF16),
            pltpu.VMEM((8, rows, win), BF16),
            pltpu.VMEM((side, side), BF16),
            pltpu.VMEM((2, side, side), BF16),
            dma((1,)), dma((1,)), dma((2,)), dma((2,)),
            dma((7,)), dma((8,)), dma((8,)), dma((4,)), dma((4,)), dma((8,)), dma((8,)), dma((8,)),
            dma((16,)), dma((6,)), dma((6,)), dma((16,)), dma((8,)), dma((1,)), dma((1,)), dma((8,)), dma((8,)),
        ],
        compiler_params=pltpu.CompilerParams(
            collective_id=0, has_side_effects=True, vmem_limit_bytes=VMEM_LIMIT
        ),
        name="ptychography_backward",
    )(
        offsets, transmission, probe, measured,
        jnp.asarray(rights), jnp.asarray(lefts), jnp.asarray(transforms),
    )
    gradient = pl.pallas_call(
        sum_kernel,
        out_shape=jax.ShapeDtypeStruct((2 * layers, rows, win), F32),
        in_specs=[vmem()],
        out_specs=vmem(),
        name="sum_halves",
    )(arrived)
    return gradient.reshape(layers, 2, rows, win)


def solution(mesh):
    in_specs = (P("depth", None, "pos", None), P(), P("pos", None), P("pos", None, None))
    out_specs = P("depth", None, "pos", None)
    return jax.shard_map(
        per_device, mesh=mesh, in_specs=in_specs, out_specs=out_specs, check_vma=False
    )
```
